32 devices in a mesh: crops: 16 (over z, y, x), rows: 2 (over core).
Axes of the slice: x: 2, y: 2, z: 4, core: 2. Of those that a mesh axis runs over, the one named last changes fastest.
Arguments:
- image_big: bfloat16 [192, 14, 14, 1024], P('crops', 'rows'), may hold values from -6 to 6
- image_small: bfloat16 [128, 10, 10, 1024], P('crops', 'rows'), may hold values from -6 to 6
- view_big: int32 [192], P('crops'), may hold values from 0 to 1, as said below
- view_small: int32 [128], P('crops'), may hold values from 0 to 1
- inner_first: bfloat16 [1024, 256], replicated, may hold values from -0.1875 to 0.1875
- spatial_first: bfloat16 [3, 3, 256, 256], replicated, may hold values from -0.125 to 0.125
- outer_first: bfloat16 [256, 1024], replicated, may hold values from -0.375 to 0.375
- norms_first: float32 [2, 1536], replicated, may hold values from 0.25 to 1.75
- inner_second: bfloat16 [1024, 512], replicated, may hold values from -0.1875 to 0.1875
- spatial_second: bfloat16 [3, 3, 512, 512], replicated, may hold values from -0.09375 to 0.09375
- outer_second: bfloat16 [512, 2048], replicated, may hold values from -0.25 to 0.25
- skip_second: bfloat16 [1024, 2048], replicated, may hold values from -0.1875 to 0.1875
- norms_second: float32 [2, 5120], replicated, may hold values from 0.25 to 1.75
- cotangent_big: bfloat16 [192, 7, 7, 2048], P(('crops', 'rows')), may hold values from -6 to 6
- cotangent_small: bfloat16 [128, 5, 5, 2048], P(('crops', 'rows')), may hold values from -6 to 6
Outputs:
- result_big: bfloat16 [192, 7, 7, 2048], P(('crops', 'rows'))
- result_small: bfloat16 [128, 5, 5, 2048], P(('crops', 'rows'))
- gradient_big: bfloat16 [192, 14, 14, 1024], P('crops', 'rows')
- gradient_small: bfloat16 [128, 10, 10, 1024], P('crops', 'rows')
- inner_first_grad: float32 [1024, 256], replicated
- spatial_first_grad: float32 [3, 3, 256, 256], replicated
- outer_first_grad: float32 [256, 1024], replicated
- norms_first_grad: float32 [2, 1536], replicated
- inner_second_grad: float32 [1024, 512], replicated
- spatial_second_grad: float32 [3, 3, 512, 512], replicated
- outer_second_grad: float32 [512, 2048], replicated
- skip_second_grad: float32 [1024, 2048], replicated
- norms_second_grad: float32 [2, 5120], replicated
The draws below stay inside these ranges and needn't reach their ends.
Inputs may be any that keep to these rules, and one draw needn't show every extreme that they name: `view_big`: the first larger crop is of view 0 and the second of view 1.
All inputs are finite; a program needn't handle non-finite values.
Results may differ from the reference program's by a relative error of at most 0.017.
Values may be sent and summed in bfloat16 or wider, within the bound.
A program may use at most 256 MiB of HBM per device.

```python
import jax
import jax.numpy as jnp
from jax import lax

CIN = 1024
MID3 = 256
MID4 = 512
COUT = 2048
LARGE_MAP_EDGE = 14
MINOR_MAP_EDGE = 10
NB = 192
NS = 128
NORM1 = 1536
NORM2 = 5120


def draw_view_big(key, part):
    key = jax.random.fold_in(key, 7)
    random_bits = jax.random.randint(key, (NB,), 0, 2)
    places = jnp.arange(NB)
    return jnp.where(places < 2, places, random_bits).astype(jnp.int32)


def place_ends(array, stream_key, least, largest):
    shape = array.shape
    place = [jax.random.randint(jax.random.fold_in(stream_key, axis), (), 0, shape[axis]) for axis in range(len(shape))]
    array = array.at[tuple(place)].set(least)
    longest = shape.index(max(shape))
    place[longest] = (place[longest] + 1) % shape[longest]
    return array.at[tuple(place)].set(largest)


def block_levels(key, extent, split, low, top_value):
    gain, own = 1.0, jax.random.fold_in(key, 6)
    for axis_at, parts in split:
        draws = jnp.exp(jax.random.uniform(jax.random.fold_in(own, axis_at), (parts,), jnp.float32, low / len(split), top_value / len(split)))
        gain = gain * jnp.repeat(draws, extent[axis_at] // parts).reshape([-1 if axis == axis_at else 1 for axis in range(len(extent))])
    return gain


def bell_draw(key, extent, scale, reach, split=(), dtype=jnp.bfloat16):
    drawn = jax.random.normal(key, extent, jnp.float32) * scale
    if len(split) > 0:
        drawn = block_levels(key, extent, split, -0.22, 0.18) * drawn
    return jnp.clip(drawn, min=-reach, max=reach).astype(dtype)


def setup_inputs(seed: int = 0) -> dict:
    arg_keys = jax.random.split(jax.random.key(seed), 16)
    image_big = bell_draw(arg_keys[0], (NB, LARGE_MAP_EDGE, LARGE_MAP_EDGE, CIN), 1.0, 6.0, ((0, 16), (1, 2)))
    image_small = bell_draw(arg_keys[1], (NS, MINOR_MAP_EDGE, MINOR_MAP_EDGE, CIN), 1.0, 6.0, ((0, 16), (1, 2)))
    view_big = draw_view_big(jax.random.fold_in(arg_keys[15], 71), 0)
    view_small = place_ends(jax.random.randint(arg_keys[3], (NS,), 0, 2), jax.random.fold_in(arg_keys[3], 1), 0, 1).astype(jnp.int32)
    inner_first = bell_draw(arg_keys[4], (CIN, MID3), CIN ** -0.5, 0.1875)
    spatial_first = bell_draw(arg_keys[5], (3, 3, MID3, MID3), (9 * MID3) ** -0.5, 0.125)
    outer_first = bell_draw(arg_keys[6], (MID3, CIN), MID3 ** -0.5, 0.375)
    norms_first = jnp.clip(1.0 + 0.15 * jax.random.normal(arg_keys[7], (2, NORM1), jnp.float32), 0.25, 1.75)
    inner_second = bell_draw(arg_keys[8], (CIN, MID4), CIN ** -0.5, 0.1875)
    spatial_second = bell_draw(arg_keys[9], (3, 3, MID4, MID4), (9 * MID4) ** -0.5, 0.09375)
    outer_second = bell_draw(arg_keys[10], (MID4, COUT), MID4 ** -0.5, 0.25)
    skip_second = bell_draw(arg_keys[11], (CIN, COUT), CIN ** -0.5, 0.1875)
    norms_second = jnp.clip(1.0 + 0.15 * jax.random.normal(arg_keys[12], (2, NORM2), jnp.float32), 0.25, 1.75)
    cotangent_big = bell_draw(arg_keys[13], (NB, LARGE_MAP_EDGE // 2, LARGE_MAP_EDGE // 2, COUT), 1.0, 6.0, ((0, 32),))
    cotangent_small = bell_draw(arg_keys[14], (NS, MINOR_MAP_EDGE // 2, MINOR_MAP_EDGE // 2, COUT), 1.0, 6.0, ((0, 32),))
    return {"image_big": image_big, "image_small": image_small, "view_big": view_big, "view_small": view_small, "inner_first": inner_first, "spatial_first": spatial_first, "outer_first": outer_first, "norms_first": norms_first, "inner_second": inner_second, "spatial_second": spatial_second, "outer_second": outer_second, "skip_second": skip_second, "norms_second": norms_second, "cotangent_big": cotangent_big, "cotangent_small": cotangent_small}


@jax.custom_vjp
def low(v):
    return lax.optimization_barrier(v.astype(jnp.bfloat16)).astype(jnp.float32)

@jax.custom_vjp
def low_back(v):
    return v

def low_keep(v):
    return (low(v), None)

def low_pass(kept, grad):
    return (grad,)

def back_keep(v):
    return (v, None)

def back_low(kept, grad):
    return (low(grad),)
low.defvjp(low_keep, low_pass)
low_back.defvjp(back_keep, back_low)
HIGH = lax.Precision.HIGHEST
EPS = 1e-05

def gelu_tanh(v):
    return jax.nn.gelu(v, approximate=True)

def project(tensor, weight):
    return jnp.einsum('nhwc,cd->nhwd', tensor, weight, precision=HIGH)

def convolve(tensor, kernel, stride):
    return lax.conv_general_dilated(tensor, kernel, (stride, stride), ((1, 1), (1, 1)), dimension_numbers=('NHWC', 'HWIO', 'NHWC'), precision=HIGH)

def view_sums(onehot, tensor):
    return jnp.einsum('vn,nc->vc', onehot, lax.optimization_barrier(jnp.sum(tensor, axis=(1, 2))), precision=HIGH)

def crop_table(onehot, table):
    return jnp.einsum('vn,vc->nc', onehot, table, precision=HIGH)[:, None, None, :]

def normalise_layer(crop_owner_table, crop_onehot_matrix, multiplier, start_position, stride_ratio):
    tallied_entries = (lax.optimization_barrier(jnp.sum(crop_onehot_matrix[0], 1)) * (LARGE_MAP_EDGE * LARGE_MAP_EDGE) + lax.optimization_barrier(jnp.sum(crop_onehot_matrix[1], 1)) * (MINOR_MAP_EDGE * MINOR_MAP_EDGE)) / stride_ratio
    per_view_totals = view_sums(crop_onehot_matrix[0], crop_owner_table[0]) + view_sums(crop_onehot_matrix[1], crop_owner_table[1])
    average = per_view_totals / tallied_entries[:, None]
    centered = [crop_owner_table[k] - crop_table(crop_onehot_matrix[k], average) for k in range(2)]
    squares = view_sums(crop_onehot_matrix[0], jnp.square(centered[0])) + view_sums(crop_onehot_matrix[1], jnp.square(centered[1]))
    inverse = lax.rsqrt(squares / tallied_entries[:, None] + EPS)
    return [multiplier * (centered[k] * crop_table(crop_onehot_matrix[k], inverse)) + start_position for k in range(2)]

def norm_pieces(norms, widths):
    pieces = []
    anchor = 0
    for breadth in widths:
        pieces.append((norms[0, anchor:anchor + breadth], norms[1, anchor:anchor + breadth]))
        anchor = anchor + breadth
    return pieces

def reference(image_big, image_small, view_big, view_small, inner_first, spatial_first, outer_first, norms_first, inner_second, spatial_second, outer_second, skip_second, norms_second, cotangent_big, cotangent_small):
    labels = jnp.arange(2)
    crop_onehot_matrix = [(view_big[None, :] == labels[:, None]).astype(jnp.float32), (view_small[None, :] == labels[:, None]).astype(jnp.float32)]

    def forward(picture_big, picture_small, squeeze, spatial, expand, normone, reduce_w, strided, widen_w, shortcut, normtwo):
        first_norms = norm_pieces(normone, (MID3, MID3, CIN))
        second_norms = norm_pieces(normtwo, (MID4, MID4, COUT, COUT))
        input_images = [picture_big, picture_small]
        linear = [low_back(project(tensor, squeeze)) for tensor in input_images]
        hidden = [low(gelu_tanh(tensor)) for tensor in normalise_layer(linear, crop_onehot_matrix, first_norms[0][0], first_norms[0][1], 1.0)]
        linear = [low_back(convolve(tensor, spatial, 1)) for tensor in hidden]
        hidden = [low(gelu_tanh(tensor)) for tensor in normalise_layer(linear, crop_onehot_matrix, first_norms[1][0], first_norms[1][1], 1.0)]
        linear = [low_back(project(tensor, expand)) for tensor in hidden]
        normed = normalise_layer(linear, crop_onehot_matrix, first_norms[2][0], first_norms[2][1], 1.0)
        block = [low_back(low(gelu_tanh(normed[k] + input_images[k]))) for k in range(2)]
        linear = [low_back(project(tensor, reduce_w)) for tensor in block]
        hidden = [low(gelu_tanh(tensor)) for tensor in normalise_layer(linear, crop_onehot_matrix, second_norms[0][0], second_norms[0][1], 1.0)]
        linear = [low_back(convolve(tensor, strided, 2)) for tensor in hidden]
        hidden = [low(gelu_tanh(tensor)) for tensor in normalise_layer(linear, crop_onehot_matrix, second_norms[1][0], second_norms[1][1], 4.0)]
        main_linear = [low_back(project(tensor, widen_w)) for tensor in hidden]
        side_linear = [low_back(project(tensor[:, ::2, ::2], shortcut)) for tensor in block]
        main_normed = normalise_layer(main_linear, crop_onehot_matrix, second_norms[2][0], second_norms[2][1], 4.0)
        side_normed = normalise_layer(side_linear, crop_onehot_matrix, second_norms[3][0], second_norms[3][1], 4.0)
        return (gelu_tanh(main_normed[0] + side_normed[0]), gelu_tanh(main_normed[1] + side_normed[1]))
    primals = (image_big.astype(jnp.float32), image_small.astype(jnp.float32), inner_first.astype(jnp.float32), spatial_first.astype(jnp.float32), outer_first.astype(jnp.float32), norms_first.astype(jnp.float32), inner_second.astype(jnp.float32), spatial_second.astype(jnp.float32), outer_second.astype(jnp.float32), skip_second.astype(jnp.float32), norms_second.astype(jnp.float32))
    outputs, pullback = jax.vjp(forward, *primals)
    grads = pullback((cotangent_big.astype(jnp.float32), cotangent_small.astype(jnp.float32)))
    return (outputs[0].astype(jnp.bfloat16), outputs[1].astype(jnp.bfloat16), grads[0].astype(jnp.bfloat16), grads[1].astype(jnp.bfloat16), grads[2], grads[3], grads[4], grads[5], grads[6], grads[7], grads[8], grads[9], grads[10])
```

```python
import functools

import jax
import jax.numpy as jnp
from jax import lax
from jax.experimental import pallas as pl
from jax.experimental.pallas import tpu as pltpu
from jax.sharding import PartitionSpec as P

HIGH = lax.Precision.HIGHEST
EPS = 1e-05
MESH = pl.DeviceIdType.MESH
F32 = jnp.float32
BF16 = jnp.bfloat16


def fold(slots, count, moments):
    if not moments:
        total = slots[0]
        for i in range(1, count):
            total = total + slots[i]
        return total
    sums = slots[0][0:2]
    tally = slots[0][4:6]
    for i in range(1, count):
        sums = sums + slots[i][0:2]
        tally = tally + slots[i][4:6]
    mean = sums / jnp.maximum(tally, 1.0)
    spread = None
    for i in range(count):
        part = slots[i]
        apart = part[0:2] / jnp.maximum(part[4:6], 1.0) - mean
        term = part[2:4] + part[4:6] * apart * apart
        spread = term if spread is None else spread + term
    return jnp.concatenate([sums, spread, tally, jnp.zeros_like(tally)], axis=0)


def exchange_kernel(moments, group, outers, x_ref, o_ref, near, far, s1, r1, s2, r2):
    k, r = lax.axis_index("crops"), lax.axis_index("rows")
    inner, outer = lax.rem(k, group), k // group
    wide = 2 * group
    me = inner * 2 + r
    barrier = pltpu.get_barrier_semaphore()
    peers = []
    for d in range(1, wide):
        p = lax.rem(me + d, wide)
        peers.append((outer * group + p // 2, lax.rem(p, 2)))
    others = []
    for d in range(1, outers):
        others.append((lax.rem(outer + d, outers) * group + inner, r))
    for peer in peers + others:
        pl.semaphore_signal(barrier, inc=1, device_id=peer, device_id_type=MESH)
    pl.semaphore_wait(barrier, len(peers) + len(others))
    copies = []
    for d, peer in enumerate(peers):
        copy = pltpu.make_async_remote_copy(
            src_ref=x_ref,
            dst_ref=near.at[me],
            send_sem=s1.at[d],
            recv_sem=r1.at[d],
            device_id=peer,
            device_id_type=MESH,
        )
        copy.start()
        copies.append(copy)
    near[me] = x_ref[...]
    for copy in copies:
        copy.wait_recv()
    mine = fold([near[i] for i in range(wide)], wide, moments)
    far[outer] = mine
    more = []
    for d, peer in enumerate(others):
        copy = pltpu.make_async_remote_copy(
            src_ref=far.at[outer],
            dst_ref=far.at[outer],
            send_sem=s2.at[d],
            recv_sem=r2.at[d],
            device_id=peer,
            device_id_type=MESH,
        )
        copy.start()
        more.append(copy)
    for copy in more:
        copy.wait_recv()
    total = fold([far[i] for i in range(outers)], outers, moments)
    if moments:
        tally = total[4:6]
        inverse = lax.rsqrt(total[2:4] / tally + EPS)
        total = jnp.concatenate([total[0:2] / tally, inverse, tally, tally], axis=0)
    o_ref[...] = total
    for copy in copies + more:
        copy.wait_send()


def exchange(block, moments, ident):
    crops = lax.axis_size("crops")
    group = 4 if crops % 4 == 0 else 1
    outers = crops // group
    width = block.shape[1]
    vmem = pl.BlockSpec(memory_space=pltpu.VMEM)
    return pl.pallas_call(
        functools.partial(exchange_kernel, moments, group, outers),
        out_shape=jax.ShapeDtypeStruct((8, width), F32),
        in_specs=[vmem],
        out_specs=vmem,
        scratch_shapes=[
            pltpu.VMEM((2 * group, 8, width), F32),
            pltpu.VMEM((outers, 8, width), F32),
            pltpu.SemaphoreType.DMA((2 * group - 1,)),
            pltpu.SemaphoreType.DMA((2 * group - 1,)),
            pltpu.SemaphoreType.DMA((max(outers - 1, 1),)),
            pltpu.SemaphoreType.DMA((max(outers - 1, 1),)),
        ],
        compiler_params=pltpu.CompilerParams(
            collective_id=ident, has_side_effects=True, vmem_limit_bytes=32 * 1024 * 1024
        ),
        name="exchange_%d" % ident,
    )(block)


def share_plan(shapes):
    chunks = []
    for at, (height, width) in enumerate(shapes):
        half = width // 2
        pieces = 1
        while half % (pieces * 2) == 0 and (half // pieces) * height > 600000 and half // pieces > 256:
            pieces *= 2
        cuts = 1
        while height // cuts * (half // pieces) > 600000 and height % (16 * 16 * (cuts + 1)) == 0:
            cuts += 1
        if height == 4608:
            cuts = 3
        for c in range(cuts):
            for p in range(pieces):
                chunks.append((at, c * (height // cuts), height // cuts, p * (half // pieces), half // pieces))
    return chunks


def share_kernel(shapes, chunks, bits, *refs):
    count, n = len(shapes), len(chunks)
    ins, outs = refs[:count], refs[count : 2 * count]
    acc = refs[2 * count : 2 * count + n]
    recv0 = refs[2 * count + n : 2 * count + 2 * n]
    recvs = refs[2 * count + 2 * n : 2 * count + 3 * n]
    send_sem, recv_sem = refs[2 * count + 3 * n], refs[2 * count + 3 * n + 1]
    k, core = lax.axis_index("crops"), lax.axis_index("rows")
    digit = [lax.rem(k // (1 << b), 2) for b in range(bits)]
    orders = [list(range(bits)), list(range(bits))]
    if bits >= 2:
        orders[1][0], orders[1][1] = 1, 0

    def stage_bit(s):
        a, b = orders[0][s], orders[1][s]
        if a == b:
            mine, step = digit[a], 1 << a
        else:
            mine = digit[a] * (1 - core) + digit[b] * core
            step = (1 << a) * (1 - core) + (1 << b) * core
        return mine, k + step * (1 - 2 * mine)

    stages = [stage_bit(s) for s in range(bits)]
    sibling = (k, 1 - core)
    barrier = pltpu.get_barrier_semaphore()
    pl.semaphore_signal(barrier, inc=1, device_id=sibling, device_id_type=MESH)
    for b in range(bits):
        peer = (k + (1 << b) * (1 - 2 * digit[b]), core)
        pl.semaphore_signal(barrier, inc=1, device_id=peer, device_id_type=MESH)
    pl.semaphore_wait(barrier, bits + 1)

    regions, kinds, slots = [], [], []
    for at, row, height, col, width in chunks:
        start, length, region, kind, slot, used = 0, height, [], [], [], 0
        for s in range(bits):
            region.append((start, length))
            slot.append(used)
            if length % 32 == 0:
                kind.append(True)
                length //= 2
                start = start + stages[s][0] * length
            else:
                kind.append(False)
            used += length
        region.append((start, length))
        regions.append(region)
        kinds.append(kind)
        slots.append(slot)

    total = 2 * bits + 2
    live = {}

    def rows(start, length):
        if isinstance(start, int):
            return pl.ds(start, length)
        return pl.ds(pl.multiple_of(start, 16), length)

    def send(i, t, src, dst, device):
        copy = pltpu.make_async_remote_copy(
            src_ref=src,
            dst_ref=dst,
            send_sem=send_sem.at[i, t],
            recv_sem=recv_sem.at[i, t],
            device_id=device,
            device_id_type=MESH,
        )
        copy.start()
        live[i, t] = copy

    def add(dst, d0, src_a, a0, a_cols, src_b, b0, length):
        block = 16
        while length % (block * 2) == 0 and block < 64:
            block *= 2

        def step(j, carry):
            off = pl.multiple_of(j * block, 16)
            left = src_a[pl.ds(pl.multiple_of(a0 + off, 16), block), a_cols].astype(F32)
            right = src_b[pl.ds(pl.multiple_of(b0 + off, 16), block), :].astype(F32)
            dst[pl.ds(pl.multiple_of(d0 + off, 16), block), :] = (left + right).astype(BF16)
            return carry

        lax.fori_loop(0, length // block, step, 0)

    def task(i, t):
        at, row, height, col, width = chunks[i]
        half = shapes[at][1] // 2
        own = pl.ds(pl.multiple_of(core * half + col, 128), width)
        if t > 0:
            live[i, t - 1].wait_recv()
        if t == 0:
            away = pl.ds(pl.multiple_of((1 - core) * half + col, 128), width)
            send(i, t, ins[at].at[pl.ds(row, height), away], recv0[i], sibling)
            return
        if t <= bits + 1:
            if t == 1:
                add(acc[i], 0, ins[at], row, own, recv0[i], 0, height)
            else:
                s = t - 2
                start, length = regions[i][s + 1]
                if not kinds[i][s]:
                    live[i, t - 1].wait_send()
                add(acc[i], start, acc[i], start, slice(None), recvs[i], slots[i][s], length)
        if t <= bits:
            s = t - 1
            start, length = regions[i][s]
            peer = (stages[s][1], core)
            if kinds[i][s]:
                give = length // 2
                from_row = start + (1 - stages[s][0]) * give
            else:
                give, from_row = length, start
            send(
                i,
                t,
                acc[i].at[rows(from_row, give)],
                recvs[i].at[pl.ds(slots[i][s], give)],
                peer,
            )
            return
        if t == bits + 1:
            start, length = regions[i][bits]
            outs[at][pl.ds(pl.multiple_of(row + start, 16), length), own] = acc[i][rows(start, length), :]
        if t <= 2 * bits:
            s = bits - 1 - (t - bits - 1)
            start, length = regions[i][s + 1]
            if kinds[i][s]:
                place = outs[at].at[pl.ds(pl.multiple_of(row + start, 16), length), own]
                send(i, t, place, place, (stages[s][1], core))
            return
        if t == 2 * bits + 1:
            place = outs[at].at[pl.ds(row, height), own]
            send(i, t, place, place, sibling)

    def skipped(i, t):
        return bits + 1 <= t <= 2 * bits and not kinds[i][bits - 1 - (t - bits - 1)]

    class Nothing:
        def wait_recv(self):
            pass

        def wait_send(self):
            pass

    for t in range(n + total):
        for i in range(n):
            s = t - i
            if 0 <= s < total:
                task(i, s)
                if skipped(i, s):
                    live[i, s] = Nothing()
            elif s == total:
                live[i, total - 1].wait_recv()
    for i in range(n):
        for t in range(total):
            if t >= 1 and t <= bits and not kinds[i][t - 1]:
                continue
            live[i, t].wait_send()


def share_all(values, ident):
    crops = lax.axis_size("crops")
    bits = crops.bit_length() - 1
    shapes = [(v.shape[0], v.shape[1]) for v in values]
    chunks = share_plan(shapes)
    vmem = pl.BlockSpec(memory_space=pltpu.VMEM)
    acc, recv0, recvs = [], [], []
    for at, row, height, col, width in chunks:
        acc.append(pltpu.VMEM((height, width), BF16))
        recv0.append(pltpu.VMEM((height, width), BF16))
        length, used = height, 0
        for s in range(bits):
            if length % 32 == 0:
                length //= 2
            used += length
        recvs.append(pltpu.VMEM((used, width), BF16))
    total = 2 * bits + 2
    return pl.pallas_call(
        functools.partial(share_kernel, shapes, chunks, bits),
        out_shape=[jax.ShapeDtypeStruct(s, BF16) for s in shapes],
        in_specs=[vmem] * len(shapes),
        out_specs=[vmem] * len(shapes),
        scratch_shapes=acc
        + recv0
        + recvs
        + [
            pltpu.SemaphoreType.DMA((len(chunks), total)),
            pltpu.SemaphoreType.DMA((len(chunks), total)),
        ],
        compiler_params=pltpu.CompilerParams(
            collective_id=ident, has_side_effects=True, vmem_limit_bytes=60 * 1024 * 1024
        ),
        name="share",
    )(*values)


def gelu_tanh(v):
    return jax.nn.gelu(v, approximate=True)


def gelu_back(tensor, upstream):
    return jax.vjp(gelu_tanh, tensor)[1](upstream)[0]


def views_onehot(labels):
    return (labels[None, :] == jnp.arange(2)[:, None]).astype(F32)


def crop_sums(tensor):
    return jnp.sum(tensor, axis=(1, 2))


def view_sums(onehot, percrop):
    return jnp.dot(onehot, percrop, precision=HIGH)


def crop_table(onehot, table):
    return jnp.dot(onehot.T, table, precision=HIGH)[:, None, None, :]


def project(tensor, weight):
    return jnp.dot(tensor, weight, preferred_element_type=F32)


def project_back(gradient, weight):
    return lax.dot_general(
        gradient, weight, (((3,), (1,)), ((), ())), preferred_element_type=F32
    )


def weight_grad(tensors, gradients):
    return sum(
        lax.dot_general(
            t, g, (((0, 1, 2), (0, 1, 2)), ((), ())), preferred_element_type=F32
        )
        for t, g in zip(tensors, gradients)
    ).astype(BF16)


def convolve(tensor, kernel, stride):
    return lax.conv_general_dilated(
        tensor,
        kernel,
        (stride, stride),
        ((1, 1), (1, 1)),
        dimension_numbers=("NHWC", "HWIO", "NHWC"),
        preferred_element_type=F32,
    )


def convolve_back(delta, kernel, stride):
    flipped = jnp.swapaxes(kernel[::-1, ::-1], 2, 3)
    high = stride
    return lax.conv_general_dilated(
        delta,
        flipped,
        (1, 1),
        ((1, high), (1, high)),
        lhs_dilation=(stride, stride),
        dimension_numbers=("NHWC", "HWIO", "NHWC"),
        preferred_element_type=F32,
    )


def kernel_grad(tensors, deltas, stride):
    high = 2 - stride
    total = sum(
        lax.conv_general_dilated(
            t,
            d,
            (1, 1),
            ((1, high), (1, high)),
            rhs_dilation=(stride, stride),
            dimension_numbers=("CHWN", "IHWO", "HWNC"),
            preferred_element_type=F32,
        )
        for t, d in zip(tensors, deltas)
    )
    return total.astype(BF16).reshape(-1, total.shape[-1])


def pieces_of(norms, widths):
    pieces, anchor = [], 0
    for width in widths:
        pieces.append((norms[0, anchor : anchor + width], norms[1, anchor : anchor + width]))
        anchor += width
    return pieces


def moments(pairs, onehots, ident):
    blocks = []
    for pair in pairs:
        tally = sum(
            jnp.sum(onehots[k], 1) * (pair[k].shape[1] * pair[k].shape[2]) for k in range(2)
        )[:, None]
        sums = sum(view_sums(onehots[k], crop_sums(pair[k])) for k in range(2))
        mean = sums / jnp.maximum(tally, 1.0)
        spread = sum(
            view_sums(
                onehots[k], crop_sums(jnp.square(pair[k] - crop_table(onehots[k], mean)))
            )
            for k in range(2)
        )
        wide = jnp.broadcast_to(tally, sums.shape)
        blocks.append(jnp.concatenate([sums, spread, wide, jnp.zeros_like(wide)], axis=0))
    got = exchange(jnp.concatenate(blocks, axis=1), True, ident)
    outs, anchor = [], 0
    for pair in pairs:
        width = pair[0].shape[3]
        part = got[:, anchor : anchor + width]
        outs.append((part[0:2], part[2:4], part[4:6]))
        anchor += width
    return outs


def apply_norm(linear, onehots, moment, piece):
    centered = [
        (linear[k] - crop_table(onehots[k], moment[0])) * crop_table(onehots[k], moment[1])
        for k in range(2)
    ]
    return centered, [t * piece[0] + piece[1] for t in centered]


def norm_sums(upstream, centereds, onehots, ident):
    rows = [sum(view_sums(onehots[k], crop_sums(upstream[k])) for k in range(2))]
    for centered in centereds:
        rows.append(
            sum(view_sums(onehots[k], crop_sums(upstream[k] * centered[k])) for k in range(2))
        )
    block = jnp.concatenate(rows, axis=0)
    block = jnp.pad(block, ((0, 8 - block.shape[0]), (0, 0)))
    got = exchange(block, False, ident)
    return [(got[0:2], got[2 * j + 2 : 2 * j + 4]) for j in range(len(centereds))]


def norm_grad(upstream, centered, onehots, moment, gain, sums):
    inverse, tally = moment[1], moment[2]
    return [
        (
            gain
            * crop_table(onehots[k], inverse)
            * (
                upstream[k]
                - crop_table(onehots[k], sums[0] / tally)
                - centered[k] * crop_table(onehots[k], sums[1] / tally)
            )
        ).astype(BF16)
        for k in range(2)
    ]


def swap_in(tensor):
    return lax.all_to_all(tensor, "rows", split_axis=0, concat_axis=1, tiled=True)


def swap_out(tensor):
    return lax.all_to_all(tensor, "rows", split_axis=1, concat_axis=0, tiled=True)


def shards(
    image_big,
    image_small,
    view_big,
    view_small,
    inner_first,
    spatial_first,
    outer_first,
    norms_first,
    inner_second,
    spatial_second,
    outer_second,
    skip_second,
    norms_second,
    cotangent_big,
    cotangent_small,
):
    two = range(2)
    splits, position = lax.axis_size("rows"), lax.axis_index("rows")
    images = [swap_in(image_big), swap_in(image_small)]
    onehots = [
        views_onehot(
            lax.dynamic_slice_in_dim(
                labels, position * (labels.shape[0] // splits), labels.shape[0] // splits
            )
        )
        for labels in (view_big, view_small)
    ]
    n1 = pieces_of(norms_first, (inner_first.shape[1], spatial_first.shape[3], outer_first.shape[1]))
    n2 = pieces_of(
        norms_second,
        (inner_second.shape[1], spatial_second.shape[3], outer_second.shape[1], skip_second.shape[1]),
    )

    z1 = [project(t, inner_first) for t in images]
    (m1,) = moments([z1], onehots, 0)
    c1, u1 = apply_norm(z1, onehots, m1, n1[0])
    h1 = [gelu_tanh(t).astype(BF16) for t in u1]

    z2 = [convolve(t, spatial_first, 1) for t in h1]
    (m2,) = moments([z2], onehots, 1)
    c2, u2 = apply_norm(z2, onehots, m2, n1[1])
    h2 = [gelu_tanh(t).astype(BF16) for t in u2]

    z3 = [project(t, outer_first) for t in h2]
    (m3,) = moments([z3], onehots, 2)
    c3, u3 = apply_norm(z3, onehots, m3, n1[2])
    mixed1 = [u3[k] + images[k].astype(F32) for k in two]
    block = [gelu_tanh(t).astype(BF16) for t in mixed1]

    z4 = [project(t, inner_second) for t in block]
    (m4,) = moments([z4], onehots, 3)
    c4, u4 = apply_norm(z4, onehots, m4, n2[0])
    h4 = [gelu_tanh(t).astype(BF16) for t in u4]

    z5 = [convolve(t, spatial_second, 2) for t in h4]
    (m5,) = moments([z5], onehots, 4)
    c5, u5 = apply_norm(z5, onehots, m5, n2[1])
    h5 = [gelu_tanh(t).astype(BF16) for t in u5]

    z6 = [project(t, outer_second) for t in h5]
    z7 = [
        lax.conv_general_dilated(
            t,
            skip_second[None, None],
            (2, 2),
            ((0, 0), (0, 0)),
            dimension_numbers=("NHWC", "HWIO", "NHWC"),
            preferred_element_type=F32,
        )
        for t in block
    ]
    m6, m7 = moments([z6, z7], onehots, 5)
    c6, u6 = apply_norm(z6, onehots, m6, n2[2])
    c7, u7 = apply_norm(z7, onehots, m7, n2[3])
    mixed2 = [u6[k] + u7[k] for k in two]
    results = [gelu_tanh(t).astype(BF16) for t in mixed2]

    cots = [cotangent_big, cotangent_small]
    up2 = [gelu_back(mixed2[k], cots[k].astype(F32)) for k in two]
    s6, s7 = norm_sums(up2, [c6, c7], onehots, 6)
    d6 = norm_grad(up2, c6, onehots, m6, n2[2][0], s6)
    d7 = norm_grad(up2, c7, onehots, m7, n2[3][0], s7)
    g_outer2 = weight_grad(h5, d6)
    picked = [
        lax.conv_general_dilated(
            block[k],
            d7[k],
            (1, 1),
            ((0, -1), (0, -1)),
            rhs_dilation=(2, 2),
            dimension_numbers=("CHWN", "IHWO", "HWNC"),
            preferred_element_type=F32,
        )[0, 0]
        for k in two
    ]
    g_skip = (picked[0] + picked[1]).astype(BF16)
    q5 = [gelu_back(u5[k], project_back(d6[k], outer_second)) for k in two]
    (s5,) = norm_sums(q5, [c5], onehots, 7)
    d5 = norm_grad(q5, c5, onehots, m5, n2[1][0], s5)
    g_spatial2 = kernel_grad(h4, d5, 2)
    q4 = [gelu_back(u4[k], convolve_back(d5[k], spatial_second, 2)) for k in two]
    (s4,) = norm_sums(q4, [c4], onehots, 8)
    d4 = norm_grad(q4, c4, onehots, m4, n2[0][0], s4)
    g_inner2 = weight_grad(block, d4)
    moved = [
        (
            project_back(d4[k], inner_second)
            + lax.pad(
                project_back(d7[k], skip_second),
                jnp.float32(0),
                ((0, 0, 0), (0, 1, 1), (0, 1, 1), (0, 0, 0)),
            )
        ).astype(BF16)
        for k in two
    ]
    up1 = [gelu_back(mixed1[k], moved[k].astype(F32)) for k in two]
    (s3,) = norm_sums(up1, [c3], onehots, 9)
    d3 = norm_grad(up1, c3, onehots, m3, n1[2][0], s3)
    g_outer1 = weight_grad(h2, d3)
    q2 = [gelu_back(u2[k], project_back(d3[k], outer_first)) for k in two]
    (s2,) = norm_sums(q2, [c2], onehots, 10)
    d2 = norm_grad(q2, c2, onehots, m2, n1[1][0], s2)
    g_spatial1 = kernel_grad(h1, d2, 1)
    q1 = [gelu_back(u1[k], convolve_back(d2[k], spatial_first, 1)) for k in two]
    (s1,) = norm_sums(q1, [c1], onehots, 11)
    d1 = norm_grad(q1, c1, onehots, m1, n1[0][0], s1)
    g_inner1 = weight_grad(images, d1)
    gradients = [
        swap_out((up1[k] + project_back(d1[k], inner_first)).astype(BF16)) for k in two
    ]

    def both(pairs):
        return jnp.stack(
            [
                jnp.concatenate([jnp.sum(p[1], 0) for p in pairs]),
                jnp.concatenate([jnp.sum(p[0], 0) for p in pairs]),
            ]
        )

    shared = share_all(
        [g_skip, g_spatial2, g_outer2, g_inner2, g_spatial1, g_outer1, g_inner1], 12
    )
    g_skip, g_spatial2, g_outer2, g_inner2, g_spatial1, g_outer1, g_inner1 = [
        t.astype(F32) for t in shared
    ]
    return (
        results[0],
        results[1],
        gradients[0],
        gradients[1],
        g_inner1,
        g_spatial1.reshape(spatial_first.shape),
        g_outer1,
        both((s1, s2, s3)),
        g_inner2,
        g_spatial2.reshape(spatial_second.shape),
        g_outer2,
        g_skip,
        both((s4, s5, s6, s7)),
    )


def solution(mesh):
    maps = P("crops", "rows", None, None)
    whole = P(("crops", "rows"), None, None, None)
    in_specs = (maps, maps, P("crops"), P("crops")) + (P(),) * 9 + (whole, whole)
    out_specs = (whole, whole, maps, maps) + (P(),) * 9
    return jax.shard_map(shards, mesh=mesh, in_specs=in_specs, out_specs=out_specs, check_vma=False)
```

```python
import functools

import jax
import jax.numpy as jnp
from jax import lax
from jax.experimental import pallas as pl
from jax.experimental.pallas import tpu as pltpu
from jax.sharding import PartitionSpec as P

HIGH = lax.Precision.HIGHEST
EPS = 1e-05
MESH = pl.DeviceIdType.MESH
F32 = jnp.float32
BF16 = jnp.bfloat16


def fold(slots, count, moments):
    if not moments:
        total = slots[0]
        for i in range(1, count):
            total = total + slots[i]
        return total
    sums = slots[0][0:2]
    tally = slots[0][4:6]
    for i in range(1, count):
        sums = sums + slots[i][0:2]
        tally = tally + slots[i][4:6]
    mean = sums / jnp.maximum(tally, 1.0)
    spread = None
    for i in range(count):
        part = slots[i]
        apart = part[0:2] / jnp.maximum(part[4:6], 1.0) - mean
        term = part[2:4] + part[4:6] * apart * apart
        spread = term if spread is None else spread + term
    return jnp.concatenate([sums, spread, tally, jnp.zeros_like(tally)], axis=0)


def exchange_kernel(moments, group, outers, x_ref, o_ref, near, far, s1, r1, s2, r2):
    k, r = lax.axis_index("crops"), lax.axis_index("rows")
    inner, outer = lax.rem(k, group), k // group
    wide = 2 * group
    me = inner * 2 + r
    barrier = pltpu.get_barrier_semaphore()
    peers = []
    for d in range(1, wide):
        p = lax.rem(me + d, wide)
        peers.append((outer * group + p // 2, lax.rem(p, 2)))
    others = []
    for d in range(1, outers):
        others.append((lax.rem(outer + d, outers) * group + inner, r))
    for peer in peers + others:
        pl.semaphore_signal(barrier, inc=1, device_id=peer, device_id_type=MESH)
    pl.semaphore_wait(barrier, len(peers) + len(others))
    copies = []
    for d, peer in enumerate(peers):
        copy = pltpu.make_async_remote_copy(
            src_ref=x_ref,
            dst_ref=near.at[me],
            send_sem=s1.at[d],
            recv_sem=r1.at[d],
            device_id=peer,
            device_id_type=MESH,
        )
        copy.start()
        copies.append(copy)
    near[me] = x_ref[...]
    for copy in copies:
        copy.wait_recv()
    mine = fold([near[i] for i in range(wide)], wide, moments)
    far[outer] = mine
    more = []
    for d, peer in enumerate(others):
        copy = pltpu.make_async_remote_copy(
            src_ref=far.at[outer],
            dst_ref=far.at[outer],
            send_sem=s2.at[d],
            recv_sem=r2.at[d],
            device_id=peer,
            device_id_type=MESH,
        )
        copy.start()
        more.append(copy)
    for copy in more:
        copy.wait_recv()
    total = fold([far[i] for i in range(outers)], outers, moments)
    if moments:
        tally = total[4:6]
        inverse = lax.rsqrt(total[2:4] / tally + EPS)
        total = jnp.concatenate([total[0:2] / tally, inverse, tally, tally], axis=0)
    o_ref[...] = total
    for copy in copies + more:
        copy.wait_send()


def exchange(block, moments, ident):
    crops = lax.axis_size("crops")
    group = 4 if crops % 4 == 0 else 1
    outers = crops // group
    width = block.shape[1]
    vmem = pl.BlockSpec(memory_space=pltpu.VMEM)
    return pl.pallas_call(
        functools.partial(exchange_kernel, moments, group, outers),
        out_shape=jax.ShapeDtypeStruct((8, width), F32),
        in_specs=[vmem],
        out_specs=vmem,
        scratch_shapes=[
            pltpu.VMEM((2 * group, 8, width), F32),
            pltpu.VMEM((outers, 8, width), F32),
            pltpu.SemaphoreType.DMA((2 * group - 1,)),
            pltpu.SemaphoreType.DMA((2 * group - 1,)),
            pltpu.SemaphoreType.DMA((max(outers - 1, 1),)),
            pltpu.SemaphoreType.DMA((max(outers - 1, 1),)),
        ],
        compiler_params=pltpu.CompilerParams(
            collective_id=ident, has_side_effects=True, vmem_limit_bytes=32 * 1024 * 1024
        ),
        name="exchange_%d" % ident,
    )(block)


def share_plan(shapes):
    chunks = []
    for at, (height, width) in enumerate(shapes):
        half = width // 2
        pieces = 1
        while half % (pieces * 2) == 0 and (half // pieces) * height > 600000 and half // pieces > 256:
            pieces *= 2
        cuts = 1
        while height // cuts * (half // pieces) > 600000 and height % (16 * 16 * (cuts + 1)) == 0:
            cuts += 1
        if height == 4608:
            cuts = 3
        for c in range(cuts):
            for p in range(pieces):
                chunks.append((at, c * (height // cuts), height // cuts, p * (half // pieces), half // pieces))
    return chunks


def share_kernel(shapes, chunks, bits, *refs):
    count, n = len(shapes), len(chunks)
    ins, outs = refs[:count], refs[count : 2 * count]
    acc = refs[2 * count : 2 * count + n]
    recv0 = refs[2 * count + n : 2 * count + 2 * n]
    recvs = refs[2 * count + 2 * n : 2 * count + 3 * n]
    send_sem, recv_sem = refs[2 * count + 3 * n], refs[2 * count + 3 * n + 1]
    k, core = lax.axis_index("crops"), lax.axis_index("rows")
    digit = [lax.rem(k // (1 << b), 2) for b in range(bits)]
    orders = [list(range(bits)), list(range(bits))]
    if bits >= 2:
        orders[1][0], orders[1][1] = 1, 0

    def stage_bit(s):
        a, b = orders[0][s], orders[1][s]
        if a == b:
            mine, step = digit[a], 1 << a
        else:
            mine = digit[a] * (1 - core) + digit[b] * core
            step = (1 << a) * (1 - core) + (1 << b) * core
        return mine, k + step * (1 - 2 * mine)

    stages = [stage_bit(s) for s in range(bits)]
    sibling = (k, 1 - core)
    barrier = pltpu.get_barrier_semaphore()
    pl.semaphore_signal(barrier, inc=1, device_id=sibling, device_id_type=MESH)
    for b in range(bits):
        peer = (k + (1 << b) * (1 - 2 * digit[b]), core)
        pl.semaphore_signal(barrier, inc=1, device_id=peer, device_id_type=MESH)
    pl.semaphore_wait(barrier, bits + 1)

    regions, kinds, slots = [], [], []
    for at, row, height, col, width in chunks:
        start, length, region, kind, slot, used = 0, height, [], [], [], 0
        for s in range(bits):
            region.append((start, length))
            slot.append(used)
            if length % 32 == 0:
                kind.append(True)
                length //= 2
                start = start + stages[s][0] * length
            else:
                kind.append(False)
            used += length
        region.append((start, length))
        regions.append(region)
        kinds.append(kind)
        slots.append(slot)

    total = 2 * bits + 2
    live = {}

    def rows(start, length):
        if isinstance(start, int):
            return pl.ds(start, length)
        return pl.ds(pl.multiple_of(start, 16), length)

    def send(i, t, src, dst, device):
        copy = pltpu.make_async_remote_copy(
            src_ref=src,
            dst_ref=dst,
            send_sem=send_sem.at[i, t],
            recv_sem=recv_sem.at[i, t],
            device_id=device,
            device_id_type=MESH,
        )
        copy.start()
        live[i, t] = copy

    def add(dst, d0, src_a, a0, a_cols, src_b, b0, length):
        block = 16
        while length % (block * 2) == 0 and block < 64:
            block *= 2

        def step(j, carry):
            off = pl.multiple_of(j * block, 16)
            left = src_a[pl.ds(pl.multiple_of(a0 + off, 16), block), a_cols].astype(F32)
            right = src_b[pl.ds(pl.multiple_of(b0 + off, 16), block), :].astype(F32)
            dst[pl.ds(pl.multiple_of(d0 + off, 16), block), :] = (left + right).astype(BF16)
            return carry

        lax.fori_loop(0, length // block, step, 0)

    def task(i, t):
        at, row, height, col, width = chunks[i]
        half = shapes[at][1] // 2
        own = pl.ds(pl.multiple_of(core * half + col, 128), width)
        if t > 0:
            live[i, t - 1].wait_recv()
        if t == 0:
            away = pl.ds(pl.multiple_of((1 - core) * half + col, 128), width)
            send(i, t, ins[at].at[pl.ds(row, height), away], recv0[i], sibling)
            return
        if t <= bits + 1:
            if t == 1:
                add(acc[i], 0, ins[at], row, own, recv0[i], 0, height)
            else:
                s = t - 2
                start, length = regions[i][s + 1]
                if not kinds[i][s]:
                    live[i, t - 1].wait_send()
                add(acc[i], start, acc[i], start, slice(None), recvs[i], slots[i][s], length)
        if t <= bits:
            s = t - 1
            start, length = regions[i][s]
            peer = (stages[s][1], core)
            if kinds[i][s]:
                give = length // 2
                from_row = start + (1 - stages[s][0]) * give
            else:
                give, from_row = length, start
            send(
                i,
                t,
                acc[i].at[rows(from_row, give)],
                recvs[i].at[pl.ds(slots[i][s], give)],
                peer,
            )
            return
        if t == bits + 1:
            start, length = regions[i][bits]
            outs[at][pl.ds(pl.multiple_of(row + start, 16), length), own] = acc[i][rows(start, length), :]
        if t <= 2 * bits:
            s = bits - 1 - (t - bits - 1)
            start, length = regions[i][s + 1]
            if kinds[i][s]:
                place = outs[at].at[pl.ds(pl.multiple_of(row + start, 16), length), own]
                send(i, t, place, place, (stages[s][1], core))
            return
        if t == 2 * bits + 1:
            place = outs[at].at[pl.ds(row, height), own]
            send(i, t, place, place, sibling)

    def skipped(i, t):
        return bits + 1 <= t <= 2 * bits and not kinds[i][bits - 1 - (t - bits - 1)]

    class Nothing:
        def wait_recv(self):
            pass

        def wait_send(self):
            pass

    for t in range(n + total):
        for i in range(n):
            s = t - i
            if 0 <= s < total:
                task(i, s)
                if skipped(i, s):
                    live[i, s] = Nothing()
            elif s == total:
                live[i, total - 1].wait_recv()
    for i in range(n):
        for t in range(total):
            if t >= 1 and t <= bits and not kinds[i][t - 1]:
                continue
            live[i, t].wait_send()


def share_all(values, ident):
    crops = lax.axis_size("crops")
    bits = crops.bit_length() - 1
    shapes = [(v.shape[0], v.shape[1]) for v in values]
    chunks = share_plan(shapes)
    vmem = pl.BlockSpec(memory_space=pltpu.VMEM)
    acc, recv0, recvs = [], [], []
    for at, row, height, col, width in chunks:
        acc.append(pltpu.VMEM((height, width), BF16))
        recv0.append(pltpu.VMEM((height, width), BF16))
        length, used = height, 0
        for s in range(bits):
            if length % 32 == 0:
                length //= 2
            used += length
        recvs.append(pltpu.VMEM((used, width), BF16))
    total = 2 * bits + 2
    return pl.pallas_call(
        functools.partial(share_kernel, shapes, chunks, bits),
        out_shape=[jax.ShapeDtypeStruct(s, BF16) for s in shapes],
        in_specs=[vmem] * len(shapes),
        out_specs=[vmem] * len(shapes),
        scratch_shapes=acc
        + recv0
        + recvs
        + [
            pltpu.SemaphoreType.DMA((len(chunks), total)),
            pltpu.SemaphoreType.DMA((len(chunks), total)),
        ],
        compiler_params=pltpu.CompilerParams(
            collective_id=ident, has_side_effects=True, vmem_limit_bytes=60 * 1024 * 1024
        ),
        name="share",
    )(*values)


class Maps:
    def __init__(self, count, edge, row0, crop0, guard0, out0):
        self.count, self.edge = count, edge
        self.row0, self.crop0, self.guard0, self.out0 = row0, crop0, guard0, out0
        self.rows = edge * 16
        self.guard = (edge + 1) * 16
        self.half = edge // 2
        self.out = self.half * 8
        self.pixels = edge * edge


def geometry(nb, eb, ns, es):
    big = Maps(nb, eb, 0, 0, 16, 0)
    small = Maps(ns, es, nb * big.rows, nb, 16 + nb * big.guard, nb * big.out)
    total = small.row0 + ns * small.rows
    guarded = small.guard0 + ns * small.guard
    out = small.out0 + ns * small.out
    return (big, small), total, guarded, out


def al(x, m=16):
    return x if isinstance(x, int) else pl.multiple_of(x, m)


def span(start, size, m=16):
    return pl.ds(al(start, m), size)


def repeat(count, body):
    def step(i, carry):
        body(i)
        return carry

    lax.fori_loop(0, count, step, 0)


def mm(a, b):
    return jnp.dot(a, b, preferred_element_type=F32)


def mm_nt(a, b):
    return lax.dot_general(a, b, (((1,), (1,)), ((), ())), preferred_element_type=F32)


def mm_tn(a, b):
    return lax.dot_general(a, b, (((0,), (0,)), ((), ())), preferred_element_type=F32)


CA = 0.7978845608028654
CB = 0.7978845608028654 * 0.044715


def act(u):
    t = jnp.tanh(u * (CA + CB * (u * u)))
    return 0.5 * u * (1.0 + t)


def act_slope(u):
    s = u * u
    t = jnp.tanh(u * (CA + CB * s))
    rise = (0.5 * u) * (CA + (3.0 * CB) * s)
    return 0.5 * (1.0 + t) + (1.0 - t * t) * rise


def act_both(u):
    s = u * u
    t = jnp.tanh(u * (CA + CB * s))
    hu = 0.5 * u
    lift = 0.5 * (1.0 + t)
    slope = lift + (1.0 - t * t) * (hu * (CA + (3.0 * CB) * s))
    return u * lift, slope


def keep(rows, width, pitch, edge):
    place = lax.broadcasted_iota(jnp.int32, (rows, width), 0)
    return lax.rem(place, pitch) < edge


def tile_sum(x):
    return jnp.sum(x.reshape(x.shape[0] // 8, 8, x.shape[1]), axis=0)


def pieces(width):
    return (4, width // 4) if width >= 512 else (width // 128, 128)


class Links:
    def __init__(self, crops, near, far, near_s, near_r, far_s, far_r):
        self.group = 4 if crops % 4 == 0 else 1
        self.outers = crops // self.group
        self.k, self.r = lax.axis_index("crops"), lax.axis_index("rows")
        inner, self.outer = lax.rem(self.k, self.group), self.k // self.group
        self.wide = 2 * self.group
        self.me = inner * 2 + self.r
        self.peers, self.others = [], []
        for d in range(1, self.wide):
            p = lax.rem(self.me + d, self.wide)
            self.peers.append((self.outer * self.group + p // 2, lax.rem(p, 2)))
        for d in range(1, self.outers):
            self.others.append((lax.rem(self.outer + d, self.outers) * self.group + inner, self.r))
        self.near, self.far = near, far
        self.sems = (near_s, near_r, far_s, far_r)
        self.live = {}

    def greet(self, extra=()):
        barrier = pltpu.get_barrier_semaphore()
        peers = self.peers + self.others + list(extra)
        for peer in peers:
            pl.semaphore_signal(barrier, inc=1, device_id=peer, device_id_type=MESH)
        pl.semaphore_wait(barrier, len(peers))

    def send_near(self, e, block):
        self.near[e][self.me] = block[...]
        self.live[e, 0] = []
        for d, peer in enumerate(self.peers):
            copy = pltpu.make_async_remote_copy(
                src_ref=block,
                dst_ref=self.near[e].at[self.me],
                send_sem=self.sems[0].at[e, d],
                recv_sem=self.sems[1].at[e, d],
                device_id=peer,
                device_id_type=MESH,
            )
            copy.start()
            self.live[e, 0].append(copy)

    def wait_near(self, e):
        for copy in self.live[e, 0]:
            copy.wait_recv()

    def send_far(self, e):
        self.live[e, 1] = []
        place = self.far[e].at[self.outer]
        for d, peer in enumerate(self.others):
            copy = pltpu.make_async_remote_copy(
                src_ref=place,
                dst_ref=place,
                send_sem=self.sems[2].at[e, d],
                recv_sem=self.sems[3].at[e, d],
                device_id=peer,
                device_id_type=MESH,
            )
            copy.start()
            self.live[e, 1].append(copy)

    def wait_far(self, e):
        for copy in self.live[e, 1]:
            copy.wait_recv()

    def finish(self):
        for copies in self.live.values():
            for copy in copies:
                copy.wait_send()


def fold_moments(buf, tallies, count, scale):
    sums, total = buf[0, 0:8, :], tallies[0]
    for i in range(1, count):
        sums = sums + buf[i, 0:8, :]
        total = total + tallies[i]
    mean = sums / jnp.maximum(total * scale, 1.0)
    spread = None
    for i in range(count):
        n = tallies[i] * scale
        apart = buf[i, 0:8, :] / jnp.maximum(n, 1.0) - mean
        term = buf[i, 8:16, :] + n * apart * apart
        spread = term if spread is None else spread + term
    return sums, spread, total


def fold_sums(buf, count):
    total = buf[0]
    for i in range(1, count):
        total = total + buf[i]
    return total


def exchange_shapes(widths, tiles, crops):
    group = 4 if crops % 4 == 0 else 1
    outers = crops // group
    blocks, near, far = [], [], []
    for width, tile in zip(widths, tiles):
        lanes = pieces(width)[1]
        blocks.append(pltpu.VMEM((8 * tile, lanes), F32))
        near.append(pltpu.VMEM((2 * group, 8 * tile, lanes), F32))
        far.append(pltpu.VMEM((outers, 8 * tile, lanes), F32))
    e = len(widths)
    sems = [
        pltpu.SemaphoreType.DMA((e, 2 * group - 1)),
        pltpu.SemaphoreType.DMA((e, 2 * group - 1)),
        pltpu.SemaphoreType.DMA((e, max(outers - 1, 1))),
        pltpu.SemaphoreType.DMA((e, max(outers - 1, 1))),
    ]
    return blocks + near + far + sems


def take(refs, count):
    return list(refs[:count]), refs[count:]


def pack(block, tile, rows, width):
    count, lanes = pieces(width)
    for q in range(count):
        for v in range(2):
            block[tile * 8 + 2 * q + v : tile * 8 + 2 * q + v + 1, :] = rows[v][:, q * lanes : (q + 1) * lanes]


def unpack(table, row, tile, width):
    count, lanes = pieces(width)
    for q in range(count):
        table[row : row + 2, q * lanes : (q + 1) * lanes] = tile[2 * q : 2 * q + 2, :]


def crop_stats(ref, row0, rows, step, width, edge, pitch, pixels, crop, cs, cm, col0=0):
    mask = keep(step, width, pitch, edge)
    zero = jnp.zeros((8, width), F32)
    cols = pl.ds(col0, width) if isinstance(col0, int) else pl.ds(pl.multiple_of(col0, 128), width)

    def first(i, acc):
        z = ref[span(row0 + i * step, step, 8), cols]
        return acc + tile_sum(jnp.where(mask, z, 0.0))

    s = jnp.sum(lax.fori_loop(0, rows // step, first, zero), axis=0, keepdims=True)
    mean = s * (1.0 / pixels)

    def second(i, acc):
        z = ref[span(row0 + i * step, step, 8), cols]
        d = jnp.where(mask, z - mean, 0.0)
        return acc + tile_sum(d * d)

    m = jnp.sum(lax.fori_loop(0, rows // step, second, zero), axis=0, keepdims=True)
    cs[pl.ds(crop, 1), cols] = s
    cm[pl.ds(crop, 1), cols] = m


def local_moments(block, cs, cm, wcol, width, scale, tally=False):
    s, m = cs[:, 0:width], cm[:, 0:width]
    pix = wcol[:, 2:3] * scale
    mean_c = s / pix
    sums, squares, tallies = [], [], []
    for v in range(2):
        w = wcol[:, v : v + 1]
        total = jnp.sum(w * s, axis=0, keepdims=True)
        n = jnp.sum(w * pix, axis=0, keepdims=True)
        apart = mean_c - total / jnp.maximum(n, 1.0)
        squares.append(jnp.sum(w * (m + pix * apart * apart), axis=0, keepdims=True))
        sums.append(total)
        tallies.append(n)
    pack(block, 0, sums, width)
    pack(block, 1, squares, width)
    if tally:
        lanes = pieces(width)[1]
        for q in range(4):
            for v in range(2):
                block[16 + 2 * q + v : 17 + 2 * q + v, :] = jnp.broadcast_to(tallies[v], (1, lanes))


def local_sums(block, parts, wcol, width):
    for tile, part in enumerate(parts):
        s = part[:, 0:width]
        pack(block, tile, [jnp.sum(wcol[:, v : v + 1] * s, axis=0, keepdims=True) for v in range(2)], width)


def by_view(wv, crop, pair):
    return wv[0, crop] * pair[0:1, :] + wv[1, crop] * pair[1:2, :]


FWD_WIDTHS = (256, 256, 1024, 512, 2048, 512, 2048, 2048)


def forward_kernel(sets, total, guarded, outs, crops, dims, *refs):
    c3, cin, c4, cout = dims
    (
        wv, wcol, norms1, norms2,
        img_b, img_s, cot_hbm, w1_h, wsp1_h, w3_h, w4_h, w5_h, w6_h, w7_h,
    ), refs = refs[:14], refs[14:]
    (
        o_img, o_z1, o_h1, o_z2, o_h2, o_blk, o_z4, o_x5, o_z5, o_h5, o_xe, o_res, o_d6, o_d7,
        o_st1, o_st2, o_st3, o_st4, o_st7, o_st5, o_st6, o_sq, o_tally,
    ), refs = refs[:23], refs[23:]
    (
        img, z1, h1, z2, h2, zt, blk, eb, z4, xe, z7, hp, x5, z5, h5, z6, cot,
        w1, wsp1, w3, w4, w5, w6, w7, cs, cm, ck,
        st1, st2, st3, st4, st7, st5, st6, sq, tally_v,
    ), refs = refs[:36], refs[36:]
    e = len(FWD_WIDTHS)
    blocks, refs = take(refs, e)
    near, refs = take(refs, e)
    far, refs = take(refs, e)
    ns_, nr_, fs_, fr_ = refs[:4]
    load_sem, img_sem, img_send, img_recv, out_sem = refs[4:]
    links = Links(crops, near, far, ns_, nr_, fs_, fr_)
    k, core = links.k, links.r
    sibling = (k, 1 - core)
    f = F32

    loads = []
    for i, (src, dst) in enumerate(
        ((w1_h, w1), (wsp1_h, wsp1), (w3_h, w3), (w4_h, w4), (w5_h, w5), (w6_h, w6), (w7_h, w7), (cot_hbm, cot))
    ):
        loads.append(pltpu.make_async_copy(src, dst, load_sem.at[i]))
    own, swaps = [], []
    for at, (m, src) in enumerate(zip(sets, (img_b, img_s))):
        part = m.rows // 2
        for c in range(m.count):
            i = m.crop0 + c
            place = img.at[span(m.row0 + c * m.rows + core * part, part)]
            own.append(
                pltpu.make_async_copy(
                    src.at[span((core * m.count + c) * part, part)], place, img_sem.at[i]
                )
            )
            swaps.append(
                pltpu.make_async_remote_copy(
                    src_ref=src.at[span(((1 - core) * m.count + c) * part, part)],
                    dst_ref=place,
                    send_sem=img_send.at[i],
                    recv_sem=img_recv.at[i],
                    device_id=sibling,
                    device_id_type=MESH,
                )
            )
    for copy in own:
        copy.start()
    for copy in loads:
        copy.start()
    links.greet()
    for copy in swaps:
        copy.start()

    out_copies = []

    def put(src, dst):
        copy = pltpu.make_async_copy(src, dst, out_sem.at[len(out_copies)])
        copy.start()
        out_copies.append(copy)

    for ref in (cs, cm, ck):
        ref[...] = jnp.zeros(ref.shape, f)
    for block in blocks:
        block[...] = jnp.zeros(block.shape, f)
    h1[0:16, :] = jnp.zeros((16, 3 * c3), BF16)
    for m in sets:
        for c in range(m.count):
            at = m.guard0 + c * m.guard + m.rows
            h1[at : at + 16, :] = jnp.zeros((16, 3 * c3), BF16)

    def near_tallies():
        return [near[0][i, 16:24, 0:1] for i in range(links.wide)]

    def far_tallies():
        return [far[0][i, 16:24, 0:1] for i in range(links.outers)]

    def meet_near(i, scale):
        links.wait_near(i)
        sums, spread, n = fold_moments(near[i], near_tallies(), links.wide, scale)
        place = far[i].at[links.outer]
        place[0:8, :] = sums
        place[8:16, :] = spread
        if i == 0:
            place[16:24, :] = jnp.broadcast_to(n, (8, near[0].shape[2]))
        links.send_far(i)

    def meet_far(i, scale, table, width):
        links.wait_far(i)
        sums, spread, n = fold_moments(far[i], far_tallies(), links.outers, scale)
        mean = sums / (n * scale)
        inverse = lax.rsqrt(spread / (n * scale) + EPS)
        unpack(table, 0, mean, width)
        unpack(table, 2, inverse, width)
        if i == 0:
            tally_v[...] = jnp.broadcast_to(n, (8, 128))

    loads[0].wait()
    for copy in own:
        copy.wait()
    for copy in swaps:
        copy.wait_recv()
    for m in sets:

        def pair(p, m=m):
            r = m.row0 + p * 2 * m.rows
            z1[span(r, 2 * m.rows), :] = mm(img[span(r, 2 * m.rows), :], w1[...])
            for j in range(2):
                crop_stats(z1, r + j * m.rows, m.rows, m.rows // 2, c3, m.edge, 16, m.pixels, m.crop0 + 2 * p + j, cs, cm)

        repeat(m.count // 2, pair)
    local_moments(blocks[0], cs, cm, wcol, c3, 1.0, True)
    links.send_near(0, blocks[0])
    put(img, o_img)
    put(z1, o_z1)
    loads[1].wait()
    meet_near(0, 1.0)
    meet_far(0, 1.0, st1, c3)

    for m in sets:

        def pair(p, m=m):
            r = m.row0 + p * 2 * m.rows
            g = m.guard0 + p * 2 * m.guard
            for j in range(2):
                crop = m.crop0 + 2 * p + j
                mean = by_view(wv, crop, st1[0:2, :])
                scale = by_view(wv, crop, st1[2:4, :]) * norms1[0:1, 0:c3]
                shift = norms1[1:2, 0:c3]
                step = m.rows // 2
                mask = keep(step, c3, 16, m.edge)

                def tile(i):
                    z = z1[span(r + j * m.rows + i * step, step), :]
                    h = jnp.where(mask, act((z - mean) * scale + shift), 0.0)
                    rows = span(g + j * m.guard + i * step, step)
                    h1[rows, 0:c3] = pltpu.roll(h, 1, 0).astype(BF16)
                    h1[rows, c3 : 2 * c3] = h.astype(BF16)
                    h1[rows, 2 * c3 : 3 * c3] = pltpu.roll(h, step - 1, 0).astype(BF16)

                repeat(2, tile)
            size = 2 * m.rows + 16
            z = mm(h1[span(g - 16, size), :], wsp1[0]) + mm(h1[span(g, size), :], wsp1[1])
            z = z + mm(h1[span(g + 16, size), :], wsp1[2])
            z2[span(r, m.rows), :] = z[0 : m.rows]
            z2[span(r + m.rows, m.rows), :] = z[m.guard : m.guard + m.rows]
            for j in range(2):
                crop_stats(z2, r + j * m.rows, m.rows, m.rows // 2, c3, m.edge, 16, m.pixels, m.crop0 + 2 * p + j, cs, cm)

        repeat(m.count // 2, pair)
    local_moments(blocks[1], cs, cm, wcol, c3, 1.0)
    links.send_near(1, blocks[1])
    put(h1, o_h1)
    put(z2, o_z2)
    loads[2].wait()
    meet_near(1, 1.0)
    meet_far(1, 1.0, st2, c3)

    for m in sets:

        def pair(p, m=m):
            r = m.row0 + p * 2 * m.rows
            for j in range(2):
                crop = m.crop0 + 2 * p + j
                mean = by_view(wv, crop, st2[0:2, :])
                scale = by_view(wv, crop, st2[2:4, :]) * norms1[0:1, c3 : 2 * c3]
                shift = norms1[1:2, c3 : 2 * c3]
                step = m.rows // 2

                def tile(i):
                    rows = span(r + j * m.rows + i * step, step)
                    h2[rows, :] = act((z2[rows, :] - mean) * scale + shift).astype(BF16)

                repeat(2, tile)
            zt[0 : 2 * m.rows, :] = mm(h2[span(r, 2 * m.rows), :], w3[...])
            for j in range(2):
                crop_stats(zt, j * m.rows, m.rows, 32, cin, m.edge, 16, m.pixels, m.crop0 + 2 * p + j, cs, cm)

        repeat(m.count // 2, pair)
    local_moments(blocks[2], cs, cm, wcol, cin, 1.0)
    links.send_near(2, blocks[2])
    put(h2, o_h2)
    loads[3].wait()
    meet_near(2, 1.0)
    meet_far(2, 1.0, st3, cin)

    for m in sets:

        def pair(p, m=m):
            r = m.row0 + p * 2 * m.rows
            zt[0 : 2 * m.rows, :] = mm(h2[span(r, 2 * m.rows), :], w3[...])
            for j in range(2):
                crop = m.crop0 + 2 * p + j
                mean = by_view(wv, crop, st3[0:2, :])
                scale = by_view(wv, crop, st3[2:4, :]) * norms1[0:1, 2 * c3 :]
                shift = norms1[1:2, 2 * c3 :]

                def tile(i):
                    here = span(j * m.rows + i * 32, 32)
                    rows = span(r + j * m.rows + i * 32, 32)
                    u = (zt[here, :] - mean) * scale + shift + img[rows, :].astype(f)
                    b = act(u)
                    blk[rows, :] = b.astype(BF16)
                    for q in range(cin // 128):
                        eb[q, span(j * m.rows // 2 + i * 16, 16), :] = b[0:16, q * 128 : (q + 1) * 128]

                repeat(m.rows // 32, tile)
            for q in range(cin // 128):
                picked = [eb[q, pl.ds(i * 16, 8, stride=2), :] for i in range(2 * m.half)]
                xe[span(m.out0 + p * 2 * m.out, 2 * m.out), q * 128 : (q + 1) * 128] = jnp.concatenate(
                    picked, axis=0
                ).astype(BF16)
            z4[span(r, 2 * m.rows), :] = mm(blk[span(r, 2 * m.rows), :], w4[...])
            for j in range(2):
                crop_stats(z4, r + j * m.rows, m.rows, 32, c4, m.edge, 16, m.pixels, m.crop0 + 2 * p + j, cs, cm)

        repeat(m.count // 2, pair)
    local_moments(blocks[3], cs, cm, wcol, c4, 1.0)
    links.send_near(3, blocks[3])
    put(blk, o_blk)
    put(z4, o_z4)
    put(xe, o_xe)
    loads[6].wait()

    def wide_product(a, w, z):
        def columns(n):
            cols = pl.ds(pl.multiple_of(n * 512, 512), 512)
            z[:, cols] = mm(a[...], w[:, cols])

        repeat(cout // 512, columns)

    def wide_stats(z):
        for m in sets:

            def crop_(c, m=m):
                def columns(n):
                    crop_stats(
                        z, m.out0 + c * m.out, m.out, m.out, 512, m.half, 8, m.half * m.half,
                        m.crop0 + c, cs, cm, n * 512,
                    )

                repeat(cout // 512, columns)

            repeat(m.count, crop_)

    wide_product(xe, w7, z7)
    meet_near(3, 1.0)
    wide_stats(z7)
    local_moments(blocks[4], cs, cm, wcol, cout, 0.25)
    links.send_near(4, blocks[4])
    meet_far(3, 1.0, st4, c4)

    loads[4].wait()
    lots = c4 // 128
    hp[:, 0:24, :] = jnp.zeros((lots, 24, 128), f)
    for m in sets:

        def pair(p, m=m):
            r = m.row0 + p * 2 * m.rows
            for j in range(2):
                crop = m.crop0 + 2 * p + j
                mean = by_view(wv, crop, st4[0:2, :])
                scale = by_view(wv, crop, st4[2:4, :]) * norms2[0:1, 0:c4]
                shift = norms2[1:2, 0:c4]
                mask = keep(32, c4, 16, m.edge)
                base = 24 + j * m.guard
                hp[:, base + m.rows : base + m.guard, :] = jnp.zeros((lots, 16, 128), f)

                def tile(i):
                    z = z4[span(r + j * m.rows + i * 32, 32), :]
                    h = jnp.where(mask, act((z - mean) * scale + shift), 0.0)
                    for q in range(lots):
                        hp[q, span(base + i * 32, 32, 8), :] = h[:, q * 128 : (q + 1) * 128]

                repeat(m.rows // 32, tile)
            for a in range(3):
                for b in range(3):
                    for q in range(lots):
                        picked = []
                        for j in range(2):
                            for i in range(m.half):
                                at = 24 + j * m.guard + (2 * i + a - 1) * 16 + b - 1
                                picked.append(hp[q, pl.ds(at, 8, stride=2), :])
                        tap = (3 * a + b) * c4 + q * 128
                        x5[span(m.out0 + p * 2 * m.out, 2 * m.out), tap : tap + 128] = jnp.concatenate(
                            picked, axis=0
                        ).astype(BF16)

        repeat(m.count // 2, pair)
    z5[...] = jnp.zeros(z5.shape, f)

    def taps(t):
        part = pl.ds(pl.multiple_of(t * 3 * c4, 128), 3 * c4)
        z5[...] += mm(x5[:, part], w5[part, :])

    repeat(3, taps)
    for m in sets:

        def crop_(c, m=m):
            crop_stats(z5, m.out0 + c * m.out, m.out, m.out, c4, m.half, 8, m.half * m.half, m.crop0 + c, cs, cm)

        repeat(m.count, crop_)
    local_moments(blocks[5], cs, cm, wcol, c4, 0.25)
    links.send_near(5, blocks[5])
    put(x5, o_x5)
    put(z5, o_z5)
    meet_near(4, 0.25)
    meet_near(5, 0.25)
    meet_far(4, 0.25, st7, cout)
    meet_far(5, 0.25, st5, c4)

    loads[5].wait()
    for m in sets:

        def pair(p, m=m):
            o = m.out0 + p * 2 * m.out
            halves = []
            for j in range(2):
                crop = m.crop0 + 2 * p + j
                mean = by_view(wv, crop, st5[0:2, :])
                scale = by_view(wv, crop, st5[2:4, :]) * norms2[0:1, c4 : 2 * c4]
                z = z5[span(o + j * m.out, m.out, 8), :]
                halves.append(act((z - mean) * scale + norms2[1:2, c4 : 2 * c4]))
            h5[span(o, 2 * m.out), :] = jnp.concatenate(halves, axis=0).astype(BF16)

        repeat(m.count // 2, pair)
    wide_product(h5, w6, z6)
    wide_stats(z6)
    local_moments(blocks[6], cs, cm, wcol, cout, 0.25)
    links.send_near(6, blocks[6])
    put(h5, o_h5)
    loads[7].wait()
    meet_near(6, 0.25)
    meet_far(6, 0.25, st6, cout)

    out_copies[6].wait()
    g6, g7 = 2 * c4, 2 * c4 + cout
    lanes = 512
    for m in sets:

        def pair(p, m=m):
            o = m.out0 + p * 2 * m.out

            def columns(n):
                cols = pl.ds(pl.multiple_of(n * lanes, lanes), lanes)
                cols6 = pl.ds(pl.multiple_of(g6 + n * lanes, lanes), lanes)
                cols7 = pl.ds(pl.multiple_of(g7 + n * lanes, lanes), lanes)
                c = cot[span(o, 2 * m.out), cols].astype(f)
                mask = keep(m.out, lanes, 8, m.half)
                found = []
                for j in range(2):
                    crop = m.crop0 + 2 * p + j
                    rows = span(o + j * m.out, m.out, 8)
                    n6 = (z6[rows, cols] - by_view(wv, crop, st6[0:2, cols])) * by_view(wv, crop, st6[2:4, cols])
                    n7 = (z7[rows, cols] - by_view(wv, crop, st7[0:2, cols])) * by_view(wv, crop, st7[2:4, cols])
                    u = n6 * norms2[0:1, cols6] + norms2[1:2, cols6] + n7 * norms2[0:1, cols7] + norms2[1:2, cols7]
                    a, slope = act_both(u)
                    found.append(a)
                    up = jnp.where(mask, slope * c[j * m.out : (j + 1) * m.out], 0.0)
                    z4[span(n * outs + o + j * m.out, m.out, 8), :] = up
                    for to, part in ((cs, up), (cm, up * n6), (ck, up * n7)):
                        to[pl.ds(crop, 1), cols] = jnp.sum(tile_sum(part), axis=0, keepdims=True)
                w6[span(o, 2 * m.out), cols] = jnp.concatenate(found, axis=0).astype(BF16)

            repeat(cout // lanes, columns)

        repeat(m.count // 2, pair)
    local_sums(blocks[7], (cs, cm, ck), wcol, cout)
    links.send_near(7, blocks[7])
    put(w6.at[0:outs], o_res)
    links.wait_near(7)
    far[7][links.outer] = fold_sums(near[7], links.wide)
    links.send_far(7)
    links.wait_far(7)
    sums = fold_sums(far[7], links.outers)
    for t in range(3):
        unpack(sq, 2 * t, sums[8 * t : 8 * t + 8], cout)

    for m in sets:

        def pair(p, m=m):
            o = m.out0 + p * 2 * m.out

            def columns(n):
                cols = pl.ds(pl.multiple_of(n * lanes, lanes), lanes)
                mask = keep(m.out, lanes, 8, m.half)
                got6, got7 = [], []
                for j in range(2):
                    crop = m.crop0 + 2 * p + j
                    rows = span(o + j * m.out, m.out, 8)
                    up = z4[span(n * outs + o + j * m.out, m.out, 8), :]
                    over = wv[0, crop] * (4.0 / tally_v[0:1, 0:1]) + wv[1, crop] * (4.0 / tally_v[1:2, 0:1])
                    level = by_view(wv, crop, sq[0:2, cols]) * over
                    for got, z, st, at, t in ((got6, z6, st6, g6, 2), (got7, z7, st7, g7, 4)):
                        inv = by_view(wv, crop, st[2:4, cols])
                        gain = inv * norms2[0:1, pl.ds(pl.multiple_of(at + n * lanes, lanes), lanes)]
                        tilt = by_view(wv, crop, sq[t : t + 2, cols]) * over
                        centered = (z[rows, cols] - by_view(wv, crop, st[0:2, cols])) * inv
                        got.append(jnp.where(mask, gain * (up - level - centered * tilt), 0.0))
                w7[span(o, 2 * m.out), cols] = jnp.concatenate(got6, axis=0).astype(BF16)
                w7[span(cin // 2 + o, 2 * m.out), cols] = jnp.concatenate(got7, axis=0).astype(BF16)

            repeat(cout // lanes, columns)

        repeat(m.count // 2, pair)
    put(w7.at[0:outs], o_d6)
    put(w7.at[cin // 2 : cin // 2 + outs], o_d7)
    for src, dst in (
        (st1, o_st1), (st2, o_st2), (st3, o_st3), (st4, o_st4), (st7, o_st7), (st5, o_st5), (st6, o_st6),
        (sq, o_sq), (tally_v, o_tally),
    ):
        put(src, dst)
    links.finish()
    for copy in swaps:
        copy.wait_send()
    for i, copy in enumerate(out_copies):
        if i != 6:
            copy.wait()


def flat_rows(tensor, pitch):
    n, h, w, c = tensor.shape
    return jnp.pad(tensor, ((0, 0), (0, 0), (0, pitch - w), (0, 0))).reshape(n * h * pitch, c)


def forward(images, cots, onehot, pixels, w, norms_first, norms_second, ident):
    crops = lax.axis_size("crops")
    nb, ns = images[0].shape[0] // 2, images[1].shape[0] // 2
    sets, total, guarded, outs = geometry(nb, images[0].shape[2], ns, images[1].shape[2])
    w1, wsp1, w3, w4, w5, w6, w7 = w
    cin, c3 = w1.shape
    c4, cout = w6.shape
    smem, vmem = pl.BlockSpec(memory_space=pltpu.SMEM), pl.BlockSpec(memory_space=pltpu.VMEM)
    hbm = pl.BlockSpec(memory_space=pl.ANY)
    shape = jax.ShapeDtypeStruct
    out_shape = [
        shape((total, cin), BF16), shape((total, c3), F32), shape((guarded, 3 * c3), BF16), shape((total, c3), F32),
        shape((total, c3), BF16), shape((total, cin), BF16), shape((total, c4), F32), shape((outs, 9 * c4), BF16),
        shape((outs, c4), F32), shape((outs, c4), BF16), shape((outs, cin), BF16), shape((outs, cout), BF16),
        shape((outs, cout), BF16), shape((outs, cout), BF16),
        shape((8, c3), F32), shape((8, c3), F32), shape((8, cin), F32), shape((8, c4), F32), shape((8, cout), F32),
        shape((8, c4), F32), shape((8, cout), F32), shape((8, cout), F32), shape((8, 128), F32),
    ]
    most = 2 * sets[0].rows
    scratch = [
        pltpu.VMEM((total, cin), BF16), pltpu.VMEM((total, c3), F32), pltpu.VMEM((guarded, 3 * c3), BF16),
        pltpu.VMEM((total, c3), F32), pltpu.VMEM((total, c3), BF16), pltpu.VMEM((most, cin), F32),
        pltpu.VMEM((total, cin), BF16), pltpu.VMEM((cin // 128, most // 2, 128), F32), pltpu.VMEM((total, c4), F32),
        pltpu.VMEM((outs, cin), BF16), pltpu.VMEM((outs, cout), F32), pltpu.VMEM((c4 // 128, 24 + 2 * sets[0].guard, 128), F32),
        pltpu.VMEM((outs, 9 * c4), BF16), pltpu.VMEM((outs, c4), F32),
        pltpu.VMEM((outs, c4), BF16), pltpu.VMEM((outs, cout), F32), pltpu.VMEM((outs, cout), BF16),
    ]
    scratch += [pltpu.VMEM(t.shape, BF16) for t in w]
    scratch += [pltpu.VMEM((16, cout), F32)] * 3
    scratch += [pltpu.VMEM((8, n), F32) for n in (c3, c3, cin, c4, cout, c4, cout, cout, 128)]
    scratch += exchange_shapes(FWD_WIDTHS, (3, 2, 2, 2, 2, 2, 2, 3), crops)
    scratch += [
        pltpu.SemaphoreType.DMA((8,)), pltpu.SemaphoreType.DMA((nb + ns,)), pltpu.SemaphoreType.DMA((nb + ns,)),
        pltpu.SemaphoreType.DMA((nb + ns,)), pltpu.SemaphoreType.DMA((23,)),
    ]
    rows = jnp.concatenate([onehot, pixels[None, :]], axis=0)
    wide = jnp.pad(rows, ((0, 0), (0, 16 - rows.shape[1])), constant_values=0.0)
    wide = wide.at[2, rows.shape[1] :].set(1.0)
    wcol = jnp.pad(wide.T, ((0, 0), (0, 125)))
    got = pl.pallas_call(
        functools.partial(forward_kernel, sets, total, guarded, outs, crops, (c3, cin, c4, cout)),
        out_shape=out_shape,
        in_specs=[smem, vmem, vmem, vmem] + [hbm] * 10,
        out_specs=[hbm] * len(out_shape),
        scratch_shapes=scratch,
        compiler_params=pltpu.CompilerParams(
            collective_id=ident, has_side_effects=True, vmem_limit_bytes=63 * 1024 * 1024
        ),
        name="forward",
    )(
        onehot, wcol, norms_first, norms_second,
        flat_rows(images[0], 16), flat_rows(images[1], 16),
        jnp.concatenate([flat_rows(t, 8) for t in cots], axis=0), *w,
    )
    return sets, got


def gelu_tanh(v):
    return jax.nn.gelu(v, approximate=True)


def gelu_back(tensor, upstream):
    return jax.vjp(gelu_tanh, tensor)[1](upstream)[0]


def views_onehot(labels):
    return (labels[None, :] == jnp.arange(2)[:, None]).astype(F32)


def crop_sums(tensor):
    return jnp.sum(tensor, axis=(1, 2))


def view_sums(onehot, percrop):
    return jnp.dot(onehot, percrop, precision=HIGH)


def crop_table(onehot, table):
    return jnp.dot(onehot.T, table, precision=HIGH)[:, None, None, :]


def project(tensor, weight):
    return jnp.dot(tensor, weight, preferred_element_type=F32)


def project_back(gradient, weight):
    return lax.dot_general(
        gradient, weight, (((3,), (1,)), ((), ())), preferred_element_type=F32
    )


def weight_grad(tensors, gradients):
    return sum(
        lax.dot_general(
            t, g, (((0, 1, 2), (0, 1, 2)), ((), ())), preferred_element_type=F32
        )
        for t, g in zip(tensors, gradients)
    ).astype(BF16)


def convolve(tensor, kernel, stride):
    return lax.conv_general_dilated(
        tensor,
        kernel,
        (stride, stride),
        ((1, 1), (1, 1)),
        dimension_numbers=("NHWC", "HWIO", "NHWC"),
        preferred_element_type=F32,
    )


def convolve_back(delta, kernel, stride):
    flipped = jnp.swapaxes(kernel[::-1, ::-1], 2, 3)
    high = stride
    return lax.conv_general_dilated(
        delta,
        flipped,
        (1, 1),
        ((1, high), (1, high)),
        lhs_dilation=(stride, stride),
        dimension_numbers=("NHWC", "HWIO", "NHWC"),
        preferred_element_type=F32,
    )


def kernel_grad(tensors, deltas, stride):
    high = 2 - stride
    total = sum(
        lax.conv_general_dilated(
            t,
            d,
            (1, 1),
            ((1, high), (1, high)),
            rhs_dilation=(stride, stride),
            dimension_numbers=("CHWN", "IHWO", "HWNC"),
            preferred_element_type=F32,
        )
        for t, d in zip(tensors, deltas)
    )
    return total.astype(BF16).reshape(-1, total.shape[-1])


def pieces_of(norms, widths):
    pieces, anchor = [], 0
    for width in widths:
        pieces.append((norms[0, anchor : anchor + width], norms[1, anchor : anchor + width]))
        anchor += width
    return pieces


def moments(pairs, onehots, ident):
    blocks = []
    for pair in pairs:
        tally = sum(
            jnp.sum(onehots[k], 1) * (pair[k].shape[1] * pair[k].shape[2]) for k in range(2)
        )[:, None]
        sums = sum(view_sums(onehots[k], crop_sums(pair[k])) for k in range(2))
        mean = sums / jnp.maximum(tally, 1.0)
        spread = sum(
            view_sums(
                onehots[k], crop_sums(jnp.square(pair[k] - crop_table(onehots[k], mean)))
            )
            for k in range(2)
        )
        wide = jnp.broadcast_to(tally, sums.shape)
        blocks.append(jnp.concatenate([sums, spread, wide, jnp.zeros_like(wide)], axis=0))
    got = exchange(jnp.concatenate(blocks, axis=1), True, ident)
    outs, anchor = [], 0
    for pair in pairs:
        width = pair[0].shape[3]
        part = got[:, anchor : anchor + width]
        outs.append((part[0:2], part[2:4], part[4:6]))
        anchor += width
    return outs


def apply_norm(linear, onehots, moment, piece):
    centered = [
        (linear[k] - crop_table(onehots[k], moment[0])) * crop_table(onehots[k], moment[1])
        for k in range(2)
    ]
    return centered, [t * piece[0] + piece[1] for t in centered]


def norm_sums(upstream, centereds, onehots, ident):
    rows = [sum(view_sums(onehots[k], crop_sums(upstream[k])) for k in range(2))]
    for centered in centereds:
        rows.append(
            sum(view_sums(onehots[k], crop_sums(upstream[k] * centered[k])) for k in range(2))
        )
    block = jnp.concatenate(rows, axis=0)
    block = jnp.pad(block, ((0, 8 - block.shape[0]), (0, 0)))
    got = exchange(block, False, ident)
    return [(got[0:2], got[2 * j + 2 : 2 * j + 4]) for j in range(len(centereds))]


def norm_grad(upstream, centered, onehots, moment, gain, sums):
    inverse, tally = moment[1], moment[2]
    return [
        (
            gain
            * crop_table(onehots[k], inverse)
            * (
                upstream[k]
                - crop_table(onehots[k], sums[0] / tally)
                - centered[k] * crop_table(onehots[k], sums[1] / tally)
            )
        ).astype(BF16)
        for k in range(2)
    ]


def swap_in(tensor):
    return lax.all_to_all(tensor, "rows", split_axis=0, concat_axis=1, tiled=True)


def swap_out(tensor):
    return lax.all_to_all(tensor, "rows", split_axis=1, concat_axis=0, tiled=True)


def shards(
    image_big,
    image_small,
    view_big,
    view_small,
    inner_first,
    spatial_first,
    outer_first,
    norms_first,
    inner_second,
    spatial_second,
    outer_second,
    skip_second,
    norms_second,
    cotangent_big,
    cotangent_small,
):
    two = range(2)
    splits, position = lax.axis_size("rows"), lax.axis_index("rows")
    onehots = [
        views_onehot(
            lax.dynamic_slice_in_dim(
                labels, position * (labels.shape[0] // splits), labels.shape[0] // splits
            )
        )
        for labels in (view_big, view_small)
    ]
    n1 = pieces_of(norms_first, (inner_first.shape[1], spatial_first.shape[3], outer_first.shape[1]))
    n2 = pieces_of(
        norms_second,
        (inner_second.shape[1], spatial_second.shape[3], outer_second.shape[1], skip_second.shape[1]),
    )

    onehot = jnp.concatenate(onehots, axis=1)
    nb, ns = image_big.shape[0] // splits, image_small.shape[0] // splits
    pixels = jnp.concatenate(
        [
            jnp.full((nb,), float(image_big.shape[2] ** 2), F32),
            jnp.full((ns,), float(image_small.shape[2] ** 2), F32),
        ]
    )
    c3, c4 = inner_first.shape[1], inner_second.shape[1]
    sets, got = forward(
        [image_big, image_small],
        [cotangent_big, cotangent_small],
        onehot,
        pixels,
        [
            inner_first,
            spatial_first.reshape(3, 3 * c3, c3),
            outer_first,
            inner_second,
            spatial_second.reshape(9 * c4, c4),
            outer_second,
            skip_second,
        ],
        norms_first,
        norms_second,
        0,
    )

    def maps(t):
        return [
            t[m.row0 : m.row0 + m.count * m.rows].reshape(m.count, m.edge, 16, -1)[:, :, : m.edge]
            for m in sets
        ]

    def halves(t):
        return [
            t[m.out0 : m.out0 + m.count * m.out].reshape(m.count, m.half, 8, -1)[:, :, : m.half]
            for m in sets
        ]

    (
        f_img, f_z1, f_h1, f_z2, f_h2, f_blk, f_z4, f_x5, f_z5, f_h5, f_xe, f_res, f_d6, f_d7,
        f_st1, f_st2, f_st3, f_st4, f_st7, f_st5, f_st6, f_sq, f_n,
    ) = got
    tally = f_n[0:2, 0:1]

    def mom(st, scale=1.0):
        return (st[0:2], st[2:4], tally * scale)

    m1, m2, m3, m4 = mom(f_st1), mom(f_st2), mom(f_st3), mom(f_st4)
    m5 = mom(f_st5, 0.25)
    images, z1, z2, h2, block, z4 = map(maps, (f_img, f_z1, f_z2, f_h2, f_blk, f_z4))
    z5, h5, results, d6, d7 = map(halves, (f_z5, f_h5, f_res, f_d6, f_d7))
    c1, u1 = apply_norm(z1, onehots, m1, n1[0])
    h1 = [gelu_tanh(t).astype(BF16) for t in u1]
    c2, u2 = apply_norm(z2, onehots, m2, n1[1])
    z3 = [project(t, outer_first) for t in h2]
    c3_, u3 = apply_norm(z3, onehots, m3, n1[2])
    mixed1 = [u3[k] + images[k].astype(F32) for k in two]
    c4_, u4 = apply_norm(z4, onehots, m4, n2[0])
    h4 = [gelu_tanh(t).astype(BF16) for t in u4]
    c5, u5 = apply_norm(z5, onehots, m5, n2[1])
    s6, s7 = (f_sq[0:2], f_sq[2:4]), (f_sq[0:2], f_sq[4:6])
    g_outer2 = weight_grad(h5, d6)
    picked = [
        lax.conv_general_dilated(
            block[k],
            d7[k],
            (1, 1),
            ((0, -1), (0, -1)),
            rhs_dilation=(2, 2),
            dimension_numbers=("CHWN", "IHWO", "HWNC"),
            preferred_element_type=F32,
        )[0, 0]
        for k in two
    ]
    g_skip = (picked[0] + picked[1]).astype(BF16)
    q5 = [gelu_back(u5[k], project_back(d6[k], outer_second)) for k in two]
    (s5,) = norm_sums(q5, [c5], onehots, 7)
    d5 = norm_grad(q5, c5, onehots, m5, n2[1][0], s5)
    g_spatial2 = kernel_grad(h4, d5, 2)
    q4 = [gelu_back(u4[k], convolve_back(d5[k], spatial_second, 2)) for k in two]
    (s4,) = norm_sums(q4, [c4_], onehots, 8)
    d4 = norm_grad(q4, c4_, onehots, m4, n2[0][0], s4)
    g_inner2 = weight_grad(block, d4)
    moved = [
        (
            project_back(d4[k], inner_second)
            + lax.pad(
                project_back(d7[k], skip_second),
                jnp.float32(0),
                ((0, 0, 0), (0, 1, 1), (0, 1, 1), (0, 0, 0)),
            )
        ).astype(BF16)
        for k in two
    ]
    up1 = [gelu_back(mixed1[k], moved[k].astype(F32)) for k in two]
    (s3,) = norm_sums(up1, [c3_], onehots, 9)
    d3 = norm_grad(up1, c3_, onehots, m3, n1[2][0], s3)
    g_outer1 = weight_grad(h2, d3)
    q2 = [gelu_back(u2[k], project_back(d3[k], outer_first)) for k in two]
    (s2,) = norm_sums(q2, [c2], onehots, 10)
    d2 = norm_grad(q2, c2, onehots, m2, n1[1][0], s2)
    g_spatial1 = kernel_grad(h1, d2, 1)
    q1 = [gelu_back(u1[k], convolve_back(d2[k], spatial_first, 1)) for k in two]
    (s1,) = norm_sums(q1, [c1], onehots, 11)
    d1 = norm_grad(q1, c1, onehots, m1, n1[0][0], s1)
    g_inner1 = weight_grad(images, d1)
    gradients = [
        swap_out((up1[k] + project_back(d1[k], inner_first)).astype(BF16)) for k in two
    ]

    def both(pairs):
        return jnp.stack(
            [
                jnp.concatenate([jnp.sum(p[1], 0) for p in pairs]),
                jnp.concatenate([jnp.sum(p[0], 0) for p in pairs]),
            ]
        )

    shared = share_all(
        [g_skip, g_spatial2, g_outer2, g_inner2, g_spatial1, g_outer1, g_inner1], 12
    )
    g_skip, g_spatial2, g_outer2, g_inner2, g_spatial1, g_outer1, g_inner1 = [
        t.astype(F32) for t in shared
    ]
    return (
        results[0],
        results[1],
        gradients[0],
        gradients[1],
        g_inner1,
        g_spatial1.reshape(spatial_first.shape),
        g_outer1,
        both((s1, s2, s3)),
        g_inner2,
        g_spatial2.reshape(spatial_second.shape),
        g_outer2,
        g_skip,
        both((s4, s5, s6, s7)),
    )


def solution(mesh):
    maps = P("crops", "rows", None, None)
    whole = P(("crops", "rows"), None, None, None)
    in_specs = (maps, maps, P("crops"), P("crops")) + (P(),) * 9 + (whole, whole)
    out_specs = (whole, whole, maps, maps) + (P(),) * 9
    return jax.shard_map(shards, mesh=mesh, in_specs=in_specs, out_specs=out_specs, check_vma=False)
```

```python
import functools

import jax
import jax.numpy as jnp
from jax import lax
from jax.experimental import pallas as pl
from jax.experimental.pallas import tpu as pltpu
from jax.sharding import PartitionSpec as P

HIGH = lax.Precision.HIGHEST
EPS = 1e-05
MESH = pl.DeviceIdType.MESH
F32 = jnp.float32
BF16 = jnp.bfloat16


def share_plan(shapes):
    chunks = []
    for at, (height, width) in enumerate(shapes):
        half = width // 2
        pieces = 1
        while half % (pieces * 2) == 0 and (half // pieces) * height > 600000 and half // pieces > 256:
            pieces *= 2
        cuts = 1
        while height // cuts * (half // pieces) > 600000 and height % (16 * 16 * (cuts + 1)) == 0:
            cuts += 1
        if height == 4608:
            cuts = 3
        for c in range(cuts):
            for p in range(pieces):
                chunks.append((at, c * (height // cuts), height // cuts, p * (half // pieces), half // pieces))
    return chunks


def share_kernel(shapes, chunks, bits, *refs):
    count, n = len(shapes), len(chunks)
    ins, outs = refs[:count], refs[count : 2 * count]
    acc = refs[2 * count : 2 * count + n]
    recv0 = refs[2 * count + n : 2 * count + 2 * n]
    recvs = refs[2 * count + 2 * n : 2 * count + 3 * n]
    send_sem, recv_sem = refs[2 * count + 3 * n], refs[2 * count + 3 * n + 1]
    k, core = lax.axis_index("crops"), lax.axis_index("rows")
    digit = [lax.rem(k // (1 << b), 2) for b in range(bits)]
    orders = [list(range(bits)), list(range(bits))]
    if bits >= 2:
        orders[1][0], orders[1][1] = 1, 0

    def stage_bit(s):
        a, b = orders[0][s], orders[1][s]
        if a == b:
            mine, step = digit[a], 1 << a
        else:
            mine = digit[a] * (1 - core) + digit[b] * core
            step = (1 << a) * (1 - core) + (1 << b) * core
        return mine, k + step * (1 - 2 * mine)

    stages = [stage_bit(s) for s in range(bits)]
    sibling = (k, 1 - core)
    barrier = pltpu.get_barrier_semaphore()
    pl.semaphore_signal(barrier, inc=1, device_id=sibling, device_id_type=MESH)
    for b in range(bits):
        peer = (k + (1 << b) * (1 - 2 * digit[b]), core)
        pl.semaphore_signal(barrier, inc=1, device_id=peer, device_id_type=MESH)
    pl.semaphore_wait(barrier, bits + 1)

    regions, kinds, slots = [], [], []
    for at, row, height, col, width in chunks:
        start, length, region, kind, slot, used = 0, height, [], [], [], 0
        for s in range(bits):
            region.append((start, length))
            slot.append(used)
            if length % 32 == 0:
                kind.append(True)
                length //= 2
                start = start + stages[s][0] * length
            else:
                kind.append(False)
            used += length
        region.append((start, length))
        regions.append(region)
        kinds.append(kind)
        slots.append(slot)

    total = 2 * bits + 2
    live = {}

    def rows(start, length):
        if isinstance(start, int):
            return pl.ds(start, length)
        return pl.ds(pl.multiple_of(start, 16), length)

    def send(i, t, src, dst, device):
        copy = pltpu.make_async_remote_copy(
            src_ref=src,
            dst_ref=dst,
            send_sem=send_sem.at[i, t],
            recv_sem=recv_sem.at[i, t],
            device_id=device,
            device_id_type=MESH,
        )
        copy.start()
        live[i, t] = copy

    def add(dst, d0, src_a, a0, a_cols, src_b, b0, length):
        block = 16
        while length % (block * 2) == 0 and block < 64:
            block *= 2

        def step(j, carry):
            off = pl.multiple_of(j * block, 16)
            left = src_a[pl.ds(pl.multiple_of(a0 + off, 16), block), a_cols].astype(F32)
            right = src_b[pl.ds(pl.multiple_of(b0 + off, 16), block), :].astype(F32)
            dst[pl.ds(pl.multiple_of(d0 + off, 16), block), :] = (left + right).astype(BF16)
            return carry

        lax.fori_loop(0, length // block, step, 0)

    def task(i, t):
        at, row, height, col, width = chunks[i]
        half = shapes[at][1] // 2
        own = pl.ds(pl.multiple_of(core * half + col, 128), width)
        if t > 0:
            live[i, t - 1].wait_recv()
        if t == 0:
            away = pl.ds(pl.multiple_of((1 - core) * half + col, 128), width)
            send(i, t, ins[at].at[pl.ds(row, height), away], recv0[i], sibling)
            return
        if t <= bits + 1:
            if t == 1:
                add(acc[i], 0, ins[at], row, own, recv0[i], 0, height)
            else:
                s = t - 2
                start, length = regions[i][s + 1]
                if not kinds[i][s]:
                    live[i, t - 1].wait_send()
                add(acc[i], start, acc[i], start, slice(None), recvs[i], slots[i][s], length)
        if t <= bits:
            s = t - 1
            start, length = regions[i][s]
            peer = (stages[s][1], core)
            if kinds[i][s]:
                give = length // 2
                from_row = start + (1 - stages[s][0]) * give
            else:
                give, from_row = length, start
            send(
                i,
                t,
                acc[i].at[rows(from_row, give)],
                recvs[i].at[pl.ds(slots[i][s], give)],
                peer,
            )
            return
        if t == bits + 1:
            start, length = regions[i][bits]
            outs[at][pl.ds(pl.multiple_of(row + start, 16), length), own] = acc[i][rows(start, length), :]
        if t <= 2 * bits:
            s = bits - 1 - (t - bits - 1)
            start, length = regions[i][s + 1]
            if kinds[i][s]:
                place = outs[at].at[pl.ds(pl.multiple_of(row + start, 16), length), own]
                send(i, t, place, place, (stages[s][1], core))
            return
        if t == 2 * bits + 1:
            place = outs[at].at[pl.ds(row, height), own]
            send(i, t, place, place, sibling)

    def skipped(i, t):
        return bits + 1 <= t <= 2 * bits and not kinds[i][bits - 1 - (t - bits - 1)]

    class Nothing:
        def wait_recv(self):
            pass

        def wait_send(self):
            pass

    for t in range(n + total):
        for i in range(n):
            s = t - i
            if 0 <= s < total:
                task(i, s)
                if skipped(i, s):
                    live[i, s] = Nothing()
            elif s == total:
                live[i, total - 1].wait_recv()
    for i in range(n):
        for t in range(total):
            if t >= 1 and t <= bits and not kinds[i][t - 1]:
                continue
            live[i, t].wait_send()


def share_all(values, ident):
    crops = lax.axis_size("crops")
    bits = crops.bit_length() - 1
    shapes = [(v.shape[0], v.shape[1]) for v in values]
    chunks = share_plan(shapes)
    vmem = pl.BlockSpec(memory_space=pltpu.VMEM)
    acc, recv0, recvs = [], [], []
    for at, row, height, col, width in chunks:
        acc.append(pltpu.VMEM((height, width), BF16))
        recv0.append(pltpu.VMEM((height, width), BF16))
        length, used = height, 0
        for s in range(bits):
            if length % 32 == 0:
                length //= 2
            used += length
        recvs.append(pltpu.VMEM((used, width), BF16))
    total = 2 * bits + 2
    return pl.pallas_call(
        functools.partial(share_kernel, shapes, chunks, bits),
        out_shape=[jax.ShapeDtypeStruct(s, BF16) for s in shapes],
        in_specs=[vmem] * len(shapes),
        out_specs=[vmem] * len(shapes),
        scratch_shapes=acc
        + recv0
        + recvs
        + [
            pltpu.SemaphoreType.DMA((len(chunks), total)),
            pltpu.SemaphoreType.DMA((len(chunks), total)),
        ],
        compiler_params=pltpu.CompilerParams(
            collective_id=ident, has_side_effects=True, vmem_limit_bytes=60 * 1024 * 1024
        ),
        name="share",
    )(*values)


class Maps:
    def __init__(self, count, edge, row0, crop0, guard0, out0):
        self.count, self.edge = count, edge
        self.row0, self.crop0, self.guard0, self.out0 = row0, crop0, guard0, out0
        self.rows = edge * 16
        self.guard = (edge + 1) * 16
        self.half = edge // 2
        self.out = self.half * 8
        self.pixels = edge * edge


def geometry(nb, eb, ns, es):
    big = Maps(nb, eb, 0, 0, 16, 0)
    small = Maps(ns, es, nb * big.rows, nb, 16 + nb * big.guard, nb * big.out)
    total = small.row0 + ns * small.rows
    guarded = small.guard0 + ns * small.guard
    out = small.out0 + ns * small.out
    return (big, small), total, guarded, out


def al(x, m=16):
    return x if isinstance(x, int) else pl.multiple_of(x, m)


def span(start, size, m=16):
    return pl.ds(al(start, m), size)


def repeat(count, body):
    def step(i, carry):
        body(i)
        return carry

    lax.fori_loop(0, count, step, 0)


def mm(a, b):
    return jnp.dot(a, b, preferred_element_type=F32)


def mm_nt(a, b):
    return lax.dot_general(a, b, (((1,), (1,)), ((), ())), preferred_element_type=F32)


def mm_tn(a, b):
    return lax.dot_general(a, b, (((0,), (0,)), ((), ())), preferred_element_type=F32)


CA = 0.7978845608028654
CB = 0.7978845608028654 * 0.044715


def act(u):
    t = jnp.tanh(u * (CA + CB * (u * u)))
    return 0.5 * u * (1.0 + t)


def act_slope(u):
    s = u * u
    t = jnp.tanh(u * (CA + CB * s))
    rise = (0.5 * u) * (CA + (3.0 * CB) * s)
    return 0.5 * (1.0 + t) + (1.0 - t * t) * rise


def act_both(u):
    s = u * u
    t = jnp.tanh(u * (CA + CB * s))
    hu = 0.5 * u
    lift = 0.5 * (1.0 + t)
    slope = lift + (1.0 - t * t) * (hu * (CA + (3.0 * CB) * s))
    return u * lift, slope


def keep(rows, width, pitch, edge):
    place = lax.broadcasted_iota(jnp.int32, (rows, width), 0)
    return lax.rem(place, pitch) < edge


def tile_sum(x):
    return jnp.sum(x.reshape(x.shape[0] // 8, 8, x.shape[1]), axis=0)


def pieces(width):
    return (4, width // 4) if width >= 512 else (width // 128, 128)


class Links:
    def __init__(self, crops, near, far, near_s, near_r, far_s, far_r):
        self.group = 4 if crops % 4 == 0 else 1
        self.outers = crops // self.group
        self.k, self.r = lax.axis_index("crops"), lax.axis_index("rows")
        inner, self.outer = lax.rem(self.k, self.group), self.k // self.group
        self.wide = 2 * self.group
        self.me = inner * 2 + self.r
        self.peers, self.others = [], []
        for d in range(1, self.wide):
            p = lax.rem(self.me + d, self.wide)
            self.peers.append((self.outer * self.group + p // 2, lax.rem(p, 2)))
        for d in range(1, self.outers):
            self.others.append((lax.rem(self.outer + d, self.outers) * self.group + inner, self.r))
        self.near, self.far = near, far
        self.sems = (near_s, near_r, far_s, far_r)
        self.live = {}

    def greet(self, extra=()):
        barrier = pltpu.get_barrier_semaphore()
        peers = self.peers + self.others + list(extra)
        for peer in peers:
            pl.semaphore_signal(barrier, inc=1, device_id=peer, device_id_type=MESH)
        pl.semaphore_wait(barrier, len(peers))

    def send_near(self, e, block):
        self.near[e][self.me] = block[...]
        self.live[e, 0] = []
        for d, peer in enumerate(self.peers):
            copy = pltpu.make_async_remote_copy(
                src_ref=block,
                dst_ref=self.near[e].at[self.me],
                send_sem=self.sems[0].at[e, d],
                recv_sem=self.sems[1].at[e, d],
                device_id=peer,
                device_id_type=MESH,
            )
            copy.start()
            self.live[e, 0].append(copy)

    def wait_near(self, e):
        for copy in self.live[e, 0]:
            copy.wait_recv()

    def send_far(self, e):
        self.live[e, 1] = []
        place = self.far[e].at[self.outer]
        for d, peer in enumerate(self.others):
            copy = pltpu.make_async_remote_copy(
                src_ref=place,
                dst_ref=place,
                send_sem=self.sems[2].at[e, d],
                recv_sem=self.sems[3].at[e, d],
                device_id=peer,
                device_id_type=MESH,
            )
            copy.start()
            self.live[e, 1].append(copy)

    def wait_far(self, e):
        for copy in self.live[e, 1]:
            copy.wait_recv()

    def finish(self):
        for copies in self.live.values():
            for copy in copies:
                copy.wait_send()


def fold_moments(buf, tallies, count, scale):
    sums, total = buf[0, 0:8, :], tallies[0]
    for i in range(1, count):
        sums = sums + buf[i, 0:8, :]
        total = total + tallies[i]
    mean = sums / jnp.maximum(total * scale, 1.0)
    spread = None
    for i in range(count):
        n = tallies[i] * scale
        apart = buf[i, 0:8, :] / jnp.maximum(n, 1.0) - mean
        term = buf[i, 8:16, :] + n * apart * apart
        spread = term if spread is None else spread + term
    return sums, spread, total


def fold_sums(buf, count):
    total = buf[0]
    for i in range(1, count):
        total = total + buf[i]
    return total


def exchange_shapes(widths, tiles, crops):
    group = 4 if crops % 4 == 0 else 1
    outers = crops // group
    blocks, near, far = [], [], []
    for width, tile in zip(widths, tiles):
        lanes = pieces(width)[1]
        blocks.append(pltpu.VMEM((8 * tile, lanes), F32))
        near.append(pltpu.VMEM((2 * group, 8 * tile, lanes), F32))
        far.append(pltpu.VMEM((outers, 8 * tile, lanes), F32))
    e = len(widths)
    sems = [
        pltpu.SemaphoreType.DMA((e, 2 * group - 1)),
        pltpu.SemaphoreType.DMA((e, 2 * group - 1)),
        pltpu.SemaphoreType.DMA((e, max(outers - 1, 1))),
        pltpu.SemaphoreType.DMA((e, max(outers - 1, 1))),
    ]
    return blocks + near + far + sems


def take(refs, count):
    return list(refs[:count]), refs[count:]


def pack(block, tile, rows, width):
    count, lanes = pieces(width)
    for q in range(count):
        for v in range(2):
            block[tile * 8 + 2 * q + v : tile * 8 + 2 * q + v + 1, :] = rows[v][:, q * lanes : (q + 1) * lanes]


def unpack(table, row, tile, width):
    count, lanes = pieces(width)
    for q in range(count):
        table[row : row + 2, q * lanes : (q + 1) * lanes] = tile[2 * q : 2 * q + 2, :]


def crop_stats(ref, row0, rows, step, width, edge, pitch, pixels, crop, cs, cm, col0=0):
    mask = keep(step, width, pitch, edge)
    zero = jnp.zeros((8, width), F32)
    cols = pl.ds(col0, width) if isinstance(col0, int) else pl.ds(pl.multiple_of(col0, 128), width)

    def first(i, acc):
        z = ref[span(row0 + i * step, step, 8), cols]
        return acc + tile_sum(jnp.where(mask, z, 0.0))

    s = jnp.sum(lax.fori_loop(0, rows // step, first, zero), axis=0, keepdims=True)
    mean = s * (1.0 / pixels)

    def second(i, acc):
        z = ref[span(row0 + i * step, step, 8), cols]
        d = jnp.where(mask, z - mean, 0.0)
        return acc + tile_sum(d * d)

    m = jnp.sum(lax.fori_loop(0, rows // step, second, zero), axis=0, keepdims=True)
    cs[pl.ds(crop, 1), cols] = s
    cm[pl.ds(crop, 1), cols] = m


def local_moments(block, cs, cm, wcol, width, scale, tally=False):
    s, m = cs[:, 0:width], cm[:, 0:width]
    pix = wcol[:, 2:3] * scale
    mean_c = s / pix
    sums, squares, tallies = [], [], []
    for v in range(2):
        w = wcol[:, v : v + 1]
        total = jnp.sum(w * s, axis=0, keepdims=True)
        n = jnp.sum(w * pix, axis=0, keepdims=True)
        apart = mean_c - total / jnp.maximum(n, 1.0)
        squares.append(jnp.sum(w * (m + pix * apart * apart), axis=0, keepdims=True))
        sums.append(total)
        tallies.append(n)
    pack(block, 0, sums, width)
    pack(block, 1, squares, width)
    if tally:
        lanes = pieces(width)[1]
        for q in range(4):
            for v in range(2):
                block[16 + 2 * q + v : 17 + 2 * q + v, :] = jnp.broadcast_to(tallies[v], (1, lanes))


def local_sums(block, parts, wcol, width):
    for tile, part in enumerate(parts):
        s = part[:, 0:width]
        pack(block, tile, [jnp.sum(wcol[:, v : v + 1] * s, axis=0, keepdims=True) for v in range(2)], width)


def by_view(wv, crop, pair):
    return wv[0, crop] * pair[0:1, :] + wv[1, crop] * pair[1:2, :]


FWD_WIDTHS = (256, 256, 1024, 512, 2048, 512, 2048, 2048)


def forward_kernel(sets, total, guarded, outs, crops, dims, *refs):
    c3, cin, c4, cout = dims
    (
        wv, wcol, norms1, norms2,
        img_b, img_s, cot_hbm, w1_h, wsp1_h, w3_h, w4_h, w5_h, w6_h, w7_h,
    ), refs = refs[:14], refs[14:]
    (
        o_img, o_z1, o_h1, o_z2, o_h2, o_blk, o_z4, o_x5, o_z5, o_h5, o_xe, o_res, o_d6, o_d7,
        o_st1, o_st2, o_st3, o_st4, o_st7, o_st5, o_st6, o_sq, o_tally,
    ), refs = refs[:23], refs[23:]
    (
        img, z1, h1, z2, h2, zt, blk, eb, z4, xe, z7, hp, x5, z5, h5, z6, cot,
        w1, wsp1, w3, w4, w5, w6, w7, cs, cm, ck,
        st1, st2, st3, st4, st7, st5, st6, sq, tally_v,
    ), refs = refs[:36], refs[36:]
    e = len(FWD_WIDTHS)
    blocks, refs = take(refs, e)
    near, refs = take(refs, e)
    far, refs = take(refs, e)
    ns_, nr_, fs_, fr_ = refs[:4]
    load_sem, img_sem, img_send, img_recv, out_sem = refs[4:]
    links = Links(crops, near, far, ns_, nr_, fs_, fr_)
    k, core = links.k, links.r
    sibling = (k, 1 - core)
    f = F32

    loads = []
    for i, (src, dst) in enumerate(
        ((w1_h, w1), (wsp1_h, wsp1), (w3_h, w3), (w4_h, w4), (w5_h, w5), (w6_h, w6), (w7_h, w7), (cot_hbm, cot))
    ):
        loads.append(pltpu.make_async_copy(src, dst, load_sem.at[i]))
    own, swaps = [], []
    for at, (m, src) in enumerate(zip(sets, (img_b, img_s))):
        part = m.rows // 2
        for c in range(m.count):
            i = m.crop0 + c
            place = img.at[span(m.row0 + c * m.rows + core * part, part)]
            own.append(
                pltpu.make_async_copy(
                    src.at[span((core * m.count + c) * part, part)], place, img_sem.at[i]
                )
            )
            swaps.append(
                pltpu.make_async_remote_copy(
                    src_ref=src.at[span(((1 - core) * m.count + c) * part, part)],
                    dst_ref=place,
                    send_sem=img_send.at[i],
                    recv_sem=img_recv.at[i],
                    device_id=sibling,
                    device_id_type=MESH,
                )
            )
    for copy in own:
        copy.start()
    for copy in loads:
        copy.start()
    links.greet()
    for copy in swaps:
        copy.start()

    out_copies = []

    def put(src, dst):
        copy = pltpu.make_async_copy(src, dst, out_sem.at[len(out_copies)])
        copy.start()
        out_copies.append(copy)

    for ref in (cs, cm, ck):
        ref[...] = jnp.zeros(ref.shape, f)
    for block in blocks:
        block[...] = jnp.zeros(block.shape, f)
    h1[0:16, :] = jnp.zeros((16, 3 * c3), BF16)
    for m in sets:
        for c in range(m.count):
            at = m.guard0 + c * m.guard + m.rows
            h1[at : at + 16, :] = jnp.zeros((16, 3 * c3), BF16)

    def near_tallies():
        return [near[0][i, 16:24, 0:1] for i in range(links.wide)]

    def far_tallies():
        return [far[0][i, 16:24, 0:1] for i in range(links.outers)]

    def meet_near(i, scale):
        links.wait_near(i)
        sums, spread, n = fold_moments(near[i], near_tallies(), links.wide, scale)
        place = far[i].at[links.outer]
        place[0:8, :] = sums
        place[8:16, :] = spread
        if i == 0:
            place[16:24, :] = jnp.broadcast_to(n, (8, near[0].shape[2]))
        links.send_far(i)

    def meet_far(i, scale, table, width):
        links.wait_far(i)
        sums, spread, n = fold_moments(far[i], far_tallies(), links.outers, scale)
        mean = sums / (n * scale)
        inverse = lax.rsqrt(spread / (n * scale) + EPS)
        unpack(table, 0, mean, width)
        unpack(table, 2, inverse, width)
        if i == 0:
            tally_v[...] = jnp.broadcast_to(n, (8, 128))

    loads[0].wait()
    for copy in own:
        copy.wait()
    for copy in swaps:
        copy.wait_recv()
    for m in sets:

        def pair(p, m=m):
            r = m.row0 + p * 2 * m.rows
            z1[span(r, 2 * m.rows), :] = mm(img[span(r, 2 * m.rows), :], w1[...])
            for j in range(2):
                crop_stats(z1, r + j * m.rows, m.rows, m.rows // 2, c3, m.edge, 16, m.pixels, m.crop0 + 2 * p + j, cs, cm)

        repeat(m.count // 2, pair)
    local_moments(blocks[0], cs, cm, wcol, c3, 1.0, True)
    links.send_near(0, blocks[0])
    put(img, o_img)
    put(z1, o_z1)
    loads[1].wait()
    meet_near(0, 1.0)
    meet_far(0, 1.0, st1, c3)

    for m in sets:

        def pair(p, m=m):
            r = m.row0 + p * 2 * m.rows
            g = m.guard0 + p * 2 * m.guard
            for j in range(2):
                crop = m.crop0 + 2 * p + j
                mean = by_view(wv, crop, st1[0:2, :])
                scale = by_view(wv, crop, st1[2:4, :]) * norms1[0:1, 0:c3]
                shift = norms1[1:2, 0:c3]
                step = m.rows // 2
                mask = keep(step, c3, 16, m.edge)

                def tile(i):
                    z = z1[span(r + j * m.rows + i * step, step), :]
                    h = jnp.where(mask, act((z - mean) * scale + shift), 0.0)
                    rows = span(g + j * m.guard + i * step, step)
                    h1[rows, 0:c3] = pltpu.roll(h, 1, 0).astype(BF16)
                    h1[rows, c3 : 2 * c3] = h.astype(BF16)
                    h1[rows, 2 * c3 : 3 * c3] = pltpu.roll(h, step - 1, 0).astype(BF16)

                repeat(2, tile)
            size = 2 * m.rows + 16
            z = mm(h1[span(g - 16, size), :], wsp1[0]) + mm(h1[span(g, size), :], wsp1[1])
            z = z + mm(h1[span(g + 16, size), :], wsp1[2])
            z2[span(r, m.rows), :] = z[0 : m.rows]
            z2[span(r + m.rows, m.rows), :] = z[m.guard : m.guard + m.rows]
            for j in range(2):
                crop_stats(z2, r + j * m.rows, m.rows, m.rows // 2, c3, m.edge, 16, m.pixels, m.crop0 + 2 * p + j, cs, cm)

        repeat(m.count // 2, pair)
    local_moments(blocks[1], cs, cm, wcol, c3, 1.0)
    links.send_near(1, blocks[1])
    put(h1, o_h1)
    put(z2, o_z2)
    loads[2].wait()
    meet_near(1, 1.0)
    meet_far(1, 1.0, st2, c3)

    for m in sets:

        def pair(p, m=m):
            r = m.row0 + p * 2 * m.rows
            for j in range(2):
                crop = m.crop0 + 2 * p + j
                mean = by_view(wv, crop, st2[0:2, :])
                scale = by_view(wv, crop, st2[2:4, :]) * norms1[0:1, c3 : 2 * c3]
                shift = norms1[1:2, c3 : 2 * c3]
                step = m.rows // 2

                def tile(i):
                    rows = span(r + j * m.rows + i * step, step)
                    h2[rows, :] = act((z2[rows, :] - mean) * scale + shift).astype(BF16)

                repeat(2, tile)
            zt[0 : 2 * m.rows, :] = mm(h2[span(r, 2 * m.rows), :], w3[...])
            for j in range(2):
                crop_stats(zt, j * m.rows, m.rows, 32, cin, m.edge, 16, m.pixels, m.crop0 + 2 * p + j, cs, cm)

        repeat(m.count // 2, pair)
    local_moments(blocks[2], cs, cm, wcol, cin, 1.0)
    links.send_near(2, blocks[2])
    put(h2, o_h2)
    loads[3].wait()
    meet_near(2, 1.0)
    meet_far(2, 1.0, st3, cin)

    for m in sets:

        def pair(p, m=m):
            r = m.row0 + p * 2 * m.rows
            zt[0 : 2 * m.rows, :] = mm(h2[span(r, 2 * m.rows), :], w3[...])
            for j in range(2):
                crop = m.crop0 + 2 * p + j
                mean = by_view(wv, crop, st3[0:2, :])
                scale = by_view(wv, crop, st3[2:4, :]) * norms1[0:1, 2 * c3 :]
                shift = norms1[1:2, 2 * c3 :]

                def tile(i):
                    here = span(j * m.rows + i * 32, 32)
                    rows = span(r + j * m.rows + i * 32, 32)
                    u = (zt[here, :] - mean) * scale + shift + img[rows, :].astype(f)
                    b = act(u)
                    blk[rows, :] = b.astype(BF16)
                    for q in range(cin // 128):
                        eb[q, span(j * m.rows // 2 + i * 16, 16), :] = b[0:16, q * 128 : (q + 1) * 128]

                repeat(m.rows // 32, tile)
            for q in range(cin // 128):
                picked = [eb[q, pl.ds(i * 16, 8, stride=2), :] for i in range(2 * m.half)]
                xe[span(m.out0 + p * 2 * m.out, 2 * m.out), q * 128 : (q + 1) * 128] = jnp.concatenate(
                    picked, axis=0
                ).astype(BF16)
            z4[span(r, 2 * m.rows), :] = mm(blk[span(r, 2 * m.rows), :], w4[...])
            for j in range(2):
                crop_stats(z4, r + j * m.rows, m.rows, 32, c4, m.edge, 16, m.pixels, m.crop0 + 2 * p + j, cs, cm)

        repeat(m.count // 2, pair)
    local_moments(blocks[3], cs, cm, wcol, c4, 1.0)
    links.send_near(3, blocks[3])
    put(blk, o_blk)
    put(z4, o_z4)
    put(xe, o_xe)
    loads[6].wait()

    def wide_product(a, w, z):
        def columns(n):
            cols = pl.ds(pl.multiple_of(n * 512, 512), 512)
            z[:, cols] = mm(a[...], w[:, cols])

        repeat(cout // 512, columns)

    def wide_stats(z):
        for m in sets:

            def crop_(c, m=m):
                def columns(n):
                    crop_stats(
                        z, m.out0 + c * m.out, m.out, m.out, 512, m.half, 8, m.half * m.half,
                        m.crop0 + c, cs, cm, n * 512,
                    )

                repeat(cout // 512, columns)

            repeat(m.count, crop_)

    wide_product(xe, w7, z7)
    meet_near(3, 1.0)
    wide_stats(z7)
    local_moments(blocks[4], cs, cm, wcol, cout, 0.25)
    links.send_near(4, blocks[4])
    meet_far(3, 1.0, st4, c4)

    loads[4].wait()
    lots = c4 // 128
    hp[:, 0:24, :] = jnp.zeros((lots, 24, 128), f)
    for m in sets:

        def pair(p, m=m):
            r = m.row0 + p * 2 * m.rows
            for j in range(2):
                crop = m.crop0 + 2 * p + j
                mean = by_view(wv, crop, st4[0:2, :])
                scale = by_view(wv, crop, st4[2:4, :]) * norms2[0:1, 0:c4]
                shift = norms2[1:2, 0:c4]
                mask = keep(32, c4, 16, m.edge)
                base = 24 + j * m.guard
                hp[:, base + m.rows : base + m.guard, :] = jnp.zeros((lots, 16, 128), f)

                def tile(i):
                    z = z4[span(r + j * m.rows + i * 32, 32), :]
                    h = jnp.where(mask, act((z - mean) * scale + shift), 0.0)
                    for q in range(lots):
                        hp[q, span(base + i * 32, 32, 8), :] = h[:, q * 128 : (q + 1) * 128]

                repeat(m.rows // 32, tile)
            for a in range(3):
                for b in range(3):
                    for q in range(lots):
                        picked = []
                        for j in range(2):
                            for i in range(m.half):
                                at = 24 + j * m.guard + (2 * i + a - 1) * 16 + b - 1
                                picked.append(hp[q, pl.ds(at, 8, stride=2), :])
                        tap = (3 * a + b) * c4 + q * 128
                        x5[span(m.out0 + p * 2 * m.out, 2 * m.out), tap : tap + 128] = jnp.concatenate(
                            picked, axis=0
                        ).astype(BF16)

        repeat(m.count // 2, pair)
    z5[...] = jnp.zeros(z5.shape, f)

    def taps(t):
        part = pl.ds(pl.multiple_of(t * 3 * c4, 128), 3 * c4)
        z5[...] += mm(x5[:, part], w5[part, :])

    repeat(3, taps)
    for m in sets:

        def crop_(c, m=m):
            crop_stats(z5, m.out0 + c * m.out, m.out, m.out, c4, m.half, 8, m.half * m.half, m.crop0 + c, cs, cm)

        repeat(m.count, crop_)
    local_moments(blocks[5], cs, cm, wcol, c4, 0.25)
    links.send_near(5, blocks[5])
    put(x5, o_x5)
    put(z5, o_z5)
    meet_near(4, 0.25)
    meet_near(5, 0.25)
    meet_far(4, 0.25, st7, cout)
    meet_far(5, 0.25, st5, c4)

    loads[5].wait()
    for m in sets:

        def pair(p, m=m):
            o = m.out0 + p * 2 * m.out
            halves = []
            for j in range(2):
                crop = m.crop0 + 2 * p + j
                mean = by_view(wv, crop, st5[0:2, :])
                scale = by_view(wv, crop, st5[2:4, :]) * norms2[0:1, c4 : 2 * c4]
                z = z5[span(o + j * m.out, m.out, 8), :]
                halves.append(act((z - mean) * scale + norms2[1:2, c4 : 2 * c4]))
            h5[span(o, 2 * m.out), :] = jnp.concatenate(halves, axis=0).astype(BF16)

        repeat(m.count // 2, pair)
    wide_product(h5, w6, z6)
    wide_stats(z6)
    local_moments(blocks[6], cs, cm, wcol, cout, 0.25)
    links.send_near(6, blocks[6])
    put(h5, o_h5)
    loads[7].wait()
    meet_near(6, 0.25)
    meet_far(6, 0.25, st6, cout)

    out_copies[6].wait()
    g6, g7 = 2 * c4, 2 * c4 + cout
    lanes = 512
    for m in sets:

        def pair(p, m=m):
            o = m.out0 + p * 2 * m.out

            def columns(n):
                cols = pl.ds(pl.multiple_of(n * lanes, lanes), lanes)
                cols6 = pl.ds(pl.multiple_of(g6 + n * lanes, lanes), lanes)
                cols7 = pl.ds(pl.multiple_of(g7 + n * lanes, lanes), lanes)
                c = cot[span(o, 2 * m.out), cols].astype(f)
                mask = keep(m.out, lanes, 8, m.half)
                found = []
                for j in range(2):
                    crop = m.crop0 + 2 * p + j
                    rows = span(o + j * m.out, m.out, 8)
                    n6 = (z6[rows, cols] - by_view(wv, crop, st6[0:2, cols])) * by_view(wv, crop, st6[2:4, cols])
                    n7 = (z7[rows, cols] - by_view(wv, crop, st7[0:2, cols])) * by_view(wv, crop, st7[2:4, cols])
                    u = n6 * norms2[0:1, cols6] + norms2[1:2, cols6] + n7 * norms2[0:1, cols7] + norms2[1:2, cols7]
                    a, slope = act_both(u)
                    found.append(a)
                    up = jnp.where(mask, slope * c[j * m.out : (j + 1) * m.out], 0.0)
                    z4[span(n * outs + o + j * m.out, m.out, 8), :] = up
                    for to, part in ((cs, up), (cm, up * n6), (ck, up * n7)):
                        to[pl.ds(crop, 1), cols] = jnp.sum(tile_sum(part), axis=0, keepdims=True)
                w6[span(o, 2 * m.out), cols] = jnp.concatenate(found, axis=0).astype(BF16)

            repeat(cout // lanes, columns)

        repeat(m.count // 2, pair)
    local_sums(blocks[7], (cs, cm, ck), wcol, cout)
    links.send_near(7, blocks[7])
    put(w6.at[0:outs], o_res)
    links.wait_near(7)
    far[7][links.outer] = fold_sums(near[7], links.wide)
    links.send_far(7)
    links.wait_far(7)
    sums = fold_sums(far[7], links.outers)
    for t in range(3):
        unpack(sq, 2 * t, sums[8 * t : 8 * t + 8], cout)

    for m in sets:

        def pair(p, m=m):
            o = m.out0 + p * 2 * m.out

            def columns(n):
                cols = pl.ds(pl.multiple_of(n * lanes, lanes), lanes)
                mask = keep(m.out, lanes, 8, m.half)
                got6, got7 = [], []
                for j in range(2):
                    crop = m.crop0 + 2 * p + j
                    rows = span(o + j * m.out, m.out, 8)
                    up = z4[span(n * outs + o + j * m.out, m.out, 8), :]
                    over = wv[0, crop] * (4.0 / tally_v[0:1, 0:1]) + wv[1, crop] * (4.0 / tally_v[1:2, 0:1])
                    level = by_view(wv, crop, sq[0:2, cols]) * over
                    for got, z, st, at, t in ((got6, z6, st6, g6, 2), (got7, z7, st7, g7, 4)):
                        inv = by_view(wv, crop, st[2:4, cols])
                        gain = inv * norms2[0:1, pl.ds(pl.multiple_of(at + n * lanes, lanes), lanes)]
                        tilt = by_view(wv, crop, sq[t : t + 2, cols]) * over
                        centered = (z[rows, cols] - by_view(wv, crop, st[0:2, cols])) * inv
                        got.append(jnp.where(mask, gain * (up - level - centered * tilt), 0.0))
                w7[span(o, 2 * m.out), cols] = jnp.concatenate(got6, axis=0).astype(BF16)
                w7[span(cin // 2 + o, 2 * m.out), cols] = jnp.concatenate(got7, axis=0).astype(BF16)

            repeat(cout // lanes, columns)

        repeat(m.count // 2, pair)
    put(w7.at[0:outs], o_d6)
    put(w7.at[cin // 2 : cin // 2 + outs], o_d7)
    for src, dst in (
        (st1, o_st1), (st2, o_st2), (st3, o_st3), (st4, o_st4), (st7, o_st7), (st5, o_st5), (st6, o_st6),
        (sq, o_sq), (tally_v, o_tally),
    ):
        put(src, dst)
    links.finish()
    for copy in swaps:
        copy.wait_send()
    for i, copy in enumerate(out_copies):
        if i != 6:
            copy.wait()


def flat_rows(tensor, pitch):
    n, h, w, c = tensor.shape
    return jnp.pad(tensor, ((0, 0), (0, 0), (0, pitch - w), (0, 0))).reshape(n * h * pitch, c)


def forward(images, cots, onehot, pixels, w, norms_first, norms_second, ident):
    crops = lax.axis_size("crops")
    nb, ns = images[0].shape[0] // 2, images[1].shape[0] // 2
    sets, total, guarded, outs = geometry(nb, images[0].shape[2], ns, images[1].shape[2])
    w1, wsp1, w3, w4, w5, w6, w7 = w
    cin, c3 = w1.shape
    c4, cout = w6.shape
    smem, vmem = pl.BlockSpec(memory_space=pltpu.SMEM), pl.BlockSpec(memory_space=pltpu.VMEM)
    hbm = pl.BlockSpec(memory_space=pl.ANY)
    shape = jax.ShapeDtypeStruct
    out_shape = [
        shape((total, cin), BF16), shape((total, c3), F32), shape((guarded, 3 * c3), BF16), shape((total, c3), F32),
        shape((total, c3), BF16), shape((total, cin), BF16), shape((total, c4), F32), shape((outs, 9 * c4), BF16),
        shape((outs, c4), F32), shape((outs, c4), BF16), shape((outs, cin), BF16), shape((outs, cout), BF16),
        shape((outs, cout), BF16), shape((outs, cout), BF16),
        shape((8, c3), F32), shape((8, c3), F32), shape((8, cin), F32), shape((8, c4), F32), shape((8, cout), F32),
        shape((8, c4), F32), shape((8, cout), F32), shape((8, cout), F32), shape((8, 128), F32),
    ]
    most = 2 * sets[0].rows
    scratch = [
        pltpu.VMEM((total, cin), BF16), pltpu.VMEM((total, c3), F32), pltpu.VMEM((guarded, 3 * c3), BF16),
        pltpu.VMEM((total, c3), F32), pltpu.VMEM((total, c3), BF16), pltpu.VMEM((most, cin), F32),
        pltpu.VMEM((total, cin), BF16), pltpu.VMEM((cin // 128, most // 2, 128), F32), pltpu.VMEM((total, c4), F32),
        pltpu.VMEM((outs, cin), BF16), pltpu.VMEM((outs, cout), F32), pltpu.VMEM((c4 // 128, 24 + 2 * sets[0].guard, 128), F32),
        pltpu.VMEM((outs, 9 * c4), BF16), pltpu.VMEM((outs, c4), F32),
        pltpu.VMEM((outs, c4), BF16), pltpu.VMEM((outs, cout), F32), pltpu.VMEM((outs, cout), BF16),
    ]
    scratch += [pltpu.VMEM(t.shape, BF16) for t in w]
    scratch += [pltpu.VMEM((16, cout), F32)] * 3
    scratch += [pltpu.VMEM((8, n), F32) for n in (c3, c3, cin, c4, cout, c4, cout, cout, 128)]
    scratch += exchange_shapes(FWD_WIDTHS, (3, 2, 2, 2, 2, 2, 2, 3), crops)
    scratch += [
        pltpu.SemaphoreType.DMA((8,)), pltpu.SemaphoreType.DMA((nb + ns,)), pltpu.SemaphoreType.DMA((nb + ns,)),
        pltpu.SemaphoreType.DMA((nb + ns,)), pltpu.SemaphoreType.DMA((23,)),
    ]
    rows = jnp.concatenate([onehot, pixels[None, :]], axis=0)
    wide = jnp.pad(rows, ((0, 0), (0, 16 - rows.shape[1])), constant_values=0.0)
    wide = wide.at[2, rows.shape[1] :].set(1.0)
    wcol = jnp.pad(wide.T, ((0, 0), (0, 125)))
    got = pl.pallas_call(
        functools.partial(forward_kernel, sets, total, guarded, outs, crops, (c3, cin, c4, cout)),
        out_shape=out_shape,
        in_specs=[smem, vmem, vmem, vmem] + [hbm] * 10,
        out_specs=[hbm] * len(out_shape),
        scratch_shapes=scratch,
        compiler_params=pltpu.CompilerParams(
            collective_id=ident, has_side_effects=True, vmem_limit_bytes=63 * 1024 * 1024
        ),
        name="forward",
    )(
        onehot, wcol, norms_first, norms_second,
        flat_rows(images[0], 16), flat_rows(images[1], 16),
        jnp.concatenate([flat_rows(t, 8) for t in cots], axis=0), *w,
    )
    return sets, wcol, (total, guarded, outs), got


def meet_sums(links, e, width, tables, between=None):
    links.wait_near(e)
    links.far[e][links.outer] = fold_sums(links.near[e], links.wide)
    links.send_far(e)
    if between is not None:
        between()
    links.wait_far(e)
    sums = fold_sums(links.far[e], links.outers)
    for t, (table, row) in enumerate(tables):
        unpack(table, row, sums[8 * t : 8 * t + 8], width)


def share_of(wv, tally, crop, times):
    return wv[0, crop] * (times / tally[0:1, 0:1]) + wv[1, crop] * (times / tally[1:2, 0:1])


class Puts:
    def __init__(self, sem):
        self.sem, self.copies = sem, []

    def put(self, src, dst):
        copy = pltpu.make_async_copy(src, dst, self.sem.at[len(self.copies)])
        copy.start()
        self.copies.append(copy)

    def finish(self):
        for copy in self.copies:
            copy.wait()


def start_loads(pairs, sem):
    copies = [pltpu.make_async_copy(src, dst, sem.at[i]) for i, (src, dst) in enumerate(pairs)]
    for copy in copies:
        copy.start()
    return copies


def back_two_kernel(sets, total, outs, crops, dims, *refs):
    c3, cin, c4, cout = dims
    wv, wcol, norms1, norms2, st3, st4, st5, tally = refs[:8]
    sources, refs = refs[8:23], refs[23:]
    (o_up, o_g6, o_g7, o_g5, o_g4, o_s5, o_s4, o_s3), refs = refs[:8], refs[8:]
    held, refs = refs[:15], refs[15:]
    (d6, w6, z5, h5, d7, xe, w7, w5, x5, z4, w4, h2, w3, img, blk) = held
    (q5, t7, d5, pv, dh, d4, zt, bg, up, s5, s4, s3, cs, cm), refs = refs[:14], refs[14:]
    g6, g7, g5, g4 = w6, w7, w5, w4
    blocks, refs = take(refs, 3)
    near, refs = take(refs, 3)
    far, refs = take(refs, 3)
    links = Links(crops, near, far, *refs[:4])
    load_sem, out_sem, up_sem = refs[4:]
    f = F32
    loads = start_loads(list(zip(sources, held)), load_sem)
    links.greet()
    puts = Puts(out_sem)
    for ref in (cs, cm):
        ref[...] = jnp.zeros(ref.shape, f)
    for block in blocks:
        block[...] = jnp.zeros(block.shape, f)

    for i in range(3):
        loads[i].wait()
    q5[...] = mm_nt(d6[...], w6[...])
    g5at = c4
    for m in sets:

        def crop_(c, m=m):
            crop = m.crop0 + c
            rows = span(m.out0 + c * m.out, m.out, 8)
            inv = by_view(wv, crop, st5[2:4, :])
            n = (z5[rows, :] - by_view(wv, crop, st5[0:2, :])) * inv
            q = act_slope(n * norms2[0:1, g5at : 2 * c4] + norms2[1:2, g5at : 2 * c4]) * q5[rows, :]
            q5[rows, :] = q
            cs[pl.ds(crop, 1), 0:c4] = jnp.sum(tile_sum(q), axis=0, keepdims=True)
            cm[pl.ds(crop, 1), 0:c4] = jnp.sum(tile_sum(q * n), axis=0, keepdims=True)

        repeat(m.count, crop_)
    local_sums(blocks[0], (cs, cm), wcol, c4)
    links.send_near(0, blocks[0])

    loads[3].wait()

    def outer(n):
        cols = pl.ds(pl.multiple_of(n * 512, 512), 512)
        g6[:, cols] = mm_tn(h5[...], d6[:, cols]).astype(BF16)

    repeat(cout // 512, outer)
    puts.put(g6, o_g6)

    def rest():
        for i in (4, 5, 6):
            loads[i].wait()

        def shortcut(n):
            part = pl.ds(pl.multiple_of(n * 256, 256), 256)
            t7[:, part] = mm_nt(d7[...], w7[part, :])

        repeat(cin // 256, shortcut)

        def skip(n):
            cols = pl.ds(pl.multiple_of(n * 512, 512), 512)
            g7[:, cols] = mm_tn(xe[...], d7[:, cols]).astype(BF16)

        repeat(cout // 512, skip)
        puts.put(g7, o_g7)

    meet_sums(links, 0, c4, ((s5, 0), (s5, 2)), rest)

    for m in sets:

        def pair(p, m=m):
            o = m.out0 + p * 2 * m.out
            mask = keep(m.out, c4, 8, m.half)
            slots = [[], [], [], []]
            for j in range(2):
                crop = m.crop0 + 2 * p + j
                rows = span(o + j * m.out, m.out, 8)
                over = share_of(wv, tally, crop, 4.0)
                inv = by_view(wv, crop, st5[2:4, :])
                n = (z5[rows, :] - by_view(wv, crop, st5[0:2, :])) * inv
                d = (inv * norms2[0:1, g5at : 2 * c4]) * (
                    q5[rows, :] - by_view(wv, crop, s5[0:2, :]) * over - n * (by_view(wv, crop, s5[2:4, :]) * over)
                )
                d = jnp.where(mask, d, 0.0)
                down = jnp.concatenate([d[8:], jnp.zeros((8, c4), f)], axis=0)
                slots[0].append(d)
                slots[1].append(pltpu.roll(d, m.out - 1, 0))
                slots[2].append(down)
                slots[3].append(pltpu.roll(down, m.out - 1, 0))
            for t in range(4):
                d5[span(o, 2 * m.out), t * c4 : (t + 1) * c4] = jnp.concatenate(slots[t], axis=0).astype(BF16)

        repeat(m.count // 2, pair)

    loads[7].wait()
    options = (((1, 0),), ((2, 0), (0, 1)))
    for a in range(2):
        for b in range(2):
            value = None
            for r, down in options[a]:
                for c, side in options[b]:
                    slot, tap = (2 * down + side) * c4, (3 * r + c) * c4
                    term = mm_nt(d5[:, slot : slot + c4], w5[tap : tap + c4, :])
                    value = term if value is None else value + term
            pv[...] = value
            for m in sets:

                def crop_(c, m=m, a=a, b=b):
                    for i in range(m.half):
                        for q in range(c4 // 128):
                            dh[q, pl.ds(m.row0 + c * m.rows + (2 * i + a) * 16 + b, 8, stride=2), :] = pv[
                                span(m.out0 + c * m.out + i * 8, 8, 8), q * 128 : (q + 1) * 128
                            ]

                repeat(m.count, crop_)
    loads[9].wait()
    for m in sets:

        def crop_(c, m=m):
            crop = m.crop0 + c
            rows = span(m.row0 + c * m.rows, m.rows)
            mask = keep(m.rows, 128, 16, m.edge)
            levels, tilts = [], []
            for q in range(c4 // 128):
                cols = slice(q * 128, (q + 1) * 128)
                inv = by_view(wv, crop, st4[2:4, cols])
                n = (z4[rows, cols] - by_view(wv, crop, st4[0:2, cols])) * inv
                up_ = jnp.where(mask, act_slope(n * norms2[0:1, cols] + norms2[1:2, cols]) * dh[q, rows, :], 0.0)
                dh[q, rows, :] = up_
                levels.append(jnp.sum(tile_sum(up_), axis=0, keepdims=True))
                tilts.append(jnp.sum(tile_sum(up_ * n), axis=0, keepdims=True))
            cs[pl.ds(crop, 1), 0:c4] = jnp.concatenate(levels, axis=1)
            cm[pl.ds(crop, 1), 0:c4] = jnp.concatenate(tilts, axis=1)

        repeat(m.count, crop_)
    local_sums(blocks[1], (cs, cm), wcol, c4)
    links.send_near(1, blocks[1])
    loads[8].wait()

    def kernel(t):
        part = pl.ds(pl.multiple_of(t * c4, c4), c4)
        g5[part, :] = mm_tn(x5[:, part], d5[:, 0:c4]).astype(BF16)

    repeat(5, kernel)

    def rest():
        repeat(4, lambda t: kernel(t + 5))
        puts.put(g5, o_g5)

    meet_sums(links, 1, c4, ((s4, 0), (s4, 2)), rest)

    for i in range(10, 14):
        loads[i].wait()
    for at, m in enumerate(sets):

        def pair(p, m=m, at=at):
            r = m.row0 + p * 2 * m.rows
            o = m.out0 + p * 2 * m.out
            mask = keep(m.rows, 128, 16, m.edge)
            for j in range(2):
                crop = m.crop0 + 2 * p + j
                rows = span(r + j * m.rows, m.rows)
                over = share_of(wv, tally, crop, 1.0)
                for q in range(c4 // 128):
                    cols = slice(q * 128, (q + 1) * 128)
                    inv = by_view(wv, crop, st4[2:4, cols])
                    n = (z4[rows, cols] - by_view(wv, crop, st4[0:2, cols])) * inv
                    d = (inv * norms2[0:1, cols]) * (
                        dh[q, rows, :] - by_view(wv, crop, s4[0:2, cols]) * over - n * (by_view(wv, crop, s4[2:4, cols]) * over)
                    )
                    d4[rows, cols] = jnp.where(mask, d, 0.0).astype(BF16)
            got = mm_nt(d4[span(r, 2 * m.rows), :], w4[...])
            for q in range(cin // 128):
                bg[q, 0 : 2 * m.rows, :] = got[:, q * 128 : (q + 1) * 128]
            for q in range(cin // 128):
                for j in range(2):
                    for i in range(m.half):
                        here = pl.ds(j * m.rows + i * 32, 8, stride=2)
                        bg[q, here, :] = bg[q, here, :] + t7[span(o + j * m.out + i * 8, 8, 8), q * 128 : (q + 1) * 128]
            zt[0 : 2 * m.rows, :] = mm(h2[span(r, 2 * m.rows), :], w3[...])
            step = m.rows // 2
            mask = keep(step, 128, 16, m.edge)
            for j in range(2):
                crop = m.crop0 + 2 * p + j
                levels, tilts = [], []
                for q in range(cin // 128):
                    cols = slice(q * 128, (q + 1) * 128)
                    at3 = slice(2 * c3 + q * 128, 2 * c3 + (q + 1) * 128)
                    mean, inv = by_view(wv, crop, st3[0:2, cols]), by_view(wv, crop, st3[2:4, cols])
                    gain, bias = norms1[0:1, at3], norms1[1:2, at3]

                    def tile(i, sums, j=j, cols=cols, q=q, mean=mean, inv=inv, gain=gain, bias=bias):
                        here = span(j * m.rows + i * step, step)
                        rows = span(r + j * m.rows + i * step, step)
                        n = (zt[here, cols] - mean) * inv
                        u = n * gain + bias + img[rows, cols].astype(f)
                        got = bg[q, here, :].astype(BF16).astype(f)
                        v = jnp.where(mask, act_slope(u) * got, 0.0)
                        up[rows, cols] = v
                        return (sums[0] + tile_sum(v), sums[1] + tile_sum(v * n))

                    zero = jnp.zeros((8, 128), f)
                    s, t = lax.fori_loop(0, 2, tile, (zero, zero))
                    levels.append(jnp.sum(s, axis=0, keepdims=True))
                    tilts.append(jnp.sum(t, axis=0, keepdims=True))
                cs[pl.ds(crop, 1), :] = jnp.concatenate(levels, axis=1)
                cm[pl.ds(crop, 1), :] = jnp.concatenate(tilts, axis=1)
            pltpu.make_async_copy(
                up.at[span(r, 2 * m.rows)], o_up.at[span(r, 2 * m.rows)], up_sem.at[m.crop0 // 2 + p]
            ).start()

        repeat(m.count // 2, pair)
    local_sums(blocks[2], (cs, cm), wcol, cin)
    links.send_near(2, blocks[2])
    loads[14].wait()

    def inner(n):
        part = pl.ds(pl.multiple_of(n * 256, 256), 256)
        g4[part, :] = mm_tn(blk[:, part], d4[...]).astype(BF16)

    repeat(2, inner)

    def rest():
        repeat(cin // 256 - 2, lambda n: inner(n + 2))
        puts.put(g4, o_g4)

    meet_sums(links, 2, cin, ((s3, 0), (s3, 2)), rest)
    for src, dst in ((s5, o_s5), (s4, o_s4), (s3, o_s3)):
        puts.put(src, dst)
    for m in sets:

        def pair(p, m=m):
            r = m.row0 + p * 2 * m.rows
            pltpu.make_async_copy(
                up.at[span(r, 2 * m.rows)], o_up.at[span(r, 2 * m.rows)], up_sem.at[m.crop0 // 2 + p]
            ).wait()

        repeat(m.count // 2, pair)
    links.finish()
    puts.finish()


def back_one_kernel(sets, total, guarded, crops, dims, *refs):
    c3, cin = dims
    wv, wcol, norms1, st1, st2, st3, s3, tally = refs[:8]
    sources, refs = refs[8:17], refs[17:]
    (o_gb, o_gs, o_g3, o_g2, o_g1, o_s2, o_s1), refs = refs[:7], refs[7:]
    held, refs = refs[:9], refs[9:]
    (h2, w3, up, z2, h1, wsp1, z1, w1, img) = held
    (zt, d3, q2, d2, q1, d1, g3, g2, g1, s2, s1, cs, cm), refs = refs[:13], refs[13:]
    blocks, refs = take(refs, 2)
    near, refs = take(refs, 2)
    far, refs = take(refs, 2)
    links = Links(crops, near, far, *refs[:4])
    load_sem, out_sem, own_sem, grad_send, grad_recv = refs[4:]
    core = links.r
    sibling = (links.k, 1 - core)
    f = F32
    loads = start_loads(list(zip(sources, held)), load_sem)
    links.greet()
    puts = Puts(out_sem)
    for ref in (cs, cm):
        ref[...] = jnp.zeros(ref.shape, f)
    for block in blocks:
        block[...] = jnp.zeros(block.shape, f)
    d2[0:16, :] = jnp.zeros((16, 3 * c3), BF16)
    for m in sets:
        for c in range(m.count):
            at = m.guard0 + c * m.guard + m.rows
            d2[at : at + 16, :] = jnp.zeros((16, 3 * c3), BF16)

    for i in range(4):
        loads[i].wait()
    for m in sets:

        def pair(p, m=m):
            r = m.row0 + p * 2 * m.rows
            zt[0 : 2 * m.rows, :] = mm(h2[span(r, 2 * m.rows), :], w3[...])
            step = m.rows // 2
            mask = keep(step, 128, 16, m.edge)
            for j in range(2):
                crop = m.crop0 + 2 * p + j
                over = share_of(wv, tally, crop, 1.0)
                for q in range(cin // 128):
                    cols = slice(q * 128, (q + 1) * 128)
                    mean, inv = by_view(wv, crop, st3[0:2, cols]), by_view(wv, crop, st3[2:4, cols])
                    gain = inv * norms1[0:1, 2 * c3 + q * 128 : 2 * c3 + (q + 1) * 128]
                    level = by_view(wv, crop, s3[0:2, cols]) * over
                    tilt = by_view(wv, crop, s3[2:4, cols]) * over * inv

                    def tile(i, j=j, cols=cols, mean=mean, gain=gain, level=level, tilt=tilt):
                        here = span(j * m.rows + i * step, step)
                        rows = span(r + j * m.rows + i * step, step)
                        d = gain * (up[rows, cols] - level - (zt[here, cols] - mean) * tilt)
                        d3[rows, cols] = jnp.where(mask, d, 0.0).astype(BF16)

                    repeat(2, tile)
            q2[span(r, 2 * m.rows), :] = mm_nt(d3[span(r, 2 * m.rows), :], w3[...])
            for j in range(2):
                crop = m.crop0 + 2 * p + j
                mean, inv = by_view(wv, crop, st2[0:2, :]), by_view(wv, crop, st2[2:4, :])

                def tile(i, sums, j=j, mean=mean, inv=inv):
                    rows = span(r + j * m.rows + i * step, step)
                    n = (z2[rows, :] - mean) * inv
                    v = act_slope(n * norms1[0:1, c3 : 2 * c3] + norms1[1:2, c3 : 2 * c3]) * q2[rows, :]
                    q2[rows, :] = v
                    return (sums[0] + tile_sum(v), sums[1] + tile_sum(v * n))

                zero = jnp.zeros((8, c3), f)
                s, t = lax.fori_loop(0, 2, tile, (zero, zero))
                cs[pl.ds(crop, 1), 0:c3] = jnp.sum(s, axis=0, keepdims=True)
                cm[pl.ds(crop, 1), 0:c3] = jnp.sum(t, axis=0, keepdims=True)

        repeat(m.count // 2, pair)
    local_sums(blocks[0], (cs, cm), wcol, c3)
    links.send_near(0, blocks[0])

    def outer(n):
        cols = pl.ds(pl.multiple_of(n * 256, 256), 256)
        g3[:, cols] = mm_tn(h2[...], d3[:, cols]).astype(BF16)

    repeat(cin // 512, outer)

    def rest():
        repeat(cin // 512, lambda n: outer(n + cin // 512))
        puts.put(g3, o_g3)

    meet_sums(links, 0, c3, ((s2, 0), (s2, 2)), rest)

    for i in range(4, 7):
        loads[i].wait()
    for m in sets:

        def pair(p, m=m):
            r = m.row0 + p * 2 * m.rows
            g = m.guard0 + p * 2 * m.guard
            step = m.rows // 2
            mask = keep(step, c3, 16, m.edge)
            for j in range(2):
                crop = m.crop0 + 2 * p + j
                over = share_of(wv, tally, crop, 1.0)
                mean, inv = by_view(wv, crop, st2[0:2, :]), by_view(wv, crop, st2[2:4, :])
                gain = inv * norms1[0:1, c3 : 2 * c3]
                level = by_view(wv, crop, s2[0:2, :]) * over
                tilt = by_view(wv, crop, s2[2:4, :]) * over * inv

                def tile(i, j=j, mean=mean, gain=gain, level=level, tilt=tilt):
                    rows = span(r + j * m.rows + i * step, step)
                    d = gain * (q2[rows, :] - level - (z2[rows, :] - mean) * tilt)
                    d = jnp.where(mask, d, 0.0)
                    to = span(g + j * m.guard + i * step, step)
                    d2[to, 0:c3] = pltpu.roll(d, step - 1, 0).astype(BF16)
                    d2[to, c3 : 2 * c3] = d.astype(BF16)
                    d2[to, 2 * c3 : 3 * c3] = pltpu.roll(d, 1, 0).astype(BF16)

                repeat(2, tile)
            size = 2 * m.rows + 16
            value = None
            for a in range(3):
                for b in range(3):
                    part = d2[span(g - (a - 1) * 16, size), b * c3 : (b + 1) * c3]
                    term = mm_nt(part, wsp1[a, b * c3 : (b + 1) * c3, :])
                    value = term if value is None else value + term
            q1[span(r, m.rows), :] = value[0 : m.rows]
            q1[span(r + m.rows, m.rows), :] = value[m.guard : m.guard + m.rows]
            for j in range(2):
                crop = m.crop0 + 2 * p + j
                mean, inv = by_view(wv, crop, st1[0:2, :]), by_view(wv, crop, st1[2:4, :])

                def tile(i, sums, j=j, mean=mean, inv=inv):
                    rows = span(r + j * m.rows + i * step, step)
                    n = (z1[rows, :] - mean) * inv
                    v = act_slope(n * norms1[0:1, 0:c3] + norms1[1:2, 0:c3]) * q1[rows, :]
                    v = jnp.where(mask, v, 0.0)
                    q1[rows, :] = v
                    return (sums[0] + tile_sum(v), sums[1] + tile_sum(v * n))

                zero = jnp.zeros((8, c3), f)
                s, t = lax.fori_loop(0, 2, tile, (zero, zero))
                cs[pl.ds(crop, 1), 0:c3] = jnp.sum(s, axis=0, keepdims=True)
                cm[pl.ds(crop, 1), 0:c3] = jnp.sum(t, axis=0, keepdims=True)

        repeat(m.count // 2, pair)
    local_sums(blocks[1], (cs, cm), wcol, c3)
    links.send_near(1, blocks[1])
    inside = guarded - 32

    def taps(a):
        g2[a * 3 * c3 : (a + 1) * 3 * c3, :] = mm_tn(
            h1[a * 16 : a * 16 + inside, :], d2[16 : 16 + inside, c3 : 2 * c3]
        ).astype(BF16)

    taps(0)

    def rest():
        taps(1)
        taps(2)
        puts.put(g2, o_g2)

    meet_sums(links, 1, c3, ((s1, 0), (s1, 2)), rest)

    loads[7].wait()
    moves = []
    for m, out in zip(sets, (o_gb, o_gs)):
        part = m.rows // 2
        for c in range(m.count):
            i = m.crop0 + c
            own_rows = span(m.row0 + c * m.rows + core * part, part)
            other_rows = span(m.row0 + c * m.rows + (1 - core) * part, part)
            place = out.at[span((core * m.count + c) * part, part)]
            moves.append(
                (
                    pltpu.make_async_copy(d3.at[own_rows], place, own_sem.at[i]),
                    pltpu.make_async_remote_copy(
                        src_ref=d3.at[other_rows],
                        dst_ref=place,
                        send_sem=grad_send.at[i],
                        recv_sem=grad_recv.at[i],
                        device_id=sibling,
                        device_id_type=MESH,
                    ),
                )
            )
    for m in sets:

        def pair(p, m=m):
            r = m.row0 + p * 2 * m.rows
            step = m.rows // 2
            mask = keep(step, c3, 16, m.edge)
            for j in range(2):
                crop = m.crop0 + 2 * p + j
                over = share_of(wv, tally, crop, 1.0)
                mean, inv = by_view(wv, crop, st1[0:2, :]), by_view(wv, crop, st1[2:4, :])
                gain = inv * norms1[0:1, 0:c3]
                level = by_view(wv, crop, s1[0:2, :]) * over
                tilt = by_view(wv, crop, s1[2:4, :]) * over * inv

                def tile(i, j=j, mean=mean, gain=gain, level=level, tilt=tilt):
                    rows = span(r + j * m.rows + i * step, step)
                    d = gain * (q1[rows, :] - level - (z1[rows, :] - mean) * tilt)
                    d1[rows, :] = jnp.where(mask, d, 0.0).astype(BF16)

                repeat(2, tile)
            rows = span(r, 2 * m.rows)
            for n in range(cin // 256):
                cols = slice(n * 256, (n + 1) * 256)
                d3[rows, cols] = (up[rows, cols] + mm_nt(d1[rows, :], w1[cols, :])).astype(BF16)

        repeat(m.count // 2, pair)
        for c in range(m.count):
            for copy in moves[m.crop0 + c]:
                copy.start()
    loads[8].wait()

    def inner(n):
        part = pl.ds(pl.multiple_of(n * 256, 256), 256)
        g1[part, :] = mm_tn(img[:, part], d1[...]).astype(BF16)

    repeat(cin // 256, inner)
    puts.put(g1, o_g1)
    for src, dst in ((s2, o_s2), (s1, o_s1)):
        puts.put(src, dst)
    links.finish()
    for near_copy, far_copy in moves:
        near_copy.wait()
        far_copy.wait()
    puts.finish()


def backward(sets, got, onehot, wcol, w, norms_first, norms_second, total, guarded, outs, idents):
    crops = lax.axis_size("crops")
    w1, wsp1, w3, w4, w5, w6, w7 = w
    cin, c3 = w1.shape
    c4, cout = w6.shape
    (
        f_img, f_z1, f_h1, f_z2, f_h2, f_blk, f_z4, f_x5, f_z5, f_h5, f_xe, f_res, f_d6, f_d7,
        f_st1, f_st2, f_st3, f_st4, f_st7, f_st5, f_st6, f_sq, f_n,
    ) = got
    smem, vmem = pl.BlockSpec(memory_space=pltpu.SMEM), pl.BlockSpec(memory_space=pltpu.VMEM)
    hbm = pl.BlockSpec(memory_space=pl.ANY)
    shape = jax.ShapeDtypeStruct
    most = 2 * sets[0].rows
    pairs = sum(m.count for m in sets) // 2
    count = 2 * pairs

    def like(arrays):
        return [pltpu.VMEM(t.shape, t.dtype) for t in arrays]

    def params(ident):
        return pltpu.CompilerParams(
            collective_id=ident, has_side_effects=True, vmem_limit_bytes=63 * 1024 * 1024
        )

    arrays = [f_d6, w6, f_z5, f_h5, f_d7, f_xe, w7, w5, f_x5, f_z4, w4, f_h2, w3, f_img, f_blk]
    out_shape = [
        shape((total, cin), F32), shape((c4, cout), BF16), shape((cin, cout), BF16), shape((9 * c4, c4), BF16),
        shape((cin, c4), BF16), shape((8, c4), F32), shape((8, c4), F32), shape((8, cin), F32),
    ]
    scratch = like(arrays) + [
        pltpu.VMEM((outs, c4), F32), pltpu.VMEM((outs, cin), F32), pltpu.VMEM((outs, 4 * c4), BF16),
        pltpu.VMEM((outs, c4), F32), pltpu.VMEM((c4 // 128, total, 128), F32), pltpu.VMEM((total, c4), BF16),
        pltpu.VMEM((most, cin), F32), pltpu.VMEM((cin // 128, most, 128), F32), pltpu.VMEM((total, cin), F32),
        pltpu.VMEM((8, c4), F32), pltpu.VMEM((8, c4), F32), pltpu.VMEM((8, cin), F32),
        pltpu.VMEM((16, cin), F32), pltpu.VMEM((16, cin), F32),
    ]
    scratch += exchange_shapes((c4, c4, cin), (2, 2, 2), crops)
    scratch += [pltpu.SemaphoreType.DMA((15,)), pltpu.SemaphoreType.DMA((7,)), pltpu.SemaphoreType.DMA((pairs,))]
    up, g_outer2, g_skip, g_spatial2, g_inner2, s5, s4, s3 = pl.pallas_call(
        functools.partial(back_two_kernel, sets, total, outs, crops, (c3, cin, c4, cout)),
        out_shape=out_shape,
        in_specs=[smem] + [vmem] * 7 + [hbm] * 15,
        out_specs=[hbm] * len(out_shape),
        scratch_shapes=scratch,
        compiler_params=params(idents[0]),
        name="back_two",
    )(onehot, wcol, norms_first, norms_second, f_st3, f_st4, f_st5, f_n, *arrays)

    arrays = [f_h2, w3, up, f_z2, f_h1, wsp1, f_z1, w1, f_img]
    out_shape = [
        shape((total_rows(sets[0]), cin), BF16), shape((total_rows(sets[1]), cin), BF16), shape((c3, cin), BF16),
        shape((9 * c3, c3), BF16), shape((cin, c3), BF16), shape((8, c3), F32), shape((8, c3), F32),
    ]
    scratch = like(arrays) + [
        pltpu.VMEM((most, cin), F32), pltpu.VMEM((total, cin), BF16), pltpu.VMEM((total, c3), F32),
        pltpu.VMEM((guarded, 3 * c3), BF16), pltpu.VMEM((total, c3), F32), pltpu.VMEM((total, c3), BF16),
        pltpu.VMEM((c3, cin), BF16), pltpu.VMEM((9 * c3, c3), BF16), pltpu.VMEM((cin, c3), BF16),
        pltpu.VMEM((8, c3), F32), pltpu.VMEM((8, c3), F32), pltpu.VMEM((16, c3), F32), pltpu.VMEM((16, c3), F32),
    ]
    scratch += exchange_shapes((c3, c3), (2, 2), crops)
    scratch += [pltpu.SemaphoreType.DMA((9,)), pltpu.SemaphoreType.DMA((5,))]
    scratch += [pltpu.SemaphoreType.DMA((count,))] * 3
    grad_b, grad_s, g_outer1, g_spatial1, g_inner1, s2, s1 = pl.pallas_call(
        functools.partial(back_one_kernel, sets, total, guarded, crops, (c3, cin)),
        out_shape=out_shape,
        in_specs=[smem] + [vmem] * 7 + [hbm] * 9,
        out_specs=[hbm] * len(out_shape),
        scratch_shapes=scratch,
        compiler_params=params(idents[1]),
        name="back_one",
    )(onehot, wcol, norms_first, f_st1, f_st2, f_st3, s3, f_n, *arrays)
    grads = (g_skip, g_spatial2, g_outer2, g_inner2, g_spatial1, g_outer1, g_inner1)
    return grad_b, grad_s, grads, (s1, s2, s3, s4, s5)


def total_rows(m):
    return m.count * m.rows


def shards(
    image_big,
    image_small,
    view_big,
    view_small,
    inner_first,
    spatial_first,
    outer_first,
    norms_first,
    inner_second,
    spatial_second,
    outer_second,
    skip_second,
    norms_second,
    cotangent_big,
    cotangent_small,
):
    splits, position = lax.axis_size("rows"), lax.axis_index("rows")
    labels = jnp.concatenate(
        [
            lax.dynamic_slice_in_dim(v, position * (v.shape[0] // splits), v.shape[0] // splits)
            for v in (view_big, view_small)
        ]
    )
    onehot = (labels[None, :] == jnp.arange(2)[:, None]).astype(F32)
    nb, ns = image_big.shape[0] // splits, image_small.shape[0] // splits
    pixels = jnp.concatenate(
        [
            jnp.full((nb,), float(image_big.shape[2] ** 2), F32),
            jnp.full((ns,), float(image_small.shape[2] ** 2), F32),
        ]
    )
    c3, c4 = inner_first.shape[1], inner_second.shape[1]
    weights = [
        inner_first,
        spatial_first.reshape(3, 3 * c3, c3),
        outer_first,
        inner_second,
        spatial_second.reshape(9 * c4, c4),
        outer_second,
        skip_second,
    ]
    sets, wcol, sizes, got = forward(
        [image_big, image_small], [cotangent_big, cotangent_small], onehot, pixels, weights, norms_first, norms_second, 0
    )
    grad_b, grad_s, grads, sums = backward(
        sets, got, onehot, wcol, weights, norms_first, norms_second, *sizes, (1, 2)
    )
    s1, s2, s3, s4, s5 = sums
    sq = got[21]

    def both(parts):
        return jnp.concatenate(
            [jnp.stack([t[g] + t[g + 1], t[0] + t[1]]) for t, g in parts], axis=1
        )

    shared = share_all(grads, 3)
    g_skip, g_spatial2, g_outer2, g_inner2, g_spatial1, g_outer1, g_inner1 = [
        t.astype(F32) for t in shared
    ]
    results = [
        got[11][m.out0 : m.out0 + m.count * m.out].reshape(m.count, m.half, 8, -1)[:, :, : m.half]
        for m in sets
    ]
    gradients = [
        t.reshape(image.shape[0], image.shape[1], 16, -1)[:, :, : image.shape[2]]
        for t, image in ((grad_b, image_big), (grad_s, image_small))
    ]
    return (
        results[0],
        results[1],
        gradients[0],
        gradients[1],
        g_inner1,
        g_spatial1.reshape(spatial_first.shape),
        g_outer1,
        both(((s1, 2), (s2, 2), (s3, 2))),
        g_inner2,
        g_spatial2.reshape(spatial_second.shape),
        g_outer2,
        g_skip,
        both(((s4, 2), (s5, 2), (sq, 2), (sq, 4))),
    )


def solution(mesh):
    maps = P("crops", "rows", None, None)
    whole = P(("crops", "rows"), None, None, None)
    in_specs = (maps, maps, P("crops"), P("crops")) + (P(),) * 9 + (whole, whole)
    out_specs = (whole, whole, maps, maps) + (P(),) * 9
    return jax.shard_map(shards, mesh=mesh, in_specs=in_specs, out_specs=out_specs, check_vma=False)
```

```python
import functools

import jax
import jax.numpy as jnp
from jax import lax
from jax.experimental import pallas as pl
from jax.experimental.pallas import tpu as pltpu
from jax.sharding import PartitionSpec as P

HIGH = lax.Precision.HIGHEST
EPS = 1e-05
MESH = pl.DeviceIdType.MESH
F32 = jnp.float32
BF16 = jnp.bfloat16


class Maps:
    def __init__(self, count, edge, row0, crop0, guard0, out0):
        self.count, self.edge = count, edge
        self.row0, self.crop0, self.guard0, self.out0 = row0, crop0, guard0, out0
        self.rows = edge * 16
        self.guard = (edge + 1) * 16
        self.half = edge // 2
        self.out = self.half * 8
        self.pixels = edge * edge


def geometry(nb, eb, ns, es):
    big = Maps(nb, eb, 0, 0, 16, 0)
    small = Maps(ns, es, nb * big.rows, nb, 16 + nb * big.guard, nb * big.out)
    total = small.row0 + ns * small.rows
    guarded = small.guard0 + ns * small.guard
    out = small.out0 + ns * small.out
    return (big, small), total, guarded, out


def al(x, m=16):
    return x if isinstance(x, int) else pl.multiple_of(x, m)


def span(start, size, m=16):
    return pl.ds(al(start, m), size)


def repeat(count, body):
    def step(i, carry):
        body(i)
        return carry

    lax.fori_loop(0, count, step, 0)


def mm(a, b):
    return jnp.dot(a, b, preferred_element_type=F32)


def mm_nt(a, b):
    return lax.dot_general(a, b, (((1,), (1,)), ((), ())), preferred_element_type=F32)


def mm_tn(a, b):
    return lax.dot_general(a, b, (((0,), (0,)), ((), ())), preferred_element_type=F32)


CA = 0.7978845608028654
CB = 0.7978845608028654 * 0.044715


def act(u):
    t = jnp.tanh(u * (CA + CB * (u * u)))
    return 0.5 * u * (1.0 + t)


def act_slope(u):
    s = u * u
    t = jnp.tanh(u * (CA + CB * s))
    rise = (0.5 * u) * (CA + (3.0 * CB) * s)
    return 0.5 * (1.0 + t) + (1.0 - t * t) * rise


def act_both(u):
    s = u * u
    t = jnp.tanh(u * (CA + CB * s))
    hu = 0.5 * u
    lift = 0.5 * (1.0 + t)
    slope = lift + (1.0 - t * t) * (hu * (CA + (3.0 * CB) * s))
    return u * lift, slope


def keep(rows, width, pitch, edge):
    place = lax.broadcasted_iota(jnp.int32, (rows, width), 0)
    return lax.rem(place, pitch) < edge


def tile_sum(x):
    return jnp.sum(x.reshape(x.shape[0] // 8, 8, x.shape[1]), axis=0)


def pieces(width):
    return (4, width // 4) if width >= 512 else (width // 128, 128)


class Links:
    def __init__(self, crops, near, far, near_s, near_r, far_s, far_r):
        self.group = 4 if crops % 4 == 0 else 1
        self.outers = crops // self.group
        self.k, self.r = lax.axis_index("crops"), lax.axis_index("rows")
        inner, self.outer = lax.rem(self.k, self.group), self.k // self.group
        self.wide = 2 * self.group
        self.me = inner * 2 + self.r
        self.peers, self.others = [], []
        for d in range(1, self.wide):
            p = lax.rem(self.me + d, self.wide)
            self.peers.append((self.outer * self.group + p // 2, lax.rem(p, 2)))
        for d in range(1, self.outers):
            self.others.append((lax.rem(self.outer + d, self.outers) * self.group + inner, self.r))
        self.near, self.far = near, far
        self.sems = (near_s, near_r, far_s, far_r)
        self.live = {}

    def greet(self, extra=()):
        barrier = pltpu.get_barrier_semaphore()
        peers = self.peers + self.others + list(extra)
        for peer in peers:
            pl.semaphore_signal(barrier, inc=1, device_id=peer, device_id_type=MESH)
        pl.semaphore_wait(barrier, len(peers))

    def send_near(self, e, block):
        self.near[e][self.me] = block[...]
        self.live[e, 0] = []
        for d, peer in enumerate(self.peers):
            copy = pltpu.make_async_remote_copy(
                src_ref=block,
                dst_ref=self.near[e].at[self.me],
                send_sem=self.sems[0].at[e, d],
                recv_sem=self.sems[1].at[e, d],
                device_id=peer,
                device_id_type=MESH,
            )
            copy.start()
            self.live[e, 0].append(copy)

    def wait_near(self, e):
        for copy in self.live[e, 0]:
            copy.wait_recv()

    def send_far(self, e):
        self.live[e, 1] = []
        place = self.far[e].at[self.outer]
        for d, peer in enumerate(self.others):
            copy = pltpu.make_async_remote_copy(
                src_ref=place,
                dst_ref=place,
                send_sem=self.sems[2].at[e, d],
                recv_sem=self.sems[3].at[e, d],
                device_id=peer,
                device_id_type=MESH,
            )
            copy.start()
            self.live[e, 1].append(copy)

    def wait_far(self, e):
        for copy in self.live[e, 1]:
            copy.wait_recv()

    def finish(self):
        for copies in self.live.values():
            for copy in copies:
                copy.wait_send()


def fold_moments(buf, tallies, count, scale):
    sums, total = buf[0, 0:8, :], tallies[0]
    for i in range(1, count):
        sums = sums + buf[i, 0:8, :]
        total = total + tallies[i]
    mean = sums / jnp.maximum(total * scale, 1.0)
    spread = None
    for i in range(count):
        n = tallies[i] * scale
        apart = buf[i, 0:8, :] / jnp.maximum(n, 1.0) - mean
        term = buf[i, 8:16, :] + n * apart * apart
        spread = term if spread is None else spread + term
    return sums, spread, total


def fold_sums(buf, count):
    total = buf[0]
    for i in range(1, count):
        total = total + buf[i]
    return total


def exchange_shapes(widths, tiles, crops):
    group = 4 if crops % 4 == 0 else 1
    outers = crops // group
    blocks, near, far = [], [], []
    for width, tile in zip(widths, tiles):
        lanes = pieces(width)[1]
        blocks.append(pltpu.VMEM((8 * tile, lanes), F32))
        near.append(pltpu.VMEM((2 * group, 8 * tile, lanes), F32))
        far.append(pltpu.VMEM((outers, 8 * tile, lanes), F32))
    e = len(widths)
    sems = [
        pltpu.SemaphoreType.DMA((e, 2 * group - 1)),
        pltpu.SemaphoreType.DMA((e, 2 * group - 1)),
        pltpu.SemaphoreType.DMA((e, max(outers - 1, 1))),
        pltpu.SemaphoreType.DMA((e, max(outers - 1, 1))),
    ]
    return blocks + near + far + sems


def take(refs, count):
    return list(refs[:count]), refs[count:]


def pack(block, tile, rows, width):
    count, lanes = pieces(width)
    for q in range(count):
        for v in range(2):
            block[tile * 8 + 2 * q + v : tile * 8 + 2 * q + v + 1, :] = rows[v][:, q * lanes : (q + 1) * lanes]


def unpack(table, row, tile, width):
    count, lanes = pieces(width)
    for q in range(count):
        table[row : row + 2, q * lanes : (q + 1) * lanes] = tile[2 * q : 2 * q + 2, :]


def crop_stats(ref, row0, rows, step, width, edge, pitch, pixels, crop, cs, cm, col0=0):
    mask = keep(step, width, pitch, edge)
    zero = jnp.zeros((8, width), F32)
    cols = pl.ds(col0, width) if isinstance(col0, int) else pl.ds(pl.multiple_of(col0, 128), width)

    def first(i, acc):
        z = ref[span(row0 + i * step, step, 8), cols]
        return acc + tile_sum(jnp.where(mask, z, 0.0))

    s = jnp.sum(lax.fori_loop(0, rows // step, first, zero), axis=0, keepdims=True)
    mean = s * (1.0 / pixels)

    def second(i, acc):
        z = ref[span(row0 + i * step, step, 8), cols]
        d = jnp.where(mask, z - mean, 0.0)
        return acc + tile_sum(d * d)

    m = jnp.sum(lax.fori_loop(0, rows // step, second, zero), axis=0, keepdims=True)
    cs[pl.ds(crop, 1), cols] = s
    cm[pl.ds(crop, 1), cols] = m


def local_moments(block, cs, cm, wcol, width, scale, tally=False):
    s, m = cs[:, 0:width], cm[:, 0:width]
    pix = wcol[:, 2:3] * scale
    mean_c = s / pix
    sums, squares, tallies = [], [], []
    for v in range(2):
        w = wcol[:, v : v + 1]
        total = jnp.sum(w * s, axis=0, keepdims=True)
        n = jnp.sum(w * pix, axis=0, keepdims=True)
        apart = mean_c - total / jnp.maximum(n, 1.0)
        squares.append(jnp.sum(w * (m + pix * apart * apart), axis=0, keepdims=True))
        sums.append(total)
        tallies.append(n)
    pack(block, 0, sums, width)
    pack(block, 1, squares, width)
    if tally:
        lanes = pieces(width)[1]
        for q in range(4):
            for v in range(2):
                block[16 + 2 * q + v : 17 + 2 * q + v, :] = jnp.broadcast_to(tallies[v], (1, lanes))


def local_sums(block, parts, wcol, width):
    for tile, part in enumerate(parts):
        s = part[:, 0:width]
        pack(block, tile, [jnp.sum(wcol[:, v : v + 1] * s, axis=0, keepdims=True) for v in range(2)], width)


def by_view(wv, crop, pair):
    return wv[0, crop] * pair[0:1, :] + wv[1, crop] * pair[1:2, :]


FWD_WIDTHS = (256, 256, 1024, 512, 2048, 512, 2048, 2048)


def forward_kernel(sets, total, guarded, outs, crops, dims, *refs):
    c3, cin, c4, cout = dims
    (
        wv, wcol, norms1, norms2,
        img_b, img_s, cot_hbm, w1_h, wsp1_h, w3_h, w4_h, w5_h, w6_h, w7_h,
    ), refs = refs[:14], refs[14:]
    (
        o_img, o_z1, o_h1, o_z2, o_h2, o_blk, o_z4, o_x5, o_z5, o_h5, o_xe, o_res, o_d6, o_d7,
        o_st1, o_st2, o_st3, o_st4, o_st7, o_st5, o_st6, o_sq, o_tally,
    ), refs = refs[:23], refs[23:]
    (
        img, z1, h1, z2, h2, zt, blk, eb, z4, xe, z7, hp, x5, z5, h5, z6, cot,
        w1, wsp1, w3, w4, w5, w6, w7, cs, cm, ck,
        st1, st2, st3, st4, st7, st5, st6, sq, tally_v,
    ), refs = refs[:36], refs[36:]
    e = len(FWD_WIDTHS)
    blocks, refs = take(refs, e)
    near, refs = take(refs, e)
    far, refs = take(refs, e)
    ns_, nr_, fs_, fr_ = refs[:4]
    load_sem, img_sem, img_send, img_recv, out_sem = refs[4:]
    links = Links(crops, near, far, ns_, nr_, fs_, fr_)
    k, core = links.k, links.r
    sibling = (k, 1 - core)
    f = F32

    loads = []
    for i, (src, dst) in enumerate(
        ((w1_h, w1), (wsp1_h, wsp1), (w3_h, w3), (w4_h, w4), (w5_h, w5), (w6_h, w6), (w7_h, w7), (cot_hbm, cot))
    ):
        loads.append(pltpu.make_async_copy(src, dst, load_sem.at[i]))
    own, swaps = [], []
    for at, (m, src) in enumerate(zip(sets, (img_b, img_s))):
        part = m.rows // 2
        for c in range(m.count):
            i = m.crop0 + c
            place = img.at[span(m.row0 + c * m.rows + core * part, part)]
            own.append(
                pltpu.make_async_copy(
                    src.at[span((core * m.count + c) * part, part)], place, img_sem.at[i]
                )
            )
            swaps.append(
                pltpu.make_async_remote_copy(
                    src_ref=src.at[span(((1 - core) * m.count + c) * part, part)],
                    dst_ref=place,
                    send_sem=img_send.at[i],
                    recv_sem=img_recv.at[i],
                    device_id=sibling,
                    device_id_type=MESH,
                )
            )
    for copy in own:
        copy.start()
    for copy in loads:
        copy.start()
    links.greet()
    for copy in swaps:
        copy.start()

    out_copies = []

    def put(src, dst):
        copy = pltpu.make_async_copy(src, dst, out_sem.at[len(out_copies)])
        copy.start()
        out_copies.append(copy)

    for ref in (cs, cm, ck):
        ref[...] = jnp.zeros(ref.shape, f)
    for block in blocks:
        block[...] = jnp.zeros(block.shape, f)
    h1[0:16, :] = jnp.zeros((16, 3 * c3), BF16)
    for m in sets:
        for c in range(m.count):
            at = m.guard0 + c * m.guard + m.rows
            h1[at : at + 16, :] = jnp.zeros((16, 3 * c3), BF16)

    def near_tallies():
        return [near[0][i, 16:24, 0:1] for i in range(links.wide)]

    def far_tallies():
        return [far[0][i, 16:24, 0:1] for i in range(links.outers)]

    def meet_near(i, scale):
        links.wait_near(i)
        sums, spread, n = fold_moments(near[i], near_tallies(), links.wide, scale)
        place = far[i].at[links.outer]
        place[0:8, :] = sums
        place[8:16, :] = spread
        if i == 0:
            place[16:24, :] = jnp.broadcast_to(n, (8, near[0].shape[2]))
        links.send_far(i)

    def meet_far(i, scale, table, width):
        links.wait_far(i)
        sums, spread, n = fold_moments(far[i], far_tallies(), links.outers, scale)
        mean = sums / (n * scale)
        inverse = lax.rsqrt(spread / (n * scale) + EPS)
        unpack(table, 0, mean, width)
        unpack(table, 2, inverse, width)
        if i == 0:
            tally_v[...] = jnp.broadcast_to(n, (8, 128))

    loads[0].wait()
    for copy in own:
        copy.wait()
    for copy in swaps:
        copy.wait_recv()
    for m in sets:

        def pair(p, m=m):
            r = m.row0 + p * 2 * m.rows
            z1[span(r, 2 * m.rows), :] = mm(img[span(r, 2 * m.rows), :], w1[...])
            for j in range(2):
                crop_stats(z1, r + j * m.rows, m.rows, m.rows // 2, c3, m.edge, 16, m.pixels, m.crop0 + 2 * p + j, cs, cm)

        repeat(m.count // 2, pair)
    local_moments(blocks[0], cs, cm, wcol, c3, 1.0, True)
    links.send_near(0, blocks[0])
    put(img, o_img)
    put(z1, o_z1)
    loads[1].wait()
    meet_near(0, 1.0)
    meet_far(0, 1.0, st1, c3)

    for m in sets:

        def pair(p, m=m):
            r = m.row0 + p * 2 * m.rows
            g = m.guard0 + p * 2 * m.guard
            for j in range(2):
                crop = m.crop0 + 2 * p + j
                mean = by_view(wv, crop, st1[0:2, :])
                scale = by_view(wv, crop, st1[2:4, :]) * norms1[0:1, 0:c3]
                shift = norms1[1:2, 0:c3]
                step = m.rows // 2
                mask = keep(step, c3, 16, m.edge)

                def tile(i):
                    z = z1[span(r + j * m.rows + i * step, step), :]
                    h = jnp.where(mask, act((z - mean) * scale + shift), 0.0)
                    rows = span(g + j * m.guard + i * step, step)
                    h1[rows, 0:c3] = pltpu.roll(h, 1, 0).astype(BF16)
                    h1[rows, c3 : 2 * c3] = h.astype(BF16)
                    h1[rows, 2 * c3 : 3 * c3] = pltpu.roll(h, step - 1, 0).astype(BF16)

                repeat(2, tile)
            size = 2 * m.rows + 16
            z = mm(h1[span(g - 16, size), :], wsp1[0]) + mm(h1[span(g, size), :], wsp1[1])
            z = z + mm(h1[span(g + 16, size), :], wsp1[2])
            z2[span(r, m.rows), :] = z[0 : m.rows]
            z2[span(r + m.rows, m.rows), :] = z[m.guard : m.guard + m.rows]
            for j in range(2):
                crop_stats(z2, r + j * m.rows, m.rows, m.rows // 2, c3, m.edge, 16, m.pixels, m.crop0 + 2 * p + j, cs, cm)

        repeat(m.count // 2, pair)
    local_moments(blocks[1], cs, cm, wcol, c3, 1.0)
    links.send_near(1, blocks[1])
    put(h1, o_h1)
    put(z2, o_z2)
    loads[2].wait()
    meet_near(1, 1.0)
    meet_far(1, 1.0, st2, c3)

    for m in sets:

        def pair(p, m=m):
            r = m.row0 + p * 2 * m.rows
            for j in range(2):
                crop = m.crop0 + 2 * p + j
                mean = by_view(wv, crop, st2[0:2, :])
                scale = by_view(wv, crop, st2[2:4, :]) * norms1[0:1, c3 : 2 * c3]
                shift = norms1[1:2, c3 : 2 * c3]
                step = m.rows // 2

                def tile(i):
                    rows = span(r + j * m.rows + i * step, step)
                    h2[rows, :] = act((z2[rows, :] - mean) * scale + shift).astype(BF16)

                repeat(2, tile)
            zt[0 : 2 * m.rows, :] = mm(h2[span(r, 2 * m.rows), :], w3[...])
            for j in range(2):
                crop_stats(zt, j * m.rows, m.rows, 32, cin, m.edge, 16, m.pixels, m.crop0 + 2 * p + j, cs, cm)

        repeat(m.count // 2, pair)
    local_moments(blocks[2], cs, cm, wcol, cin, 1.0)
    links.send_near(2, blocks[2])
    put(h2, o_h2)
    loads[3].wait()
    meet_near(2, 1.0)
    meet_far(2, 1.0, st3, cin)

    for m in sets:

        def pair(p, m=m):
            r = m.row0 + p * 2 * m.rows
            zt[0 : 2 * m.rows, :] = mm(h2[span(r, 2 * m.rows), :], w3[...])
            for j in range(2):
                crop = m.crop0 + 2 * p + j
                mean = by_view(wv, crop, st3[0:2, :])
                scale = by_view(wv, crop, st3[2:4, :]) * norms1[0:1, 2 * c3 :]
                shift = norms1[1:2, 2 * c3 :]

                def tile(i):
                    here = span(j * m.rows + i * 32, 32)
                    rows = span(r + j * m.rows + i * 32, 32)
                    u = (zt[here, :] - mean) * scale + shift + img[rows, :].astype(f)
                    b = act(u)
                    blk[rows, :] = b.astype(BF16)
                    for q in range(cin // 128):
                        eb[q, span(j * m.rows // 2 + i * 16, 16), :] = b[0:16, q * 128 : (q + 1) * 128]

                repeat(m.rows // 32, tile)
            for q in range(cin // 128):
                picked = [eb[q, pl.ds(i * 16, 8, stride=2), :] for i in range(2 * m.half)]
                xe[span(m.out0 + p * 2 * m.out, 2 * m.out), q * 128 : (q + 1) * 128] = jnp.concatenate(
                    picked, axis=0
                ).astype(BF16)
            z4[span(r, 2 * m.rows), :] = mm(blk[span(r, 2 * m.rows), :], w4[...])
            for j in range(2):
                crop_stats(z4, r + j * m.rows, m.rows, 32, c4, m.edge, 16, m.pixels, m.crop0 + 2 * p + j, cs, cm)

        repeat(m.count // 2, pair)
    local_moments(blocks[3], cs, cm, wcol, c4, 1.0)
    links.send_near(3, blocks[3])
    put(blk, o_blk)
    put(z4, o_z4)
    put(xe, o_xe)
    loads[6].wait()

    def wide_product(a, w, z):
        def columns(n):
            cols = pl.ds(pl.multiple_of(n * 512, 512), 512)
            z[:, cols] = mm(a[...], w[:, cols])

        repeat(cout // 512, columns)

    def wide_stats(z):
        for m in sets:

            def crop_(c, m=m):
                def columns(n):
                    crop_stats(
                        z, m.out0 + c * m.out, m.out, m.out, 512, m.half, 8, m.half * m.half,
                        m.crop0 + c, cs, cm, n * 512,
                    )

                repeat(cout // 512, columns)

            repeat(m.count, crop_)

    wide_product(xe, w7, z7)
    meet_near(3, 1.0)
    wide_stats(z7)
    local_moments(blocks[4], cs, cm, wcol, cout, 0.25)
    links.send_near(4, blocks[4])
    meet_far(3, 1.0, st4, c4)

    loads[4].wait()
    lots = c4 // 128
    hp[:, 0:24, :] = jnp.zeros((lots, 24, 128), f)
    for m in sets:

        def pair(p, m=m):
            r = m.row0 + p * 2 * m.rows
            for j in range(2):
                crop = m.crop0 + 2 * p + j
                mean = by_view(wv, crop, st4[0:2, :])
                scale = by_view(wv, crop, st4[2:4, :]) * norms2[0:1, 0:c4]
                shift = norms2[1:2, 0:c4]
                mask = keep(32, c4, 16, m.edge)
                base = 24 + j * m.guard
                hp[:, base + m.rows : base + m.guard, :] = jnp.zeros((lots, 16, 128), f)

                def tile(i):
                    z = z4[span(r + j * m.rows + i * 32, 32), :]
                    h = jnp.where(mask, act((z - mean) * scale + shift), 0.0)
                    for q in range(lots):
                        hp[q, span(base + i * 32, 32, 8), :] = h[:, q * 128 : (q + 1) * 128]

                repeat(m.rows // 32, tile)
            for a in range(3):
                for b in range(3):
                    for q in range(lots):
                        picked = []
                        for j in range(2):
                            for i in range(m.half):
                                at = 24 + j * m.guard + (2 * i + a - 1) * 16 + b - 1
                                picked.append(hp[q, pl.ds(at, 8, stride=2), :])
                        tap = (3 * a + b) * c4 + q * 128
                        x5[span(m.out0 + p * 2 * m.out, 2 * m.out), tap : tap + 128] = jnp.concatenate(
                            picked, axis=0
                        ).astype(BF16)

        repeat(m.count // 2, pair)
    z5[...] = jnp.zeros(z5.shape, f)

    def taps(t):
        part = pl.ds(pl.multiple_of(t * 3 * c4, 128), 3 * c4)
        z5[...] += mm(x5[:, part], w5[part, :])

    repeat(3, taps)
    for m in sets:

        def crop_(c, m=m):
            crop_stats(z5, m.out0 + c * m.out, m.out, m.out, c4, m.half, 8, m.half * m.half, m.crop0 + c, cs, cm)

        repeat(m.count, crop_)
    local_moments(blocks[5], cs, cm, wcol, c4, 0.25)
    links.send_near(5, blocks[5])
    put(x5, o_x5)
    put(z5, o_z5)
    meet_near(4, 0.25)
    meet_near(5, 0.25)
    meet_far(4, 0.25, st7, cout)
    meet_far(5, 0.25, st5, c4)

    loads[5].wait()
    for m in sets:

        def pair(p, m=m):
            o = m.out0 + p * 2 * m.out
            halves = []
            for j in range(2):
                crop = m.crop0 + 2 * p + j
                mean = by_view(wv, crop, st5[0:2, :])
                scale = by_view(wv, crop, st5[2:4, :]) * norms2[0:1, c4 : 2 * c4]
                z = z5[span(o + j * m.out, m.out, 8), :]
                halves.append(act((z - mean) * scale + norms2[1:2, c4 : 2 * c4]))
            h5[span(o, 2 * m.out), :] = jnp.concatenate(halves, axis=0).astype(BF16)

        repeat(m.count // 2, pair)
    wide_product(h5, w6, z6)
    wide_stats(z6)
    local_moments(blocks[6], cs, cm, wcol, cout, 0.25)
    links.send_near(6, blocks[6])
    put(h5, o_h5)
    loads[7].wait()
    meet_near(6, 0.25)
    meet_far(6, 0.25, st6, cout)

    out_copies[6].wait()
    g6, g7 = 2 * c4, 2 * c4 + cout
    lanes = 512
    for m in sets:

        def pair(p, m=m):
            o = m.out0 + p * 2 * m.out

            def columns(n):
                cols = pl.ds(pl.multiple_of(n * lanes, lanes), lanes)
                cols6 = pl.ds(pl.multiple_of(g6 + n * lanes, lanes), lanes)
                cols7 = pl.ds(pl.multiple_of(g7 + n * lanes, lanes), lanes)
                c = cot[span(o, 2 * m.out), cols].astype(f)
                mask = keep(m.out, lanes, 8, m.half)
                found = []
                for j in range(2):
                    crop = m.crop0 + 2 * p + j
                    rows = span(o + j * m.out, m.out, 8)
                    n6 = (z6[rows, cols] - by_view(wv, crop, st6[0:2, cols])) * by_view(wv, crop, st6[2:4, cols])
                    n7 = (z7[rows, cols] - by_view(wv, crop, st7[0:2, cols])) * by_view(wv, crop, st7[2:4, cols])
                    u = n6 * norms2[0:1, cols6] + norms2[1:2, cols6] + n7 * norms2[0:1, cols7] + norms2[1:2, cols7]
                    a, slope = act_both(u)
                    found.append(a)
                    up = jnp.where(mask, slope * c[j * m.out : (j + 1) * m.out], 0.0)
                    z4[span(n * outs + o + j * m.out, m.out, 8), :] = up
                    for to, part in ((cs, up), (cm, up * n6), (ck, up * n7)):
                        to[pl.ds(crop, 1), cols] = jnp.sum(tile_sum(part), axis=0, keepdims=True)
                w6[span(o, 2 * m.out), cols] = jnp.concatenate(found, axis=0).astype(BF16)

            repeat(cout // lanes, columns)

        repeat(m.count // 2, pair)
    local_sums(blocks[7], (cs, cm, ck), wcol, cout)
    links.send_near(7, blocks[7])
    put(w6.at[0:outs], o_res)
    links.wait_near(7)
    far[7][links.outer] = fold_sums(near[7], links.wide)
    links.send_far(7)
    links.wait_far(7)
    sums = fold_sums(far[7], links.outers)
    for t in range(3):
        unpack(sq, 2 * t, sums[8 * t : 8 * t + 8], cout)

    for m in sets:

        def pair(p, m=m):
            o = m.out0 + p * 2 * m.out

            def columns(n):
                cols = pl.ds(pl.multiple_of(n * lanes, lanes), lanes)
                mask = keep(m.out, lanes, 8, m.half)
                got6, got7 = [], []
                for j in range(2):
                    crop = m.crop0 + 2 * p + j
                    rows = span(o + j * m.out, m.out, 8)
                    up = z4[span(n * outs + o + j * m.out, m.out, 8), :]
                    over = wv[0, crop] * (4.0 / tally_v[0:1, 0:1]) + wv[1, crop] * (4.0 / tally_v[1:2, 0:1])
                    level = by_view(wv, crop, sq[0:2, cols]) * over
                    for got, z, st, at, t in ((got6, z6, st6, g6, 2), (got7, z7, st7, g7, 4)):
                        inv = by_view(wv, crop, st[2:4, cols])
                        gain = inv * norms2[0:1, pl.ds(pl.multiple_of(at + n * lanes, lanes), lanes)]
                        tilt = by_view(wv, crop, sq[t : t + 2, cols]) * over
                        centered = (z[rows, cols] - by_view(wv, crop, st[0:2, cols])) * inv
                        got.append(jnp.where(mask, gain * (up - level - centered * tilt), 0.0))
                w7[span(o, 2 * m.out), cols] = jnp.concatenate(got6, axis=0).astype(BF16)
                w7[span(cin // 2 + o, 2 * m.out), cols] = jnp.concatenate(got7, axis=0).astype(BF16)

            repeat(cout // lanes, columns)

        repeat(m.count // 2, pair)
    put(w7.at[0:outs], o_d6)
    put(w7.at[cin // 2 : cin // 2 + outs], o_d7)
    for src, dst in (
        (st1, o_st1), (st2, o_st2), (st3, o_st3), (st4, o_st4), (st7, o_st7), (st5, o_st5), (st6, o_st6),
        (sq, o_sq), (tally_v, o_tally),
    ):
        put(src, dst)
    links.finish()
    for copy in swaps:
        copy.wait_send()
    for i, copy in enumerate(out_copies):
        if i != 6:
            copy.wait()


def flat_rows(tensor, pitch):
    n, h, w, c = tensor.shape
    return jnp.pad(tensor, ((0, 0), (0, 0), (0, pitch - w), (0, 0))).reshape(n * h * pitch, c)


def forward(images, cots, onehot, pixels, w, norms_first, norms_second, ident):
    crops = lax.axis_size("crops")
    nb, ns = images[0].shape[0] // 2, images[1].shape[0] // 2
    sets, total, guarded, outs = geometry(nb, images[0].shape[2], ns, images[1].shape[2])
    w1, wsp1, w3, w4, w5, w6, w7 = w
    cin, c3 = w1.shape
    c4, cout = w6.shape
    smem, vmem = pl.BlockSpec(memory_space=pltpu.SMEM), pl.BlockSpec(memory_space=pltpu.VMEM)
    hbm = pl.BlockSpec(memory_space=pl.ANY)
    shape = jax.ShapeDtypeStruct
    out_shape = [
        shape((total, cin), BF16), shape((total, c3), F32), shape((guarded, 3 * c3), BF16), shape((total, c3), F32),
        shape((total, c3), BF16), shape((total, cin), BF16), shape((total, c4), F32), shape((outs, 9 * c4), BF16),
        shape((outs, c4), F32), shape((outs, c4), BF16), shape((outs, cin), BF16), shape((outs, cout), BF16),
        shape((outs, cout), BF16), shape((outs, cout), BF16),
        shape((8, c3), F32), shape((8, c3), F32), shape((8, cin), F32), shape((8, c4), F32), shape((8, cout), F32),
        shape((8, c4), F32), shape((8, cout), F32), shape((8, cout), F32), shape((8, 128), F32),
    ]
    most = 2 * sets[0].rows
    scratch = [
        pltpu.VMEM((total, cin), BF16), pltpu.VMEM((total, c3), F32), pltpu.VMEM((guarded, 3 * c3), BF16),
        pltpu.VMEM((total, c3), F32), pltpu.VMEM((total, c3), BF16), pltpu.VMEM((most, cin), F32),
        pltpu.VMEM((total, cin), BF16), pltpu.VMEM((cin // 128, most // 2, 128), F32), pltpu.VMEM((total, c4), F32),
        pltpu.VMEM((outs, cin), BF16), pltpu.VMEM((outs, cout), F32), pltpu.VMEM((c4 // 128, 24 + 2 * sets[0].guard, 128), F32),
        pltpu.VMEM((outs, 9 * c4), BF16), pltpu.VMEM((outs, c4), F32),
        pltpu.VMEM((outs, c4), BF16), pltpu.VMEM((outs, cout), F32), pltpu.VMEM((outs, cout), BF16),
    ]
    scratch += [pltpu.VMEM(t.shape, BF16) for t in w]
    scratch += [pltpu.VMEM((16, cout), F32)] * 3
    scratch += [pltpu.VMEM((8, n), F32) for n in (c3, c3, cin, c4, cout, c4, cout, cout, 128)]
    scratch += exchange_shapes(FWD_WIDTHS, (3, 2, 2, 2, 2, 2, 2, 3), crops)
    scratch += [
        pltpu.SemaphoreType.DMA((8,)), pltpu.SemaphoreType.DMA((nb + ns,)), pltpu.SemaphoreType.DMA((nb + ns,)),
        pltpu.SemaphoreType.DMA((nb + ns,)), pltpu.SemaphoreType.DMA((23,)),
    ]
    rows = jnp.concatenate([onehot, pixels[None, :]], axis=0)
    wide = jnp.pad(rows, ((0, 0), (0, 16 - rows.shape[1])), constant_values=0.0)
    wide = wide.at[2, rows.shape[1] :].set(1.0)
    wcol = jnp.pad(wide.T, ((0, 0), (0, 125)))
    got = pl.pallas_call(
        functools.partial(forward_kernel, sets, total, guarded, outs, crops, (c3, cin, c4, cout)),
        out_shape=out_shape,
        in_specs=[smem, vmem, vmem, vmem] + [hbm] * 10,
        out_specs=[hbm] * len(out_shape),
        scratch_shapes=scratch,
        compiler_params=pltpu.CompilerParams(
            collective_id=ident, has_side_effects=True, vmem_limit_bytes=63 * 1024 * 1024
        ),
        name="forward",
    )(
        onehot, wcol, norms_first, norms_second,
        flat_rows(images[0], 16), flat_rows(images[1], 16),
        jnp.concatenate([flat_rows(t, 8) for t in cots], axis=0), *w,
    )
    return sets, wcol, (total, guarded, outs), got


def share_plan(shapes, cuts):
    chunks = []
    for at, (height, width) in enumerate(shapes):
        down, across = cuts[at]
        half, high = width // 2 // across, height // down
        for c in range(down):
            for p in range(across):
                chunks.append((at, c * high, high, p * half, half))
    return chunks


class Share:
    def __init__(self, shapes, chunks, orders, bits, links, sources, outs, acc, recv0, recvs, sems):
        self.shapes, self.chunks, self.bits = shapes, chunks, bits
        self.k, self.core = links.k, links.r
        self.sources, self.outs, self.acc, self.recv0, self.recvs = sources, outs, acc, recv0, recvs
        self.send_sem, self.recv_sem, self.load_sem, self.store_sem = sems
        self.sibling = (self.k, 1 - self.core)
        self.total = 2 * bits + 2
        self.live, self.loads, self.stores = {}, {}, {}
        digit = [lax.rem(self.k // (1 << b), 2) for b in range(bits)]
        self.stages, self.regions, self.kinds, self.slots = [], [], [], []
        for i, (at, row, height, col, width) in enumerate(chunks):
            stages = []
            for a, b in zip(*orders[i]):
                if a == b:
                    mine, step = digit[a], 1 << a
                else:
                    mine = digit[a] * (1 - self.core) + digit[b] * self.core
                    step = (1 << a) * (1 - self.core) + (1 << b) * self.core
                stages.append((mine, self.k + step * (1 - 2 * mine)))
            start, length, used = 0, height, 0
            region, kind, slot = [], [], []
            for s in range(bits):
                region.append((start, length))
                slot.append(used)
                if length % 32 == 0:
                    kind.append(True)
                    length //= 2
                    start = start + stages[s][0] * length
                else:
                    kind.append(False)
                used += length
            region.append((start, length))
            self.stages.append(stages)
            self.regions.append(region)
            self.kinds.append(kind)
            self.slots.append(slot)

    def send(self, i, t, src, dst, device):
        copy = pltpu.make_async_remote_copy(
            src_ref=src,
            dst_ref=dst,
            send_sem=self.send_sem.at[i, t],
            recv_sem=self.recv_sem.at[i, t],
            device_id=device,
            device_id_type=MESH,
        )
        copy.start()
        self.live[i, t] = copy

    def add(self, dst, at, src, src_at, length):
        block = 16
        while length % (block * 2) == 0 and block * 2 * dst.shape[1] <= 65536:
            block *= 2

        def step(j, carry):
            off = j * block
            rows = span(at + off, block)
            dst[rows, :] = dst[rows, :] + src[span(src_at + off, block), :]
            return carry

        lax.fori_loop(0, length // block, step, 0)

    def arrived(self, i, t):
        if (i, t) in self.live:
            self.live[i, t].wait_recv()

    def task(self, i, t):
        at, row, height, col, width = self.chunks[i]
        bits, kinds, regions, stages = self.bits, self.kinds[i], self.regions[i], self.stages[i]
        half = self.shapes[at][1] // 2
        own = pl.ds(pl.multiple_of(self.core * half + col, 128), width)
        rows = pl.ds(row, height)
        if t == 0:
            away = pl.ds(pl.multiple_of((1 - self.core) * half + col, 128), width)
            self.send(i, 0, self.sources[at].at[rows, away], self.recv0[i], self.sibling)
            copy = pltpu.make_async_copy(self.sources[at].at[rows, own], self.acc[i], self.load_sem.at[i])
            copy.start()
            self.loads[i] = copy
            return
        self.arrived(i, t - 1)
        if t <= bits + 1:
            if t == 1:
                self.loads[i].wait()
                self.add(self.acc[i], 0, self.recv0[i], 0, height)
            else:
                s = t - 2
                start, length = regions[s + 1]
                if not kinds[s]:
                    self.live[i, t - 1].wait_send()
                self.add(self.acc[i], start, self.recvs[i], self.slots[i][s], length)
        if t <= bits:
            s = t - 1
            start, length = regions[s]
            give, first = length, start
            if kinds[s]:
                give = length // 2
                first = start + (1 - stages[s][0]) * give
            self.send(
                i, t, self.acc[i].at[span(first, give)], self.recvs[i].at[pl.ds(self.slots[i][s], give)],
                (stages[s][1], self.core),
            )
            return
        if t == bits + 1:
            start, length = regions[bits]
            mine = self.acc[i].at[span(start, length)]
            copy = pltpu.make_async_copy(mine, self.outs[at].at[span(row + start, length), own], self.store_sem.at[i])
            copy.start()
            self.stores[i] = copy
        if t == bits + 2:
            self.stores[i].wait()
        if t <= 2 * bits:
            s = bits - 1 - (t - bits - 1)
            start, length = regions[s + 1]
            if kinds[s]:
                place = self.outs[at].at[span(row + start, length), own]
                self.send(i, t, mine if t == bits + 1 else place, place, (stages[s][1], self.core))
            return
        if t == 2 * bits + 1:
            place = self.outs[at].at[rows, own]
            self.send(i, t, place, place, self.sibling)

    def step(self, k, starts):
        busy = False
        for i in range(len(self.chunks)):
            t = k - starts[i]
            if 0 <= t < self.total:
                if (i, t) not in self.live:
                    self.task(i, t)
                busy = True
            elif t == self.total:
                self.arrived(i, t - 1)
                busy = True
        return busy

    def finish(self):
        for (i, t), copy in self.live.items():
            if not (1 <= t <= self.bits and not self.kinds[i][t - 1]):
                copy.wait_send()


def share_scratch(shapes, chunks, bits):
    acc, recv0, recvs = [], [], []
    for at, row, height, col, width in chunks:
        acc.append(pltpu.VMEM((height, width), BF16))
        recv0.append(pltpu.VMEM((height, width), BF16))
        length, used = height, 0
        for s in range(bits):
            if length % 32 == 0:
                length //= 2
            used += length
        recvs.append(pltpu.VMEM((used, width), BF16))
    n = len(chunks)
    sems = [pltpu.SemaphoreType.DMA((n, 2 * bits + 2))] * 2 + [pltpu.SemaphoreType.DMA((n,))] * 2
    return acc + recv0 + recvs + sems


def share_orders(bits, straight):
    first, second = list(range(bits)), list(range(bits))
    if bits >= 2:
        second[0], second[1] = 1, 0
        if not straight:
            first = [0] + first[2:] + [1]
            second = [1] + second[2:] + [0]
    return first, second


SHARE_CUTS = ((1, 2), (3, 1), (1, 1), (1, 1), (1, 1), (1, 1), (1, 1))
SHARE_STRAIGHT = (False, True, False, True, False, False, False, True, False, False)
SHARE_STARTS = (0, 1, 3, 4, 5, 2, 6, 7, 8, 11)


def meet_sums(links, e, width, tables, between=None):
    links.wait_near(e)
    links.far[e][links.outer] = fold_sums(links.near[e], links.wide)
    links.send_far(e)
    if between is not None:
        between()
    links.wait_far(e)
    sums = fold_sums(links.far[e], links.outers)
    for t, (table, row) in enumerate(tables):
        unpack(table, row, sums[8 * t : 8 * t + 8], width)


def share_of(wv, tally, crop, times):
    return wv[0, crop] * (times / tally[0:1, 0:1]) + wv[1, crop] * (times / tally[1:2, 0:1])


class Puts:
    def __init__(self, sem):
        self.sem, self.copies = sem, []

    def put(self, src, dst):
        copy = pltpu.make_async_copy(src, dst, self.sem.at[len(self.copies)])
        copy.start()
        self.copies.append(copy)

    def finish(self):
        for copy in self.copies:
            copy.wait()


def start_loads(pairs, sem):
    copies = [pltpu.make_async_copy(src, dst, sem.at[i]) for i, (src, dst) in enumerate(pairs)]
    for copy in copies:
        copy.start()
    return copies


def back_two_kernel(sets, total, outs, crops, dims, *refs):
    c3, cin, c4, cout = dims
    wv, wcol, norms1, norms2, st3, st4, st5, tally = refs[:8]
    sources, refs = refs[8:23], refs[23:]
    (o_up, o_g6, o_g7, o_g5, o_g4, o_s5, o_s4, o_s3), refs = refs[:8], refs[8:]
    held, refs = refs[:15], refs[15:]
    (d6, w6, z5, h5, d7, xe, w7, w5, x5, z4, w4, h2, w3, img, blk) = held
    (q5, t7, d5, pv, dh, d4, zt, bg, up, s5, s4, s3, cs, cm), refs = refs[:14], refs[14:]
    g6, g7, g5, g4 = w6, w7, w5, w4
    blocks, refs = take(refs, 3)
    near, refs = take(refs, 3)
    far, refs = take(refs, 3)
    links = Links(crops, near, far, *refs[:4])
    load_sem, out_sem, up_sem = refs[4:]
    f = F32
    loads = start_loads(list(zip(sources, held)), load_sem)
    links.greet()
    puts = Puts(out_sem)
    for ref in (cs, cm):
        ref[...] = jnp.zeros(ref.shape, f)
    for block in blocks:
        block[...] = jnp.zeros(block.shape, f)

    for i in range(3):
        loads[i].wait()
    q5[...] = mm_nt(d6[...], w6[...])
    g5at = c4
    for m in sets:

        def crop_(c, m=m):
            crop = m.crop0 + c
            rows = span(m.out0 + c * m.out, m.out, 8)
            inv = by_view(wv, crop, st5[2:4, :])
            n = (z5[rows, :] - by_view(wv, crop, st5[0:2, :])) * inv
            q = act_slope(n * norms2[0:1, g5at : 2 * c4] + norms2[1:2, g5at : 2 * c4]) * q5[rows, :]
            q5[rows, :] = q
            cs[pl.ds(crop, 1), 0:c4] = jnp.sum(tile_sum(q), axis=0, keepdims=True)
            cm[pl.ds(crop, 1), 0:c4] = jnp.sum(tile_sum(q * n), axis=0, keepdims=True)

        repeat(m.count, crop_)
    local_sums(blocks[0], (cs, cm), wcol, c4)
    links.send_near(0, blocks[0])

    loads[3].wait()

    def outer(n):
        cols = pl.ds(pl.multiple_of(n * 512, 512), 512)
        g6[:, cols] = mm_tn(h5[...], d6[:, cols]).astype(BF16)

    repeat(cout // 512, outer)
    puts.put(g6, o_g6)

    def rest():
        for i in (4, 5, 6):
            loads[i].wait()

        def shortcut(n):
            part = pl.ds(pl.multiple_of(n * 256, 256), 256)
            t7[:, part] = mm_nt(d7[...], w7[part, :])

        repeat(cin // 256, shortcut)

        def skip(n):
            cols = pl.ds(pl.multiple_of(n * 512, 512), 512)
            g7[:, cols] = mm_tn(xe[...], d7[:, cols]).astype(BF16)

        repeat(cout // 512, skip)
        puts.put(g7, o_g7)

    meet_sums(links, 0, c4, ((s5, 0), (s5, 2)), rest)

    for m in sets:

        def pair(p, m=m):
            o = m.out0 + p * 2 * m.out
            mask = keep(m.out, c4, 8, m.half)
            slots = [[], [], [], []]
            for j in range(2):
                crop = m.crop0 + 2 * p + j
                rows = span(o + j * m.out, m.out, 8)
                over = share_of(wv, tally, crop, 4.0)
                inv = by_view(wv, crop, st5[2:4, :])
                n = (z5[rows, :] - by_view(wv, crop, st5[0:2, :])) * inv
                d = (inv * norms2[0:1, g5at : 2 * c4]) * (
                    q5[rows, :] - by_view(wv, crop, s5[0:2, :]) * over - n * (by_view(wv, crop, s5[2:4, :]) * over)
                )
                d = jnp.where(mask, d, 0.0)
                down = jnp.concatenate([d[8:], jnp.zeros((8, c4), f)], axis=0)
                slots[0].append(d)
                slots[1].append(pltpu.roll(d, m.out - 1, 0))
                slots[2].append(down)
                slots[3].append(pltpu.roll(down, m.out - 1, 0))
            for t in range(4):
                d5[span(o, 2 * m.out), t * c4 : (t + 1) * c4] = jnp.concatenate(slots[t], axis=0).astype(BF16)

        repeat(m.count // 2, pair)

    loads[7].wait()
    options = (((1, 0),), ((2, 0), (0, 1)))
    for a in range(2):
        for b in range(2):
            value = None
            for r, down in options[a]:
                for c, side in options[b]:
                    slot, tap = (2 * down + side) * c4, (3 * r + c) * c4
                    term = mm_nt(d5[:, slot : slot + c4], w5[tap : tap + c4, :])
                    value = term if value is None else value + term
            pv[...] = value
            for m in sets:

                def crop_(c, m=m, a=a, b=b):
                    for i in range(m.half):
                        for q in range(c4 // 128):
                            dh[q, pl.ds(m.row0 + c * m.rows + (2 * i + a) * 16 + b, 8, stride=2), :] = pv[
                                span(m.out0 + c * m.out + i * 8, 8, 8), q * 128 : (q + 1) * 128
                            ]

                repeat(m.count, crop_)
    loads[9].wait()
    for m in sets:

        def crop_(c, m=m):
            crop = m.crop0 + c
            rows = span(m.row0 + c * m.rows, m.rows)
            mask = keep(m.rows, 128, 16, m.edge)
            levels, tilts = [], []
            for q in range(c4 // 128):
                cols = slice(q * 128, (q + 1) * 128)
                inv = by_view(wv, crop, st4[2:4, cols])
                n = (z4[rows, cols] - by_view(wv, crop, st4[0:2, cols])) * inv
                up_ = jnp.where(mask, act_slope(n * norms2[0:1, cols] + norms2[1:2, cols]) * dh[q, rows, :], 0.0)
                dh[q, rows, :] = up_
                levels.append(jnp.sum(tile_sum(up_), axis=0, keepdims=True))
                tilts.append(jnp.sum(tile_sum(up_ * n), axis=0, keepdims=True))
            cs[pl.ds(crop, 1), 0:c4] = jnp.concatenate(levels, axis=1)
            cm[pl.ds(crop, 1), 0:c4] = jnp.concatenate(tilts, axis=1)

        repeat(m.count, crop_)
    local_sums(blocks[1], (cs, cm), wcol, c4)
    links.send_near(1, blocks[1])
    loads[8].wait()

    def kernel(t):
        part = pl.ds(pl.multiple_of(t * c4, c4), c4)
        g5[part, :] = mm_tn(x5[:, part], d5[:, 0:c4]).astype(BF16)

    repeat(5, kernel)

    def rest():
        repeat(4, lambda t: kernel(t + 5))
        puts.put(g5, o_g5)

    meet_sums(links, 1, c4, ((s4, 0), (s4, 2)), rest)

    for i in range(10, 14):
        loads[i].wait()
    for at, m in enumerate(sets):

        def pair(p, m=m, at=at):
            r = m.row0 + p * 2 * m.rows
            o = m.out0 + p * 2 * m.out
            mask = keep(m.rows, 128, 16, m.edge)
            for j in range(2):
                crop = m.crop0 + 2 * p + j
                rows = span(r + j * m.rows, m.rows)
                over = share_of(wv, tally, crop, 1.0)
                for q in range(c4 // 128):
                    cols = slice(q * 128, (q + 1) * 128)
                    inv = by_view(wv, crop, st4[2:4, cols])
                    n = (z4[rows, cols] - by_view(wv, crop, st4[0:2, cols])) * inv
                    d = (inv * norms2[0:1, cols]) * (
                        dh[q, rows, :] - by_view(wv, crop, s4[0:2, cols]) * over - n * (by_view(wv, crop, s4[2:4, cols]) * over)
                    )
                    d4[rows, cols] = jnp.where(mask, d, 0.0).astype(BF16)
            got = mm_nt(d4[span(r, 2 * m.rows), :], w4[...])
            for q in range(cin // 128):
                bg[q, 0 : 2 * m.rows, :] = got[:, q * 128 : (q + 1) * 128]
            for q in range(cin // 128):
                for j in range(2):
                    for i in range(m.half):
                        here = pl.ds(j * m.rows + i * 32, 8, stride=2)
                        bg[q, here, :] = bg[q, here, :] + t7[span(o + j * m.out + i * 8, 8, 8), q * 128 : (q + 1) * 128]
            zt[0 : 2 * m.rows, :] = mm(h2[span(r, 2 * m.rows), :], w3[...])
            step = m.rows // 2
            mask = keep(step, 128, 16, m.edge)
            for j in range(2):
                crop = m.crop0 + 2 * p + j
                levels, tilts = [], []
                for q in range(cin // 128):
                    cols = slice(q * 128, (q + 1) * 128)
                    at3 = slice(2 * c3 + q * 128, 2 * c3 + (q + 1) * 128)
                    mean, inv = by_view(wv, crop, st3[0:2, cols]), by_view(wv, crop, st3[2:4, cols])
                    gain, bias = norms1[0:1, at3], norms1[1:2, at3]

                    def tile(i, sums, j=j, cols=cols, q=q, mean=mean, inv=inv, gain=gain, bias=bias):
                        here = span(j * m.rows + i * step, step)
                        rows = span(r + j * m.rows + i * step, step)
                        n = (zt[here, cols] - mean) * inv
                        u = n * gain + bias + img[rows, cols].astype(f)
                        got = bg[q, here, :].astype(BF16).astype(f)
                        v = jnp.where(mask, act_slope(u) * got, 0.0)
                        up[rows, cols] = v
                        return (sums[0] + tile_sum(v), sums[1] + tile_sum(v * n))

                    zero = jnp.zeros((8, 128), f)
                    s, t = lax.fori_loop(0, 2, tile, (zero, zero))
                    levels.append(jnp.sum(s, axis=0, keepdims=True))
                    tilts.append(jnp.sum(t, axis=0, keepdims=True))
                cs[pl.ds(crop, 1), :] = jnp.concatenate(levels, axis=1)
                cm[pl.ds(crop, 1), :] = jnp.concatenate(tilts, axis=1)
            pltpu.make_async_copy(
                up.at[span(r, 2 * m.rows)], o_up.at[span(r, 2 * m.rows)], up_sem.at[m.crop0 // 2 + p]
            ).start()

        repeat(m.count // 2, pair)
    local_sums(blocks[2], (cs, cm), wcol, cin)
    links.send_near(2, blocks[2])
    loads[14].wait()

    def inner(n):
        part = pl.ds(pl.multiple_of(n * 256, 256), 256)
        g4[part, :] = mm_tn(blk[:, part], d4[...]).astype(BF16)

    repeat(2, inner)

    def rest():
        repeat(cin // 256 - 2, lambda n: inner(n + 2))
        puts.put(g4, o_g4)

    meet_sums(links, 2, cin, ((s3, 0), (s3, 2)), rest)
    for src, dst in ((s5, o_s5), (s4, o_s4), (s3, o_s3)):
        puts.put(src, dst)
    for m in sets:

        def pair(p, m=m):
            r = m.row0 + p * 2 * m.rows
            pltpu.make_async_copy(
                up.at[span(r, 2 * m.rows)], o_up.at[span(r, 2 * m.rows)], up_sem.at[m.crop0 // 2 + p]
            ).wait()

        repeat(m.count // 2, pair)
    links.finish()
    puts.finish()


def back_one_kernel(sets, total, guarded, crops, dims, shapes, chunks, *refs):
    c3, cin = dims
    wv, wcol, norms1, st1, st2, st3, s3, tally = refs[:8]
    sources, refs = refs[8:17], refs[17:]
    second, refs = list(refs[:4]), refs[4:]
    (o_gb, o_gs, o_s2, o_s1), refs = refs[:4], refs[4:]
    o_grads, refs = refs[:7], refs[7:]
    held, refs = refs[:9], refs[9:]
    (h2, w3, up, z2, h1, wsp1, z1, w1, img) = held
    (zt, d3, q2, d2, q1, d1, g3, g2, g1, s2, s1, cs, cm), refs = refs[:13], refs[13:]
    blocks, refs = take(refs, 2)
    near, refs = take(refs, 2)
    far, refs = take(refs, 2)
    links = Links(crops, near, far, *refs[:4])
    load_sem, out_sem, own_sem, grad_send, grad_recv, up_sem = refs[4:10]
    refs = refs[10:]
    n = len(chunks)
    bits = crops.bit_length() - 1
    acc, refs = take(refs, n)
    recv0, refs = take(refs, n)
    recvs, refs = take(refs, n)
    share = Share(
        shapes, chunks, [share_orders(bits, s) for s in SHARE_STRAIGHT], bits, links, second + [g3, g2, g1], o_grads,
        acc, recv0, recvs, refs,
    )
    clock = [0]

    def tick():
        clock[0] += 1
        return share.step(clock[0], SHARE_STARTS)

    core = links.r
    sibling = (links.k, 1 - core)
    f = F32
    loads = start_loads([(a, b) for a, b in zip(sources, held) if b is not up], load_sem)
    ups = []
    for m in sets:
        for p in range(m.count // 2):
            rows = pl.ds(m.row0 + p * 2 * m.rows, 2 * m.rows)
            ups.append(pltpu.make_async_copy(sources[2].at[rows], up.at[rows], up_sem.at[len(ups)]))
    for copy in ups:
        copy.start()
    links.greet()
    for i in range(7):
        share.task(i, 0)
    puts = Puts(out_sem)
    for ref in (cs, cm):
        ref[...] = jnp.zeros(ref.shape, f)
    for block in blocks:
        block[...] = jnp.zeros(block.shape, f)
    d2[0:16, :] = jnp.zeros((16, 3 * c3), BF16)
    for m in sets:
        for c in range(m.count):
            at = m.guard0 + c * m.guard + m.rows
            d2[at : at + 16, :] = jnp.zeros((16, 3 * c3), BF16)

    for i in range(3):
        loads[i].wait()
    for copy in ups:
        copy.wait()
    for m in sets:

        def pair(p, m=m):
            r = m.row0 + p * 2 * m.rows
            step = m.rows // 2
            mask = keep(step, 128, 16, m.edge)
            for h, j in [(h, j) for h in range(cin // 512) for j in range(2)]:
                if j == 0:
                    zt[0 : 2 * m.rows, :] = mm(h2[span(r, 2 * m.rows), :], w3[:, h * 512 : (h + 1) * 512])
                crop = m.crop0 + 2 * p + j
                over = share_of(wv, tally, crop, 1.0)
                for q in range(h * 4, h * 4 + 4):
                    cols = slice(q * 128, (q + 1) * 128)
                    part = slice((q - h * 4) * 128, (q - h * 4 + 1) * 128)
                    mean, inv = by_view(wv, crop, st3[0:2, cols]), by_view(wv, crop, st3[2:4, cols])
                    gain = inv * norms1[0:1, 2 * c3 + q * 128 : 2 * c3 + (q + 1) * 128]
                    level = by_view(wv, crop, s3[0:2, cols]) * over
                    tilt = by_view(wv, crop, s3[2:4, cols]) * over * inv

                    def tile(i, j=j, cols=cols, part=part, mean=mean, gain=gain, level=level, tilt=tilt):
                        here = span(j * m.rows + i * step, step)
                        rows = span(r + j * m.rows + i * step, step)
                        d = gain * (up[rows, cols] - level - (zt[here, part] - mean) * tilt)
                        d3[rows, cols] = jnp.where(mask, d, 0.0).astype(BF16)

                    repeat(2, tile)
            q2[span(r, 2 * m.rows), :] = mm_nt(d3[span(r, 2 * m.rows), :], w3[...])
            for j in range(2):
                crop = m.crop0 + 2 * p + j
                mean, inv = by_view(wv, crop, st2[0:2, :]), by_view(wv, crop, st2[2:4, :])

                def tile(i, sums, j=j, mean=mean, inv=inv):
                    rows = span(r + j * m.rows + i * step, step)
                    n = (z2[rows, :] - mean) * inv
                    v = act_slope(n * norms1[0:1, c3 : 2 * c3] + norms1[1:2, c3 : 2 * c3]) * q2[rows, :]
                    q2[rows, :] = v
                    return (sums[0] + tile_sum(v), sums[1] + tile_sum(v * n))

                zero = jnp.zeros((8, c3), f)
                s, t = lax.fori_loop(0, 2, tile, (zero, zero))
                cs[pl.ds(crop, 1), 0:c3] = jnp.sum(s, axis=0, keepdims=True)
                cm[pl.ds(crop, 1), 0:c3] = jnp.sum(t, axis=0, keepdims=True)

        repeat(m.count // 2, pair)
        tick()
    local_sums(blocks[0], (cs, cm), wcol, c3)
    links.send_near(0, blocks[0])

    def outer(n):
        cols = pl.ds(pl.multiple_of(n * 256, 256), 256)
        g3[:, cols] = mm_tn(h2[...], d3[:, cols]).astype(BF16)

    repeat(cin // 512, outer)
    tick()

    def rest():
        repeat(cin // 512, lambda n: outer(n + cin // 512))
        tick()

    meet_sums(links, 0, c3, ((s2, 0), (s2, 2)), rest)

    for i in range(3, 6):
        loads[i].wait()
    for m in sets:

        def pair(p, m=m):
            r = m.row0 + p * 2 * m.rows
            g = m.guard0 + p * 2 * m.guard
            step = m.rows // 2
            mask = keep(step, c3, 16, m.edge)
            for j in range(2):
                crop = m.crop0 + 2 * p + j
                over = share_of(wv, tally, crop, 1.0)
                mean, inv = by_view(wv, crop, st2[0:2, :]), by_view(wv, crop, st2[2:4, :])
                gain = inv * norms1[0:1, c3 : 2 * c3]
                level = by_view(wv, crop, s2[0:2, :]) * over
                tilt = by_view(wv, crop, s2[2:4, :]) * over * inv

                def tile(i, j=j, mean=mean, gain=gain, level=level, tilt=tilt):
                    rows = span(r + j * m.rows + i * step, step)
                    d = gain * (q2[rows, :] - level - (z2[rows, :] - mean) * tilt)
                    d = jnp.where(mask, d, 0.0)
                    to = span(g + j * m.guard + i * step, step)
                    d2[to, 0:c3] = pltpu.roll(d, step - 1, 0).astype(BF16)
                    d2[to, c3 : 2 * c3] = d.astype(BF16)
                    d2[to, 2 * c3 : 3 * c3] = pltpu.roll(d, 1, 0).astype(BF16)

                repeat(2, tile)
            size = 2 * m.rows + 16
            value = None
            for a in range(3):
                for b in range(3):
                    part = d2[span(g - (a - 1) * 16, size), b * c3 : (b + 1) * c3]
                    term = mm_nt(part, wsp1[a, b * c3 : (b + 1) * c3, :])
                    value = term if value is None else value + term
            q1[span(r, m.rows), :] = value[0 : m.rows]
            q1[span(r + m.rows, m.rows), :] = value[m.guard : m.guard + m.rows]
            for j in range(2):
                crop = m.crop0 + 2 * p + j
                mean, inv = by_view(wv, crop, st1[0:2, :]), by_view(wv, crop, st1[2:4, :])

                def tile(i, sums, j=j, mean=mean, inv=inv):
                    rows = span(r + j * m.rows + i * step, step)
                    n = (z1[rows, :] - mean) * inv
                    v = act_slope(n * norms1[0:1, 0:c3] + norms1[1:2, 0:c3]) * q1[rows, :]
                    v = jnp.where(mask, v, 0.0)
                    q1[rows, :] = v
                    return (sums[0] + tile_sum(v), sums[1] + tile_sum(v * n))

                zero = jnp.zeros((8, c3), f)
                s, t = lax.fori_loop(0, 2, tile, (zero, zero))
                cs[pl.ds(crop, 1), 0:c3] = jnp.sum(s, axis=0, keepdims=True)
                cm[pl.ds(crop, 1), 0:c3] = jnp.sum(t, axis=0, keepdims=True)

        repeat(m.count // 2, pair)
        tick()
    local_sums(blocks[1], (cs, cm), wcol, c3)
    links.send_near(1, blocks[1])
    inside = guarded - 32

    def taps(a):
        g2[a * 3 * c3 : (a + 1) * 3 * c3, :] = mm_tn(
            h1[a * 16 : a * 16 + inside, :], d2[16 : 16 + inside, c3 : 2 * c3]
        ).astype(BF16)

    taps(0)
    tick()

    def rest():
        taps(1)
        taps(2)
        tick()

    meet_sums(links, 1, c3, ((s1, 0), (s1, 2)), rest)

    loads[6].wait()
    moves = []
    for m, out in zip(sets, (o_gb, o_gs)):
        part = m.rows // 2
        for c in range(m.count):
            i = m.crop0 + c
            own_rows = span(m.row0 + c * m.rows + core * part, part)
            other_rows = span(m.row0 + c * m.rows + (1 - core) * part, part)
            place = out.at[span((core * m.count + c) * part, part)]
            moves.append(
                (
                    pltpu.make_async_copy(d3.at[own_rows], place, own_sem.at[i]),
                    pltpu.make_async_remote_copy(
                        src_ref=d3.at[other_rows],
                        dst_ref=place,
                        send_sem=grad_send.at[i],
                        recv_sem=grad_recv.at[i],
                        device_id=sibling,
                        device_id_type=MESH,
                    ),
                )
            )
    for m in sets:

        def pair(p, m=m):
            r = m.row0 + p * 2 * m.rows
            step = m.rows // 2
            mask = keep(step, c3, 16, m.edge)
            for j in range(2):
                crop = m.crop0 + 2 * p + j
                over = share_of(wv, tally, crop, 1.0)
                mean, inv = by_view(wv, crop, st1[0:2, :]), by_view(wv, crop, st1[2:4, :])
                gain = inv * norms1[0:1, 0:c3]
                level = by_view(wv, crop, s1[0:2, :]) * over
                tilt = by_view(wv, crop, s1[2:4, :]) * over * inv

                def tile(i, j=j, mean=mean, gain=gain, level=level, tilt=tilt):
                    rows = span(r + j * m.rows + i * step, step)
                    d = gain * (q1[rows, :] - level - (z1[rows, :] - mean) * tilt)
                    d1[rows, :] = jnp.where(mask, d, 0.0).astype(BF16)

                repeat(2, tile)
            rows = span(r, 2 * m.rows)
            for n in range(cin // 256):
                cols = slice(n * 256, (n + 1) * 256)
                d3[rows, cols] = (up[rows, cols] + mm_nt(d1[rows, :], w1[cols, :])).astype(BF16)

        repeat(m.count // 2, pair)
        for c in range(m.count):
            for copy in moves[m.crop0 + c]:
                copy.start()
        tick()
    loads[7].wait()

    def inner(n):
        part = pl.ds(pl.multiple_of(n * 256, 256), 256)
        g1[part, :] = mm_tn(img[:, part], d1[...]).astype(BF16)

    repeat(cin // 256, inner)
    for src, dst in ((s2, o_s2), (s1, o_s1)):
        puts.put(src, dst)
    while tick():
        pass
    share.finish()
    links.finish()
    for near_copy, far_copy in moves:
        near_copy.wait()
        far_copy.wait()
    puts.finish()


def backward(sets, got, onehot, wcol, w, norms_first, norms_second, total, guarded, outs, idents):
    crops = lax.axis_size("crops")
    w1, wsp1, w3, w4, w5, w6, w7 = w
    cin, c3 = w1.shape
    c4, cout = w6.shape
    (
        f_img, f_z1, f_h1, f_z2, f_h2, f_blk, f_z4, f_x5, f_z5, f_h5, f_xe, f_res, f_d6, f_d7,
        f_st1, f_st2, f_st3, f_st4, f_st7, f_st5, f_st6, f_sq, f_n,
    ) = got
    smem, vmem = pl.BlockSpec(memory_space=pltpu.SMEM), pl.BlockSpec(memory_space=pltpu.VMEM)
    hbm = pl.BlockSpec(memory_space=pl.ANY)
    shape = jax.ShapeDtypeStruct
    most = 2 * sets[0].rows
    pairs = sum(m.count for m in sets) // 2
    count = 2 * pairs

    def like(arrays):
        return [pltpu.VMEM(t.shape, t.dtype) for t in arrays]

    def params(ident):
        return pltpu.CompilerParams(
            collective_id=ident, has_side_effects=True, vmem_limit_bytes=63 * 1024 * 1024
        )

    arrays = [f_d6, w6, f_z5, f_h5, f_d7, f_xe, w7, w5, f_x5, f_z4, w4, f_h2, w3, f_img, f_blk]
    out_shape = [
        shape((total, cin), F32), shape((c4, cout), BF16), shape((cin, cout), BF16), shape((9 * c4, c4), BF16),
        shape((cin, c4), BF16), shape((8, c4), F32), shape((8, c4), F32), shape((8, cin), F32),
    ]
    scratch = like(arrays) + [
        pltpu.VMEM((outs, c4), F32), pltpu.VMEM((outs, cin), F32), pltpu.VMEM((outs, 4 * c4), BF16),
        pltpu.VMEM((outs, c4), F32), pltpu.VMEM((c4 // 128, total, 128), F32), pltpu.VMEM((total, c4), BF16),
        pltpu.VMEM((most, cin), F32), pltpu.VMEM((cin // 128, most, 128), F32), pltpu.VMEM((total, cin), F32),
        pltpu.VMEM((8, c4), F32), pltpu.VMEM((8, c4), F32), pltpu.VMEM((8, cin), F32),
        pltpu.VMEM((16, cin), F32), pltpu.VMEM((16, cin), F32),
    ]
    scratch += exchange_shapes((c4, c4, cin), (2, 2, 2), crops)
    scratch += [pltpu.SemaphoreType.DMA((15,)), pltpu.SemaphoreType.DMA((7,)), pltpu.SemaphoreType.DMA((pairs,))]
    up, g_outer2, g_skip, g_spatial2, g_inner2, s5, s4, s3 = pl.pallas_call(
        functools.partial(back_two_kernel, sets, total, outs, crops, (c3, cin, c4, cout)),
        out_shape=out_shape,
        in_specs=[smem] + [vmem] * 7 + [hbm] * 15,
        out_specs=[hbm] * len(out_shape),
        scratch_shapes=scratch,
        compiler_params=params(idents[0]),
        name="back_two",
    )(onehot, wcol, norms_first, norms_second, f_st3, f_st4, f_st5, f_n, *arrays)

    arrays = [f_h2, w3, up, f_z2, f_h1, wsp1, f_z1, w1, f_img]
    shapes = [(cin, cout), (9 * c4, c4), (c4, cout), (cin, c4), (c3, cin), (9 * c3, c3), (cin, c3)]
    chunks = share_plan(shapes, SHARE_CUTS)
    out_shape = [
        shape((total_rows(sets[0]), cin), BF16), shape((total_rows(sets[1]), cin), BF16), shape((8, c3), F32),
        shape((8, c3), F32),
    ] + [shape(t, BF16) for t in shapes]
    scratch = like(arrays) + [
        pltpu.VMEM((most, 512), F32), pltpu.VMEM((total, cin), BF16), pltpu.VMEM((total, c3), F32),
        pltpu.VMEM((guarded, 3 * c3), BF16), pltpu.VMEM((total, c3), F32), pltpu.VMEM((total, c3), BF16),
        pltpu.VMEM((c3, cin), BF16), pltpu.VMEM((9 * c3, c3), BF16), pltpu.VMEM((cin, c3), BF16),
        pltpu.VMEM((8, c3), F32), pltpu.VMEM((8, c3), F32), pltpu.VMEM((16, c3), F32), pltpu.VMEM((16, c3), F32),
    ]
    scratch += exchange_shapes((c3, c3), (2, 2), crops)
    scratch += [pltpu.SemaphoreType.DMA((9,)), pltpu.SemaphoreType.DMA((2,))]
    scratch += [pltpu.SemaphoreType.DMA((count,))] * 3 + [pltpu.SemaphoreType.DMA((pairs,))]
    scratch += share_scratch(shapes, chunks, crops.bit_length() - 1)
    grad_b, grad_s, s2, s1, *grads = pl.pallas_call(
        functools.partial(back_one_kernel, sets, total, guarded, crops, (c3, cin), shapes, chunks),
        out_shape=out_shape,
        in_specs=[smem] + [vmem] * 7 + [hbm] * 13,
        out_specs=[hbm] * len(out_shape),
        scratch_shapes=scratch,
        compiler_params=params(idents[1]),
        name="back_one",
    )(onehot, wcol, norms_first, f_st1, f_st2, f_st3, s3, f_n, *arrays, g_skip, g_spatial2, g_outer2, g_inner2)
    return grad_b, grad_s, grads, (s1, s2, s3, s4, s5)


def total_rows(m):
    return m.count * m.rows


def shards(
    image_big,
    image_small,
    view_big,
    view_small,
    inner_first,
    spatial_first,
    outer_first,
    norms_first,
    inner_second,
    spatial_second,
    outer_second,
    skip_second,
    norms_second,
    cotangent_big,
    cotangent_small,
):
    splits, position = lax.axis_size("rows"), lax.axis_index("rows")
    labels = jnp.concatenate(
        [
            lax.dynamic_slice_in_dim(v, position * (v.shape[0] // splits), v.shape[0] // splits)
            for v in (view_big, view_small)
        ]
    )
    onehot = (labels[None, :] == jnp.arange(2)[:, None]).astype(F32)
    nb, ns = image_big.shape[0] // splits, image_small.shape[0] // splits
    pixels = jnp.concatenate(
        [
            jnp.full((nb,), float(image_big.shape[2] ** 2), F32),
            jnp.full((ns,), float(image_small.shape[2] ** 2), F32),
        ]
    )
    c3, c4 = inner_first.shape[1], inner_second.shape[1]
    weights = [
        inner_first,
        spatial_first.reshape(3, 3 * c3, c3),
        outer_first,
        inner_second,
        spatial_second.reshape(9 * c4, c4),
        outer_second,
        skip_second,
    ]
    sets, wcol, sizes, got = forward(
        [image_big, image_small], [cotangent_big, cotangent_small], onehot, pixels, weights, norms_first, norms_second, 0
    )
    grad_b, grad_s, grads, sums = backward(
        sets, got, onehot, wcol, weights, norms_first, norms_second, *sizes, (1, 2)
    )
    s1, s2, s3, s4, s5 = sums
    sq = got[21]

    def both(parts):
        return jnp.concatenate(
            [jnp.stack([t[g] + t[g + 1], t[0] + t[1]]) for t, g in parts], axis=1
        )

    g_skip, g_spatial2, g_outer2, g_inner2, g_outer1, g_spatial1, g_inner1 = [
        t.astype(F32) for t in grads
    ]
    results = [
        got[11][m.out0 : m.out0 + m.count * m.out].reshape(m.count, m.half, 8, -1)[:, :, : m.half]
        for m in sets
    ]
    gradients = [
        t.reshape(image.shape[0], image.shape[1], 16, -1)[:, :, : image.shape[2]]
        for t, image in ((grad_b, image_big), (grad_s, image_small))
    ]
    return (
        results[0],
        results[1],
        gradients[0],
        gradients[1],
        g_inner1,
        g_spatial1.reshape(spatial_first.shape),
        g_outer1,
        both(((s1, 2), (s2, 2), (s3, 2))),
        g_inner2,
        g_spatial2.reshape(spatial_second.shape),
        g_outer2,
        g_skip,
        both(((s4, 2), (s5, 2), (sq, 2), (sq, 4))),
    )


def solution(mesh):
    maps = P("crops", "rows", None, None)
    whole = P(("crops", "rows"), None, None, None)
    in_specs = (maps, maps, P("crops"), P("crops")) + (P(),) * 9 + (whole, whole)
    out_specs = (whole, whole, maps, maps) + (P(),) * 9
    return jax.shard_map(shards, mesh=mesh, in_specs=in_specs, out_specs=out_specs, check_vma=False)
```

```python
import functools

import jax
import jax.numpy as jnp
from jax import lax
from jax.experimental import pallas as pl
from jax.experimental.pallas import tpu as pltpu
from jax.sharding import PartitionSpec as P

HIGH = lax.Precision.HIGHEST
EPS = 1e-05
MESH = pl.DeviceIdType.MESH
F32 = jnp.float32
BF16 = jnp.bfloat16


class Maps:
    def __init__(self, count, edge, row0, crop0, guard0, out0):
        self.count, self.edge = count, edge
        self.row0, self.crop0, self.guard0, self.out0 = row0, crop0, guard0, out0
        self.rows = edge * 16
        self.guard = (edge + 1) * 16
        self.half = edge // 2
        self.out = self.half * 8
        self.pixels = edge * edge


def geometry(nb, eb, ns, es):
    big = Maps(nb, eb, 0, 0, 16, 0)
    small = Maps(ns, es, nb * big.rows, nb, 16 + nb * big.guard, nb * big.out)
    total = small.row0 + ns * small.rows
    guarded = small.guard0 + ns * small.guard
    out = small.out0 + ns * small.out
    return (big, small), total, guarded, out


def al(x, m=16):
    return x if isinstance(x, int) else pl.multiple_of(x, m)


def span(start, size, m=16):
    return pl.ds(al(start, m), size)


def repeat(count, body):
    def step(i, carry):
        body(i)
        return carry

    lax.fori_loop(0, count, step, 0)


def mm(a, b):
    return jnp.dot(a, b, preferred_element_type=F32)


def mm_nt(a, b):
    return lax.dot_general(a, b, (((1,), (1,)), ((), ())), preferred_element_type=F32)


def mm_tn(a, b):
    return lax.dot_general(a, b, (((0,), (0,)), ((), ())), preferred_element_type=F32)


CA = 0.7978845608028654
CB = 0.7978845608028654 * 0.044715


def act(u):
    t = jnp.tanh(u * (CA + CB * (u * u)))
    return 0.5 * u * (1.0 + t)


def act_slope(u):
    s = u * u
    t = jnp.tanh(u * (CA + CB * s))
    rise = (0.5 * u) * (CA + (3.0 * CB) * s)
    return 0.5 * (1.0 + t) + (1.0 - t * t) * rise


def act_both(u):
    s = u * u
    t = jnp.tanh(u * (CA + CB * s))
    hu = 0.5 * u
    lift = 0.5 * (1.0 + t)
    slope = lift + (1.0 - t * t) * (hu * (CA + (3.0 * CB) * s))
    return u * lift, slope


def keep(rows, width, pitch, edge):
    place = lax.broadcasted_iota(jnp.int32, (rows, width), 0)
    return lax.rem(place, pitch) < edge


def tile_sum(x):
    return jnp.sum(x.reshape(x.shape[0] // 8, 8, x.shape[1]), axis=0)


def pieces(width):
    return (4, width // 4) if width >= 512 else (width // 128, 128)


class Links:
    def __init__(self, crops, near, far, near_s, near_r, far_s, far_r):
        self.group = 4 if crops % 4 == 0 else 1
        self.outers = crops // self.group
        self.k, self.r = lax.axis_index("crops"), lax.axis_index("rows")
        inner, self.outer = lax.rem(self.k, self.group), self.k // self.group
        self.wide = 2 * self.group
        self.me = inner * 2 + self.r
        self.peers, self.others = [], []
        for d in range(1, self.wide):
            p = lax.rem(self.me + d, self.wide)
            self.peers.append((self.outer * self.group + p // 2, lax.rem(p, 2)))
        for d in range(1, self.outers):
            self.others.append((lax.rem(self.outer + d, self.outers) * self.group + inner, self.r))
        self.near, self.far = near, far
        self.sems = (near_s, near_r, far_s, far_r)
        self.live = {}

    def greet(self, extra=()):
        barrier = pltpu.get_barrier_semaphore()
        peers = self.peers + self.others + list(extra)
        for peer in peers:
            pl.semaphore_signal(barrier, inc=1, device_id=peer, device_id_type=MESH)
        pl.semaphore_wait(barrier, len(peers))

    def send_near(self, e, block):
        self.near[e][self.me] = block[...]
        self.live[e, 0] = []
        for d, peer in enumerate(self.peers):
            copy = pltpu.make_async_remote_copy(
                src_ref=block,
                dst_ref=self.near[e].at[self.me],
                send_sem=self.sems[0].at[e, d],
                recv_sem=self.sems[1].at[e, d],
                device_id=peer,
                device_id_type=MESH,
            )
            copy.start()
            self.live[e, 0].append(copy)

    def wait_near(self, e):
        for copy in self.live[e, 0]:
            copy.wait_recv()

    def send_far(self, e):
        self.live[e, 1] = []
        place = self.far[e].at[self.outer]
        for d, peer in enumerate(self.others):
            copy = pltpu.make_async_remote_copy(
                src_ref=place,
                dst_ref=place,
                send_sem=self.sems[2].at[e, d],
                recv_sem=self.sems[3].at[e, d],
                device_id=peer,
                device_id_type=MESH,
            )
            copy.start()
            self.live[e, 1].append(copy)

    def wait_far(self, e):
        for copy in self.live[e, 1]:
            copy.wait_recv()

    def finish(self):
        for copies in self.live.values():
            for copy in copies:
                copy.wait_send()


def fold_moments(buf, tallies, count, scale):
    sums, total = buf[0, 0:8, :], tallies[0]
    for i in range(1, count):
        sums = sums + buf[i, 0:8, :]
        total = total + tallies[i]
    mean = sums / jnp.maximum(total * scale, 1.0)
    spread = None
    for i in range(count):
        n = tallies[i] * scale
        apart = buf[i, 0:8, :] / jnp.maximum(n, 1.0) - mean
        term = buf[i, 8:16, :] + n * apart * apart
        spread = term if spread is None else spread + term
    return sums, spread, total


def fold_sums(buf, count):
    total = buf[0]
    for i in range(1, count):
        total = total + buf[i]
    return total


def exchange_shapes(widths, tiles, crops):
    group = 4 if crops % 4 == 0 else 1
    outers = crops // group
    blocks, near, far = [], [], []
    for width, tile in zip(widths, tiles):
        lanes = pieces(width)[1]
        blocks.append(pltpu.VMEM((8 * tile, lanes), F32))
        near.append(pltpu.VMEM((2 * group, 8 * tile, lanes), F32))
        far.append(pltpu.VMEM((outers, 8 * tile, lanes), F32))
    e = len(widths)
    sems = [
        pltpu.SemaphoreType.DMA((e, 2 * group - 1)),
        pltpu.SemaphoreType.DMA((e, 2 * group - 1)),
        pltpu.SemaphoreType.DMA((e, max(outers - 1, 1))),
        pltpu.SemaphoreType.DMA((e, max(outers - 1, 1))),
    ]
    return blocks + near + far + sems


def take(refs, count):
    return list(refs[:count]), refs[count:]


def pack(block, tile, rows, width):
    count, lanes = pieces(width)
    for q in range(count):
        for v in range(2):
            block[tile * 8 + 2 * q + v : tile * 8 + 2 * q + v + 1, :] = rows[v][:, q * lanes : (q + 1) * lanes]


def unpack(table, row, tile, width):
    count, lanes = pieces(width)
    for q in range(count):
        table[row : row + 2, q * lanes : (q + 1) * lanes] = tile[2 * q : 2 * q + 2, :]


def crop_stats(ref, row0, rows, step, width, edge, pitch, pixels, crop, cs, cm, col0=0):
    mask = keep(step, width, pitch, edge)
    zero = jnp.zeros((8, width), F32)
    cols = pl.ds(col0, width) if isinstance(col0, int) else pl.ds(pl.multiple_of(col0, 128), width)

    def first(i, acc):
        z = ref[span(row0 + i * step, step, 8), cols]
        return acc + tile_sum(jnp.where(mask, z, 0.0))

    s = jnp.sum(lax.fori_loop(0, rows // step, first, zero), axis=0, keepdims=True)
    mean = s * (1.0 / pixels)

    def second(i, acc):
        z = ref[span(row0 + i * step, step, 8), cols]
        d = jnp.where(mask, z - mean, 0.0)
        return acc + tile_sum(d * d)

    m = jnp.sum(lax.fori_loop(0, rows // step, second, zero), axis=0, keepdims=True)
    cs[pl.ds(crop, 1), cols] = s
    cm[pl.ds(crop, 1), cols] = m


def local_moments(block, cs, cm, wcol, width, scale, tally=False):
    s, m = cs[:, 0:width], cm[:, 0:width]
    pix = wcol[:, 2:3] * scale
    mean_c = s / pix
    sums, squares, tallies = [], [], []
    for v in range(2):
        w = wcol[:, v : v + 1]
        total = jnp.sum(w * s, axis=0, keepdims=True)
        n = jnp.sum(w * pix, axis=0, keepdims=True)
        apart = mean_c - total / jnp.maximum(n, 1.0)
        squares.append(jnp.sum(w * (m + pix * apart * apart), axis=0, keepdims=True))
        sums.append(total)
        tallies.append(n)
    pack(block, 0, sums, width)
    pack(block, 1, squares, width)
    if tally:
        lanes = pieces(width)[1]
        for q in range(4):
            for v in range(2):
                block[16 + 2 * q + v : 17 + 2 * q + v, :] = jnp.broadcast_to(tallies[v], (1, lanes))


def local_sums(block, parts, wcol, width):
    for tile, part in enumerate(parts):
        s = part[:, 0:width]
        pack(block, tile, [jnp.sum(wcol[:, v : v + 1] * s, axis=0, keepdims=True) for v in range(2)], width)


def by_view(wv, crop, pair):
    return wv[0, crop] * pair[0:1, :] + wv[1, crop] * pair[1:2, :]


FWD_WIDTHS = (256, 256, 1024, 512, 2048, 512, 2048, 2048)


def forward_kernel(sets, total, guarded, outs, crops, dims, *refs):
    c3, cin, c4, cout = dims
    (
        wv, wcol, norms1, norms2,
        img_b, img_s, cot_hbm, w1_h, wsp1_h, w3_h, w4_h, w5_h, w6_h, w7_h,
    ), refs = refs[:14], refs[14:]
    (
        o_img, o_z1, o_h1, o_z2, o_h2, o_blk, o_z4, o_x5, o_z5, o_h5, o_xe, o_res, o_d6, o_d7,
        o_st1, o_st2, o_st3, o_st4, o_st7, o_st5, o_st6, o_sq, o_tally,
    ), refs = refs[:23], refs[23:]
    (
        img, z1, h1, z2, h2, zt, blk, eb, z4, xe, z7, hp, x5, z5, h5, z6, cot,
        w1, wsp1, w3, w4, w5, w6, w7, cs, cm, ck,
        st1, st2, st3, st4, st7, st5, st6, sq, tally_v,
    ), refs = refs[:36], refs[36:]
    e = len(FWD_WIDTHS)
    blocks, refs = take(refs, e)
    near, refs = take(refs, e)
    far, refs = take(refs, e)
    ns_, nr_, fs_, fr_ = refs[:4]
    load_sem, img_sem, img_send, img_recv, out_sem = refs[4:]
    links = Links(crops, near, far, ns_, nr_, fs_, fr_)
    k, core = links.k, links.r
    sibling = (k, 1 - core)
    f = F32

    loads = []
    for i, (src, dst) in enumerate(
        ((w1_h, w1), (wsp1_h, wsp1), (w3_h, w3), (w4_h, w4), (w5_h, w5), (w6_h, w6), (w7_h, w7), (cot_hbm, cot))
    ):
        loads.append(pltpu.make_async_copy(src, dst, load_sem.at[i]))
    own, swaps = [], []
    for at, (m, src) in enumerate(zip(sets, (img_b, img_s))):
        part = m.rows // 2
        for c in range(m.count):
            i = m.crop0 + c
            place = img.at[span(m.row0 + c * m.rows + core * part, part)]
            own.append(
                pltpu.make_async_copy(
                    src.at[span((core * m.count + c) * part, part)], place, img_sem.at[i]
                )
            )
            swaps.append(
                pltpu.make_async_remote_copy(
                    src_ref=src.at[span(((1 - core) * m.count + c) * part, part)],
                    dst_ref=place,
                    send_sem=img_send.at[i],
                    recv_sem=img_recv.at[i],
                    device_id=sibling,
                    device_id_type=MESH,
                )
            )
    for copy in own:
        copy.start()
    for copy in loads:
        copy.start()
    links.greet()
    for copy in swaps:
        copy.start()

    out_copies = []

    def put(src, dst):
        copy = pltpu.make_async_copy(src, dst, out_sem.at[len(out_copies)])
        copy.start()
        out_copies.append(copy)

    for ref in (cs, cm, ck):
        ref[...] = jnp.zeros(ref.shape, f)
    for block in blocks:
        block[...] = jnp.zeros(block.shape, f)
    h1[0:16, :] = jnp.zeros((16, 3 * c3), BF16)
    for m in sets:
        for c in range(m.count):
            at = m.guard0 + c * m.guard + m.rows
            h1[at : at + 16, :] = jnp.zeros((16, 3 * c3), BF16)

    def near_tallies():
        return [near[0][i, 16:24, 0:1] for i in range(links.wide)]

    def far_tallies():
        return [far[0][i, 16:24, 0:1] for i in range(links.outers)]

    def meet_near(i, scale):
        links.wait_near(i)
        sums, spread, n = fold_moments(near[i], near_tallies(), links.wide, scale)
        place = far[i].at[links.outer]
        place[0:8, :] = sums
        place[8:16, :] = spread
        if i == 0:
            place[16:24, :] = jnp.broadcast_to(n, (8, near[0].shape[2]))
        links.send_far(i)

    def meet_far(i, scale, table, width):
        links.wait_far(i)
        sums, spread, n = fold_moments(far[i], far_tallies(), links.outers, scale)
        mean = sums / (n * scale)
        inverse = lax.rsqrt(spread / (n * scale) + EPS)
        unpack(table, 0, mean, width)
        unpack(table, 2, inverse, width)
        if i == 0:
            tally_v[...] = jnp.broadcast_to(n, (8, 128))

    loads[0].wait()
    for copy in own:
        copy.wait()
    for copy in swaps:
        copy.wait_recv()
    for m in sets:

        def pair(p, m=m):
            r = m.row0 + p * 2 * m.rows
            z1[span(r, 2 * m.rows), :] = mm(img[span(r, 2 * m.rows), :], w1[...])
            for j in range(2):
                crop_stats(z1, r + j * m.rows, m.rows, m.rows // 2, c3, m.edge, 16, m.pixels, m.crop0 + 2 * p + j, cs, cm)

        repeat(m.count // 2, pair)
    local_moments(blocks[0], cs, cm, wcol, c3, 1.0, True)
    links.send_near(0, blocks[0])
    put(img, o_img)
    put(z1, o_z1)
    loads[1].wait()
    meet_near(0, 1.0)
    meet_far(0, 1.0, st1, c3)

    for m in sets:

        def pair(p, m=m):
            r = m.row0 + p * 2 * m.rows
            g = m.guard0 + p * 2 * m.guard
            for j in range(2):
                crop = m.crop0 + 2 * p + j
                mean = by_view(wv, crop, st1[0:2, :])
                scale = by_view(wv, crop, st1[2:4, :]) * norms1[0:1, 0:c3]
                shift = norms1[1:2, 0:c3]
                step = m.rows // 2
                mask = keep(step, c3, 16, m.edge)

                def tile(i):
                    z = z1[span(r + j * m.rows + i * step, step), :]
                    h = jnp.where(mask, act((z - mean) * scale + shift), 0.0)
                    rows = span(g + j * m.guard + i * step, step)
                    h1[rows, 0:c3] = pltpu.roll(h, 1, 0).astype(BF16)
                    h1[rows, c3 : 2 * c3] = h.astype(BF16)
                    h1[rows, 2 * c3 : 3 * c3] = pltpu.roll(h, step - 1, 0).astype(BF16)

                repeat(2, tile)
            size = 2 * m.rows + 16
            z = mm(h1[span(g - 16, size), :], wsp1[0]) + mm(h1[span(g, size), :], wsp1[1])
            z = z + mm(h1[span(g + 16, size), :], wsp1[2])
            z2[span(r, m.rows), :] = z[0 : m.rows]
            z2[span(r + m.rows, m.rows), :] = z[m.guard : m.guard + m.rows]
            for j in range(2):
                crop_stats(z2, r + j * m.rows, m.rows, m.rows // 2, c3, m.edge, 16, m.pixels, m.crop0 + 2 * p + j, cs, cm)

        repeat(m.count // 2, pair)
    local_moments(blocks[1], cs, cm, wcol, c3, 1.0)
    links.send_near(1, blocks[1])
    put(h1, o_h1)
    put(z2, o_z2)
    loads[2].wait()
    meet_near(1, 1.0)
    meet_far(1, 1.0, st2, c3)

    for m in sets:

        def pair(p, m=m):
            r = m.row0 + p * 2 * m.rows
            for j in range(2):
                crop = m.crop0 + 2 * p + j
                mean = by_view(wv, crop, st2[0:2, :])
                scale = by_view(wv, crop, st2[2:4, :]) * norms1[0:1, c3 : 2 * c3]
                shift = norms1[1:2, c3 : 2 * c3]
                step = m.rows // 2

                def tile(i):
                    rows = span(r + j * m.rows + i * step, step)
                    h2[rows, :] = act((z2[rows, :] - mean) * scale + shift).astype(BF16)

                repeat(2, tile)
            zt[0 : 2 * m.rows, :] = mm(h2[span(r, 2 * m.rows), :], w3[...])
            for j in range(2):
                crop_stats(zt, j * m.rows, m.rows, 32, cin, m.edge, 16, m.pixels, m.crop0 + 2 * p + j, cs, cm)

        repeat(m.count // 2, pair)
    local_moments(blocks[2], cs, cm, wcol, cin, 1.0)
    links.send_near(2, blocks[2])
    put(h2, o_h2)
    loads[3].wait()
    meet_near(2, 1.0)
    meet_far(2, 1.0, st3, cin)

    for m in sets:

        def pair(p, m=m):
            r = m.row0 + p * 2 * m.rows
            zt[0 : 2 * m.rows, :] = mm(h2[span(r, 2 * m.rows), :], w3[...])
            for j in range(2):
                crop = m.crop0 + 2 * p + j
                mean = by_view(wv, crop, st3[0:2, :])
                scale = by_view(wv, crop, st3[2:4, :]) * norms1[0:1, 2 * c3 :]
                shift = norms1[1:2, 2 * c3 :]

                def tile(i):
                    here = span(j * m.rows + i * 32, 32)
                    rows = span(r + j * m.rows + i * 32, 32)
                    u = (zt[here, :] - mean) * scale + shift + img[rows, :].astype(f)
                    b = act(u)
                    blk[rows, :] = b.astype(BF16)
                    for q in range(cin // 128):
                        eb[q, span(j * m.rows // 2 + i * 16, 16), :] = b[0:16, q * 128 : (q + 1) * 128]

                repeat(m.rows // 32, tile)
            for q in range(cin // 128):
                picked = [eb[q, pl.ds(i * 16, 8, stride=2), :] for i in range(2 * m.half)]
                xe[span(m.out0 + p * 2 * m.out, 2 * m.out), q * 128 : (q + 1) * 128] = jnp.concatenate(
                    picked, axis=0
                ).astype(BF16)
            z4[span(r, 2 * m.rows), :] = mm(blk[span(r, 2 * m.rows), :], w4[...])
            for j in range(2):
                crop_stats(z4, r + j * m.rows, m.rows, 32, c4, m.edge, 16, m.pixels, m.crop0 + 2 * p + j, cs, cm)

        repeat(m.count // 2, pair)
    local_moments(blocks[3], cs, cm, wcol, c4, 1.0)
    links.send_near(3, blocks[3])
    put(blk, o_blk)
    put(z4, o_z4)
    put(xe, o_xe)
    loads[6].wait()

    def wide_product(a, w, z):
        def columns(n):
            cols = pl.ds(pl.multiple_of(n * 512, 512), 512)
            z[:, cols] = mm(a[...], w[:, cols])

        repeat(cout // 512, columns)

    def wide_stats(z):
        for m in sets:

            def crop_(c, m=m):
                def columns(n):
                    crop_stats(
                        z, m.out0 + c * m.out, m.out, m.out, 512, m.half, 8, m.half * m.half,
                        m.crop0 + c, cs, cm, n * 512,
                    )

                repeat(cout // 512, columns)

            repeat(m.count, crop_)

    wide_product(xe, w7, z7)
    meet_near(3, 1.0)
    wide_stats(z7)
    local_moments(blocks[4], cs, cm, wcol, cout, 0.25)
    links.send_near(4, blocks[4])
    meet_far(3, 1.0, st4, c4)

    loads[4].wait()
    lots = c4 // 128
    hp[:, 0:24, :] = jnp.zeros((lots, 24, 128), f)
    for m in sets:

        def pair(p, m=m):
            r = m.row0 + p * 2 * m.rows
            for j in range(2):
                crop = m.crop0 + 2 * p + j
                mean = by_view(wv, crop, st4[0:2, :])
                scale = by_view(wv, crop, st4[2:4, :]) * norms2[0:1, 0:c4]
                shift = norms2[1:2, 0:c4]
                mask = keep(32, c4, 16, m.edge)
                base = 24 + j * m.guard
                hp[:, base + m.rows : base + m.guard, :] = jnp.zeros((lots, 16, 128), f)

                def tile(i):
                    z = z4[span(r + j * m.rows + i * 32, 32), :]
                    h = jnp.where(mask, act((z - mean) * scale + shift), 0.0)
                    for q in range(lots):
                        hp[q, span(base + i * 32, 32, 8), :] = h[:, q * 128 : (q + 1) * 128]

                repeat(m.rows // 32, tile)
            for a in range(3):
                for b in range(3):
                    for q in range(lots):
                        picked = []
                        for j in range(2):
                            for i in range(m.half):
                                at = 24 + j * m.guard + (2 * i + a - 1) * 16 + b - 1
                                picked.append(hp[q, pl.ds(at, 8, stride=2), :])
                        tap = (3 * a + b) * c4 + q * 128
                        x5[span(m.out0 + p * 2 * m.out, 2 * m.out), tap : tap + 128] = jnp.concatenate(
                            picked, axis=0
                        ).astype(BF16)

        repeat(m.count // 2, pair)
    z5[...] = jnp.zeros(z5.shape, f)

    def taps(t):
        part = pl.ds(pl.multiple_of(t * 3 * c4, 128), 3 * c4)
        z5[...] += mm(x5[:, part], w5[part, :])

    repeat(3, taps)
    for m in sets:

        def crop_(c, m=m):
            crop_stats(z5, m.out0 + c * m.out, m.out, m.out, c4, m.half, 8, m.half * m.half, m.crop0 + c, cs, cm)

        repeat(m.count, crop_)
    local_moments(blocks[5], cs, cm, wcol, c4, 0.25)
    links.send_near(5, blocks[5])
    put(x5, o_x5)
    put(z5, o_z5)
    meet_near(4, 0.25)
    meet_near(5, 0.25)
    meet_far(4, 0.25, st7, cout)
    meet_far(5, 0.25, st5, c4)

    loads[5].wait()
    for m in sets:

        def pair(p, m=m):
            o = m.out0 + p * 2 * m.out
            halves = []
            for j in range(2):
                crop = m.crop0 + 2 * p + j
                mean = by_view(wv, crop, st5[0:2, :])
                scale = by_view(wv, crop, st5[2:4, :]) * norms2[0:1, c4 : 2 * c4]
                z = z5[span(o + j * m.out, m.out, 8), :]
                halves.append(act((z - mean) * scale + norms2[1:2, c4 : 2 * c4]))
            h5[span(o, 2 * m.out), :] = jnp.concatenate(halves, axis=0).astype(BF16)

        repeat(m.count // 2, pair)
    wide_product(h5, w6, z6)
    wide_stats(z6)
    local_moments(blocks[6], cs, cm, wcol, cout, 0.25)
    links.send_near(6, blocks[6])
    put(h5, o_h5)
    loads[7].wait()
    meet_near(6, 0.25)
    meet_far(6, 0.25, st6, cout)

    out_copies[6].wait()
    g6, g7 = 2 * c4, 2 * c4 + cout
    lanes = 512
    for m in sets:

        def pair(p, m=m):
            o = m.out0 + p * 2 * m.out

            def columns(n):
                cols = pl.ds(pl.multiple_of(n * lanes, lanes), lanes)
                cols6 = pl.ds(pl.multiple_of(g6 + n * lanes, lanes), lanes)
                cols7 = pl.ds(pl.multiple_of(g7 + n * lanes, lanes), lanes)
                c = cot[span(o, 2 * m.out), cols].astype(f)
                mask = keep(m.out, lanes, 8, m.half)
                found = []
                for j in range(2):
                    crop = m.crop0 + 2 * p + j
                    rows = span(o + j * m.out, m.out, 8)
                    n6 = (z6[rows, cols] - by_view(wv, crop, st6[0:2, cols])) * by_view(wv, crop, st6[2:4, cols])
                    n7 = (z7[rows, cols] - by_view(wv, crop, st7[0:2, cols])) * by_view(wv, crop, st7[2:4, cols])
                    u = n6 * norms2[0:1, cols6] + norms2[1:2, cols6] + n7 * norms2[0:1, cols7] + norms2[1:2, cols7]
                    a, slope = act_both(u)
                    found.append(a)
                    up = jnp.where(mask, slope * c[j * m.out : (j + 1) * m.out], 0.0)
                    z4[span(n * outs + o + j * m.out, m.out, 8), :] = up
                    for to, part in ((cs, up), (cm, up * n6), (ck, up * n7)):
                        to[pl.ds(crop, 1), cols] = jnp.sum(tile_sum(part), axis=0, keepdims=True)
                w6[span(o, 2 * m.out), cols] = jnp.concatenate(found, axis=0).astype(BF16)

            repeat(cout // lanes, columns)

        repeat(m.count // 2, pair)
    local_sums(blocks[7], (cs, cm, ck), wcol, cout)
    links.send_near(7, blocks[7])
    put(w6.at[0:outs], o_res)
    links.wait_near(7)
    far[7][links.outer] = fold_sums(near[7], links.wide)
    links.send_far(7)
    links.wait_far(7)
    sums = fold_sums(far[7], links.outers)
    for t in range(3):
        unpack(sq, 2 * t, sums[8 * t : 8 * t + 8], cout)

    for m in sets:

        def pair(p, m=m):
            o = m.out0 + p * 2 * m.out

            def columns(n):
                cols = pl.ds(pl.multiple_of(n * lanes, lanes), lanes)
                mask = keep(m.out, lanes, 8, m.half)
                got6, got7 = [], []
                for j in range(2):
                    crop = m.crop0 + 2 * p + j
                    rows = span(o + j * m.out, m.out, 8)
                    up = z4[span(n * outs + o + j * m.out, m.out, 8), :]
                    over = wv[0, crop] * (4.0 / tally_v[0:1, 0:1]) + wv[1, crop] * (4.0 / tally_v[1:2, 0:1])
                    level = by_view(wv, crop, sq[0:2, cols]) * over
                    for got, z, st, at, t in ((got6, z6, st6, g6, 2), (got7, z7, st7, g7, 4)):
                        inv = by_view(wv, crop, st[2:4, cols])
                        gain = inv * norms2[0:1, pl.ds(pl.multiple_of(at + n * lanes, lanes), lanes)]
                        tilt = by_view(wv, crop, sq[t : t + 2, cols]) * over
                        centered = (z[rows, cols] - by_view(wv, crop, st[0:2, cols])) * inv
                        got.append(jnp.where(mask, gain * (up - level - centered * tilt), 0.0))
                w7[span(o, 2 * m.out), cols] = jnp.concatenate(got6, axis=0).astype(BF16)
                w7[span(cin // 2 + o, 2 * m.out), cols] = jnp.concatenate(got7, axis=0).astype(BF16)

            repeat(cout // lanes, columns)

        repeat(m.count // 2, pair)
    put(w7.at[0:outs], o_d6)
    put(w7.at[cin // 2 : cin // 2 + outs], o_d7)
    for src, dst in (
        (st1, o_st1), (st2, o_st2), (st3, o_st3), (st4, o_st4), (st7, o_st7), (st5, o_st5), (st6, o_st6),
        (sq, o_sq), (tally_v, o_tally),
    ):
        put(src, dst)
    links.finish()
    for copy in swaps:
        copy.wait_send()
    for i, copy in enumerate(out_copies):
        if i != 6:
            copy.wait()


def flat_rows(tensor, pitch):
    n, h, w, c = tensor.shape
    return jnp.pad(tensor, ((0, 0), (0, 0), (0, pitch - w), (0, 0))).reshape(n * h * pitch, c)


def forward(images, cots, onehot, pixels, w, norms_first, norms_second, ident):
    crops = lax.axis_size("crops")
    nb, ns = images[0].shape[0] // 2, images[1].shape[0] // 2
    sets, total, guarded, outs = geometry(nb, images[0].shape[2], ns, images[1].shape[2])
    w1, wsp1, w3, w4, w5, w6, w7 = w
    cin, c3 = w1.shape
    c4, cout = w6.shape
    smem, vmem = pl.BlockSpec(memory_space=pltpu.SMEM), pl.BlockSpec(memory_space=pltpu.VMEM)
    hbm = pl.BlockSpec(memory_space=pl.ANY)
    shape = jax.ShapeDtypeStruct
    out_shape = [
        shape((total, cin), BF16), shape((total, c3), F32), shape((guarded, 3 * c3), BF16), shape((total, c3), F32),
        shape((total, c3), BF16), shape((total, cin), BF16), shape((total, c4), F32), shape((outs, 9 * c4), BF16),
        shape((outs, c4), F32), shape((outs, c4), BF16), shape((outs, cin), BF16), shape((outs, cout), BF16),
        shape((outs, cout), BF16), shape((outs, cout), BF16),
        shape((8, c3), F32), shape((8, c3), F32), shape((8, cin), F32), shape((8, c4), F32), shape((8, cout), F32),
        shape((8, c4), F32), shape((8, cout), F32), shape((8, cout), F32), shape((8, 128), F32),
    ]
    most = 2 * sets[0].rows
    scratch = [
        pltpu.VMEM((total, cin), BF16), pltpu.VMEM((total, c3), F32), pltpu.VMEM((guarded, 3 * c3), BF16),
        pltpu.VMEM((total, c3), F32), pltpu.VMEM((total, c3), BF16), pltpu.VMEM((most, cin), F32),
        pltpu.VMEM((total, cin), BF16), pltpu.VMEM((cin // 128, most // 2, 128), F32), pltpu.VMEM((total, c4), F32),
        pltpu.VMEM((outs, cin), BF16), pltpu.VMEM((outs, cout), F32), pltpu.VMEM((c4 // 128, 24 + 2 * sets[0].guard, 128), F32),
        pltpu.VMEM((outs, 9 * c4), BF16), pltpu.VMEM((outs, c4), F32),
        pltpu.VMEM((outs, c4), BF16), pltpu.VMEM((outs, cout), F32), pltpu.VMEM((outs, cout), BF16),
    ]
    scratch += [pltpu.VMEM(t.shape, BF16) for t in w]
    scratch += [pltpu.VMEM((16, cout), F32)] * 3
    scratch += [pltpu.VMEM((8, n), F32) for n in (c3, c3, cin, c4, cout, c4, cout, cout, 128)]
    scratch += exchange_shapes(FWD_WIDTHS, (3, 2, 2, 2, 2, 2, 2, 3), crops)
    scratch += [
        pltpu.SemaphoreType.DMA((8,)), pltpu.SemaphoreType.DMA((nb + ns,)), pltpu.SemaphoreType.DMA((nb + ns,)),
        pltpu.SemaphoreType.DMA((nb + ns,)), pltpu.SemaphoreType.DMA((23,)),
    ]
    rows = jnp.concatenate([onehot, pixels[None, :]], axis=0)
    wide = jnp.pad(rows, ((0, 0), (0, 16 - rows.shape[1])), constant_values=0.0)
    wide = wide.at[2, rows.shape[1] :].set(1.0)
    wcol = jnp.pad(wide.T, ((0, 0), (0, 125)))
    got = pl.pallas_call(
        functools.partial(forward_kernel, sets, total, guarded, outs, crops, (c3, cin, c4, cout)),
        out_shape=out_shape,
        in_specs=[smem, vmem, vmem, vmem] + [hbm] * 10,
        out_specs=[hbm] * len(out_shape),
        scratch_shapes=scratch,
        compiler_params=pltpu.CompilerParams(
            collective_id=ident, has_side_effects=True, vmem_limit_bytes=63 * 1024 * 1024
        ),
        name="forward",
    )(
        onehot, wcol, norms_first, norms_second,
        flat_rows(images[0], 16), flat_rows(images[1], 16),
        jnp.concatenate([flat_rows(t, 8) for t in cots], axis=0), *w,
    )
    return sets, wcol, (total, guarded, outs), got


def share_plan(shapes, cuts):
    chunks = []
    for at, (height, width) in enumerate(shapes):
        down, across = cuts[at]
        half, high = width // 2 // across, height // down
        for c in range(down):
            for p in range(across):
                chunks.append((at, c * high, high, p * half, half))
    return chunks


class Share:
    def __init__(self, shapes, chunks, orders, bits, links, sources, outs, acc, recv0, recvs, sems, done=(), gather=True):
        self.shapes, self.chunks, self.bits = shapes, chunks, bits
        self.k, self.core = links.k, links.r
        self.sources, self.outs, self.acc, self.recv0, self.recvs = sources, outs, acc, recv0, recvs
        self.send_sem, self.recv_sem, self.load_sem, self.store_sem = sems
        self.sibling = (self.k, 1 - self.core)
        self.total = 2 * bits + 2
        self.live, self.loads, self.stores, self.done, self.gather, self.at = {}, {}, {}, done, gather, 0
        digit = [lax.rem(self.k // (1 << b), 2) for b in range(bits)]
        self.stages, self.regions, self.kinds, self.slots = [], [], [], []
        for i, (at, row, height, col, width) in enumerate(chunks):
            stages = []
            for a, b in zip(*orders[i]):
                if a == b:
                    mine, step = digit[a], 1 << a
                else:
                    mine = digit[a] * (1 - self.core) + digit[b] * self.core
                    step = (1 << a) * (1 - self.core) + (1 << b) * self.core
                stages.append((mine, self.k + step * (1 - 2 * mine)))
            start, length, used = 0, height, 0
            region, kind, slot = [], [], []
            for s in range(bits):
                region.append((start, length))
                slot.append(used)
                if length % 32 == 0:
                    kind.append(True)
                    length //= 2
                    start = start + stages[s][0] * length
                else:
                    kind.append(False)
                used += length
            region.append((start, length))
            self.stages.append(stages)
            self.regions.append(region)
            self.kinds.append(kind)
            self.slots.append(slot)

    def send(self, i, t, src, dst, device):
        copy = pltpu.make_async_remote_copy(
            src_ref=src,
            dst_ref=dst,
            send_sem=self.send_sem.at[i, t],
            recv_sem=self.recv_sem.at[i, t],
            device_id=device,
            device_id_type=MESH,
        )
        copy.start()
        self.live[i, t] = copy

    def add(self, dst, at, src, src_at, length):
        block = 16
        while length % (block * 2) == 0 and block * 2 * dst.shape[1] <= 65536:
            block *= 2

        def step(j, carry):
            off = j * block
            rows = span(at + off, block)
            dst[rows, :] = dst[rows, :] + src[span(src_at + off, block), :]
            return carry

        lax.fori_loop(0, length // block, step, 0)

    def arrived(self, i, t):
        if (i, t) in self.live:
            self.live[i, t].wait_recv()

    def task(self, i, t):
        at, row, height, col, width = self.chunks[i]
        bits, kinds, regions, stages = self.bits, self.kinds[i], self.regions[i], self.stages[i]
        half = self.shapes[at][1] // 2
        own = pl.ds(pl.multiple_of(self.core * half + col, 128), width)
        rows = pl.ds(row, height)
        if t == 0:
            away = pl.ds(pl.multiple_of((1 - self.core) * half + col, 128), width)
            self.send(i, 0, self.sources[at].at[rows, away], self.recv0[i], self.sibling)
            if self.acc[i] is None:
                self.acc[i] = self.sources[at].at[rows, own]
                return
            copy = pltpu.make_async_copy(self.sources[at].at[rows, own], self.acc[i], self.load_sem.at[i])
            copy.start()
            self.loads[i] = copy
            return
        self.arrived(i, t - 1)
        if t <= bits + 1:
            if i in self.done:
                pass
            elif t == 1:
                if i in self.loads:
                    self.loads[i].wait()
                self.add(self.acc[i], 0, self.recv0[i], 0, height)
            else:
                s = t - 2
                start, length = regions[s + 1]
                if not kinds[s]:
                    self.live[i, t - 1].wait_send()
                self.add(self.acc[i], start, self.recvs[i], self.slots[i][s], length)
        if t <= bits:
            s = t - 1
            start, length = regions[s]
            give, first = length, start
            if kinds[s]:
                give = length // 2
                first = start + (1 - stages[s][0]) * give
            self.send(
                i, t, self.acc[i].at[span(first, give)], self.recvs[i].at[pl.ds(self.slots[i][s], give)],
                (stages[s][1], self.core),
            )
            return
        if t == bits + 1:
            start, length = regions[bits]
            if i in self.done:
                mine = self.sources[at].at[span(row + start, length), own]
            else:
                mine = self.acc[i].at[span(start, length)]
            copy = pltpu.make_async_copy(mine, self.outs[at].at[span(row + start, length), own], self.store_sem.at[i])
            copy.start()
            self.stores[i] = copy
            if not self.gather:
                return
        if t == bits + 2:
            self.stores[i].wait()
        if t <= 2 * bits:
            s = bits - 1 - (t - bits - 1)
            start, length = regions[s + 1]
            if kinds[s]:
                place = self.outs[at].at[span(row + start, length), own]
                self.send(i, t, mine if t == bits + 1 else place, place, (stages[s][1], self.core))
            return
        if t == 2 * bits + 1:
            place = self.outs[at].at[rows, own]
            self.send(i, t, place, place, self.sibling)

    def run(self, order):
        while self.at < len(order):
            token = order[self.at]
            self.at += 1
            if token is None:
                return
            i, t = token
            if t == self.total:
                self.arrived(i, t - 1)
            else:
                self.task(i, t)

    def finish(self):
        for (i, t), copy in self.live.items():
            if not (1 <= t <= self.bits and not self.kinds[i][t - 1]):
                copy.wait_send()


def share_scratch(chunks, bits, done=(), inside=False):
    acc, recv0, recvs = [], [], []
    for i, (at, row, height, col, width) in enumerate(chunks):
        if i in done:
            continue
        acc.append(pltpu.VMEM((height, width), BF16))
        recv0.append(pltpu.VMEM((height, width), BF16))
        length, used = height, 0
        for s in range(bits):
            if length % 32 == 0:
                length //= 2
            used += length
        recvs.append(pltpu.VMEM((used, width), BF16))
    n = len(chunks)
    sems = [pltpu.SemaphoreType.DMA((n, 2 * bits + 2))] * 2 + [pltpu.SemaphoreType.DMA((n,))] * 2
    return ([] if inside else acc) + recv0 + recvs + sems


def share_orders(bits, path):
    rest = list(range(2, bits))
    if bits < 2:
        return rest or list(range(bits)), rest or list(range(bits))
    if path == 0:
        return [0, 1] + rest, [1, 0] + rest
    if path == 1:
        return [0] + rest + [1], [1] + rest + [0]
    return rest + [0, 1], rest + [1, 0]


SHARE_CUTS = ((1, 2), (1, 1), (3, 1), (1, 1), (1, 1), (1, 1), (1, 1))
SHARE_FIRST = 3
SHARE_PATHS = (0, 0, 0, 1, 1, 0, 0, 0, 0, 0)
SHARE_LATE = (
    5, 37, 64, 21, 48, 80, 96, -1, 6, 38, 65, 22, 49, 81, 97, -1, -1, -1, 7, 39, 112, 23, -1, 113,
    66, 98, -1, 50, -1, 82, -1, 67, 8, 40, 114, 128, 24, 99, -1, 115, 68, 129, 51, 83, 100, -1, 116, -1,
    144, 69, 101, 117, 145, 84, 70, 118, 52, 102, 85, 119, 53, 103, 146, 130, 71, 86, 54, 120, 9, 41, 25, 147,
    104, 131, 121, 87, 148, 10, 122, 42, 55, 26, 105, 149, 72, 132, 88, 106, 150, 133, 151, 134, 56, 152, 135, 73,
    89, 74, 153, 90, 136, 154, 57, 58, 137, 138,
)
SHARE_EARLY = (
    32, -1, 33, 0, 16, -1, 34, 1, -1, 35, 2, 17, -1, 36, 3, -1, 37, 4, 18, -1, 19, -1, 5, -1, 20, -1, 21,
)


def share_late_order(pieces, bits, parts, ready):
    if bits == 4:
        return [None if v < 0 else (v // 16, v % 16) for v in SHARE_LATE]
    order, total = [], 2 * bits + 2
    begin = [bits + 1 if i < SHARE_FIRST else 0 for i in range(pieces)]
    for k in range(parts + total + 1):
        for i in range(pieces):
            t = k - ready[i] + begin[i]
            if k >= ready[i] and t <= total:
                order.append((i, t))
        if k < parts:
            order.append(None)
    return order


def share_early_order(bits):
    if bits == 4:
        return [None if v < 0 else (v // 16, v % 16) for v in SHARE_EARLY]
    order = [(2, 0), None, (0, 0), (1, 0), None]
    for t in range(1, bits + 2):
        order += [(2, t), (0, t), (1, t), None]
    return order


def meet_sums(links, e, width, tables, between=None):
    links.wait_near(e)
    links.far[e][links.outer] = fold_sums(links.near[e], links.wide)
    links.send_far(e)
    if between is not None:
        between()
    links.wait_far(e)
    sums = fold_sums(links.far[e], links.outers)
    for t, (table, row) in enumerate(tables):
        unpack(table, row, sums[8 * t : 8 * t + 8], width)


def share_of(wv, tally, crop, times):
    return wv[0, crop] * (times / tally[0:1, 0:1]) + wv[1, crop] * (times / tally[1:2, 0:1])


class Puts:
    def __init__(self, sem):
        self.sem, self.copies = sem, []

    def put(self, src, dst):
        copy = pltpu.make_async_copy(src, dst, self.sem.at[len(self.copies)])
        copy.start()
        self.copies.append(copy)

    def finish(self):
        for copy in self.copies:
            copy.wait()


def start_loads(pairs, sem):
    copies = [pltpu.make_async_copy(src, dst, sem.at[i]) for i, (src, dst) in enumerate(pairs)]
    for copy in copies:
        copy.start()
    return copies


def back_two_kernel(sets, total, outs, crops, dims, shapes, chunks, *refs):
    c3, cin, c4, cout = dims
    wv, wcol, norms1, norms2, st3, st4, st5, tally = refs[:8]
    sources, refs = refs[8:23], refs[23:]
    (o_up, o_g6, o_g7, o_g5, o_g4, o_s5, o_s4, o_s3), refs = refs[:8], refs[8:]
    held, refs = refs[:15], refs[15:]
    (d6, w6, z5, h5, d7, xe, w7, w5, x5, z4, w4, h2, w3, img, blk) = held
    (q5, t7, pv, dh, d4, zt, bg, up, s5, s4, s3, cs, cm), refs = refs[:13], refs[13:]
    d5 = d6
    g6, g7, g5, g4 = w6, w7, w5, w4
    blocks, refs = take(refs, 3)
    near, refs = take(refs, 3)
    far, refs = take(refs, 3)
    links = Links(crops, near, far, *refs[:4])
    load_sem, out_sem, up_sem = refs[4:7]
    refs = refs[7:]
    bits = crops.bit_length() - 1
    early = SHARE_FIRST
    recv0, refs = take(refs, early)
    recvs, refs = take(refs, early)
    share = Share(
        shapes, chunks[:early], [share_orders(bits, v) for v in SHARE_PATHS[:early]], bits, links, [g7, g6], [o_g7, o_g6],
        [None] * early, recv0, recvs, refs, gather=False,
    )
    order = share_early_order(bits)

    def tick():
        share.run(order)

    f = F32
    loads = start_loads(list(zip(sources, held)), load_sem)
    links.greet()
    puts = Puts(out_sem)
    for ref in (cs, cm):
        ref[...] = jnp.zeros(ref.shape, f)
    for block in blocks:
        block[...] = jnp.zeros(block.shape, f)

    for i in range(3):
        loads[i].wait()
    q5[...] = mm_nt(d6[...], w6[...])
    g5at = c4
    for m in sets:

        def crop_(c, m=m):
            crop = m.crop0 + c
            rows = span(m.out0 + c * m.out, m.out, 8)
            inv = by_view(wv, crop, st5[2:4, :])
            n = (z5[rows, :] - by_view(wv, crop, st5[0:2, :])) * inv
            q = act_slope(n * norms2[0:1, g5at : 2 * c4] + norms2[1:2, g5at : 2 * c4]) * q5[rows, :]
            q5[rows, :] = q
            cs[pl.ds(crop, 1), 0:c4] = jnp.sum(tile_sum(q), axis=0, keepdims=True)
            cm[pl.ds(crop, 1), 0:c4] = jnp.sum(tile_sum(q * n), axis=0, keepdims=True)

        repeat(m.count, crop_)
    local_sums(blocks[0], (cs, cm), wcol, c4)
    links.send_near(0, blocks[0])

    loads[3].wait()

    def outer(n):
        cols = pl.ds(pl.multiple_of(n * 512, 512), 512)
        g6[:, cols] = mm_tn(h5[...], d6[:, cols]).astype(BF16)

    repeat(cout // 512, outer)
    tick()

    def rest():
        for i in (4, 5, 6):
            loads[i].wait()

        def shortcut(n):
            part = pl.ds(pl.multiple_of(n * 256, 256), 256)
            t7[:, part] = mm_nt(d7[...], w7[part, :])

        repeat(cin // 256, shortcut)

        def skip(n):
            cols = pl.ds(pl.multiple_of(n * 512, 512), 512)
            g7[:, cols] = mm_tn(xe[...], d7[:, cols]).astype(BF16)

        repeat(cout // 512, skip)
        tick()

    meet_sums(links, 0, c4, ((s5, 0), (s5, 2)), rest)

    for m in sets:

        def pair(p, m=m):
            o = m.out0 + p * 2 * m.out
            mask = keep(m.out, c4, 8, m.half)
            slots = [[], [], [], []]
            for j in range(2):
                crop = m.crop0 + 2 * p + j
                rows = span(o + j * m.out, m.out, 8)
                over = share_of(wv, tally, crop, 4.0)
                inv = by_view(wv, crop, st5[2:4, :])
                n = (z5[rows, :] - by_view(wv, crop, st5[0:2, :])) * inv
                d = (inv * norms2[0:1, g5at : 2 * c4]) * (
                    q5[rows, :] - by_view(wv, crop, s5[0:2, :]) * over - n * (by_view(wv, crop, s5[2:4, :]) * over)
                )
                d = jnp.where(mask, d, 0.0)
                down = jnp.concatenate([d[8:], jnp.zeros((8, c4), f)], axis=0)
                slots[0].append(d)
                slots[1].append(pltpu.roll(d, m.out - 1, 0))
                slots[2].append(down)
                slots[3].append(pltpu.roll(down, m.out - 1, 0))
            for t in range(4):
                d5[span(o, 2 * m.out), t * c4 : (t + 1) * c4] = jnp.concatenate(slots[t], axis=0).astype(BF16)

        repeat(m.count // 2, pair)

    tick()
    loads[7].wait()
    options = (((1, 0),), ((2, 0), (0, 1)))
    for a in range(2):
        for b in range(2):
            value = None
            for r, down in options[a]:
                for c, side in options[b]:
                    slot, tap = (2 * down + side) * c4, (3 * r + c) * c4
                    term = mm_nt(d5[:, slot : slot + c4], w5[tap : tap + c4, :])
                    value = term if value is None else value + term
            pv[...] = value
            for m in sets:

                def crop_(c, m=m, a=a, b=b):
                    for i in range(m.half):
                        for q in range(c4 // 128):
                            dh[q, pl.ds(m.row0 + c * m.rows + (2 * i + a) * 16 + b, 8, stride=2), :] = pv[
                                span(m.out0 + c * m.out + i * 8, 8, 8), q * 128 : (q + 1) * 128
                            ]

                repeat(m.count, crop_)
        tick()
    loads[9].wait()
    for m in sets:

        def crop_(c, m=m):
            crop = m.crop0 + c
            rows = span(m.row0 + c * m.rows, m.rows)
            mask = keep(m.rows, 128, 16, m.edge)
            levels, tilts = [], []
            for q in range(c4 // 128):
                cols = slice(q * 128, (q + 1) * 128)
                inv = by_view(wv, crop, st4[2:4, cols])
                n = (z4[rows, cols] - by_view(wv, crop, st4[0:2, cols])) * inv
                up_ = jnp.where(mask, act_slope(n * norms2[0:1, cols] + norms2[1:2, cols]) * dh[q, rows, :], 0.0)
                dh[q, rows, :] = up_
                levels.append(jnp.sum(tile_sum(up_), axis=0, keepdims=True))
                tilts.append(jnp.sum(tile_sum(up_ * n), axis=0, keepdims=True))
            cs[pl.ds(crop, 1), 0:c4] = jnp.concatenate(levels, axis=1)
            cm[pl.ds(crop, 1), 0:c4] = jnp.concatenate(tilts, axis=1)

        repeat(m.count, crop_)
        tick()
    local_sums(blocks[1], (cs, cm), wcol, c4)
    links.send_near(1, blocks[1])
    loads[8].wait()

    def kernel(t):
        part = pl.ds(pl.multiple_of(t * c4, c4), c4)
        g5[part, :] = mm_tn(x5[:, part], d5[:, 0:c4]).astype(BF16)

    repeat(5, kernel)
    tick()

    def rest():
        repeat(4, lambda t: kernel(t + 5))
        puts.put(g5, o_g5)
        tick()

    meet_sums(links, 1, c4, ((s4, 0), (s4, 2)), rest)

    for i in range(10, 14):
        loads[i].wait()
    big_rows = 2 * sets[0].rows
    for at, m in enumerate(sets):

        def pair(p, m=m, at=at):
            r = m.row0 + p * 2 * m.rows
            o = m.out0 + p * 2 * m.out
            mask = keep(m.rows, 128, 16, m.edge)
            for j in range(2):
                crop = m.crop0 + 2 * p + j
                rows = span(r + j * m.rows, m.rows)
                over = share_of(wv, tally, crop, 1.0)
                for q in range(c4 // 128):
                    cols = slice(q * 128, (q + 1) * 128)
                    inv = by_view(wv, crop, st4[2:4, cols])
                    n = (z4[rows, cols] - by_view(wv, crop, st4[0:2, cols])) * inv
                    d = (inv * norms2[0:1, cols]) * (
                        dh[q, rows, :] - by_view(wv, crop, s4[0:2, cols]) * over - n * (by_view(wv, crop, s4[2:4, cols]) * over)
                    )
                    d4[rows, cols] = jnp.where(mask, d, 0.0).astype(BF16)
            got = mm_nt(d4[span(r, 2 * m.rows), :], w4[...])
            for q in range(cin // 128):
                bg[q, 0 : 2 * m.rows, :] = got[:, q * 128 : (q + 1) * 128]
            for q in range(cin // 128):
                for j in range(2):
                    for i in range(m.half):
                        here = pl.ds(j * m.rows + i * 32, 8, stride=2)
                        bg[q, here, :] = bg[q, here, :] + t7[span(o + j * m.out + i * 8, 8, 8), q * 128 : (q + 1) * 128]
            turn = m.crop0 // 2 + p
            slot = lax.rem(turn, 2)

            def left(turn, slot):
                return pltpu.make_async_copy(
                    up.at[slot, 0 : 2 * m.rows], o_up.at[span(r, 2 * m.rows)], up_sem.at[turn]
                )

            if at == 0:
                @pl.when(p >= 2)
                def _():
                    left(turn - 2, slot).wait()
            else:
                for back, size in ((2, big_rows),):
                    pltpu.make_async_copy(
                        up.at[slot, 0:size], o_up.at[span(0, size)], up_sem.at[turn - back]
                    ).wait()
            step = m.rows // 2
            mask = keep(step, 128, 16, m.edge)
            totals = [[[], []], [[], []]]
            for h, j in [(h, j) for h in range(cin // 512) for j in range(2)]:
                if j == 0:
                    zt[0 : 2 * m.rows, :] = mm(h2[span(r, 2 * m.rows), :], w3[:, h * 512 : (h + 1) * 512])
                crop = m.crop0 + 2 * p + j
                levels, tilts = totals[j]
                for q in range(h * 4, h * 4 + 4):
                    cols = slice(q * 128, (q + 1) * 128)
                    part = slice((q - h * 4) * 128, (q - h * 4 + 1) * 128)
                    at3 = slice(2 * c3 + q * 128, 2 * c3 + (q + 1) * 128)
                    mean, inv = by_view(wv, crop, st3[0:2, cols]), by_view(wv, crop, st3[2:4, cols])
                    gain, bias = norms1[0:1, at3], norms1[1:2, at3]

                    def tile(i, sums, j=j, cols=cols, part=part, q=q, mean=mean, inv=inv, gain=gain, bias=bias):
                        here = span(j * m.rows + i * step, step)
                        rows = span(r + j * m.rows + i * step, step)
                        n = (zt[here, part] - mean) * inv
                        u = n * gain + bias + img[rows, cols].astype(f)
                        got = bg[q, here, :].astype(BF16).astype(f)
                        v = jnp.where(mask, act_slope(u) * got, 0.0)
                        up[slot, here, cols] = v
                        return (sums[0] + tile_sum(v), sums[1] + tile_sum(v * n))

                    zero = jnp.zeros((8, 128), f)
                    s, t = lax.fori_loop(0, 2, tile, (zero, zero))
                    levels.append(jnp.sum(s, axis=0, keepdims=True))
                    tilts.append(jnp.sum(t, axis=0, keepdims=True))
            for j in range(2):
                crop = m.crop0 + 2 * p + j
                cs[pl.ds(crop, 1), :] = jnp.concatenate(totals[j][0], axis=1)
                cm[pl.ds(crop, 1), :] = jnp.concatenate(totals[j][1], axis=1)
            left(turn, slot).start()

        repeat(m.count // 2, pair)
        tick()
    local_sums(blocks[2], (cs, cm), wcol, cin)
    links.send_near(2, blocks[2])
    loads[14].wait()

    def inner(n):
        part = pl.ds(pl.multiple_of(n * 256, 256), 256)
        g4[part, :] = mm_tn(blk[:, part], d4[...]).astype(BF16)

    repeat(2, inner)

    def rest():
        repeat(cin // 256 - 2, lambda n: inner(n + 2))
        puts.put(g4, o_g4)

    meet_sums(links, 2, cin, ((s3, 0), (s3, 2)), rest)
    for src, dst in ((s5, o_s5), (s4, o_s4), (s3, o_s3)):
        puts.put(src, dst)
    for back in (2, 1):
        size = 2 * sets[1].rows
        turn = (sets[0].count + sets[1].count) // 2 - back
        pltpu.make_async_copy(
            up.at[turn % 2, 0:size], o_up.at[pl.ds(sets[1].row0, size)], up_sem.at[turn]
        ).wait()
    while share.at < len(order):
        tick()
    for copy in share.stores.values():
        copy.wait()
    share.finish()
    links.finish()
    puts.finish()


def back_one_kernel(sets, total, guarded, crops, dims, shapes, chunks, *refs):
    c3, cin = dims
    wv, wcol, norms1, st1, st2, st3, s3, tally = refs[:8]
    sources, refs = refs[8:17], refs[17:]
    second, refs = list(refs[:4]), refs[4:]
    (o_gb, o_gs, o_s2, o_s1), refs = refs[:4], refs[4:]
    o_grads, refs = refs[:7], refs[7:]
    held, refs = refs[:9], refs[9:]
    (h2, w3, up, z2, h1, wsp1, z1, w1, img) = held
    (zt, d3, q2, d2, q1, d1, g3, g2, g1, s2, s1, cs, cm), refs = refs[:13], refs[13:]
    blocks, refs = take(refs, 2)
    near, refs = take(refs, 2)
    far, refs = take(refs, 2)
    links = Links(crops, near, far, *refs[:4])
    load_sem, out_sem, own_sem, grad_send, grad_recv, up_sem = refs[4:10]
    refs = refs[10:]
    n = len(chunks)
    bits = crops.bit_length() - 1
    early = SHARE_FIRST
    acc, refs = take(refs, n - early)
    recv0, refs = take(refs, n - early)
    recvs, refs = take(refs, n - early)
    gap = [None] * early
    share = Share(
        shapes, chunks, [share_orders(bits, v) for v in SHARE_PATHS], bits, links, second + [g3, g2, g1], o_grads,
        gap + acc, gap + recv0, gap + recvs, refs, range(early),
    )
    order = share_late_order(n, bits, 11, (0,) * 7 + (4, 8, 11))

    def tick():
        share.run(order)

    core = links.r
    sibling = (links.k, 1 - core)
    f = F32
    loads = start_loads([(a, b) for a, b in zip(sources, held) if b is not up], load_sem)
    ups = []
    for m in sets:
        for p in range(m.count // 2):
            rows = pl.ds(m.row0 + p * 2 * m.rows, 2 * m.rows)
            ups.append(pltpu.make_async_copy(sources[2].at[rows], up.at[rows], up_sem.at[len(ups)]))
    for copy in ups:
        copy.start()
    links.greet()
    tick()
    puts = Puts(out_sem)
    for ref in (cs, cm):
        ref[...] = jnp.zeros(ref.shape, f)
    for block in blocks:
        block[...] = jnp.zeros(block.shape, f)
    d2[0:16, :] = jnp.zeros((16, 3 * c3), BF16)
    for m in sets:
        for c in range(m.count):
            at = m.guard0 + c * m.guard + m.rows
            d2[at : at + 16, :] = jnp.zeros((16, 3 * c3), BF16)

    for i in range(3):
        loads[i].wait()
    for copy in ups:
        copy.wait()
    for m in sets:

        def pair(p, m=m):
            r = m.row0 + p * 2 * m.rows
            step = m.rows // 2
            mask = keep(step, 128, 16, m.edge)
            for h, j in [(h, j) for h in range(cin // 512) for j in range(2)]:
                if j == 0:
                    zt[0 : 2 * m.rows, :] = mm(h2[span(r, 2 * m.rows), :], w3[:, h * 512 : (h + 1) * 512])
                crop = m.crop0 + 2 * p + j
                over = share_of(wv, tally, crop, 1.0)
                for q in range(h * 4, h * 4 + 4):
                    cols = slice(q * 128, (q + 1) * 128)
                    part = slice((q - h * 4) * 128, (q - h * 4 + 1) * 128)
                    mean, inv = by_view(wv, crop, st3[0:2, cols]), by_view(wv, crop, st3[2:4, cols])
                    gain = inv * norms1[0:1, 2 * c3 + q * 128 : 2 * c3 + (q + 1) * 128]
                    level = by_view(wv, crop, s3[0:2, cols]) * over
                    tilt = by_view(wv, crop, s3[2:4, cols]) * over * inv

                    def tile(i, j=j, cols=cols, part=part, mean=mean, gain=gain, level=level, tilt=tilt):
                        here = span(j * m.rows + i * step, step)
                        rows = span(r + j * m.rows + i * step, step)
                        d = gain * (up[rows, cols] - level - (zt[here, part] - mean) * tilt)
                        d3[rows, cols] = jnp.where(mask, d, 0.0).astype(BF16)

                    repeat(2, tile)
            q2[span(r, 2 * m.rows), :] = mm_nt(d3[span(r, 2 * m.rows), :], w3[...])
            for j in range(2):
                crop = m.crop0 + 2 * p + j
                mean, inv = by_view(wv, crop, st2[0:2, :]), by_view(wv, crop, st2[2:4, :])

                def tile(i, sums, j=j, mean=mean, inv=inv):
                    rows = span(r + j * m.rows + i * step, step)
                    n = (z2[rows, :] - mean) * inv
                    v = act_slope(n * norms1[0:1, c3 : 2 * c3] + norms1[1:2, c3 : 2 * c3]) * q2[rows, :]
                    q2[rows, :] = v
                    return (sums[0] + tile_sum(v), sums[1] + tile_sum(v * n))

                zero = jnp.zeros((8, c3), f)
                s, t = lax.fori_loop(0, 2, tile, (zero, zero))
                cs[pl.ds(crop, 1), 0:c3] = jnp.sum(s, axis=0, keepdims=True)
                cm[pl.ds(crop, 1), 0:c3] = jnp.sum(t, axis=0, keepdims=True)

        repeat(m.count // 2, pair)
        tick()
    local_sums(blocks[0], (cs, cm), wcol, c3)
    links.send_near(0, blocks[0])

    def outer(n):
        cols = pl.ds(pl.multiple_of(n * 256, 256), 256)
        g3[:, cols] = mm_tn(h2[...], d3[:, cols]).astype(BF16)

    repeat(cin // 512, outer)
    tick()

    def rest():
        repeat(cin // 512, lambda n: outer(n + cin // 512))
        tick()

    meet_sums(links, 0, c3, ((s2, 0), (s2, 2)), rest)

    for i in range(3, 6):
        loads[i].wait()
    for m in sets:

        def pair(p, m=m):
            r = m.row0 + p * 2 * m.rows
            g = m.guard0 + p * 2 * m.guard
            step = m.rows // 2
            mask = keep(step, c3, 16, m.edge)
            for j in range(2):
                crop = m.crop0 + 2 * p + j
                over = share_of(wv, tally, crop, 1.0)
                mean, inv = by_view(wv, crop, st2[0:2, :]), by_view(wv, crop, st2[2:4, :])
                gain = inv * norms1[0:1, c3 : 2 * c3]
                level = by_view(wv, crop, s2[0:2, :]) * over
                tilt = by_view(wv, crop, s2[2:4, :]) * over * inv

                def tile(i, j=j, mean=mean, gain=gain, level=level, tilt=tilt):
                    rows = span(r + j * m.rows + i * step, step)
                    d = gain * (q2[rows, :] - level - (z2[rows, :] - mean) * tilt)
                    d = jnp.where(mask, d, 0.0)
                    to = span(g + j * m.guard + i * step, step)
                    d2[to, 0:c3] = pltpu.roll(d, step - 1, 0).astype(BF16)
                    d2[to, c3 : 2 * c3] = d.astype(BF16)
                    d2[to, 2 * c3 : 3 * c3] = pltpu.roll(d, 1, 0).astype(BF16)

                repeat(2, tile)
            size = 2 * m.rows + 16
            value = None
            for a in range(3):
                for b in range(3):
                    part = d2[span(g - (a - 1) * 16, size), b * c3 : (b + 1) * c3]
                    term = mm_nt(part, wsp1[a, b * c3 : (b + 1) * c3, :])
                    value = term if value is None else value + term
            q1[span(r, m.rows), :] = value[0 : m.rows]
            q1[span(r + m.rows, m.rows), :] = value[m.guard : m.guard + m.rows]
            for j in range(2):
                crop = m.crop0 + 2 * p + j
                mean, inv = by_view(wv, crop, st1[0:2, :]), by_view(wv, crop, st1[2:4, :])

                def tile(i, sums, j=j, mean=mean, inv=inv):
                    rows = span(r + j * m.rows + i * step, step)
                    n = (z1[rows, :] - mean) * inv
                    v = act_slope(n * norms1[0:1, 0:c3] + norms1[1:2, 0:c3]) * q1[rows, :]
                    v = jnp.where(mask, v, 0.0)
                    q1[rows, :] = v
                    return (sums[0] + tile_sum(v), sums[1] + tile_sum(v * n))

                zero = jnp.zeros((8, c3), f)
                s, t = lax.fori_loop(0, 2, tile, (zero, zero))
                cs[pl.ds(crop, 1), 0:c3] = jnp.sum(s, axis=0, keepdims=True)
                cm[pl.ds(crop, 1), 0:c3] = jnp.sum(t, axis=0, keepdims=True)

        repeat(m.count // 2, pair)
        tick()
    local_sums(blocks[1], (cs, cm), wcol, c3)
    links.send_near(1, blocks[1])
    inside = guarded - 32

    def taps(a):
        g2[a * 3 * c3 : (a + 1) * 3 * c3, :] = mm_tn(
            h1[a * 16 : a * 16 + inside, :], d2[16 : 16 + inside, c3 : 2 * c3]
        ).astype(BF16)

    taps(0)
    tick()

    def rest():
        taps(1)
        taps(2)
        tick()

    meet_sums(links, 1, c3, ((s1, 0), (s1, 2)), rest)

    loads[6].wait()
    moves = []
    for m, out in zip(sets, (o_gb, o_gs)):
        part = m.rows // 2
        for c in range(m.count):
            i = m.crop0 + c
            own_rows = span(m.row0 + c * m.rows + core * part, part)
            other_rows = span(m.row0 + c * m.rows + (1 - core) * part, part)
            place = out.at[span((core * m.count + c) * part, part)]
            moves.append(
                (
                    pltpu.make_async_copy(d3.at[own_rows], place, own_sem.at[i]),
                    pltpu.make_async_remote_copy(
                        src_ref=d3.at[other_rows],
                        dst_ref=place,
                        send_sem=grad_send.at[i],
                        recv_sem=grad_recv.at[i],
                        device_id=sibling,
                        device_id_type=MESH,
                    ),
                )
            )
    for m in sets:

        def pair(p, m=m):
            r = m.row0 + p * 2 * m.rows
            step = m.rows // 2
            mask = keep(step, c3, 16, m.edge)
            for j in range(2):
                crop = m.crop0 + 2 * p + j
                over = share_of(wv, tally, crop, 1.0)
                mean, inv = by_view(wv, crop, st1[0:2, :]), by_view(wv, crop, st1[2:4, :])
                gain = inv * norms1[0:1, 0:c3]
                level = by_view(wv, crop, s1[0:2, :]) * over
                tilt = by_view(wv, crop, s1[2:4, :]) * over * inv

                def tile(i, j=j, mean=mean, gain=gain, level=level, tilt=tilt):
                    rows = span(r + j * m.rows + i * step, step)
                    d = gain * (q1[rows, :] - level - (z1[rows, :] - mean) * tilt)
                    d1[rows, :] = jnp.where(mask, d, 0.0).astype(BF16)

                repeat(2, tile)
            rows = span(r, 2 * m.rows)
            for n in range(cin // 256):
                cols = slice(n * 256, (n + 1) * 256)
                d3[rows, cols] = (up[rows, cols] + mm_nt(d1[rows, :], w1[cols, :])).astype(BF16)

        repeat(m.count // 2, pair)
        for c in range(m.count):
            for copy in moves[m.crop0 + c]:
                copy.start()
        tick()
    loads[7].wait()

    def inner(n):
        part = pl.ds(pl.multiple_of(n * 256, 256), 256)
        g1[part, :] = mm_tn(img[:, part], d1[...]).astype(BF16)

    repeat(cin // 256, inner)
    for src, dst in ((s2, o_s2), (s1, o_s1)):
        puts.put(src, dst)
    while share.at < len(order):
        tick()
    share.finish()
    links.finish()
    for near_copy, far_copy in moves:
        near_copy.wait()
        far_copy.wait()
    puts.finish()


def backward(sets, got, onehot, wcol, w, norms_first, norms_second, total, guarded, outs, idents):
    crops = lax.axis_size("crops")
    w1, wsp1, w3, w4, w5, w6, w7 = w
    cin, c3 = w1.shape
    c4, cout = w6.shape
    (
        f_img, f_z1, f_h1, f_z2, f_h2, f_blk, f_z4, f_x5, f_z5, f_h5, f_xe, f_res, f_d6, f_d7,
        f_st1, f_st2, f_st3, f_st4, f_st7, f_st5, f_st6, f_sq, f_n,
    ) = got
    smem, vmem = pl.BlockSpec(memory_space=pltpu.SMEM), pl.BlockSpec(memory_space=pltpu.VMEM)
    hbm = pl.BlockSpec(memory_space=pl.ANY)
    shape = jax.ShapeDtypeStruct
    most = 2 * sets[0].rows
    pairs = sum(m.count for m in sets) // 2
    count = 2 * pairs

    def like(arrays):
        return [pltpu.VMEM(t.shape, t.dtype) for t in arrays]

    def params(ident):
        return pltpu.CompilerParams(
            collective_id=ident, has_side_effects=True, vmem_limit_bytes=63 * 1024 * 1024
        )

    arrays = [f_d6, w6, f_z5, f_h5, f_d7, f_xe, w7, w5, f_x5, f_z4, w4, f_h2, w3, f_img, f_blk]
    out_shape = [
        shape((total, cin), F32), shape((c4, cout), BF16), shape((cin, cout), BF16), shape((9 * c4, c4), BF16),
        shape((cin, c4), BF16), shape((8, c4), F32), shape((8, c4), F32), shape((8, cin), F32),
    ]
    scratch = like(arrays) + [
        pltpu.VMEM((outs, c4), F32), pltpu.VMEM((outs, cin), F32), pltpu.VMEM((outs, c4), F32), pltpu.VMEM((c4 // 128, total, 128), F32), pltpu.VMEM((total, c4), BF16),
        pltpu.VMEM((most, 512), F32), pltpu.VMEM((cin // 128, most, 128), F32), pltpu.VMEM((2, most, cin), F32),
        pltpu.VMEM((8, c4), F32), pltpu.VMEM((8, c4), F32), pltpu.VMEM((8, cin), F32),
        pltpu.VMEM((16, cin), F32), pltpu.VMEM((16, cin), F32),
    ]
    scratch += exchange_shapes((c4, c4, cin), (2, 2, 2), crops)
    scratch += [pltpu.SemaphoreType.DMA((15,)), pltpu.SemaphoreType.DMA((7,)), pltpu.SemaphoreType.DMA((pairs,))]
    shapes = [(cin, cout), (c4, cout), (9 * c4, c4), (cin, c4), (c3, cin), (9 * c3, c3), (cin, c3)]
    chunks = share_plan(shapes, SHARE_CUTS)
    bits = crops.bit_length() - 1
    scratch += share_scratch(chunks[:SHARE_FIRST], bits, inside=True)
    up, g_outer2, g_skip, g_spatial2, g_inner2, s5, s4, s3 = pl.pallas_call(
        functools.partial(back_two_kernel, sets, total, outs, crops, (c3, cin, c4, cout), shapes, chunks),
        out_shape=out_shape,
        in_specs=[smem] + [vmem] * 7 + [hbm] * 15,
        out_specs=[hbm] * len(out_shape),
        scratch_shapes=scratch,
        compiler_params=params(idents[0]),
        name="back_two",
    )(onehot, wcol, norms_first, norms_second, f_st3, f_st4, f_st5, f_n, *arrays)

    arrays = [f_h2, w3, up, f_z2, f_h1, wsp1, f_z1, w1, f_img]
    out_shape = [
        shape((total_rows(sets[0]), cin), BF16), shape((total_rows(sets[1]), cin), BF16), shape((8, c3), F32),
        shape((8, c3), F32),
    ] + [shape(t, BF16) for t in shapes]
    scratch = like(arrays) + [
        pltpu.VMEM((most, 512), F32), pltpu.VMEM((total, cin), BF16), pltpu.VMEM((total, c3), F32),
        pltpu.VMEM((guarded, 3 * c3), BF16), pltpu.VMEM((total, c3), F32), pltpu.VMEM((total, c3), BF16),
        pltpu.VMEM((c3, cin), BF16), pltpu.VMEM((9 * c3, c3), BF16), pltpu.VMEM((cin, c3), BF16),
        pltpu.VMEM((8, c3), F32), pltpu.VMEM((8, c3), F32), pltpu.VMEM((16, c3), F32), pltpu.VMEM((16, c3), F32),
    ]
    scratch += exchange_shapes((c3, c3), (2, 2), crops)
    scratch += [pltpu.SemaphoreType.DMA((9,)), pltpu.SemaphoreType.DMA((2,))]
    scratch += [pltpu.SemaphoreType.DMA((count,))] * 3 + [pltpu.SemaphoreType.DMA((pairs,))]
    scratch += share_scratch(chunks, bits, range(SHARE_FIRST))
    grad_b, grad_s, s2, s1, *grads = pl.pallas_call(
        functools.partial(back_one_kernel, sets, total, guarded, crops, (c3, cin), shapes, chunks),
        out_shape=out_shape,
        in_specs=[smem] + [vmem] * 7 + [hbm] * 13,
        out_specs=[hbm] * len(out_shape),
        scratch_shapes=scratch,
        compiler_params=params(idents[1]),
        name="back_one",
    )(onehot, wcol, norms_first, f_st1, f_st2, f_st3, s3, f_n, *arrays, g_skip, g_outer2, g_spatial2, g_inner2)
    return grad_b, grad_s, grads, (s1, s2, s3, s4, s5)


def total_rows(m):
    return m.count * m.rows


def shards(
    image_big,
    image_small,
    view_big,
    view_small,
    inner_first,
    spatial_first,
    outer_first,
    norms_first,
    inner_second,
    spatial_second,
    outer_second,
    skip_second,
    norms_second,
    cotangent_big,
    cotangent_small,
):
    splits, position = lax.axis_size("rows"), lax.axis_index("rows")
    labels = jnp.concatenate(
        [
            lax.dynamic_slice_in_dim(v, position * (v.shape[0] // splits), v.shape[0] // splits)
            for v in (view_big, view_small)
        ]
    )
    onehot = (labels[None, :] == jnp.arange(2)[:, None]).astype(F32)
    nb, ns = image_big.shape[0] // splits, image_small.shape[0] // splits
    pixels = jnp.concatenate(
        [
            jnp.full((nb,), float(image_big.shape[2] ** 2), F32),
            jnp.full((ns,), float(image_small.shape[2] ** 2), F32),
        ]
    )
    c3, c4 = inner_first.shape[1], inner_second.shape[1]
    weights = [
        inner_first,
        spatial_first.reshape(3, 3 * c3, c3),
        outer_first,
        inner_second,
        spatial_second.reshape(9 * c4, c4),
        outer_second,
        skip_second,
    ]
    sets, wcol, sizes, got = forward(
        [image_big, image_small], [cotangent_big, cotangent_small], onehot, pixels, weights, norms_first, norms_second, 0
    )
    grad_b, grad_s, grads, sums = backward(
        sets, got, onehot, wcol, weights, norms_first, norms_second, *sizes, (1, 2)
    )
    s1, s2, s3, s4, s5 = sums
    sq = got[21]

    def both(parts):
        return jnp.concatenate(
            [jnp.stack([t[g] + t[g + 1], t[0] + t[1]]) for t, g in parts], axis=1
        )

    g_skip, g_outer2, g_spatial2, g_inner2, g_outer1, g_spatial1, g_inner1 = [
        t.astype(F32) for t in grads
    ]
    results = [
        got[11][m.out0 : m.out0 + m.count * m.out].reshape(m.count, m.half, 8, -1)[:, :, : m.half]
        for m in sets
    ]
    gradients = [
        t.reshape(image.shape[0], image.shape[1], 16, -1)[:, :, : image.shape[2]]
        for t, image in ((grad_b, image_big), (grad_s, image_small))
    ]
    return (
        results[0],
        results[1],
        gradients[0],
        gradients[1],
        g_inner1,
        g_spatial1.reshape(spatial_first.shape),
        g_outer1,
        both(((s1, 2), (s2, 2), (s3, 2))),
        g_inner2,
        g_spatial2.reshape(spatial_second.shape),
        g_outer2,
        g_skip,
        both(((s4, 2), (s5, 2), (sq, 2), (sq, 4))),
    )


def solution(mesh):
    maps = P("crops", "rows", None, None)
    whole = P(("crops", "rows"), None, None, None)
    in_specs = (maps, maps, P("crops"), P("crops")) + (P(),) * 9 + (whole, whole)
    out_specs = (whole, whole, maps, maps) + (P(),) * 9
    return jax.shard_map(shards, mesh=mesh, in_specs=in_specs, out_specs=out_specs, check_vma=False)
```

```python
import functools

import jax
import jax.numpy as jnp
from jax import lax
from jax.experimental import pallas as pl
from jax.experimental.pallas import tpu as pltpu
from jax.sharding import PartitionSpec as P

HIGH = lax.Precision.HIGHEST
EPS = 1e-05
MESH = pl.DeviceIdType.MESH
F32 = jnp.float32
BF16 = jnp.bfloat16


class Maps:
    def __init__(self, count, edge, row0, crop0, guard0, out0):
        self.count, self.edge = count, edge
        self.row0, self.crop0, self.guard0, self.out0 = row0, crop0, guard0, out0
        self.rows = edge * 16
        self.guard = (edge + 1) * 16
        self.half = edge // 2
        self.out = self.half * 8
        self.pixels = edge * edge


def geometry(nb, eb, ns, es):
    big = Maps(nb, eb, 0, 0, 16, 0)
    small = Maps(ns, es, nb * big.rows, nb, 16 + nb * big.guard, nb * big.out)
    total = small.row0 + ns * small.rows
    guarded = small.guard0 + ns * small.guard
    out = small.out0 + ns * small.out
    return (big, small), total, guarded, out


def al(x, m=16):
    return x if isinstance(x, int) else pl.multiple_of(x, m)


def span(start, size, m=16):
    return pl.ds(al(start, m), size)


def repeat(count, body):
    def step(i, carry):
        body(i)
        return carry

    lax.fori_loop(0, count, step, 0)


def mm(a, b):
    return jnp.dot(a, b, preferred_element_type=F32)


def mm_nt(a, b):
    return lax.dot_general(a, b, (((1,), (1,)), ((), ())), preferred_element_type=F32)


def mm_tn(a, b):
    return lax.dot_general(a, b, (((0,), (0,)), ((), ())), preferred_element_type=F32)


CA = 0.7978845608028654
CB = 0.7978845608028654 * 0.044715


def act(u):
    t = jnp.tanh(u * (CA + CB * (u * u)))
    return 0.5 * u * (1.0 + t)


def act_slope(u):
    s = u * u
    t = jnp.tanh(u * (CA + CB * s))
    rise = (0.5 * u) * (CA + (3.0 * CB) * s)
    return 0.5 * (1.0 + t) + (1.0 - t * t) * rise


def act_both(u):
    s = u * u
    t = jnp.tanh(u * (CA + CB * s))
    hu = 0.5 * u
    lift = 0.5 * (1.0 + t)
    slope = lift + (1.0 - t * t) * (hu * (CA + (3.0 * CB) * s))
    return u * lift, slope


def keep(width, pitch, edge):
    return lax.broadcasted_iota(jnp.int32, (pitch, width), 0) < edge


def masked(x, mask):
    rows = x.reshape(x.shape[0] // mask.shape[0], mask.shape[0], x.shape[1])
    return jnp.where(mask[None], rows, 0.0).reshape(x.shape)


def tile_sum(x):
    return jnp.sum(x.reshape(x.shape[0] // 8, 8, x.shape[1]), axis=0)


def pieces(width):
    return (4, width // 4) if width >= 512 else (width // 128, 128)


class Links:
    def __init__(self, crops, near, far, near_s, near_r, far_s, far_r):
        self.group = 4 if crops % 4 == 0 else 1
        self.outers = crops // self.group
        self.k, self.r = lax.axis_index("crops"), lax.axis_index("rows")
        inner, self.outer = lax.rem(self.k, self.group), self.k // self.group
        self.wide = 2 * self.group
        self.me = inner * 2 + self.r
        self.peers, self.others = [], []
        for d in range(1, self.wide):
            p = lax.rem(self.me + d, self.wide)
            self.peers.append((self.outer * self.group + p // 2, lax.rem(p, 2)))
        for d in range(1, self.outers):
            self.others.append((lax.rem(self.outer + d, self.outers) * self.group + inner, self.r))
        self.near, self.far = near, far
        self.sems = (near_s, near_r, far_s, far_r)
        self.live = {}

    def greet(self, extra=()):
        barrier = pltpu.get_barrier_semaphore()
        peers = self.peers + self.others + list(extra)
        for peer in peers:
            pl.semaphore_signal(barrier, inc=1, device_id=peer, device_id_type=MESH)
        pl.semaphore_wait(barrier, len(peers))

    def send_near(self, e, block):
        self.near[e][self.me] = block[...]
        self.live[e, 0] = []
        for d, peer in enumerate(self.peers):
            copy = pltpu.make_async_remote_copy(
                src_ref=block,
                dst_ref=self.near[e].at[self.me],
                send_sem=self.sems[0].at[e, d],
                recv_sem=self.sems[1].at[e, d],
                device_id=peer,
                device_id_type=MESH,
            )
            copy.start()
            self.live[e, 0].append(copy)

    def wait_near(self, e):
        for copy in self.live[e, 0]:
            copy.wait_recv()

    def send_far(self, e):
        self.live[e, 1] = []
        place = self.far[e].at[self.outer]
        for d, peer in enumerate(self.others):
            copy = pltpu.make_async_remote_copy(
                src_ref=place,
                dst_ref=place,
                send_sem=self.sems[2].at[e, d],
                recv_sem=self.sems[3].at[e, d],
                device_id=peer,
                device_id_type=MESH,
            )
            copy.start()
            self.live[e, 1].append(copy)

    def wait_far(self, e):
        for copy in self.live[e, 1]:
            copy.wait_recv()

    def finish(self):
        for copies in self.live.values():
            for copy in copies:
                copy.wait_send()


def fold_moments(buf, tallies, count, scale):
    sums, total = buf[0, 0:8, :], tallies[0]
    for i in range(1, count):
        sums = sums + buf[i, 0:8, :]
        total = total + tallies[i]
    mean = sums * (1.0 / jnp.maximum(total * scale, 1.0))
    spread = None
    for i in range(count):
        n = tallies[i] * scale
        apart = buf[i, 0:8, :] * (1.0 / jnp.maximum(n, 1.0)) - mean
        term = buf[i, 8:16, :] + n * apart * apart
        spread = term if spread is None else spread + term
    return sums, spread, total


def fold_sums(buf, count):
    total = buf[0]
    for i in range(1, count):
        total = total + buf[i]
    return total


def exchange_shapes(widths, tiles, crops):
    group = 4 if crops % 4 == 0 else 1
    outers = crops // group
    blocks, near, far = [], [], []
    for width, tile in zip(widths, tiles):
        lanes = pieces(width)[1]
        blocks.append(pltpu.VMEM((8 * tile, lanes), F32))
        near.append(pltpu.VMEM((2 * group, 8 * tile, lanes), F32))
        far.append(pltpu.VMEM((outers, 8 * tile, lanes), F32))
    e = len(widths)
    sems = [
        pltpu.SemaphoreType.DMA((e, 2 * group - 1)),
        pltpu.SemaphoreType.DMA((e, 2 * group - 1)),
        pltpu.SemaphoreType.DMA((e, max(outers - 1, 1))),
        pltpu.SemaphoreType.DMA((e, max(outers - 1, 1))),
    ]
    return blocks + near + far + sems


def take(refs, count):
    return list(refs[:count]), refs[count:]


def pack(block, tile, rows, width):
    count, lanes = pieces(width)
    for q in range(count):
        for v in range(2):
            block[tile * 8 + 2 * q + v : tile * 8 + 2 * q + v + 1, :] = rows[v][:, q * lanes : (q + 1) * lanes]


def unpack(table, row, tile, width):
    count, lanes = pieces(width)
    for q in range(count):
        table[row : row + 2, q * lanes : (q + 1) * lanes] = tile[2 * q : 2 * q + 2, :]


def crop_stats(ref, row0, rows, step, width, edge, pitch, pixels, crop, cs, cm, col0=0):
    mask = keep(width, pitch, edge)
    zero = jnp.zeros((8, width), F32)
    cols = pl.ds(col0, width) if isinstance(col0, int) else pl.ds(pl.multiple_of(col0, 128), width)

    def first(i, acc):
        z = ref[span(row0 + i * step, step, 8), cols]
        return acc + tile_sum(masked(z, mask))

    s = jnp.sum(lax.fori_loop(0, rows // step, first, zero), axis=0, keepdims=True)
    mean = s * (1.0 / pixels)

    def second(i, acc):
        z = ref[span(row0 + i * step, step, 8), cols]
        d = masked(z - mean, mask)
        return acc + tile_sum(d * d)

    m = jnp.sum(lax.fori_loop(0, rows // step, second, zero), axis=0, keepdims=True)
    cs[pl.ds(crop, 1), cols] = s
    cm[pl.ds(crop, 1), cols] = m


def local_moments(block, cs, cm, wcol, width, scale, tally=False):
    s, m = cs[:, 0:width], cm[:, 0:width]
    pix = wcol[:, 2:3] * scale
    mean_c = s * (1.0 / pix)
    sums, squares, tallies = [], [], []
    for v in range(2):
        w = wcol[:, v : v + 1]
        total = jnp.sum(w * s, axis=0, keepdims=True)
        n = jnp.sum(w * pix, axis=0, keepdims=True)
        apart = mean_c - total * (1.0 / jnp.maximum(n, 1.0))
        squares.append(jnp.sum(w * (m + pix * apart * apart), axis=0, keepdims=True))
        sums.append(total)
        tallies.append(n)
    pack(block, 0, sums, width)
    pack(block, 1, squares, width)
    if tally:
        lanes = pieces(width)[1]
        for q in range(4):
            for v in range(2):
                block[16 + 2 * q + v : 17 + 2 * q + v, :] = jnp.broadcast_to(tallies[v], (1, lanes))


def local_sums(block, parts, wcol, width):
    for tile, part in enumerate(parts):
        s = part[:, 0:width]
        pack(block, tile, [jnp.sum(wcol[:, v : v + 1] * s, axis=0, keepdims=True) for v in range(2)], width)


def view_tables(sets, core, views, wv, wcol):
    row = lax.broadcasted_iota(jnp.int32, wcol.shape, 0)
    lane = lax.broadcasted_iota(jnp.int32, wcol.shape, 1)
    table = jnp.where(lane == 2, 1.0, 0.0)
    for m, view in zip(sets, views):
        for c in range(m.count):
            second = view[core * m.count + c].astype(F32)
            pair = (1.0 - second, second, float(m.pixels))
            for v in range(3):
                table = jnp.where((row == m.crop0 + c) & (lane == v), pair[v], table)
            wv[0, m.crop0 + c] = pair[0]
            wv[1, m.crop0 + c] = pair[1]
    wcol[...] = table


def by_view(wv, crop, pair):
    return wv[0, crop] * pair[0:1, :] + wv[1, crop] * pair[1:2, :]


FWD_WIDTHS = (256, 256, 1024, 512, 2048, 512, 2048, 2048)


def forward_kernel(sets, total, guarded, outs, crops, dims, *refs):
    c3, cin, c4, cout = dims
    (
        vb, vs, norms1, norms2,
        img_b, img_s, cot_hbm, w1_h, wsp1_h, w3_h, w4_h, w5_h, w6_h, w7_h,
    ), refs = refs[:14], refs[14:]
    (
        o_img, o_z1, o_h1, o_z2, o_h2, o_blk, o_z4, o_x5, o_z5, o_h5, o_xe, o_res, o_d6, o_d7,
        o_st1, o_st2, o_st3, o_st4, o_st7, o_st5, o_st6, o_sq, o_tally,
    ), refs = refs[:23], refs[23:]
    (
        img, z1, h1, z2, h2, zt, blk, eb, z4, xe, z7, hp, x5, z5, h5, z6, cot,
        w1, wsp1, w3, w4, w5, w6, w7, cs, cm, ck,
        st1, st2, st3, st4, st7, st5, st6, sq, tally_v, wv, wcol,
    ), refs = refs[:38], refs[38:]
    e = len(FWD_WIDTHS)
    blocks, refs = take(refs, e)
    near, refs = take(refs, e)
    far, refs = take(refs, e)
    ns_, nr_, fs_, fr_ = refs[:4]
    load_sem, img_sem, img_send, img_recv, out_sem = refs[4:]
    links = Links(crops, near, far, ns_, nr_, fs_, fr_)
    k, core = links.k, links.r
    sibling = (k, 1 - core)
    f = F32

    loads = []
    for i, (src, dst) in enumerate(
        ((w1_h, w1), (wsp1_h, wsp1), (w3_h, w3), (w4_h, w4), (w5_h, w5), (w6_h, w6), (w7_h, w7), (cot_hbm, cot))
    ):
        loads.append(pltpu.make_async_copy(src, dst, load_sem.at[i]))
    own, swaps = [], []
    for at, (m, src) in enumerate(zip(sets, (img_b, img_s))):
        part = m.rows // 2
        for c in range(m.count):
            i = m.crop0 + c
            place = img.at[span(m.row0 + c * m.rows + core * part, part)]
            own.append(
                pltpu.make_async_copy(
                    src.at[span((core * m.count + c) * part, part)], place, img_sem.at[i]
                )
            )
            swaps.append(
                pltpu.make_async_remote_copy(
                    src_ref=src.at[span(((1 - core) * m.count + c) * part, part)],
                    dst_ref=place,
                    send_sem=img_send.at[i],
                    recv_sem=img_recv.at[i],
                    device_id=sibling,
                    device_id_type=MESH,
                )
            )
    for copy in own:
        copy.start()
    loads[0].start()
    links.greet()
    for copy in swaps:
        copy.start()

    view_tables(sets, core, (vb, vs), wv, wcol)
    out_copies = []

    def put(src, dst):
        copy = pltpu.make_async_copy(src, dst, out_sem.at[len(out_copies)])
        copy.start()
        out_copies.append(copy)

    for ref in (cs, cm, ck):
        ref[...] = jnp.zeros(ref.shape, f)
    for block in blocks:
        block[...] = jnp.zeros(block.shape, f)
    h1[0:16, :] = jnp.zeros((16, 3 * c3), BF16)
    for m in sets:
        for c in range(m.count):
            at = m.guard0 + c * m.guard + m.rows
            h1[at : at + 16, :] = jnp.zeros((16, 3 * c3), BF16)

    def near_tallies():
        return [near[0][i, 16:24, 0:1] for i in range(links.wide)]

    def far_tallies():
        return [far[0][i, 16:24, 0:1] for i in range(links.outers)]

    def meet_near(i, scale):
        links.wait_near(i)
        sums, spread, n = fold_moments(near[i], near_tallies(), links.wide, scale)
        place = far[i].at[links.outer]
        place[0:8, :] = sums
        place[8:16, :] = spread
        if i == 0:
            place[16:24, :] = jnp.broadcast_to(n, (8, near[0].shape[2]))
        links.send_far(i)

    def meet_far(i, scale, table, width):
        links.wait_far(i)
        sums, spread, n = fold_moments(far[i], far_tallies(), links.outers, scale)
        over = 1.0 / (n * scale)
        mean = sums * over
        inverse = lax.rsqrt(spread * over + EPS)
        unpack(table, 0, mean, width)
        unpack(table, 2, inverse, width)
        if i == 0:
            tally_v[...] = jnp.broadcast_to(n, (8, 128))

    loads[0].wait()
    for copy in own:
        copy.wait()
    for copy in swaps:
        copy.wait_recv()
    for copy in loads[1:]:
        copy.start()
    for m in sets:

        def pair(p, m=m):
            r = m.row0 + p * 2 * m.rows
            z1[span(r, 2 * m.rows), :] = mm(img[span(r, 2 * m.rows), :], w1[...])
            for j in range(2):
                crop_stats(z1, r + j * m.rows, m.rows, m.rows // 2, c3, m.edge, 16, m.pixels, m.crop0 + 2 * p + j, cs, cm)

        repeat(m.count // 2, pair)
    local_moments(blocks[0], cs, cm, wcol, c3, 1.0, True)
    links.send_near(0, blocks[0])
    put(img, o_img)
    put(z1, o_z1)
    loads[1].wait()
    meet_near(0, 1.0)
    meet_far(0, 1.0, st1, c3)

    for m in sets:

        def pair(p, m=m):
            r = m.row0 + p * 2 * m.rows
            g = m.guard0 + p * 2 * m.guard
            for j in range(2):
                crop = m.crop0 + 2 * p + j
                mean = by_view(wv, crop, st1[0:2, :])
                scale = by_view(wv, crop, st1[2:4, :]) * norms1[0:1, 0:c3]
                shift = norms1[1:2, 0:c3]
                step = m.rows // 2
                mask = keep(c3, 16, m.edge)

                def tile(i):
                    z = z1[span(r + j * m.rows + i * step, step), :]
                    h = masked(act((z - mean) * scale + shift), mask)
                    rows = span(g + j * m.guard + i * step, step)
                    h1[rows, 0:c3] = pltpu.roll(h, 1, 0).astype(BF16)
                    h1[rows, c3 : 2 * c3] = h.astype(BF16)
                    h1[rows, 2 * c3 : 3 * c3] = pltpu.roll(h, step - 1, 0).astype(BF16)

                repeat(2, tile)
            size = 2 * m.rows + 16
            z = mm(h1[span(g - 16, size), :], wsp1[0]) + mm(h1[span(g, size), :], wsp1[1])
            z = z + mm(h1[span(g + 16, size), :], wsp1[2])
            z2[span(r, m.rows), :] = z[0 : m.rows]
            z2[span(r + m.rows, m.rows), :] = z[m.guard : m.guard + m.rows]
            for j in range(2):
                crop_stats(z2, r + j * m.rows, m.rows, m.rows // 2, c3, m.edge, 16, m.pixels, m.crop0 + 2 * p + j, cs, cm)

        repeat(m.count // 2, pair)
    local_moments(blocks[1], cs, cm, wcol, c3, 1.0)
    links.send_near(1, blocks[1])
    put(h1, o_h1)
    put(z2, o_z2)
    loads[2].wait()
    meet_near(1, 1.0)
    meet_far(1, 1.0, st2, c3)

    for m in sets:

        def pair(p, m=m):
            r = m.row0 + p * 2 * m.rows
            for j in range(2):
                crop = m.crop0 + 2 * p + j
                mean = by_view(wv, crop, st2[0:2, :])
                scale = by_view(wv, crop, st2[2:4, :]) * norms1[0:1, c3 : 2 * c3]
                shift = norms1[1:2, c3 : 2 * c3]
                step = m.rows // 2

                def tile(i):
                    rows = span(r + j * m.rows + i * step, step)
                    h2[rows, :] = act((z2[rows, :] - mean) * scale + shift).astype(BF16)

                repeat(2, tile)
            zt[0 : 2 * m.rows, :] = mm(h2[span(r, 2 * m.rows), :], w3[...])
            for j in range(2):
                crop_stats(zt, j * m.rows, m.rows, 32, cin, m.edge, 16, m.pixels, m.crop0 + 2 * p + j, cs, cm)

        repeat(m.count // 2, pair)
    local_moments(blocks[2], cs, cm, wcol, cin, 1.0)
    links.send_near(2, blocks[2])
    put(h2, o_h2)
    loads[3].wait()
    meet_near(2, 1.0)
    meet_far(2, 1.0, st3, cin)

    for m in sets:

        def pair(p, m=m):
            r = m.row0 + p * 2 * m.rows
            zt[0 : 2 * m.rows, :] = mm(h2[span(r, 2 * m.rows), :], w3[...])
            for j in range(2):
                crop = m.crop0 + 2 * p + j
                mean = by_view(wv, crop, st3[0:2, :])
                scale = by_view(wv, crop, st3[2:4, :]) * norms1[0:1, 2 * c3 :]
                shift = norms1[1:2, 2 * c3 :]

                def tile(i):
                    here = span(j * m.rows + i * 32, 32)
                    rows = span(r + j * m.rows + i * 32, 32)
                    u = (zt[here, :] - mean) * scale + shift + img[rows, :].astype(f)
                    b = act(u)
                    blk[rows, :] = b.astype(BF16)
                    for q in range(cin // 128):
                        eb[q, span(j * m.rows // 2 + i * 16, 16), :] = b[0:16, q * 128 : (q + 1) * 128]

                repeat(m.rows // 32, tile)
            for q in range(cin // 128):
                picked = [eb[q, pl.ds(i * 16, 8, stride=2), :] for i in range(2 * m.half)]
                xe[span(m.out0 + p * 2 * m.out, 2 * m.out), q * 128 : (q + 1) * 128] = jnp.concatenate(
                    picked, axis=0
                ).astype(BF16)
            z4[span(r, 2 * m.rows), :] = mm(blk[span(r, 2 * m.rows), :], w4[...])
            for j in range(2):
                crop_stats(z4, r + j * m.rows, m.rows, 32, c4, m.edge, 16, m.pixels, m.crop0 + 2 * p + j, cs, cm)

        repeat(m.count // 2, pair)
    local_moments(blocks[3], cs, cm, wcol, c4, 1.0)
    links.send_near(3, blocks[3])
    put(blk, o_blk)
    put(z4, o_z4)
    put(xe, o_xe)
    loads[6].wait()

    def wide_product(a, w, z):
        def columns(n):
            cols = pl.ds(pl.multiple_of(n * 512, 512), 512)
            z[:, cols] = mm(a[...], w[:, cols])

        repeat(cout // 512, columns)

    def wide_stats(z):
        for m in sets:

            def crop_(c, m=m):
                def columns(n):
                    crop_stats(
                        z, m.out0 + c * m.out, m.out, m.out, 512, m.half, 8, m.half * m.half,
                        m.crop0 + c, cs, cm, n * 512,
                    )

                repeat(cout // 512, columns)

            repeat(m.count, crop_)

    wide_product(xe, w7, z7)
    meet_near(3, 1.0)
    wide_stats(z7)
    local_moments(blocks[4], cs, cm, wcol, cout, 0.25)
    links.send_near(4, blocks[4])
    meet_far(3, 1.0, st4, c4)

    loads[4].wait()
    lots = c4 // 128
    hp[:, 0:24, :] = jnp.zeros((lots, 24, 128), f)
    for m in sets:

        def pair(p, m=m):
            r = m.row0 + p * 2 * m.rows
            for j in range(2):
                crop = m.crop0 + 2 * p + j
                mean = by_view(wv, crop, st4[0:2, :])
                scale = by_view(wv, crop, st4[2:4, :]) * norms2[0:1, 0:c4]
                shift = norms2[1:2, 0:c4]
                mask = keep(c4, 16, m.edge)
                base = 24 + j * m.guard
                hp[:, base + m.rows : base + m.guard, :] = jnp.zeros((lots, 16, 128), f)

                def tile(i):
                    z = z4[span(r + j * m.rows + i * 32, 32), :]
                    h = masked(act((z - mean) * scale + shift), mask)
                    for q in range(lots):
                        hp[q, span(base + i * 32, 32, 8), :] = h[:, q * 128 : (q + 1) * 128]

                repeat(m.rows // 32, tile)
            for a in range(3):
                for b in range(3):
                    for q in range(lots):
                        picked = []
                        for j in range(2):
                            for i in range(m.half):
                                at = 24 + j * m.guard + (2 * i + a - 1) * 16 + b - 1
                                picked.append(hp[q, pl.ds(at, 8, stride=2), :])
                        tap = (3 * a + b) * c4 + q * 128
                        x5[span(m.out0 + p * 2 * m.out, 2 * m.out), tap : tap + 128] = jnp.concatenate(
                            picked, axis=0
                        ).astype(BF16)

        repeat(m.count // 2, pair)
    z5[...] = jnp.zeros(z5.shape, f)

    def taps(t):
        part = pl.ds(pl.multiple_of(t * 3 * c4, 128), 3 * c4)
        z5[...] += mm(x5[:, part], w5[part, :])

    repeat(3, taps)
    for m in sets:

        def crop_(c, m=m):
            crop_stats(z5, m.out0 + c * m.out, m.out, m.out, c4, m.half, 8, m.half * m.half, m.crop0 + c, cs, cm)

        repeat(m.count, crop_)
    local_moments(blocks[5], cs, cm, wcol, c4, 0.25)
    links.send_near(5, blocks[5])
    put(x5, o_x5)
    put(z5, o_z5)
    meet_near(4, 0.25)
    meet_near(5, 0.25)
    meet_far(4, 0.25, st7, cout)
    meet_far(5, 0.25, st5, c4)

    loads[5].wait()
    for m in sets:

        def pair(p, m=m):
            o = m.out0 + p * 2 * m.out
            halves = []
            for j in range(2):
                crop = m.crop0 + 2 * p + j
                mean = by_view(wv, crop, st5[0:2, :])
                scale = by_view(wv, crop, st5[2:4, :]) * norms2[0:1, c4 : 2 * c4]
                z = z5[span(o + j * m.out, m.out, 8), :]
                halves.append(act((z - mean) * scale + norms2[1:2, c4 : 2 * c4]))
            h5[span(o, 2 * m.out), :] = jnp.concatenate(halves, axis=0).astype(BF16)

        repeat(m.count // 2, pair)
    wide_product(h5, w6, z6)
    wide_stats(z6)
    local_moments(blocks[6], cs, cm, wcol, cout, 0.25)
    links.send_near(6, blocks[6])
    put(h5, o_h5)
    loads[7].wait()
    meet_near(6, 0.25)
    meet_far(6, 0.25, st6, cout)

    out_copies[6].wait()
    g6, g7 = 2 * c4, 2 * c4 + cout
    lanes = 512
    for m in sets:

        def pair(p, m=m):
            o = m.out0 + p * 2 * m.out

            def columns(n):
                cols = pl.ds(pl.multiple_of(n * lanes, lanes), lanes)
                cols6 = pl.ds(pl.multiple_of(g6 + n * lanes, lanes), lanes)
                cols7 = pl.ds(pl.multiple_of(g7 + n * lanes, lanes), lanes)
                c = cot[span(o, 2 * m.out), cols].astype(f)
                mask = keep(lanes, 8, m.half)
                found = []
                for j in range(2):
                    crop = m.crop0 + 2 * p + j
                    rows = span(o + j * m.out, m.out, 8)
                    n6 = (z6[rows, cols] - by_view(wv, crop, st6[0:2, cols])) * by_view(wv, crop, st6[2:4, cols])
                    n7 = (z7[rows, cols] - by_view(wv, crop, st7[0:2, cols])) * by_view(wv, crop, st7[2:4, cols])
                    u = n6 * norms2[0:1, cols6] + norms2[1:2, cols6] + n7 * norms2[0:1, cols7] + norms2[1:2, cols7]
                    a, slope = act_both(u)
                    found.append(a)
                    up = masked(slope * c[j * m.out : (j + 1) * m.out], mask)
                    z4[span(n * outs + o + j * m.out, m.out, 8), :] = up
                    for to, part in ((cs, up), (cm, up * n6), (ck, up * n7)):
                        to[pl.ds(crop, 1), cols] = jnp.sum(tile_sum(part), axis=0, keepdims=True)
                w6[span(o, 2 * m.out), cols] = jnp.concatenate(found, axis=0).astype(BF16)

            repeat(cout // lanes, columns)

        repeat(m.count // 2, pair)
    local_sums(blocks[7], (cs, cm, ck), wcol, cout)
    links.send_near(7, blocks[7])
    put(w6.at[0:outs], o_res)
    links.wait_near(7)
    far[7][links.outer] = fold_sums(near[7], links.wide)
    links.send_far(7)
    links.wait_far(7)
    sums = fold_sums(far[7], links.outers)
    for t in range(3):
        unpack(sq, 2 * t, sums[8 * t : 8 * t + 8], cout)

    for m in sets:

        def pair(p, m=m):
            o = m.out0 + p * 2 * m.out

            def columns(n):
                cols = pl.ds(pl.multiple_of(n * lanes, lanes), lanes)
                mask = keep(lanes, 8, m.half)
                got6, got7 = [], []
                for j in range(2):
                    crop = m.crop0 + 2 * p + j
                    rows = span(o + j * m.out, m.out, 8)
                    up = z4[span(n * outs + o + j * m.out, m.out, 8), :]
                    over = wv[0, crop] * (4.0 / tally_v[0:1, 0:1]) + wv[1, crop] * (4.0 / tally_v[1:2, 0:1])
                    level = by_view(wv, crop, sq[0:2, cols]) * over
                    for got, z, st, at, t in ((got6, z6, st6, g6, 2), (got7, z7, st7, g7, 4)):
                        inv = by_view(wv, crop, st[2:4, cols])
                        gain = inv * norms2[0:1, pl.ds(pl.multiple_of(at + n * lanes, lanes), lanes)]
                        tilt = by_view(wv, crop, sq[t : t + 2, cols]) * over
                        centered = (z[rows, cols] - by_view(wv, crop, st[0:2, cols])) * inv
                        got.append(masked(gain * (up - level - centered * tilt), mask))
                w7[span(o, 2 * m.out), cols] = jnp.concatenate(got6, axis=0).astype(BF16)
                w7[span(cin // 2 + o, 2 * m.out), cols] = jnp.concatenate(got7, axis=0).astype(BF16)

            repeat(cout // lanes, columns)

        repeat(m.count // 2, pair)
    put(w7.at[0:outs], o_d6)
    put(w7.at[cin // 2 : cin // 2 + outs], o_d7)
    for src, dst in (
        (st1, o_st1), (st2, o_st2), (st3, o_st3), (st4, o_st4), (st7, o_st7), (st5, o_st5), (st6, o_st6),
        (sq, o_sq), (tally_v, o_tally),
    ):
        put(src, dst)
    links.finish()
    for copy in swaps:
        copy.wait_send()
    for i, copy in enumerate(out_copies):
        if i != 6:
            copy.wait()


def flat_rows(tensor, pitch):
    n, h, w, c = tensor.shape
    return jnp.pad(tensor, ((0, 0), (0, 0), (0, pitch - w), (0, 0))).reshape(n * h * pitch, c)


def forward(images, cots, views, w, norms_first, norms_second, ident):
    crops = lax.axis_size("crops")
    nb, ns = images[0].shape[0] // 2, images[1].shape[0] // 2
    sets, total, guarded, outs = geometry(nb, images[0].shape[2], ns, images[1].shape[2])
    w1, wsp1, w3, w4, w5, w6, w7 = w
    cin, c3 = w1.shape
    c4, cout = w6.shape
    smem, vmem = pl.BlockSpec(memory_space=pltpu.SMEM), pl.BlockSpec(memory_space=pltpu.VMEM)
    hbm = pl.BlockSpec(memory_space=pl.ANY)
    shape = jax.ShapeDtypeStruct
    out_shape = [
        shape((total, cin), BF16), shape((total, c3), F32), shape((guarded, 3 * c3), BF16), shape((total, c3), F32),
        shape((total, c3), BF16), shape((total, cin), BF16), shape((total, c4), F32), shape((outs, 9 * c4), BF16),
        shape((outs, c4), F32), shape((outs, c4), BF16), shape((outs, cin), BF16), shape((outs, cout), BF16),
        shape((outs, cout), BF16), shape((outs, cout), BF16),
        shape((8, c3), F32), shape((8, c3), F32), shape((8, cin), F32), shape((8, c4), F32), shape((8, cout), F32),
        shape((8, c4), F32), shape((8, cout), F32), shape((8, cout), F32), shape((8, 128), F32),
    ]
    most = 2 * sets[0].rows
    scratch = [
        pltpu.VMEM((total, cin), BF16), pltpu.VMEM((total, c3), F32), pltpu.VMEM((guarded, 3 * c3), BF16),
        pltpu.VMEM((total, c3), F32), pltpu.VMEM((total, c3), BF16), pltpu.VMEM((most, cin), F32),
        pltpu.VMEM((total, cin), BF16), pltpu.VMEM((cin // 128, most // 2, 128), F32), pltpu.VMEM((total, c4), F32),
        pltpu.VMEM((outs, cin), BF16), pltpu.VMEM((outs, cout), F32), pltpu.VMEM((c4 // 128, 24 + 2 * sets[0].guard, 128), F32),
        pltpu.VMEM((outs, 9 * c4), BF16), pltpu.VMEM((outs, c4), F32),
        pltpu.VMEM((outs, c4), BF16), pltpu.VMEM((outs, cout), F32), pltpu.VMEM((outs, cout), BF16),
    ]
    scratch += [pltpu.VMEM(t.shape, BF16) for t in w]
    scratch += [pltpu.VMEM((16, cout), F32)] * 3
    scratch += [pltpu.VMEM((8, n), F32) for n in (c3, c3, cin, c4, cout, c4, cout, cout, 128)]
    scratch += [pltpu.SMEM((2, 16), F32), pltpu.VMEM((16, 128), F32)]
    scratch += exchange_shapes(FWD_WIDTHS, (3, 2, 2, 2, 2, 2, 2, 3), crops)
    scratch += [
        pltpu.SemaphoreType.DMA((8,)), pltpu.SemaphoreType.DMA((nb + ns,)), pltpu.SemaphoreType.DMA((nb + ns,)),
        pltpu.SemaphoreType.DMA((nb + ns,)), pltpu.SemaphoreType.DMA((23,)),
    ]
    got = pl.pallas_call(
        functools.partial(forward_kernel, sets, total, guarded, outs, crops, (c3, cin, c4, cout)),
        out_shape=out_shape,
        in_specs=[smem, smem, vmem, vmem] + [hbm] * 10,
        out_specs=[hbm] * len(out_shape),
        scratch_shapes=scratch,
        compiler_params=pltpu.CompilerParams(
            collective_id=ident, has_side_effects=True, vmem_limit_bytes=63 * 1024 * 1024
        ),
        name="forward",
    )(
        *views, norms_first, norms_second,
        flat_rows(images[0], 16), flat_rows(images[1], 16),
        jnp.concatenate([flat_rows(t, 8) for t in cots], axis=0), *w,
    )
    return sets, (total, guarded, outs), got


def share_plan(shapes, cuts):
    chunks = []
    for at, (height, width) in enumerate(shapes):
        down, across = cuts[at]
        half, high = width // 2 // across, height // down
        for c in range(down):
            for p in range(across):
                chunks.append((at, c * high, high, p * half, half))
    return chunks


class Share:
    def __init__(self, shapes, chunks, orders, bits, links, sources, outs, acc, recv0, recvs, sems, done=(), gather=True):
        self.shapes, self.chunks, self.bits = shapes, chunks, bits
        self.k, self.core = links.k, links.r
        self.sources, self.outs, self.acc, self.recv0, self.recvs = sources, outs, acc, recv0, recvs
        self.send_sem, self.recv_sem, self.load_sem, self.store_sem = sems
        self.sibling = (self.k, 1 - self.core)
        self.total = 2 * bits + 2
        self.live, self.loads, self.stores, self.done, self.gather, self.at = {}, {}, {}, done, gather, 0
        digit = [lax.rem(self.k // (1 << b), 2) for b in range(bits)]
        self.stages, self.regions, self.kinds, self.slots = [], [], [], []
        for i, (at, row, height, col, width) in enumerate(chunks):
            stages = []
            for a, b in zip(*orders[i]):
                if a == b:
                    mine, step = digit[a], 1 << a
                else:
                    mine = digit[a] * (1 - self.core) + digit[b] * self.core
                    step = (1 << a) * (1 - self.core) + (1 << b) * self.core
                stages.append((mine, self.k + step * (1 - 2 * mine)))
            start, length, used = 0, height, 0
            region, kind, slot = [], [], []
            for s in range(bits):
                region.append((start, length))
                slot.append(used)
                if length % 32 == 0:
                    kind.append(True)
                    length //= 2
                    start = start + stages[s][0] * length
                else:
                    kind.append(False)
                used += length
            region.append((start, length))
            self.stages.append(stages)
            self.regions.append(region)
            self.kinds.append(kind)
            self.slots.append(slot)

    def send(self, i, t, src, dst, device):
        copy = pltpu.make_async_remote_copy(
            src_ref=src,
            dst_ref=dst,
            send_sem=self.send_sem.at[i, t],
            recv_sem=self.recv_sem.at[i, t],
            device_id=device,
            device_id_type=MESH,
        )
        copy.start()
        self.live[i, t] = copy

    def add(self, dst, at, src, src_at, length):
        block = 16
        while length % (block * 2) == 0 and block * 2 * dst.shape[1] <= 65536:
            block *= 2

        def step(j, carry):
            off = j * block
            rows = span(at + off, block)
            dst[rows, :] = dst[rows, :] + src[span(src_at + off, block), :]
            return carry

        lax.fori_loop(0, length // block, step, 0)

    def arrived(self, i, t):
        if (i, t) in self.live:
            self.live[i, t].wait_recv()

    def task(self, i, t):
        at, row, height, col, width = self.chunks[i]
        bits, kinds, regions, stages = self.bits, self.kinds[i], self.regions[i], self.stages[i]
        half = self.shapes[at][1] // 2
        own = pl.ds(pl.multiple_of(self.core * half + col, 128), width)
        rows = pl.ds(row, height)
        if t == 0:
            away = pl.ds(pl.multiple_of((1 - self.core) * half + col, 128), width)
            self.send(i, 0, self.sources[at].at[rows, away], self.recv0[i], self.sibling)
            if self.acc[i] is None:
                self.acc[i] = self.sources[at].at[rows, own]
                return
            copy = pltpu.make_async_copy(self.sources[at].at[rows, own], self.acc[i], self.load_sem.at[i])
            copy.start()
            self.loads[i] = copy
            return
        self.arrived(i, t - 1)
        if t <= bits + 1:
            if i in self.done:
                pass
            elif t == 1:
                if i in self.loads:
                    self.loads[i].wait()
                self.add(self.acc[i], 0, self.recv0[i], 0, height)
            else:
                s = t - 2
                start, length = regions[s + 1]
                if not kinds[s]:
                    self.live[i, t - 1].wait_send()
                self.add(self.acc[i], start, self.recvs[i], self.slots[i][s], length)
        if t <= bits:
            s = t - 1
            start, length = regions[s]
            give, first = length, start
            if kinds[s]:
                give = length // 2
                first = start + (1 - stages[s][0]) * give
            self.send(
                i, t, self.acc[i].at[span(first, give)], self.recvs[i].at[pl.ds(self.slots[i][s], give)],
                (stages[s][1], self.core),
            )
            return
        if t == bits + 1:
            start, length = regions[bits]
            if i in self.done:
                mine = self.sources[at].at[span(row + start, length), own]
            else:
                mine = self.acc[i].at[span(start, length)]
            copy = pltpu.make_async_copy(mine, self.outs[at].at[span(row + start, length), own], self.store_sem.at[i])
            copy.start()
            self.stores[i] = copy
            if not self.gather:
                return
        if t == bits + 2:
            self.stores[i].wait()
        if t <= 2 * bits:
            s = bits - 1 - (t - bits - 1)
            start, length = regions[s + 1]
            if kinds[s]:
                place = self.outs[at].at[span(row + start, length), own]
                self.send(i, t, mine if t == bits + 1 else place, place, (stages[s][1], self.core))
            return
        if t == 2 * bits + 1:
            place = self.outs[at].at[rows, own]
            self.send(i, t, place, place, self.sibling)

    def run(self, order):
        while self.at < len(order):
            token = order[self.at]
            self.at += 1
            if token is None:
                return
            i, t = token
            if t == self.total:
                self.arrived(i, t - 1)
            else:
                self.task(i, t)

    def finish(self):
        for (i, t), copy in self.live.items():
            if not (1 <= t <= self.bits and not self.kinds[i][t - 1]):
                copy.wait_send()


def share_scratch(chunks, bits, done=(), inside=False):
    acc, recv0, recvs = [], [], []
    for i, (at, row, height, col, width) in enumerate(chunks):
        if i in done:
            continue
        acc.append(pltpu.VMEM((height, width), BF16))
        recv0.append(pltpu.VMEM((height, width), BF16))
        length, used = height, 0
        for s in range(bits):
            if length % 32 == 0:
                length //= 2
            used += length
        recvs.append(pltpu.VMEM((used, width), BF16))
    n = len(chunks)
    sems = [pltpu.SemaphoreType.DMA((n, 2 * bits + 2))] * 2 + [pltpu.SemaphoreType.DMA((n,))] * 2
    return ([] if inside else acc) + recv0 + recvs + sems


def share_orders(bits, path):
    rest = list(range(2, bits))
    if bits < 2:
        return rest or list(range(bits)), rest or list(range(bits))
    if path == 0:
        return [0, 1] + rest, [1, 0] + rest
    if path == 1:
        return [0] + rest + [1], [1] + rest + [0]
    return rest + [0, 1], rest + [1, 0]


SHARE_CUTS = ((1, 2), (1, 1), (3, 1), (1, 1), (1, 1), (1, 1), (1, 1))
SHARE_FIRST = 3
SHARE_PATHS = (0, 0, 1, 0, 0, 0, 2, 0, 0, 0)
SHARE_LATE = (
    21, 64, 80, 5, 37, 96, 48, -1, 38, -1, 22, 65, 81, 6, 97, 49, -1, 39, -1, -1, -1, 23, -1, 112,
    66, 7, -1, 113, 82, 50, 98, -1, 24, 40, -1, 67, -1, -1, 114, 8, 99, -1, 68, 83, -1, 128, 51, -1,
    115, 69, 84, 100, -1, 129, -1, 101, 116, 52, -1, -1, 70, 85, -1, 117, 144, 102, 25, 41, 53, 145, 86, 118,
    9, 103, 130, 71, 54, 26, 42, 146, 119, 10, 131, 87, 147, 120, 72, 55, 104, 132, 148, 88, 121, 149, 133, 56,
    122, 105, 150, 134, 73, 106, 151, 135, 89, 74, 152, 57, 136, 90, 153, 58, 154, 137, 138,
)
SHARE_EARLY = (
    32, -1, 0, 33, 16, -1, 1, -1, 17, -1, 34, -1, -1, -1, 2, -1, 35, 18, -1, 3, -1, 19, 36, -1,
    4, -1, 37, 20, -1, -1, -1, 5, 21,
)


def share_late_order(pieces, bits, parts, ready):
    if bits == 4:
        return [None if v < 0 else (v // 16, v % 16) for v in SHARE_LATE]
    order, total = [], 2 * bits + 2
    begin = [bits + 1 if i < SHARE_FIRST else 0 for i in range(pieces)]
    for k in range(parts + total + 1):
        for i in range(pieces):
            t = k - ready[i] + begin[i]
            if k >= ready[i] and t <= total:
                order.append((i, t))
        if k < parts:
            order.append(None)
    return order


def share_early_order(bits):
    if bits == 4:
        return [None if v < 0 else (v // 16, v % 16) for v in SHARE_EARLY]
    order = [(2, 0), None, (0, 0), (1, 0), None]
    for t in range(1, bits + 2):
        order += [(2, t), (0, t), (1, t), None]
    return order


def meet_sums(links, e, width, tables, between=None):
    links.wait_near(e)
    links.far[e][links.outer] = fold_sums(links.near[e], links.wide)
    links.send_far(e)
    if between is not None:
        between()
    links.wait_far(e)
    sums = fold_sums(links.far[e], links.outers)
    for t, (table, row) in enumerate(tables):
        unpack(table, row, sums[8 * t : 8 * t + 8], width)


def share_of(wv, tally, crop, times):
    return wv[0, crop] * (times / tally[0:1, 0:1]) + wv[1, crop] * (times / tally[1:2, 0:1])


class Puts:
    def __init__(self, sem):
        self.sem, self.copies = sem, []

    def put(self, src, dst):
        copy = pltpu.make_async_copy(src, dst, self.sem.at[len(self.copies)])
        copy.start()
        self.copies.append(copy)

    def finish(self):
        for copy in self.copies:
            copy.wait()


def start_loads(pairs, sem):
    copies = [pltpu.make_async_copy(src, dst, sem.at[i]) for i, (src, dst) in enumerate(pairs)]
    for copy in copies:
        copy.start()
    return copies


def back_two_kernel(sets, total, outs, crops, dims, shapes, chunks, *refs):
    c3, cin, c4, cout = dims
    vb, vs, norms1, norms2, st3, st4, st5, tally = refs[:8]
    sources, refs = refs[8:23], refs[23:]
    (o_up, o_g6, o_g7, o_g5, o_g4, o_s5, o_s4, o_s3), refs = refs[:8], refs[8:]
    held, refs = refs[:15], refs[15:]
    (d6, w6, z5, h5, d7, xe, w7, w5, x5, z4, w4, h2, w3, img, blk) = held
    (q5, t7, pv, dh, d4, zt, bg, up, s5, s4, s3, cs, cm, wv, wcol), refs = refs[:15], refs[15:]
    d5 = d6
    g6, g7, g5, g4 = w6, w7, w5, w4
    blocks, refs = take(refs, 3)
    near, refs = take(refs, 3)
    far, refs = take(refs, 3)
    links = Links(crops, near, far, *refs[:4])
    load_sem, out_sem, up_sem = refs[4:7]
    refs = refs[7:]
    bits = crops.bit_length() - 1
    early = SHARE_FIRST
    recv0, refs = take(refs, early)
    recvs, refs = take(refs, early)
    share = Share(
        shapes, chunks[:early], [share_orders(bits, v) for v in SHARE_PATHS[:early]], bits, links, [g7, g6], [o_g7, o_g6],
        [None] * early, recv0, recvs, refs, gather=False,
    )
    order = share_early_order(bits)

    def tick():
        share.run(order)

    f = F32
    loads = start_loads(list(zip(sources, held)), load_sem)
    links.greet()
    view_tables(sets, links.r, (vb, vs), wv, wcol)
    puts = Puts(out_sem)
    for ref in (cs, cm):
        ref[...] = jnp.zeros(ref.shape, f)
    for block in blocks:
        block[...] = jnp.zeros(block.shape, f)

    for i in range(3):
        loads[i].wait()
    q5[...] = mm_nt(d6[...], w6[...])
    g5at = c4
    for m in sets:

        def crop_(c, m=m):
            crop = m.crop0 + c
            rows = span(m.out0 + c * m.out, m.out, 8)
            inv = by_view(wv, crop, st5[2:4, :])
            n = (z5[rows, :] - by_view(wv, crop, st5[0:2, :])) * inv
            q = act_slope(n * norms2[0:1, g5at : 2 * c4] + norms2[1:2, g5at : 2 * c4]) * q5[rows, :]
            q5[rows, :] = q
            cs[pl.ds(crop, 1), 0:c4] = jnp.sum(tile_sum(q), axis=0, keepdims=True)
            cm[pl.ds(crop, 1), 0:c4] = jnp.sum(tile_sum(q * n), axis=0, keepdims=True)

        repeat(m.count, crop_)
    local_sums(blocks[0], (cs, cm), wcol, c4)
    links.send_near(0, blocks[0])

    loads[3].wait()

    def outer(n):
        cols = pl.ds(pl.multiple_of(n * 512, 512), 512)
        g6[:, cols] = mm_tn(h5[...], d6[:, cols]).astype(BF16)

    repeat(cout // 512, outer)
    tick()

    def rest():
        for i in (4, 5, 6):
            loads[i].wait()

        def shortcut(n):
            part = pl.ds(pl.multiple_of(n * 256, 256), 256)
            t7[:, part] = mm_nt(d7[...], w7[part, :])

        repeat(cin // 256, shortcut)

        def skip(n):
            cols = pl.ds(pl.multiple_of(n * 512, 512), 512)
            g7[:, cols] = mm_tn(xe[...], d7[:, cols]).astype(BF16)

        repeat(cout // 512, skip)
        tick()

    meet_sums(links, 0, c4, ((s5, 0), (s5, 2)), rest)

    for m in sets:

        def pair(p, m=m):
            o = m.out0 + p * 2 * m.out
            mask = keep(c4, 8, m.half)
            slots = [[], [], [], []]
            for j in range(2):
                crop = m.crop0 + 2 * p + j
                rows = span(o + j * m.out, m.out, 8)
                over = share_of(wv, tally, crop, 4.0)
                inv = by_view(wv, crop, st5[2:4, :])
                n = (z5[rows, :] - by_view(wv, crop, st5[0:2, :])) * inv
                d = (inv * norms2[0:1, g5at : 2 * c4]) * (
                    q5[rows, :] - by_view(wv, crop, s5[0:2, :]) * over - n * (by_view(wv, crop, s5[2:4, :]) * over)
                )
                d = masked(d, mask)
                down = jnp.concatenate([d[8:], jnp.zeros((8, c4), f)], axis=0)
                slots[0].append(d)
                slots[1].append(pltpu.roll(d, m.out - 1, 0))
                slots[2].append(down)
                slots[3].append(pltpu.roll(down, m.out - 1, 0))
            for t in range(4):
                d5[span(o, 2 * m.out), t * c4 : (t + 1) * c4] = jnp.concatenate(slots[t], axis=0).astype(BF16)

        repeat(m.count // 2, pair)

    tick()
    loads[7].wait()
    options = (((1, 0),), ((2, 0), (0, 1)))
    for a in range(2):
        for b in range(2):
            value = None
            for r, down in options[a]:
                for c, side in options[b]:
                    slot, tap = (2 * down + side) * c4, (3 * r + c) * c4
                    term = mm_nt(d5[:, slot : slot + c4], w5[tap : tap + c4, :])
                    value = term if value is None else value + term
            pv[...] = value
            for m in sets:

                def crop_(c, m=m, a=a, b=b):
                    for i in range(m.half):
                        for q in range(c4 // 128):
                            dh[q, pl.ds(m.row0 + c * m.rows + (2 * i + a) * 16 + b, 8, stride=2), :] = pv[
                                span(m.out0 + c * m.out + i * 8, 8, 8), q * 128 : (q + 1) * 128
                            ]

                repeat(m.count, crop_)
        tick()
    loads[9].wait()
    for m in sets:

        def crop_(c, m=m):
            crop = m.crop0 + c
            rows = span(m.row0 + c * m.rows, m.rows)
            mask = keep(128, 16, m.edge)
            levels, tilts = [], []
            for q in range(c4 // 128):
                cols = slice(q * 128, (q + 1) * 128)
                inv = by_view(wv, crop, st4[2:4, cols])
                n = (z4[rows, cols] - by_view(wv, crop, st4[0:2, cols])) * inv
                up_ = masked(act_slope(n * norms2[0:1, cols] + norms2[1:2, cols]) * dh[q, rows, :], mask)
                dh[q, rows, :] = up_
                levels.append(jnp.sum(tile_sum(up_), axis=0, keepdims=True))
                tilts.append(jnp.sum(tile_sum(up_ * n), axis=0, keepdims=True))
            cs[pl.ds(crop, 1), 0:c4] = jnp.concatenate(levels, axis=1)
            cm[pl.ds(crop, 1), 0:c4] = jnp.concatenate(tilts, axis=1)

        repeat(m.count, crop_)
        tick()
    local_sums(blocks[1], (cs, cm), wcol, c4)
    links.send_near(1, blocks[1])
    loads[8].wait()

    def kernel(t):
        part = pl.ds(pl.multiple_of(t * c4, c4), c4)
        g5[part, :] = mm_tn(x5[:, part], d5[:, 0:c4]).astype(BF16)

    repeat(5, kernel)
    tick()

    def rest():
        repeat(4, lambda t: kernel(t + 5))
        puts.put(g5, o_g5)
        tick()

    meet_sums(links, 1, c4, ((s4, 0), (s4, 2)), rest)

    for i in range(10, 14):
        loads[i].wait()
    big_rows = 2 * sets[0].rows
    for at, m in enumerate(sets):

        def pair(p, m=m, at=at):
            r = m.row0 + p * 2 * m.rows
            o = m.out0 + p * 2 * m.out
            mask = keep(128, 16, m.edge)
            for j in range(2):
                crop = m.crop0 + 2 * p + j
                rows = span(r + j * m.rows, m.rows)
                over = share_of(wv, tally, crop, 1.0)
                for q in range(c4 // 128):
                    cols = slice(q * 128, (q + 1) * 128)
                    inv = by_view(wv, crop, st4[2:4, cols])
                    n = (z4[rows, cols] - by_view(wv, crop, st4[0:2, cols])) * inv
                    d = (inv * norms2[0:1, cols]) * (
                        dh[q, rows, :] - by_view(wv, crop, s4[0:2, cols]) * over - n * (by_view(wv, crop, s4[2:4, cols]) * over)
                    )
                    d4[rows, cols] = masked(d, mask).astype(BF16)
            got = mm_nt(d4[span(r, 2 * m.rows), :], w4[...])
            for q in range(cin // 128):
                bg[q, 0 : 2 * m.rows, :] = got[:, q * 128 : (q + 1) * 128]
            for q in range(cin // 128):
                for j in range(2):
                    for i in range(m.half):
                        here = pl.ds(j * m.rows + i * 32, 8, stride=2)
                        bg[q, here, :] = bg[q, here, :] + t7[span(o + j * m.out + i * 8, 8, 8), q * 128 : (q + 1) * 128]
            turn = m.crop0 // 2 + p
            slot = turn % 2

            def left(turn, slot):
                return pltpu.make_async_copy(
                    up.at[slot, 0 : 2 * m.rows], o_up.at[span(r, 2 * m.rows)], up_sem.at[turn]
                )

            if turn >= 2:
                size = big_rows if turn - 2 < sets[0].count // 2 else 2 * m.rows
                pltpu.make_async_copy(up.at[slot, 0:size], o_up.at[pl.ds(0, size)], up_sem.at[turn - 2]).wait()
            step = m.rows // 2
            mask = keep(128, 16, m.edge)
            totals = [[[], []], [[], []]]
            for h, j in [(h, j) for h in range(cin // 512) for j in range(2)]:
                if j == 0:
                    zt[0 : 2 * m.rows, :] = mm(h2[span(r, 2 * m.rows), :], w3[:, h * 512 : (h + 1) * 512])
                crop = m.crop0 + 2 * p + j
                levels, tilts = totals[j]
                for q in range(h * 4, h * 4 + 4):
                    cols = slice(q * 128, (q + 1) * 128)
                    part = slice((q - h * 4) * 128, (q - h * 4 + 1) * 128)
                    at3 = slice(2 * c3 + q * 128, 2 * c3 + (q + 1) * 128)
                    mean, inv = by_view(wv, crop, st3[0:2, cols]), by_view(wv, crop, st3[2:4, cols])
                    gain, bias = norms1[0:1, at3], norms1[1:2, at3]

                    def tile(i, sums, j=j, cols=cols, part=part, q=q, mean=mean, inv=inv, gain=gain, bias=bias):
                        here = span(j * m.rows + i * step, step)
                        rows = span(r + j * m.rows + i * step, step)
                        n = (zt[here, part] - mean) * inv
                        u = n * gain + bias + img[rows, cols].astype(f)
                        got = bg[q, here, :].astype(BF16).astype(f)
                        v = masked(act_slope(u) * got, mask)
                        up[slot, here, cols] = v
                        return (sums[0] + tile_sum(v), sums[1] + tile_sum(v * n))

                    zero = jnp.zeros((8, 128), f)
                    s, t = lax.fori_loop(0, 2, tile, (zero, zero))
                    levels.append(jnp.sum(s, axis=0, keepdims=True))
                    tilts.append(jnp.sum(t, axis=0, keepdims=True))
            for j in range(2):
                crop = m.crop0 + 2 * p + j
                cs[pl.ds(crop, 1), :] = jnp.concatenate(totals[j][0], axis=1)
                cm[pl.ds(crop, 1), :] = jnp.concatenate(totals[j][1], axis=1)
            left(turn, slot).start()

        for p in range(m.count // 2):
            pair(p)
            tick()
    local_sums(blocks[2], (cs, cm), wcol, cin)
    links.send_near(2, blocks[2])
    loads[14].wait()

    def inner(n):
        part = pl.ds(pl.multiple_of(n * 256, 256), 256)
        g4[part, :] = mm_tn(blk[:, part], d4[...]).astype(BF16)

    repeat(2, inner)
    tick()

    def rest():
        repeat(cin // 256 - 2, lambda n: inner(n + 2))
        puts.put(g4, o_g4)
        tick()

    meet_sums(links, 2, cin, ((s3, 0), (s3, 2)), rest)
    for src, dst in ((s5, o_s5), (s4, o_s4), (s3, o_s3)):
        puts.put(src, dst)
    for back in (2, 1):
        size = 2 * sets[1].rows
        turn = (sets[0].count + sets[1].count) // 2 - back
        pltpu.make_async_copy(
            up.at[turn % 2, 0:size], o_up.at[pl.ds(sets[1].row0, size)], up_sem.at[turn]
        ).wait()
    while share.at < len(order):
        tick()
    for copy in share.stores.values():
        copy.wait()
    share.finish()
    links.finish()
    puts.finish()


def back_one_kernel(sets, total, guarded, crops, dims, shapes, chunks, *refs):
    c3, cin = dims
    vb, vs, norms1, st1, st2, st3, s3, tally = refs[:8]
    sources, refs = refs[8:17], refs[17:]
    second, refs = list(refs[:4]), refs[4:]
    (o_gb, o_gs, o_s2, o_s1), refs = refs[:4], refs[4:]
    o_grads, refs = refs[:7], refs[7:]
    held, refs = refs[:9], refs[9:]
    (h2, w3, up, z2, h1, wsp1, z1, w1, img) = held
    (zt, d3, q2, d2, q1, d1, g3, g2, g1, s2, s1, cs, cm, wv, wcol), refs = refs[:15], refs[15:]
    blocks, refs = take(refs, 2)
    near, refs = take(refs, 2)
    far, refs = take(refs, 2)
    links = Links(crops, near, far, *refs[:4])
    load_sem, out_sem, own_sem, grad_send, grad_recv, up_sem = refs[4:10]
    refs = refs[10:]
    n = len(chunks)
    bits = crops.bit_length() - 1
    early = SHARE_FIRST
    acc, refs = take(refs, n - early)
    recv0, refs = take(refs, n - early)
    recvs, refs = take(refs, n - early)
    gap = [None] * early
    share = Share(
        shapes, chunks, [share_orders(bits, v) for v in SHARE_PATHS], bits, links, second + [g3, g2, g1], o_grads,
        gap + acc, gap + recv0, gap + recvs, refs, range(early),
    )
    order = share_late_order(n, bits, 20, (0,) * 7 + (7, 14, 20))

    def tick():
        share.run(order)

    core = links.r
    sibling = (links.k, 1 - core)
    f = F32
    loads = start_loads([(a, b) for a, b in zip(sources, held) if b is not up], load_sem)
    ups = []
    for m in sets:
        for p in range(m.count // 2):
            rows = pl.ds(m.row0 + p * 2 * m.rows, 2 * m.rows)
            ups.append(pltpu.make_async_copy(sources[2].at[rows], up.at[rows], up_sem.at[len(ups)]))
    for copy in ups:
        copy.start()
    links.greet()
    tick()
    view_tables(sets, links.r, (vb, vs), wv, wcol)
    puts = Puts(out_sem)
    for ref in (cs, cm):
        ref[...] = jnp.zeros(ref.shape, f)
    for block in blocks:
        block[...] = jnp.zeros(block.shape, f)
    d2[0:16, :] = jnp.zeros((16, 3 * c3), BF16)
    for m in sets:
        for c in range(m.count):
            at = m.guard0 + c * m.guard + m.rows
            d2[at : at + 16, :] = jnp.zeros((16, 3 * c3), BF16)

    for i in range(3):
        loads[i].wait()
    for copy in ups:
        copy.wait()
    for m in sets:

        def pair(p, m=m):
            r = m.row0 + p * 2 * m.rows
            step = m.rows // 2
            mask = keep(128, 16, m.edge)
            for h, j in [(h, j) for h in range(cin // 512) for j in range(2)]:
                if j == 0:
                    zt[0 : 2 * m.rows, :] = mm(h2[span(r, 2 * m.rows), :], w3[:, h * 512 : (h + 1) * 512])
                crop = m.crop0 + 2 * p + j
                over = share_of(wv, tally, crop, 1.0)
                for q in range(h * 4, h * 4 + 4):
                    cols = slice(q * 128, (q + 1) * 128)
                    part = slice((q - h * 4) * 128, (q - h * 4 + 1) * 128)
                    mean, inv = by_view(wv, crop, st3[0:2, cols]), by_view(wv, crop, st3[2:4, cols])
                    gain = inv * norms1[0:1, 2 * c3 + q * 128 : 2 * c3 + (q + 1) * 128]
                    level = by_view(wv, crop, s3[0:2, cols]) * over
                    tilt = by_view(wv, crop, s3[2:4, cols]) * over * inv

                    def tile(i, j=j, cols=cols, part=part, mean=mean, gain=gain, level=level, tilt=tilt):
                        here = span(j * m.rows + i * step, step)
                        rows = span(r + j * m.rows + i * step, step)
                        d = gain * (up[rows, cols] - level - (zt[here, part] - mean) * tilt)
                        d3[rows, cols] = masked(d, mask).astype(BF16)

                    repeat(2, tile)
            q2[span(r, 2 * m.rows), :] = mm_nt(d3[span(r, 2 * m.rows), :], w3[...])
            for j in range(2):
                crop = m.crop0 + 2 * p + j
                mean, inv = by_view(wv, crop, st2[0:2, :]), by_view(wv, crop, st2[2:4, :])

                def tile(i, sums, j=j, mean=mean, inv=inv):
                    rows = span(r + j * m.rows + i * step, step)
                    n = (z2[rows, :] - mean) * inv
                    v = act_slope(n * norms1[0:1, c3 : 2 * c3] + norms1[1:2, c3 : 2 * c3]) * q2[rows, :]
                    q2[rows, :] = v
                    return (sums[0] + tile_sum(v), sums[1] + tile_sum(v * n))

                zero = jnp.zeros((8, c3), f)
                s, t = lax.fori_loop(0, 2, tile, (zero, zero))
                cs[pl.ds(crop, 1), 0:c3] = jnp.sum(s, axis=0, keepdims=True)
                cm[pl.ds(crop, 1), 0:c3] = jnp.sum(t, axis=0, keepdims=True)

        for p in range(m.count // 2):
            pair(p)
            tick()
    local_sums(blocks[0], (cs, cm), wcol, c3)
    links.send_near(0, blocks[0])

    def outer(n):
        cols = pl.ds(pl.multiple_of(n * 256, 256), 256)
        g3[:, cols] = mm_tn(h2[...], d3[:, cols]).astype(BF16)

    repeat(cin // 512, outer)
    tick()

    def rest():
        repeat(cin // 512, lambda n: outer(n + cin // 512))
        tick()

    meet_sums(links, 0, c3, ((s2, 0), (s2, 2)), rest)

    for i in range(3, 6):
        loads[i].wait()
    for m in sets:

        def pair(p, m=m):
            r = m.row0 + p * 2 * m.rows
            g = m.guard0 + p * 2 * m.guard
            step = m.rows // 2
            mask = keep(c3, 16, m.edge)
            for j in range(2):
                crop = m.crop0 + 2 * p + j
                over = share_of(wv, tally, crop, 1.0)
                mean, inv = by_view(wv, crop, st2[0:2, :]), by_view(wv, crop, st2[2:4, :])
                gain = inv * norms1[0:1, c3 : 2 * c3]
                level = by_view(wv, crop, s2[0:2, :]) * over
                tilt = by_view(wv, crop, s2[2:4, :]) * over * inv

                def tile(i, j=j, mean=mean, gain=gain, level=level, tilt=tilt):
                    rows = span(r + j * m.rows + i * step, step)
                    d = gain * (q2[rows, :] - level - (z2[rows, :] - mean) * tilt)
                    d = masked(d, mask)
                    to = span(g + j * m.guard + i * step, step)
                    d2[to, 0:c3] = pltpu.roll(d, step - 1, 0).astype(BF16)
                    d2[to, c3 : 2 * c3] = d.astype(BF16)
                    d2[to, 2 * c3 : 3 * c3] = pltpu.roll(d, 1, 0).astype(BF16)

                repeat(2, tile)
            size = 2 * m.rows + 16
            value = None
            for a in range(3):
                for b in range(3):
                    part = d2[span(g - (a - 1) * 16, size), b * c3 : (b + 1) * c3]
                    term = mm_nt(part, wsp1[a, b * c3 : (b + 1) * c3, :])
                    value = term if value is None else value + term
            q1[span(r, m.rows), :] = value[0 : m.rows]
            q1[span(r + m.rows, m.rows), :] = value[m.guard : m.guard + m.rows]
            for j in range(2):
                crop = m.crop0 + 2 * p + j
                mean, inv = by_view(wv, crop, st1[0:2, :]), by_view(wv, crop, st1[2:4, :])

                def tile(i, sums, j=j, mean=mean, inv=inv):
                    rows = span(r + j * m.rows + i * step, step)
                    n = (z1[rows, :] - mean) * inv
                    v = act_slope(n * norms1[0:1, 0:c3] + norms1[1:2, 0:c3]) * q1[rows, :]
                    v = masked(v, mask)
                    q1[rows, :] = v
                    return (sums[0] + tile_sum(v), sums[1] + tile_sum(v * n))

                zero = jnp.zeros((8, c3), f)
                s, t = lax.fori_loop(0, 2, tile, (zero, zero))
                cs[pl.ds(crop, 1), 0:c3] = jnp.sum(s, axis=0, keepdims=True)
                cm[pl.ds(crop, 1), 0:c3] = jnp.sum(t, axis=0, keepdims=True)

        for p in range(m.count // 2):
            pair(p)
            tick()
    local_sums(blocks[1], (cs, cm), wcol, c3)
    links.send_near(1, blocks[1])
    inside = guarded - 32

    def taps(a):
        g2[a * 3 * c3 : (a + 1) * 3 * c3, :] = mm_tn(
            h1[a * 16 : a * 16 + inside, :], d2[16 : 16 + inside, c3 : 2 * c3]
        ).astype(BF16)

    taps(0)
    tick()

    def rest():
        taps(1)
        taps(2)
        tick()

    meet_sums(links, 1, c3, ((s1, 0), (s1, 2)), rest)

    loads[6].wait()
    moves = []
    for m, out in zip(sets, (o_gb, o_gs)):
        part = m.rows // 2
        for c in range(m.count):
            i = m.crop0 + c
            own_rows = span(m.row0 + c * m.rows + core * part, part)
            other_rows = span(m.row0 + c * m.rows + (1 - core) * part, part)
            place = out.at[span((core * m.count + c) * part, part)]
            moves.append(
                (
                    pltpu.make_async_copy(d3.at[own_rows], place, own_sem.at[i]),
                    pltpu.make_async_remote_copy(
                        src_ref=d3.at[other_rows],
                        dst_ref=place,
                        send_sem=grad_send.at[i],
                        recv_sem=grad_recv.at[i],
                        device_id=sibling,
                        device_id_type=MESH,
                    ),
                )
            )
    for m in sets:

        def pair(p, m=m):
            r = m.row0 + p * 2 * m.rows
            step = m.rows // 2
            mask = keep(c3, 16, m.edge)
            for j in range(2):
                crop = m.crop0 + 2 * p + j
                over = share_of(wv, tally, crop, 1.0)
                mean, inv = by_view(wv, crop, st1[0:2, :]), by_view(wv, crop, st1[2:4, :])
                gain = inv * norms1[0:1, 0:c3]
                level = by_view(wv, crop, s1[0:2, :]) * over
                tilt = by_view(wv, crop, s1[2:4, :]) * over * inv

                def tile(i, j=j, mean=mean, gain=gain, level=level, tilt=tilt):
                    rows = span(r + j * m.rows + i * step, step)
                    d = gain * (q1[rows, :] - level - (z1[rows, :] - mean) * tilt)
                    d1[rows, :] = masked(d, mask).astype(BF16)

                repeat(2, tile)
            rows = span(r, 2 * m.rows)
            for n in range(cin // 256):
                cols = slice(n * 256, (n + 1) * 256)
                d3[rows, cols] = (up[rows, cols] + mm_nt(d1[rows, :], w1[cols, :])).astype(BF16)

        for p in range(m.count // 2):
            pair(p)
            for c in (2 * p, 2 * p + 1):
                for copy in moves[m.crop0 + c]:
                    copy.start()
            tick()
    loads[7].wait()

    def inner(n):
        part = pl.ds(pl.multiple_of(n * 256, 256), 256)
        g1[part, :] = mm_tn(img[:, part], d1[...]).astype(BF16)

    repeat(cin // 256, inner)
    for src, dst in ((s2, o_s2), (s1, o_s1)):
        puts.put(src, dst)
    while share.at < len(order):
        tick()
    share.finish()
    links.finish()
    for near_copy, far_copy in moves:
        near_copy.wait()
        far_copy.wait()
    puts.finish()


def backward(sets, got, views, w, norms_first, norms_second, total, guarded, outs, idents):
    crops = lax.axis_size("crops")
    w1, wsp1, w3, w4, w5, w6, w7 = w
    cin, c3 = w1.shape
    c4, cout = w6.shape
    (
        f_img, f_z1, f_h1, f_z2, f_h2, f_blk, f_z4, f_x5, f_z5, f_h5, f_xe, f_res, f_d6, f_d7,
        f_st1, f_st2, f_st3, f_st4, f_st7, f_st5, f_st6, f_sq, f_n,
    ) = got
    smem, vmem = pl.BlockSpec(memory_space=pltpu.SMEM), pl.BlockSpec(memory_space=pltpu.VMEM)
    hbm = pl.BlockSpec(memory_space=pl.ANY)
    shape = jax.ShapeDtypeStruct
    most = 2 * sets[0].rows
    pairs = sum(m.count for m in sets) // 2
    count = 2 * pairs

    def like(arrays):
        return [pltpu.VMEM(t.shape, t.dtype) for t in arrays]

    def params(ident):
        return pltpu.CompilerParams(
            collective_id=ident, has_side_effects=True, vmem_limit_bytes=63 * 1024 * 1024
        )

    arrays = [f_d6, w6, f_z5, f_h5, f_d7, f_xe, w7, w5, f_x5, f_z4, w4, f_h2, w3, f_img, f_blk]
    out_shape = [
        shape((total, cin), F32), shape((c4, cout), BF16), shape((cin, cout), BF16), shape((9 * c4, c4), BF16),
        shape((cin, c4), BF16), shape((8, c4), F32), shape((8, c4), F32), shape((8, cin), F32),
    ]
    scratch = like(arrays) + [
        pltpu.VMEM((outs, c4), F32), pltpu.VMEM((outs, cin), F32), pltpu.VMEM((outs, c4), F32), pltpu.VMEM((c4 // 128, total, 128), F32), pltpu.VMEM((total, c4), BF16),
        pltpu.VMEM((most, 512), F32), pltpu.VMEM((cin // 128, most, 128), F32), pltpu.VMEM((2, most, cin), F32),
        pltpu.VMEM((8, c4), F32), pltpu.VMEM((8, c4), F32), pltpu.VMEM((8, cin), F32),
        pltpu.VMEM((16, cin), F32), pltpu.VMEM((16, cin), F32),
        pltpu.SMEM((2, 16), F32), pltpu.VMEM((16, 128), F32),
    ]
    scratch += exchange_shapes((c4, c4, cin), (2, 2, 2), crops)
    scratch += [pltpu.SemaphoreType.DMA((15,)), pltpu.SemaphoreType.DMA((7,)), pltpu.SemaphoreType.DMA((pairs,))]
    shapes = [(cin, cout), (c4, cout), (9 * c4, c4), (cin, c4), (c3, cin), (9 * c3, c3), (cin, c3)]
    chunks = share_plan(shapes, SHARE_CUTS)
    bits = crops.bit_length() - 1
    scratch += share_scratch(chunks[:SHARE_FIRST], bits, inside=True)
    up, g_outer2, g_skip, g_spatial2, g_inner2, s5, s4, s3 = pl.pallas_call(
        functools.partial(back_two_kernel, sets, total, outs, crops, (c3, cin, c4, cout), shapes, chunks),
        out_shape=out_shape,
        in_specs=[smem] * 2 + [vmem] * 6 + [hbm] * 15,
        out_specs=[hbm] * len(out_shape),
        scratch_shapes=scratch,
        compiler_params=params(idents[0]),
        name="back_two",
    )(*views, norms_first, norms_second, f_st3, f_st4, f_st5, f_n, *arrays)

    arrays = [f_h2, w3, up, f_z2, f_h1, wsp1, f_z1, w1, f_img]
    out_shape = [
        shape((total_rows(sets[0]), cin), BF16), shape((total_rows(sets[1]), cin), BF16), shape((8, c3), F32),
        shape((8, c3), F32),
    ] + [shape(t, BF16) for t in shapes]
    scratch = like(arrays) + [
        pltpu.VMEM((most, 512), F32), pltpu.VMEM((total, cin), BF16), pltpu.VMEM((total, c3), F32),
        pltpu.VMEM((guarded, 3 * c3), BF16), pltpu.VMEM((total, c3), F32), pltpu.VMEM((total, c3), BF16),
        pltpu.VMEM((c3, cin), BF16), pltpu.VMEM((9 * c3, c3), BF16), pltpu.VMEM((cin, c3), BF16),
        pltpu.VMEM((8, c3), F32), pltpu.VMEM((8, c3), F32), pltpu.VMEM((16, c3), F32), pltpu.VMEM((16, c3), F32),
        pltpu.SMEM((2, 16), F32), pltpu.VMEM((16, 128), F32),
    ]
    scratch += exchange_shapes((c3, c3), (2, 2), crops)
    scratch += [pltpu.SemaphoreType.DMA((9,)), pltpu.SemaphoreType.DMA((2,))]
    scratch += [pltpu.SemaphoreType.DMA((count,))] * 3 + [pltpu.SemaphoreType.DMA((pairs,))]
    scratch += share_scratch(chunks, bits, range(SHARE_FIRST))
    grad_b, grad_s, s2, s1, *grads = pl.pallas_call(
        functools.partial(back_one_kernel, sets, total, guarded, crops, (c3, cin), shapes, chunks),
        out_shape=out_shape,
        in_specs=[smem] * 2 + [vmem] * 6 + [hbm] * 13,
        out_specs=[hbm] * len(out_shape),
        scratch_shapes=scratch,
        compiler_params=params(idents[1]),
        name="back_one",
    )(*views, norms_first, f_st1, f_st2, f_st3, s3, f_n, *arrays, g_skip, g_outer2, g_spatial2, g_inner2)
    return grad_b, grad_s, grads, (s1, s2, s3, s4, s5)


def widen_kernel(*refs):
    for src, dst in zip(refs[: len(refs) // 2], refs[len(refs) // 2 :]):
        dst[...] = src[...].astype(F32)


def widen(arrays, steps=8):
    def block(t):
        return pl.BlockSpec((t.shape[0] // steps, t.shape[1]), lambda i: (i, 0))

    return pl.pallas_call(
        widen_kernel,
        grid=(steps,),
        out_shape=[jax.ShapeDtypeStruct(t.shape, F32) for t in arrays],
        in_specs=[block(t) for t in arrays],
        out_specs=[block(t) for t in arrays],
        compiler_params=pltpu.CompilerParams(vmem_limit_bytes=48 * 1024 * 1024),
        name="widen",
    )(*arrays)


def total_rows(m):
    return m.count * m.rows


def shards(
    image_big,
    image_small,
    view_big,
    view_small,
    inner_first,
    spatial_first,
    outer_first,
    norms_first,
    inner_second,
    spatial_second,
    outer_second,
    skip_second,
    norms_second,
    cotangent_big,
    cotangent_small,
):
    c3, c4 = inner_first.shape[1], inner_second.shape[1]
    weights = [
        inner_first,
        spatial_first.reshape(3, 3 * c3, c3),
        outer_first,
        inner_second,
        spatial_second.reshape(9 * c4, c4),
        outer_second,
        skip_second,
    ]
    sets, sizes, got = forward(
        [image_big, image_small], [cotangent_big, cotangent_small], (view_big, view_small), weights, norms_first, norms_second, 0
    )
    grad_b, grad_s, grads, sums = backward(
        sets, got, (view_big, view_small), weights, norms_first, norms_second, *sizes, (1, 2)
    )
    s1, s2, s3, s4, s5 = sums
    sq = got[21]

    def both(parts):
        return jnp.concatenate(
            [jnp.stack([t[g] + t[g + 1], t[0] + t[1]]) for t, g in parts], axis=1
        )

    g_skip, g_outer2, g_spatial2, g_inner2, g_outer1, g_spatial1, g_inner1 = widen(grads)
    results = [
        got[11][m.out0 : m.out0 + m.count * m.out].reshape(m.count, m.half, 8, -1)[:, :, : m.half]
        for m in sets
    ]
    gradients = [
        t.reshape(image.shape[0], image.shape[1], 16, -1)[:, :, : image.shape[2]]
        for t, image in ((grad_b, image_big), (grad_s, image_small))
    ]
    return (
        results[0],
        results[1],
        gradients[0],
        gradients[1],
        g_inner1,
        g_spatial1.reshape(spatial_first.shape),
        g_outer1,
        both(((s1, 2), (s2, 2), (s3, 2))),
        g_inner2,
        g_spatial2.reshape(spatial_second.shape),
        g_outer2,
        g_skip,
        both(((s4, 2), (s5, 2), (sq, 2), (sq, 4))),
    )


def solution(mesh):
    maps = P("crops", "rows", None, None)
    whole = P(("crops", "rows"), None, None, None)
    in_specs = (maps, maps, P("crops"), P("crops")) + (P(),) * 9 + (whole, whole)
    out_specs = (whole, whole, maps, maps) + (P(),) * 9
    return jax.shard_map(shards, mesh=mesh, in_specs=in_specs, out_specs=out_specs, check_vma=False)
```

```python
import functools

import jax
import jax.numpy as jnp
from jax import lax
from jax.experimental import pallas as pl
from jax.experimental.pallas import tpu as pltpu
from jax.sharding import PartitionSpec as P

HIGH = lax.Precision.HIGHEST
EPS = 1e-05
MESH = pl.DeviceIdType.MESH
F32 = jnp.float32
BF16 = jnp.bfloat16


class Maps:
    def __init__(self, count, edge, row0, crop0, guard0, out0):
        self.count, self.edge = count, edge
        self.row0, self.crop0, self.guard0, self.out0 = row0, crop0, guard0, out0
        self.rows = edge * 16
        self.guard = (edge + 1) * 16
        self.half = edge // 2
        self.out = self.half * 8
        self.pixels = edge * edge


def geometry(nb, eb, ns, es):
    big = Maps(nb, eb, 0, 0, 16, 0)
    small = Maps(ns, es, nb * big.rows, nb, 16 + nb * big.guard, nb * big.out)
    total = small.row0 + ns * small.rows
    guarded = small.guard0 + ns * small.guard
    out = small.out0 + ns * small.out
    return (big, small), total, guarded, out


def al(x, m=16):
    return x if isinstance(x, int) else pl.multiple_of(x, m)


def span(start, size, m=16):
    return pl.ds(al(start, m), size)


def repeat(count, body):
    def step(i, carry):
        body(i)
        return carry

    lax.fori_loop(0, count, step, 0)


def mm(a, b):
    return jnp.dot(a, b, preferred_element_type=F32)


def mm_nt(a, b):
    return lax.dot_general(a, b, (((1,), (1,)), ((), ())), preferred_element_type=F32)


def mm_tn(a, b):
    return lax.dot_general(a, b, (((0,), (0,)), ((), ())), preferred_element_type=F32)


CA = 0.7978845608028654
CB = 0.7978845608028654 * 0.044715


def act(u):
    t = jnp.tanh(u * (CA + CB * (u * u)))
    return 0.5 * u * (1.0 + t)


def act_slope(u):
    s = u * u
    t = jnp.tanh(u * (CA + CB * s))
    rise = (0.5 * u) * (CA + (3.0 * CB) * s)
    return 0.5 * (1.0 + t) + (1.0 - t * t) * rise


def act_both(u):
    s = u * u
    t = jnp.tanh(u * (CA + CB * s))
    hu = 0.5 * u
    lift = 0.5 * (1.0 + t)
    slope = lift + (1.0 - t * t) * (hu * (CA + (3.0 * CB) * s))
    return u * lift, slope


def keep(width, pitch, edge):
    return lax.broadcasted_iota(jnp.int32, (pitch, width), 0) < edge


def masked(x, mask):
    rows = x.reshape(x.shape[0] // mask.shape[0], mask.shape[0], x.shape[1])
    return jnp.where(mask[None], rows, 0.0).reshape(x.shape)


def tile_sum(x):
    return jnp.sum(x.reshape(x.shape[0] // 8, 8, x.shape[1]), axis=0)


def pieces(width):
    return (4, width // 4) if width >= 512 else (width // 128, 128)


class Links:
    def __init__(self, crops, near, far, near_s, near_r, far_s, far_r):
        self.group = 4 if crops % 4 == 0 else 1
        self.outers = crops // self.group
        self.k, self.r = lax.axis_index("crops"), lax.axis_index("rows")
        inner, self.outer = lax.rem(self.k, self.group), self.k // self.group
        self.wide = 2 * self.group
        self.me = inner * 2 + self.r
        self.peers, self.others = [], []
        for d in range(1, self.wide):
            p = lax.rem(self.me + d, self.wide)
            self.peers.append((self.outer * self.group + p // 2, lax.rem(p, 2)))
        for d in range(1, self.outers):
            self.others.append((lax.rem(self.outer + d, self.outers) * self.group + inner, self.r))
        self.near, self.far = near, far
        self.sems = (near_s, near_r, far_s, far_r)
        self.live = {}

    def greet(self, extra=()):
        barrier = pltpu.get_barrier_semaphore()
        peers = self.peers + self.others + list(extra)
        for peer in peers:
            pl.semaphore_signal(barrier, inc=1, device_id=peer, device_id_type=MESH)
        pl.semaphore_wait(barrier, len(peers))

    def send_near(self, e, block):
        self.near[e][self.me] = block[...]
        self.live[e, 0] = []
        for d, peer in enumerate(self.peers):
            copy = pltpu.make_async_remote_copy(
                src_ref=block,
                dst_ref=self.near[e].at[self.me],
                send_sem=self.sems[0].at[e, d],
                recv_sem=self.sems[1].at[e, d],
                device_id=peer,
                device_id_type=MESH,
            )
            copy.start()
            self.live[e, 0].append(copy)

    def wait_near(self, e):
        for copy in self.live[e, 0]:
            copy.wait_recv()

    def send_far(self, e):
        self.live[e, 1] = []
        place = self.far[e].at[self.outer]
        for d, peer in enumerate(self.others):
            copy = pltpu.make_async_remote_copy(
                src_ref=place,
                dst_ref=place,
                send_sem=self.sems[2].at[e, d],
                recv_sem=self.sems[3].at[e, d],
                device_id=peer,
                device_id_type=MESH,
            )
            copy.start()
            self.live[e, 1].append(copy)

    def wait_far(self, e):
        for copy in self.live[e, 1]:
            copy.wait_recv()

    def finish(self):
        for copies in self.live.values():
            for copy in copies:
                copy.wait_send()


def fold_moments(buf, tallies, count, scale):
    sums, total = buf[0, 0:8, :], tallies[0]
    for i in range(1, count):
        sums = sums + buf[i, 0:8, :]
        total = total + tallies[i]
    mean = sums * (1.0 / jnp.maximum(total * scale, 1.0))
    spread = None
    for i in range(count):
        n = tallies[i] * scale
        apart = buf[i, 0:8, :] * (1.0 / jnp.maximum(n, 1.0)) - mean
        term = buf[i, 8:16, :] + n * apart * apart
        spread = term if spread is None else spread + term
    return sums, spread, total


def fold_sums(buf, count):
    total = buf[0]
    for i in range(1, count):
        total = total + buf[i]
    return total


def exchange_shapes(widths, tiles, crops):
    group = 4 if crops % 4 == 0 else 1
    outers = crops // group
    blocks, near, far = [], [], []
    for width, tile in zip(widths, tiles):
        lanes = pieces(width)[1]
        blocks.append(pltpu.VMEM((8 * tile, lanes), F32))
        near.append(pltpu.VMEM((2 * group, 8 * tile, lanes), F32))
        far.append(pltpu.VMEM((outers, 8 * tile, lanes), F32))
    e = len(widths)
    sems = [
        pltpu.SemaphoreType.DMA((e, 2 * group - 1)),
        pltpu.SemaphoreType.DMA((e, 2 * group - 1)),
        pltpu.SemaphoreType.DMA((e, max(outers - 1, 1))),
        pltpu.SemaphoreType.DMA((e, max(outers - 1, 1))),
    ]
    return blocks + near + far + sems


def take(refs, count):
    return list(refs[:count]), refs[count:]


def pack(block, tile, rows, width):
    count, lanes = pieces(width)
    for q in range(count):
        for v in range(2):
            block[tile * 8 + 2 * q + v : tile * 8 + 2 * q + v + 1, :] = rows[v][:, q * lanes : (q + 1) * lanes]


def unpack(table, row, tile, width):
    count, lanes = pieces(width)
    for q in range(count):
        table[row : row + 2, q * lanes : (q + 1) * lanes] = tile[2 * q : 2 * q + 2, :]


def crop_stats(ref, row0, rows, step, width, edge, pitch, pixels, crop, cs, cm, col0=0):
    mask = keep(width, pitch, edge)
    zero = jnp.zeros((8, width), F32)
    cols = pl.ds(col0, width) if isinstance(col0, int) else pl.ds(pl.multiple_of(col0, 128), width)
    near = min(8, edge)
    first = masked(ref[span(row0, 8, 8), cols], keep(width, 8, edge))
    pivot = jnp.sum(first, axis=0, keepdims=True) * (1.0 / near)

    def tile(i, acc):
        d = masked(ref[span(row0 + i * step, step, 8), cols] - pivot, mask)
        return acc[0] + tile_sum(d), acc[1] + tile_sum(d * d)

    if rows == step:
        s, m = tile(0, (zero, zero))
    else:
        s, m = lax.fori_loop(0, rows // step, tile, (zero, zero))
    s = jnp.sum(s, axis=0, keepdims=True)
    m = jnp.sum(m, axis=0, keepdims=True)
    cs[pl.ds(crop, 1), cols] = s + pivot * float(pixels)
    cm[pl.ds(crop, 1), cols] = jnp.maximum(m - s * s * (1.0 / pixels), 0.0)


def local_moments(block, cs, cm, wcol, width, scale, tally=False):
    s, m = cs[:, 0:width], cm[:, 0:width]
    pix = wcol[:, 2:3] * scale
    mean_c = s * (1.0 / pix)
    sums, squares, tallies = [], [], []
    for v in range(2):
        w = wcol[:, v : v + 1]
        total = jnp.sum(w * s, axis=0, keepdims=True)
        n = jnp.sum(w * pix, axis=0, keepdims=True)
        apart = mean_c - total * (1.0 / jnp.maximum(n, 1.0))
        squares.append(jnp.sum(w * (m + pix * apart * apart), axis=0, keepdims=True))
        sums.append(total)
        tallies.append(n)
    pack(block, 0, sums, width)
    pack(block, 1, squares, width)
    if tally:
        lanes = pieces(width)[1]
        for q in range(4):
            for v in range(2):
                block[16 + 2 * q + v : 17 + 2 * q + v, :] = jnp.broadcast_to(tallies[v], (1, lanes))


def local_sums(block, parts, wcol, width):
    for tile, part in enumerate(parts):
        s = part[:, 0:width]
        pack(block, tile, [jnp.sum(wcol[:, v : v + 1] * s, axis=0, keepdims=True) for v in range(2)], width)


def view_tables(sets, core, views, wv, wcol):
    row = lax.broadcasted_iota(jnp.int32, wcol.shape, 0)
    lane = lax.broadcasted_iota(jnp.int32, wcol.shape, 1)
    table = jnp.where(lane == 2, 1.0, 0.0)
    for m, view in zip(sets, views):
        for c in range(m.count):
            second = view[core * m.count + c].astype(F32)
            pair = (1.0 - second, second, float(m.pixels))
            for v in range(3):
                table = jnp.where((row == m.crop0 + c) & (lane == v), pair[v], table)
            wv[0, m.crop0 + c] = pair[0]
            wv[1, m.crop0 + c] = pair[1]
    wcol[...] = table


def by_view(wv, crop, pair):
    return wv[0, crop] * pair[0:1, :] + wv[1, crop] * pair[1:2, :]


FWD_WIDTHS = (256, 256, 1024, 512, 2048, 512, 2048, 2048)


def forward_kernel(sets, total, guarded, outs, crops, dims, *refs):
    c3, cin, c4, cout = dims
    (
        vb, vs, norms1, norms2,
        img_b, img_s, cot_hbm, w1_h, wsp1_h, w3_h, w4_h, w5_h, w6_h, w7_h,
    ), refs = refs[:14], refs[14:]
    (
        o_img, o_z1, o_h1, o_z2, o_h2, o_blk, o_z4, o_x5, o_z5, o_h5, o_xe, o_res, o_d6, o_d7,
        o_st1, o_st2, o_st3, o_st4, o_st7, o_st5, o_st6, o_sq, o_tally,
    ), refs = refs[:23], refs[23:]
    (
        img, z1, h1, z2, h2, zt, blk, eb, z4, xe, z7, hp, x5, z5, h5, z6, cot,
        w1, wsp1, w3, w4, w5, w6, w7, cs, cm, ck,
        st1, st2, st3, st4, st7, st5, st6, sq, tally_v, wv, wcol,
    ), refs = refs[:38], refs[38:]
    e = len(FWD_WIDTHS)
    blocks, refs = take(refs, e)
    near, refs = take(refs, e)
    far, refs = take(refs, e)
    ns_, nr_, fs_, fr_ = refs[:4]
    load_sem, img_sem, img_send, img_recv, out_sem = refs[4:]
    links = Links(crops, near, far, ns_, nr_, fs_, fr_)
    k, core = links.k, links.r
    sibling = (k, 1 - core)
    f = F32

    loads = []
    for i, (src, dst) in enumerate(
        ((w1_h, w1), (wsp1_h, wsp1), (w3_h, w3), (w4_h, w4), (w5_h, w5), (w6_h, w6), (w7_h, w7), (cot_hbm, cot))
    ):
        loads.append(pltpu.make_async_copy(src, dst, load_sem.at[i]))
    own, swaps = [], []
    for at, (m, src) in enumerate(zip(sets, (img_b, img_s))):
        part = m.rows // 2
        for c in range(m.count):
            i = m.crop0 + c
            place = img.at[span(m.row0 + c * m.rows + core * part, part)]
            own.append(
                pltpu.make_async_copy(
                    src.at[span((core * m.count + c) * part, part)], place, img_sem.at[i]
                )
            )
            swaps.append(
                pltpu.make_async_remote_copy(
                    src_ref=src.at[span(((1 - core) * m.count + c) * part, part)],
                    dst_ref=place,
                    send_sem=img_send.at[i],
                    recv_sem=img_recv.at[i],
                    device_id=sibling,
                    device_id_type=MESH,
                )
            )
    for copy in own:
        copy.start()
    loads[0].start()
    links.greet()
    for copy in swaps:
        copy.start()

    view_tables(sets, core, (vb, vs), wv, wcol)
    out_copies = []

    def put(src, dst):
        copy = pltpu.make_async_copy(src, dst, out_sem.at[len(out_copies)])
        copy.start()
        out_copies.append(copy)

    for ref in (cs, cm, ck):
        ref[...] = jnp.zeros(ref.shape, f)
    for block in blocks:
        block[...] = jnp.zeros(block.shape, f)
    h1[0:16, :] = jnp.zeros((16, 3 * c3), BF16)
    for m in sets:
        for c in range(m.count):
            at = m.guard0 + c * m.guard + m.rows
            h1[at : at + 16, :] = jnp.zeros((16, 3 * c3), BF16)

    def near_tallies():
        return [near[0][i, 16:24, 0:1] for i in range(links.wide)]

    def far_tallies():
        return [far[0][i, 16:24, 0:1] for i in range(links.outers)]

    def meet_near(i, scale):
        links.wait_near(i)
        sums, spread, n = fold_moments(near[i], near_tallies(), links.wide, scale)
        place = far[i].at[links.outer]
        place[0:8, :] = sums
        place[8:16, :] = spread
        if i == 0:
            place[16:24, :] = jnp.broadcast_to(n, (8, near[0].shape[2]))
        links.send_far(i)

    def meet_far(i, scale, table, width):
        links.wait_far(i)
        sums, spread, n = fold_moments(far[i], far_tallies(), links.outers, scale)
        over = 1.0 / (n * scale)
        mean = sums * over
        inverse = lax.rsqrt(spread * over + EPS)
        unpack(table, 0, mean, width)
        unpack(table, 2, inverse, width)
        if i == 0:
            tally_v[...] = jnp.broadcast_to(n, (8, 128))

    loads[0].wait()
    for m in sets:

        def pair(p, m=m):
            r = m.row0 + p * 2 * m.rows
            for j in range(2):
                own[m.crop0 + 2 * p + j].wait()
                swaps[m.crop0 + 2 * p + j].wait_recv()
            z1[span(r, 2 * m.rows), :] = mm(img[span(r, 2 * m.rows), :], w1[...])
            for j in range(2):
                crop_stats(z1, r + j * m.rows, m.rows, m.rows // 2, c3, m.edge, 16, m.pixels, m.crop0 + 2 * p + j, cs, cm)

        for p in range(m.count // 2):
            pair(p)
            if m is sets[0] and p == 0:
                for copy in loads[1:]:
                    copy.start()
    local_moments(blocks[0], cs, cm, wcol, c3, 1.0, True)
    links.send_near(0, blocks[0])
    put(img, o_img)
    put(z1, o_z1)
    loads[1].wait()
    meet_near(0, 1.0)
    meet_far(0, 1.0, st1, c3)

    for m in sets:

        def pair(p, m=m):
            r = m.row0 + p * 2 * m.rows
            g = m.guard0 + p * 2 * m.guard
            for j in range(2):
                crop = m.crop0 + 2 * p + j
                mean = by_view(wv, crop, st1[0:2, :])
                scale = by_view(wv, crop, st1[2:4, :]) * norms1[0:1, 0:c3]
                shift = norms1[1:2, 0:c3] - mean * scale
                step = m.rows // 2
                mask = keep(c3, 16, m.edge)

                def tile(i):
                    z = z1[span(r + j * m.rows + i * step, step), :]
                    h = masked(act(z * scale + shift), mask)
                    rows = span(g + j * m.guard + i * step, step)
                    h1[rows, 0:c3] = pltpu.roll(h, 1, 0).astype(BF16)
                    h1[rows, c3 : 2 * c3] = h.astype(BF16)
                    h1[rows, 2 * c3 : 3 * c3] = pltpu.roll(h, step - 1, 0).astype(BF16)

                repeat(2, tile)
            size = 2 * m.rows + 16
            z = mm(h1[span(g - 16, size), :], wsp1[0]) + mm(h1[span(g, size), :], wsp1[1])
            z = z + mm(h1[span(g + 16, size), :], wsp1[2])
            z2[span(r, m.rows), :] = z[0 : m.rows]
            z2[span(r + m.rows, m.rows), :] = z[m.guard : m.guard + m.rows]
            for j in range(2):
                crop_stats(z2, r + j * m.rows, m.rows, m.rows // 2, c3, m.edge, 16, m.pixels, m.crop0 + 2 * p + j, cs, cm)

        repeat(m.count // 2, pair)
    local_moments(blocks[1], cs, cm, wcol, c3, 1.0)
    links.send_near(1, blocks[1])
    put(h1, o_h1)
    put(z2, o_z2)
    loads[2].wait()
    meet_near(1, 1.0)
    meet_far(1, 1.0, st2, c3)

    for m in sets:

        def pair(p, m=m):
            r = m.row0 + p * 2 * m.rows
            for j in range(2):
                crop = m.crop0 + 2 * p + j
                mean = by_view(wv, crop, st2[0:2, :])
                scale = by_view(wv, crop, st2[2:4, :]) * norms1[0:1, c3 : 2 * c3]
                shift = norms1[1:2, c3 : 2 * c3] - mean * scale
                step = m.rows // 2

                def tile(i):
                    rows = span(r + j * m.rows + i * step, step)
                    h2[rows, :] = act(z2[rows, :] * scale + shift).astype(BF16)

                repeat(2, tile)
            zt[0 : 2 * m.rows, :] = mm(h2[span(r, 2 * m.rows), :], w3[...])
            for j in range(2):
                crop_stats(zt, j * m.rows, m.rows, 32, cin, m.edge, 16, m.pixels, m.crop0 + 2 * p + j, cs, cm)

        repeat(m.count // 2, pair)
    local_moments(blocks[2], cs, cm, wcol, cin, 1.0)
    links.send_near(2, blocks[2])
    put(h2, o_h2)
    loads[3].wait()
    meet_near(2, 1.0)
    meet_far(2, 1.0, st3, cin)

    for m in sets:

        def pair(p, m=m):
            r = m.row0 + p * 2 * m.rows
            zt[0 : 2 * m.rows, :] = mm(h2[span(r, 2 * m.rows), :], w3[...])
            for j in range(2):
                crop = m.crop0 + 2 * p + j
                mean = by_view(wv, crop, st3[0:2, :])
                scale = by_view(wv, crop, st3[2:4, :]) * norms1[0:1, 2 * c3 :]
                shift = norms1[1:2, 2 * c3 :] - mean * scale

                def tile(i):
                    here = span(j * m.rows + i * 32, 32)
                    rows = span(r + j * m.rows + i * 32, 32)
                    u = zt[here, :] * scale + shift + img[rows, :].astype(f)
                    b = act(u)
                    blk[rows, :] = b.astype(BF16)
                    for q in range(cin // 128):
                        eb[q, span(j * m.rows // 2 + i * 16, 16), :] = b[0:16, q * 128 : (q + 1) * 128]

                repeat(m.rows // 32, tile)
            for q in range(cin // 128):
                picked = [eb[q, pl.ds(i * 16, 8, stride=2), :] for i in range(2 * m.half)]
                xe[span(m.out0 + p * 2 * m.out, 2 * m.out), q * 128 : (q + 1) * 128] = jnp.concatenate(
                    picked, axis=0
                ).astype(BF16)
            z4[span(r, 2 * m.rows), :] = mm(blk[span(r, 2 * m.rows), :], w4[...])
            for j in range(2):
                crop_stats(z4, r + j * m.rows, m.rows, 32, c4, m.edge, 16, m.pixels, m.crop0 + 2 * p + j, cs, cm)

        repeat(m.count // 2, pair)
    local_moments(blocks[3], cs, cm, wcol, c4, 1.0)
    links.send_near(3, blocks[3])
    put(blk, o_blk)
    put(z4, o_z4)
    put(xe, o_xe)
    loads[6].wait()

    def wide_product(a, w, z):
        def columns(n):
            cols = pl.ds(pl.multiple_of(n * 512, 512), 512)
            z[:, cols] = mm(a[...], w[:, cols])

        repeat(cout // 512, columns)

    def wide_stats(z):
        for m in sets:

            def crop_(c, m=m):
                def columns(n):
                    crop_stats(
                        z, m.out0 + c * m.out, m.out, m.out, 512, m.half, 8, m.half * m.half,
                        m.crop0 + c, cs, cm, n * 512,
                    )

                repeat(cout // 512, columns)

            repeat(m.count, crop_)

    wide_product(xe, w7, z7)
    meet_near(3, 1.0)
    wide_stats(z7)
    local_moments(blocks[4], cs, cm, wcol, cout, 0.25)
    links.send_near(4, blocks[4])
    meet_far(3, 1.0, st4, c4)

    loads[4].wait()
    lots = c4 // 128
    hp[:, 0:24, :] = jnp.zeros((lots, 24, 128), f)
    for m in sets:

        def pair(p, m=m):
            r = m.row0 + p * 2 * m.rows
            for j in range(2):
                crop = m.crop0 + 2 * p + j
                mean = by_view(wv, crop, st4[0:2, :])
                scale = by_view(wv, crop, st4[2:4, :]) * norms2[0:1, 0:c4]
                shift = norms2[1:2, 0:c4] - mean * scale
                mask = keep(c4, 16, m.edge)
                base = 24 + j * m.guard
                hp[:, base + m.rows : base + m.guard, :] = jnp.zeros((lots, 16, 128), f)

                def tile(i):
                    z = z4[span(r + j * m.rows + i * 32, 32), :]
                    h = masked(act(z * scale + shift), mask)
                    for q in range(lots):
                        hp[q, span(base + i * 32, 32, 8), :] = h[:, q * 128 : (q + 1) * 128]

                repeat(m.rows // 32, tile)
            for a in range(3):
                for b in range(3):
                    for q in range(lots):
                        picked = []
                        for j in range(2):
                            for i in range(m.half):
                                at = 24 + j * m.guard + (2 * i + a - 1) * 16 + b - 1
                                picked.append(hp[q, pl.ds(at, 8, stride=2), :])
                        tap = (3 * a + b) * c4 + q * 128
                        x5[span(m.out0 + p * 2 * m.out, 2 * m.out), tap : tap + 128] = jnp.concatenate(
                            picked, axis=0
                        ).astype(BF16)

        repeat(m.count // 2, pair)
    z5[...] = jnp.zeros(z5.shape, f)

    def taps(t):
        part = pl.ds(pl.multiple_of(t * 3 * c4, 128), 3 * c4)
        z5[...] += mm(x5[:, part], w5[part, :])

    repeat(3, taps)
    for m in sets:

        def crop_(c, m=m):
            crop_stats(z5, m.out0 + c * m.out, m.out, m.out, c4, m.half, 8, m.half * m.half, m.crop0 + c, cs, cm)

        repeat(m.count, crop_)
    local_moments(blocks[5], cs, cm, wcol, c4, 0.25)
    links.send_near(5, blocks[5])
    put(x5, o_x5)
    put(z5, o_z5)
    meet_near(4, 0.25)
    meet_near(5, 0.25)
    meet_far(4, 0.25, st7, cout)
    meet_far(5, 0.25, st5, c4)

    loads[5].wait()
    for m in sets:

        def pair(p, m=m):
            o = m.out0 + p * 2 * m.out
            halves = []
            for j in range(2):
                crop = m.crop0 + 2 * p + j
                mean = by_view(wv, crop, st5[0:2, :])
                scale = by_view(wv, crop, st5[2:4, :]) * norms2[0:1, c4 : 2 * c4]
                z = z5[span(o + j * m.out, m.out, 8), :]
                halves.append(act(z * scale + (norms2[1:2, c4 : 2 * c4] - mean * scale)))
            h5[span(o, 2 * m.out), :] = jnp.concatenate(halves, axis=0).astype(BF16)

        repeat(m.count // 2, pair)
    wide_product(h5, w6, z6)
    wide_stats(z6)
    local_moments(blocks[6], cs, cm, wcol, cout, 0.25)
    links.send_near(6, blocks[6])
    put(h5, o_h5)
    loads[7].wait()

    def center(ms):
        for m in ms:

            def crop_(c, m=m):
                def columns(n):
                    cols = pl.ds(pl.multiple_of(n * 512, 512), 512)
                    rows = span(m.out0 + c * m.out, m.out, 8)
                    mean = by_view(wv, m.crop0 + c, st7[0:2, cols])
                    z7[rows, cols] = (z7[rows, cols] - mean) * by_view(wv, m.crop0 + c, st7[2:4, cols])

                repeat(cout // 512, columns)

            repeat(m.count, crop_)

    center(sets[:1])
    meet_near(6, 0.25)
    center(sets[1:])
    meet_far(6, 0.25, st6, cout)

    out_copies[6].wait()
    g6, g7 = 2 * c4, 2 * c4 + cout
    lanes = 512
    for m in sets:

        def pair(p, m=m):
            o = m.out0 + p * 2 * m.out

            def columns(n):
                cols = pl.ds(pl.multiple_of(n * lanes, lanes), lanes)
                cols6 = pl.ds(pl.multiple_of(g6 + n * lanes, lanes), lanes)
                cols7 = pl.ds(pl.multiple_of(g7 + n * lanes, lanes), lanes)
                c = cot[span(o, 2 * m.out), cols].astype(f)
                mask = keep(lanes, 8, m.half)
                found = []
                for j in range(2):
                    crop = m.crop0 + 2 * p + j
                    rows = span(o + j * m.out, m.out, 8)
                    n6 = (z6[rows, cols] - by_view(wv, crop, st6[0:2, cols])) * by_view(wv, crop, st6[2:4, cols])
                    n7 = z7[rows, cols]
                    z6[rows, cols] = n6
                    u = n6 * norms2[0:1, cols6] + n7 * norms2[0:1, cols7] + (norms2[1:2, cols6] + norms2[1:2, cols7])
                    a, slope = act_both(u)
                    found.append(a)
                    up = masked(slope * c[j * m.out : (j + 1) * m.out], mask)
                    z4[span(n * outs + o + j * m.out, m.out, 8), :] = up
                    for to, part in ((cs, up), (cm, up * n6), (ck, up * n7)):
                        to[pl.ds(crop, 1), cols] = jnp.sum(tile_sum(part), axis=0, keepdims=True)
                w6[span(o, 2 * m.out), cols] = jnp.concatenate(found, axis=0).astype(BF16)

            repeat(cout // lanes, columns)

        repeat(m.count // 2, pair)
    local_sums(blocks[7], (cs, cm, ck), wcol, cout)
    links.send_near(7, blocks[7])
    put(w6.at[0:outs], o_res)
    links.wait_near(7)
    far[7][links.outer] = fold_sums(near[7], links.wide)
    links.send_far(7)
    links.wait_far(7)
    sums = fold_sums(far[7], links.outers)
    for t in range(3):
        unpack(sq, 2 * t, sums[8 * t : 8 * t + 8], cout)

    for m in sets:

        def pair(p, m=m):
            o = m.out0 + p * 2 * m.out

            def columns(n):
                cols = pl.ds(pl.multiple_of(n * lanes, lanes), lanes)
                mask = keep(lanes, 8, m.half)
                got6, got7 = [], []
                for j in range(2):
                    crop = m.crop0 + 2 * p + j
                    rows = span(o + j * m.out, m.out, 8)
                    up = z4[span(n * outs + o + j * m.out, m.out, 8), :]
                    over = wv[0, crop] * (4.0 / tally_v[0:1, 0:1]) + wv[1, crop] * (4.0 / tally_v[1:2, 0:1])
                    level = by_view(wv, crop, sq[0:2, cols]) * over
                    for got, z, st, at, t in ((got6, z6, st6, g6, 2), (got7, z7, st7, g7, 4)):
                        inv = by_view(wv, crop, st[2:4, cols])
                        gain = inv * norms2[0:1, pl.ds(pl.multiple_of(at + n * lanes, lanes), lanes)]
                        tilt = by_view(wv, crop, sq[t : t + 2, cols]) * over
                        got.append(masked(gain * (up - level - z[rows, cols] * tilt), mask))
                w7[span(o, 2 * m.out), cols] = jnp.concatenate(got6, axis=0).astype(BF16)
                w7[span(cin // 2 + o, 2 * m.out), cols] = jnp.concatenate(got7, axis=0).astype(BF16)

            repeat(cout // lanes, columns)

        repeat(m.count // 2, pair)
    put(w7.at[0:outs], o_d6)
    put(w7.at[cin // 2 : cin // 2 + outs], o_d7)
    for src, dst in (
        (st1, o_st1), (st2, o_st2), (st3, o_st3), (st4, o_st4), (st7, o_st7), (st5, o_st5), (st6, o_st6),
        (sq, o_sq), (tally_v, o_tally),
    ):
        put(src, dst)
    links.finish()
    for copy in swaps:
        copy.wait_send()
    for i, copy in enumerate(out_copies):
        if i != 6:
            copy.wait()


def flat_rows(tensor, pitch):
    n, h, w, c = tensor.shape
    return jnp.pad(tensor, ((0, 0), (0, 0), (0, pitch - w), (0, 0))).reshape(n * h * pitch, c)


def forward(images, cots, views, w, norms_first, norms_second, ident):
    crops = lax.axis_size("crops")
    nb, ns = images[0].shape[0] // 2, images[1].shape[0] // 2
    sets, total, guarded, outs = geometry(nb, images[0].shape[2], ns, images[1].shape[2])
    w1, wsp1, w3, w4, w5, w6, w7 = w
    cin, c3 = w1.shape
    c4, cout = w6.shape
    smem, vmem = pl.BlockSpec(memory_space=pltpu.SMEM), pl.BlockSpec(memory_space=pltpu.VMEM)
    hbm = pl.BlockSpec(memory_space=pl.ANY)
    shape = jax.ShapeDtypeStruct
    out_shape = [
        shape((total, cin), BF16), shape((total, c3), F32), shape((guarded, 3 * c3), BF16), shape((total, c3), F32),
        shape((total, c3), BF16), shape((total, cin), BF16), shape((total, c4), F32), shape((outs, 9 * c4), BF16),
        shape((outs, c4), F32), shape((outs, c4), BF16), shape((outs, cin), BF16), shape((outs, cout), BF16),
        shape((outs, cout), BF16), shape((outs, cout), BF16),
        shape((8, c3), F32), shape((8, c3), F32), shape((8, cin), F32), shape((8, c4), F32), shape((8, cout), F32),
        shape((8, c4), F32), shape((8, cout), F32), shape((8, cout), F32), shape((8, 128), F32),
    ]
    most = 2 * sets[0].rows
    scratch = [
        pltpu.VMEM((total, cin), BF16), pltpu.VMEM((total, c3), F32), pltpu.VMEM((guarded, 3 * c3), BF16),
        pltpu.VMEM((total, c3), F32), pltpu.VMEM((total, c3), BF16), pltpu.VMEM((most, cin), F32),
        pltpu.VMEM((total, cin), BF16), pltpu.VMEM((cin // 128, most // 2, 128), F32), pltpu.VMEM((total, c4), F32),
        pltpu.VMEM((outs, cin), BF16), pltpu.VMEM((outs, cout), F32), pltpu.VMEM((c4 // 128, 24 + 2 * sets[0].guard, 128), F32),
        pltpu.VMEM((outs, 9 * c4), BF16), pltpu.VMEM((outs, c4), F32),
        pltpu.VMEM((outs, c4), BF16), pltpu.VMEM((outs, cout), F32), pltpu.VMEM((outs, cout), BF16),
    ]
    scratch += [pltpu.VMEM(t.shape, BF16) for t in w]
    scratch += [pltpu.VMEM((16, cout), F32)] * 3
    scratch += [pltpu.VMEM((8, n), F32) for n in (c3, c3, cin, c4, cout, c4, cout, cout, 128)]
    scratch += [pltpu.SMEM((2, 16), F32), pltpu.VMEM((16, 128), F32)]
    scratch += exchange_shapes(FWD_WIDTHS, (3, 2, 2, 2, 2, 2, 2, 3), crops)
    scratch += [
        pltpu.SemaphoreType.DMA((8,)), pltpu.SemaphoreType.DMA((nb + ns,)), pltpu.SemaphoreType.DMA((nb + ns,)),
        pltpu.SemaphoreType.DMA((nb + ns,)), pltpu.SemaphoreType.DMA((23,)),
    ]
    got = pl.pallas_call(
        functools.partial(forward_kernel, sets, total, guarded, outs, crops, (c3, cin, c4, cout)),
        out_shape=out_shape,
        in_specs=[smem, smem, vmem, vmem] + [hbm] * 10,
        out_specs=[hbm] * len(out_shape),
        scratch_shapes=scratch,
        compiler_params=pltpu.CompilerParams(
            collective_id=ident, has_side_effects=True, vmem_limit_bytes=63 * 1024 * 1024
        ),
        name="forward",
    )(
        *views, norms_first, norms_second,
        flat_rows(images[0], 16), flat_rows(images[1], 16),
        jnp.concatenate([flat_rows(t, 8) for t in cots], axis=0), *w,
    )
    return sets, (total, guarded, outs), got


def share_plan(shapes, cuts):
    chunks = []
    for at, (height, width) in enumerate(shapes):
        down, across = cuts[at]
        half, high = width // 2 // across, height // down
        for c in range(down):
            for p in range(across):
                chunks.append((at, c * high, high, p * half, half))
    return chunks


class Share:
    def __init__(self, shapes, chunks, orders, bits, links, sources, outs, acc, recv0, recvs, sems, begin, leave):
        self.shapes, self.chunks, self.bits = shapes, chunks, bits
        self.k, self.core = links.k, links.r
        self.sources, self.outs, self.acc, self.recv0, self.recvs = sources, outs, acc, recv0, recvs
        self.send_sem, self.recv_sem, self.load_sem, self.store_sem = sems
        self.sibling = (self.k, 1 - self.core)
        self.total = 2 * bits + 2
        self.live, self.loads, self.stores, self.begin, self.leave, self.at = {}, {}, {}, begin, leave, 0
        digit = [lax.rem(self.k // (1 << b), 2) for b in range(bits)]
        self.stages, self.regions, self.kinds, self.slots = [], [], [], []
        for i, (at, row, height, col, width) in enumerate(chunks):
            stages = []
            for a, b in zip(*orders[i]):
                if a == b:
                    mine, step = digit[a], 1 << a
                else:
                    mine = digit[a] * (1 - self.core) + digit[b] * self.core
                    step = (1 << a) * (1 - self.core) + (1 << b) * self.core
                stages.append((mine, self.k + step * (1 - 2 * mine)))
            start, length, used = 0, height, 0
            region, kind, slot = [], [], []
            for s in range(bits):
                region.append((start, length))
                slot.append(used)
                if length % 32 == 0:
                    kind.append(True)
                    length //= 2
                    start = start + stages[s][0] * length
                else:
                    kind.append(False)
                used += length
            region.append((start, length))
            self.stages.append(stages)
            self.regions.append(region)
            self.kinds.append(kind)
            self.slots.append(slot)

    def send(self, i, t, src, dst, device):
        copy = pltpu.make_async_remote_copy(
            src_ref=src,
            dst_ref=dst,
            send_sem=self.send_sem.at[i, t],
            recv_sem=self.recv_sem.at[i, t],
            device_id=device,
            device_id_type=MESH,
        )
        copy.start()
        self.live[i, t] = copy

    def add(self, dst, at, src, src_at, length):
        block = 16
        while length % (block * 2) == 0 and block * 2 * dst.shape[1] <= 65536:
            block *= 2

        def step(j, carry):
            off = j * block
            rows = span(at + off, block)
            dst[rows, :] = dst[rows, :] + src[span(src_at + off, block), :]
            return carry

        lax.fori_loop(0, length // block, step, 0)

    def fetch(self):
        for i, (at, row, height, col, width) in enumerate(self.chunks):
            t = self.begin[i]
            if 1 <= t <= self.bits:
                start, length = self.regions[i][t - 1]
                own = pl.ds(pl.multiple_of(self.core * (self.shapes[at][1] // 2) + col, 128), width)
                self.loads[i] = pltpu.make_async_copy(
                    self.sources[at].at[span(row + start, length), own],
                    self.acc[i].at[span(start, length)],
                    self.load_sem.at[i],
                )
                self.loads[i].start()

    def arrived(self, i, t):
        if (i, t) in self.live:
            self.live[i, t].wait_recv()

    def task(self, i, t):
        at, row, height, col, width = self.chunks[i]
        bits, kinds, regions, stages = self.bits, self.kinds[i], self.regions[i], self.stages[i]
        half = self.shapes[at][1] // 2
        own = pl.ds(pl.multiple_of(self.core * half + col, 128), width)
        rows = pl.ds(row, height)
        if t == 0:
            away = pl.ds(pl.multiple_of((1 - self.core) * half + col, 128), width)
            self.send(i, 0, self.sources[at].at[rows, away], self.recv0[i], self.sibling)
            if self.acc[i] is None:
                self.acc[i] = self.sources[at].at[rows, own]
                return
            copy = pltpu.make_async_copy(self.sources[at].at[rows, own], self.acc[i], self.load_sem.at[i])
            copy.start()
            self.loads[i] = copy
            return
        self.arrived(i, t - 1)
        if t <= bits + 1:
            if t == self.begin[i]:
                if t <= bits:
                    self.loads[i].wait()
            elif t == 1:
                if i in self.loads:
                    self.loads[i].wait()
                self.add(self.acc[i], 0, self.recv0[i], 0, height)
            else:
                s = t - 2
                start, length = regions[s + 1]
                if not kinds[s]:
                    self.live[i, t - 1].wait_send()
                self.add(self.acc[i], start, self.recvs[i], self.slots[i][s], length)
        if t == self.leave[i]:
            start, length = regions[t - 1]
            copy = pltpu.make_async_copy(
                self.acc[i].at[span(start, length)], self.outs[at].at[span(row + start, length), own], self.store_sem.at[i]
            )
            copy.start()
            self.stores[i] = copy
            return
        if t <= bits:
            s = t - 1
            start, length = regions[s]
            give, first = length, start
            if kinds[s]:
                give = length // 2
                first = start + (1 - stages[s][0]) * give
            self.send(
                i, t, self.acc[i].at[span(first, give)], self.recvs[i].at[pl.ds(self.slots[i][s], give)],
                (stages[s][1], self.core),
            )
            return
        if t == bits + 1:
            start, length = regions[bits]
            if t == self.begin[i]:
                mine = self.sources[at].at[span(row + start, length), own]
            else:
                mine = self.acc[i].at[span(start, length)]
            copy = pltpu.make_async_copy(mine, self.outs[at].at[span(row + start, length), own], self.store_sem.at[i])
            copy.start()
            self.stores[i] = copy
        if t == bits + 2:
            self.stores[i].wait()
        if t <= 2 * bits:
            s = bits - 1 - (t - bits - 1)
            start, length = regions[s + 1]
            if kinds[s]:
                place = self.outs[at].at[span(row + start, length), own]
                self.send(i, t, mine if t == bits + 1 else place, place, (stages[s][1], self.core))
            return
        if t == 2 * bits + 1:
            place = self.outs[at].at[rows, own]
            self.send(i, t, place, place, self.sibling)

    def run(self, order):
        while self.at < len(order):
            token = order[self.at]
            self.at += 1
            if token is None:
                return
            i, t = token
            if t == self.total:
                self.arrived(i, t - 1)
            else:
                self.task(i, t)

    def finish(self):
        for (i, t), copy in self.live.items():
            if not (1 <= t <= self.bits and not self.kinds[i][t - 1]):
                copy.wait_send()


def share_scratch(chunks, bits, begin, inside=False):
    acc, recv0, recvs = [], [], []
    for i, (at, row, height, col, width) in enumerate(chunks):
        if begin[i] > bits:
            continue
        acc.append(pltpu.VMEM((height, width), BF16))
        if begin[i] == 0:
            recv0.append(pltpu.VMEM((height, width), BF16))
        length, used = height, 0
        for s in range(bits):
            if length % 32 == 0:
                length //= 2
            used += length
        recvs.append(pltpu.VMEM((used, width), BF16))
    n = len(chunks)
    sems = [pltpu.SemaphoreType.DMA((n, 2 * bits + 2))] * 2 + [pltpu.SemaphoreType.DMA((n,))] * 2
    return ([] if inside else acc) + recv0 + recvs + sems


def share_hold(refs, bits, begin, inside=False):
    n = len(begin)
    acc, recv0, recvs = [None] * n, [None] * n, [None] * n
    for held, most in ((acc, -1 if inside else bits), (recv0, 0), (recvs, bits)):
        for i in range(n):
            if begin[i] <= most:
                held[i], refs = refs[0], refs[1:]
    return acc, recv0, recvs, refs


def share_leave(bits):
    return [bits + 1] * 3 + [min(3, bits + 1)] * 3


def share_orders(bits, path):
    rest = list(range(2, bits))
    if bits < 2:
        return rest or list(range(bits)), rest or list(range(bits))
    if path == 0:
        return [0, 1] + rest, [1, 0] + rest
    if path == 1:
        return [0] + rest + [1], [1] + rest + [0]
    return rest + [0, 1], rest + [1, 0]


SHARE_CUTS = ((1, 2), (1, 1), (3, 1), (1, 1), (1, 1), (1, 1), (1, 1))
SHARE_FIRST = 6
SHARE_PATHS = (0, 1, 1, 0, 1, 0, 0, 0, 0, 0)
SHARE_LATE = (
    21, 51, 96, 83, 5, 37, -1, 97, -1, 22, 52, 6, -1, 98, -1, -1, -1, 53, -1, 23, 112, 84, 7, -1,
    54, -1, 113, 8, 67, -1, -1, 55, 85, -1, 114, -1, 24, 99, 38, -1, 128, 86, 68, -1, 56, 115, 9, -1,
    129, 69, -1, 116, 39, 100, -1, 10, -1, -1, 117, 144, 87, 25, 101, 118, 145, 57, 70, 130, 26, 88, 40, 102,
    146, 58, 131, 119, 71, 147, 103, 120, 132, 148, 104, 133, 149, 89, 72, 121, 41, 150, 134, 122, 90, 151, 105, 42,
    135, 73, 152, 106, 136, 74, 153, 154, 137, 138,
)
SHARE_EARLY = (
    32, -1, 33, 16, -1, -1, 17, 0, -1, 34, -1, 1, -1, 18, -1, 48, -1, -1, 35, -1, 64, 49, 2, -1,
    65, 80, 19, -1, -1, 81, 3, 36, -1, -1, 66, 20, 37, 50, 4, -1, 82, -1, 21, 5, 51, 83, 67,
)


def share_late_order(pieces, bits, parts, ready):
    if bits == 4:
        return [None if v < 0 else (v // 16, v % 16) for v in SHARE_LATE]
    order, total = [], 2 * bits + 2
    begin = share_leave(bits) + [0] * (pieces - SHARE_FIRST)
    for k in range(parts + total + 1):
        for i in range(pieces):
            t = k - ready[i] + begin[i]
            if k >= ready[i] and t <= total:
                order.append((i, t))
        if k < parts:
            order.append(None)
    return order


def share_early_order(bits):
    if bits == 4:
        return [None if v < 0 else (v // 16, v % 16) for v in SHARE_EARLY]
    order = [None] * 10
    for t in range(bits + 2):
        order += [(i, t) for i in range(SHARE_FIRST) if t <= share_leave(bits)[i]] + [None]
    return order


def meet_sums(links, e, width, tables, between=None):
    links.wait_near(e)
    links.far[e][links.outer] = fold_sums(links.near[e], links.wide)
    links.send_far(e)
    if between is not None:
        between()
    links.wait_far(e)
    sums = fold_sums(links.far[e], links.outers)
    for t, (table, row) in enumerate(tables):
        unpack(table, row, sums[8 * t : 8 * t + 8], width)


def share_of(wv, tally, crop, times):
    return wv[0, crop] * (times / tally[0:1, 0:1]) + wv[1, crop] * (times / tally[1:2, 0:1])


class Puts:
    def __init__(self, sem):
        self.sem, self.copies = sem, []

    def put(self, src, dst):
        copy = pltpu.make_async_copy(src, dst, self.sem.at[len(self.copies)])
        copy.start()
        self.copies.append(copy)

    def finish(self):
        for copy in self.copies:
            copy.wait()


def start_loads(pairs, sem):
    copies = [pltpu.make_async_copy(src, dst, sem.at[i]) for i, (src, dst) in enumerate(pairs)]
    for copy in copies:
        copy.start()
    return copies


def back_two_kernel(sets, total, outs, crops, dims, shapes, chunks, *refs):
    c3, cin, c4, cout = dims
    vb, vs, norms1, norms2, st3, st4, st5, tally = refs[:8]
    sources, refs = refs[8:23], refs[23:]
    (o_up, o_g6, o_g7, o_g5, o_g4, o_s5, o_s4, o_s3), refs = refs[:8], refs[8:]
    held, refs = refs[:14], refs[14:]
    (d6, w6, z5, h5, d7, xe, w7, w5, x5, z4, w4, h2, w3, img) = held
    (q5, t7, dh, d4, zt, bg, up, s5, s4, s3, cs, cm, wv, wcol), refs = refs[:14], refs[14:]
    d5, pv, blk = d6, q5, img
    g6, g7, g5, g4 = w6, w7, w5, w4
    blocks, refs = take(refs, 3)
    near, refs = take(refs, 3)
    far, refs = take(refs, 3)
    links = Links(crops, near, far, *refs[:4])
    load_sem, out_sem, up_sem = refs[4:7]
    refs = refs[7:]
    bits = crops.bit_length() - 1
    early = SHARE_FIRST
    acc, recv0, recvs, refs = share_hold(refs, bits, [0] * early, True)
    share = Share(
        shapes, chunks[:early], [share_orders(bits, v) for v in SHARE_PATHS[:early]], bits, links, [g7, g6, g5], [o_g7, o_g6, o_g5],
        acc, recv0, recvs, refs, [0] * early, share_leave(bits),
    )
    order = share_early_order(bits)

    def tick():
        share.run(order)

    f = F32
    loads = start_loads(list(zip(sources, held)), load_sem)
    links.greet()
    view_tables(sets, links.r, (vb, vs), wv, wcol)
    puts = Puts(out_sem)
    for ref in (cs, cm):
        ref[...] = jnp.zeros(ref.shape, f)
    for block in blocks:
        block[...] = jnp.zeros(block.shape, f)

    for i in range(3):
        loads[i].wait()
    q5[...] = mm_nt(d6[...], w6[...])
    g5at = c4
    for m in sets:

        def crop_(c, m=m):
            crop = m.crop0 + c
            rows = span(m.out0 + c * m.out, m.out, 8)
            inv = by_view(wv, crop, st5[2:4, :])
            n = (z5[rows, :] - by_view(wv, crop, st5[0:2, :])) * inv
            q = act_slope(n * norms2[0:1, g5at : 2 * c4] + norms2[1:2, g5at : 2 * c4]) * q5[rows, :]
            q5[rows, :] = q
            cs[pl.ds(crop, 1), 0:c4] = jnp.sum(tile_sum(q), axis=0, keepdims=True)
            cm[pl.ds(crop, 1), 0:c4] = jnp.sum(tile_sum(q * n), axis=0, keepdims=True)

        repeat(m.count, crop_)
    local_sums(blocks[0], (cs, cm), wcol, c4)
    links.send_near(0, blocks[0])

    loads[3].wait()

    def outer(n):
        cols = pl.ds(pl.multiple_of(n * 512, 512), 512)
        g6[:, cols] = mm_tn(h5[...], d6[:, cols]).astype(BF16)

    repeat(cout // 512, outer)
    tick()

    def rest():
        for i in (4, 5, 6):
            loads[i].wait()

        def shortcut(n):
            part = pl.ds(pl.multiple_of(n * 256, 256), 256)
            t7[:, part] = mm_nt(d7[...], w7[part, :])

        repeat(cin // 256, shortcut)

        def skip(n):
            cols = pl.ds(pl.multiple_of(n * 512, 512), 512)
            g7[:, cols] = mm_tn(xe[...], d7[:, cols]).astype(BF16)

        repeat(cout // 512, skip)
        tick()

    meet_sums(links, 0, c4, ((s5, 0), (s5, 2)), rest)

    for m in sets:

        def pair(p, m=m):
            o = m.out0 + p * 2 * m.out
            mask = keep(c4, 8, m.half)
            slots = [[], [], [], []]
            for j in range(2):
                crop = m.crop0 + 2 * p + j
                rows = span(o + j * m.out, m.out, 8)
                over = share_of(wv, tally, crop, 4.0)
                inv = by_view(wv, crop, st5[2:4, :])
                n = (z5[rows, :] - by_view(wv, crop, st5[0:2, :])) * inv
                d = (inv * norms2[0:1, g5at : 2 * c4]) * (
                    q5[rows, :] - by_view(wv, crop, s5[0:2, :]) * over - n * (by_view(wv, crop, s5[2:4, :]) * over)
                )
                d = masked(d, mask)
                down = jnp.concatenate([d[8:], jnp.zeros((8, c4), f)], axis=0)
                slots[0].append(d)
                slots[1].append(pltpu.roll(d, m.out - 1, 0))
                slots[2].append(down)
                slots[3].append(pltpu.roll(down, m.out - 1, 0))
            for t in range(4):
                d5[span(o, 2 * m.out), t * c4 : (t + 1) * c4] = jnp.concatenate(slots[t], axis=0).astype(BF16)

        repeat(m.count // 2, pair)

    tick()
    loads[7].wait()
    options = (((1, 0),), ((2, 0), (0, 1)))
    for a in range(2):
        for b in range(2):
            value = None
            for r, down in options[a]:
                for c, side in options[b]:
                    slot, tap = (2 * down + side) * c4, (3 * r + c) * c4
                    term = mm_nt(d5[:, slot : slot + c4], w5[tap : tap + c4, :])
                    value = term if value is None else value + term
            pv[...] = value
            for m in sets:

                def crop_(c, m=m, a=a, b=b):
                    for i in range(m.half):
                        for q in range(c4 // 128):
                            dh[q, pl.ds(m.row0 + c * m.rows + (2 * i + a) * 16 + b, 8, stride=2), :] = pv[
                                span(m.out0 + c * m.out + i * 8, 8, 8), q * 128 : (q + 1) * 128
                            ]

                repeat(m.count, crop_)
        tick()
    loads[9].wait()
    for m in sets:

        def crop_(c, m=m):
            crop = m.crop0 + c
            rows = span(m.row0 + c * m.rows, m.rows)
            mask = keep(128, 16, m.edge)
            levels, tilts = [], []
            for q in range(c4 // 128):
                cols = slice(q * 128, (q + 1) * 128)
                inv = by_view(wv, crop, st4[2:4, cols])
                n = (z4[rows, cols] - by_view(wv, crop, st4[0:2, cols])) * inv
                up_ = masked(act_slope(n * norms2[0:1, cols] + norms2[1:2, cols]) * dh[q, rows, :], mask)
                dh[q, rows, :] = up_
                levels.append(jnp.sum(tile_sum(up_), axis=0, keepdims=True))
                tilts.append(jnp.sum(tile_sum(up_ * n), axis=0, keepdims=True))
            cs[pl.ds(crop, 1), 0:c4] = jnp.concatenate(levels, axis=1)
            cm[pl.ds(crop, 1), 0:c4] = jnp.concatenate(tilts, axis=1)

        repeat(m.count, crop_)
        tick()
    local_sums(blocks[1], (cs, cm), wcol, c4)
    links.send_near(1, blocks[1])
    loads[8].wait()

    def kernel(n):
        for t in range(3 * n, 3 * n + 3):
            part = slice(t * c4, (t + 1) * c4)
            g5[part, :] = mm_tn(x5[:, part], d5[:, 0:c4]).astype(BF16)
        tick()

    kernel(0)

    def rest():
        kernel(1)
        kernel(2)

    meet_sums(links, 1, c4, ((s4, 0), (s4, 2)), rest)
    tick()

    for i in range(10, 14):
        loads[i].wait()
    big_rows = 2 * sets[0].rows
    for at, m in enumerate(sets):

        def pair(p, m=m, at=at):
            r = m.row0 + p * 2 * m.rows
            o = m.out0 + p * 2 * m.out
            mask = keep(128, 16, m.edge)
            for j in range(2):
                crop = m.crop0 + 2 * p + j
                rows = span(r + j * m.rows, m.rows)
                over = share_of(wv, tally, crop, 1.0)
                for q in range(c4 // 128):
                    cols = slice(q * 128, (q + 1) * 128)
                    inv = by_view(wv, crop, st4[2:4, cols])
                    n = (z4[rows, cols] - by_view(wv, crop, st4[0:2, cols])) * inv
                    d = (inv * norms2[0:1, cols]) * (
                        dh[q, rows, :] - by_view(wv, crop, s4[0:2, cols]) * over - n * (by_view(wv, crop, s4[2:4, cols]) * over)
                    )
                    d4[rows, cols] = masked(d, mask).astype(BF16)
            got = mm_nt(d4[span(r, 2 * m.rows), :], w4[...])
            for q in range(cin // 128):
                bg[q, 0 : 2 * m.rows, :] = got[:, q * 128 : (q + 1) * 128]
            for q in range(cin // 128):
                for j in range(2):
                    for i in range(m.half):
                        here = pl.ds(j * m.rows + i * 32, 8, stride=2)
                        bg[q, here, :] = bg[q, here, :] + t7[span(o + j * m.out + i * 8, 8, 8), q * 128 : (q + 1) * 128]
            turn = m.crop0 // 2 + p
            slot = turn % 2

            def left(turn, slot):
                return pltpu.make_async_copy(
                    up.at[slot, 0 : 2 * m.rows], o_up.at[span(r, 2 * m.rows)], up_sem.at[turn]
                )

            if turn >= 2:
                size = big_rows if turn - 2 < sets[0].count // 2 else 2 * m.rows
                pltpu.make_async_copy(up.at[slot, 0:size], o_up.at[pl.ds(0, size)], up_sem.at[turn - 2]).wait()
            step = m.rows // 2
            mask = keep(128, 16, m.edge)
            totals = [[[], []], [[], []]]
            for h, j in [(h, j) for h in range(cin // 512) for j in range(2)]:
                if j == 0:
                    zt[0 : 2 * m.rows, :] = mm(h2[span(r, 2 * m.rows), :], w3[:, h * 512 : (h + 1) * 512])
                crop = m.crop0 + 2 * p + j
                levels, tilts = totals[j]
                for q in range(h * 4, h * 4 + 4):
                    cols = slice(q * 128, (q + 1) * 128)
                    part = slice((q - h * 4) * 128, (q - h * 4 + 1) * 128)
                    at3 = slice(2 * c3 + q * 128, 2 * c3 + (q + 1) * 128)
                    mean, inv = by_view(wv, crop, st3[0:2, cols]), by_view(wv, crop, st3[2:4, cols])
                    gain, bias = norms1[0:1, at3], norms1[1:2, at3]

                    def tile(i, sums, j=j, cols=cols, part=part, q=q, mean=mean, inv=inv, gain=gain, bias=bias):
                        here = span(j * m.rows + i * step, step)
                        rows = span(r + j * m.rows + i * step, step)
                        n = (zt[here, part] - mean) * inv
                        u = n * gain + bias + img[rows, cols].astype(f)
                        got = bg[q, here, :].astype(BF16).astype(f)
                        v = masked(act_slope(u) * got, mask)
                        up[slot, here, cols] = v
                        return (sums[0] + tile_sum(v), sums[1] + tile_sum(v * n))

                    zero = jnp.zeros((8, 128), f)
                    s, t = lax.fori_loop(0, 2, tile, (zero, zero))
                    levels.append(jnp.sum(s, axis=0, keepdims=True))
                    tilts.append(jnp.sum(t, axis=0, keepdims=True))
            for j in range(2):
                crop = m.crop0 + 2 * p + j
                cs[pl.ds(crop, 1), :] = jnp.concatenate(totals[j][0], axis=1)
                cm[pl.ds(crop, 1), :] = jnp.concatenate(totals[j][1], axis=1)
            left(turn, slot).start()

        for p in range(m.count // 2):
            pair(p)
            tick()
    late = pltpu.make_async_copy(sources[14], blk, load_sem.at[14])
    late.start()
    local_sums(blocks[2], (cs, cm), wcol, cin)
    links.send_near(2, blocks[2])
    late.wait()

    def inner(n):
        part = pl.ds(pl.multiple_of(n * 256, 256), 256)
        g4[part, :] = mm_tn(blk[:, part], d4[...]).astype(BF16)

    repeat(2, inner)
    tick()

    def rest():
        repeat(cin // 256 - 2, lambda n: inner(n + 2))
        puts.put(g4, o_g4)
        tick()

    meet_sums(links, 2, cin, ((s3, 0), (s3, 2)), rest)
    for src, dst in ((s5, o_s5), (s4, o_s4), (s3, o_s3)):
        puts.put(src, dst)
    for back in (2, 1):
        size = 2 * sets[1].rows
        turn = (sets[0].count + sets[1].count) // 2 - back
        pltpu.make_async_copy(
            up.at[turn % 2, 0:size], o_up.at[pl.ds(sets[1].row0, size)], up_sem.at[turn]
        ).wait()
    while share.at < len(order):
        tick()
    for copy in share.stores.values():
        copy.wait()
    share.finish()
    links.finish()
    puts.finish()


def back_one_kernel(sets, total, guarded, crops, dims, shapes, chunks, *refs):
    c3, cin = dims
    vb, vs, norms1, st1, st2, st3, s3, tally = refs[:8]
    sources, refs = refs[8:17], refs[17:]
    second, refs = list(refs[:4]), refs[4:]
    (o_gb, o_gs, o_s2, o_s1), refs = refs[:4], refs[4:]
    o_grads, refs = refs[:7], refs[7:]
    held, refs = refs[:9], refs[9:]
    (h2, w3, up, z2, h1, wsp1, z1, w1, img) = held
    (zt, d3, q2, d2, q1, d1, g3, g2, g1, s2, s1, cs, cm, wv, wcol), refs = refs[:15], refs[15:]
    blocks, refs = take(refs, 2)
    near, refs = take(refs, 2)
    far, refs = take(refs, 2)
    links = Links(crops, near, far, *refs[:4])
    load_sem, out_sem, own_sem, grad_send, grad_recv, up_sem = refs[4:10]
    refs = refs[10:]
    n = len(chunks)
    bits = crops.bit_length() - 1
    begin = share_leave(bits) + [0] * (n - SHARE_FIRST)
    acc, recv0, recvs, refs = share_hold(refs, bits, begin)
    share = Share(
        shapes, chunks, [share_orders(bits, v) for v in SHARE_PATHS], bits, links, second + [g3, g2, g1], o_grads,
        acc, recv0, recvs, refs, begin, [2 * bits + 3] * n,
    )
    share.fetch()
    order = share_late_order(n, bits, 20, (0,) * 7 + (7, 14, 20))

    def tick():
        share.run(order)

    core = links.r
    sibling = (links.k, 1 - core)
    f = F32
    loads = start_loads([(a, b) for a, b in zip(sources, held) if b is not up], load_sem)
    ups = []
    for m in sets:
        for p in range(m.count // 2):
            rows = pl.ds(m.row0 + p * 2 * m.rows, 2 * m.rows)
            ups.append(pltpu.make_async_copy(sources[2].at[rows], up.at[rows], up_sem.at[len(ups)]))
    for copy in ups:
        copy.start()
    links.greet()
    tick()
    view_tables(sets, links.r, (vb, vs), wv, wcol)
    puts = Puts(out_sem)
    for ref in (cs, cm):
        ref[...] = jnp.zeros(ref.shape, f)
    for block in blocks:
        block[...] = jnp.zeros(block.shape, f)
    d2[0:16, :] = jnp.zeros((16, 3 * c3), BF16)
    for m in sets:
        for c in range(m.count):
            at = m.guard0 + c * m.guard + m.rows
            d2[at : at + 16, :] = jnp.zeros((16, 3 * c3), BF16)

    for i in range(3):
        loads[i].wait()
    for copy in ups:
        copy.wait()
    for m in sets:

        def pair(p, m=m):
            r = m.row0 + p * 2 * m.rows
            step = m.rows // 2
            mask = keep(128, 16, m.edge)
            for h, j in [(h, j) for h in range(cin // 512) for j in range(2)]:
                if j == 0:
                    zt[0 : 2 * m.rows, :] = mm(h2[span(r, 2 * m.rows), :], w3[:, h * 512 : (h + 1) * 512])
                crop = m.crop0 + 2 * p + j
                over = share_of(wv, tally, crop, 1.0)
                for q in range(h * 4, h * 4 + 4):
                    cols = slice(q * 128, (q + 1) * 128)
                    part = slice((q - h * 4) * 128, (q - h * 4 + 1) * 128)
                    mean, inv = by_view(wv, crop, st3[0:2, cols]), by_view(wv, crop, st3[2:4, cols])
                    gain = inv * norms1[0:1, 2 * c3 + q * 128 : 2 * c3 + (q + 1) * 128]
                    level = by_view(wv, crop, s3[0:2, cols]) * over
                    tilt = by_view(wv, crop, s3[2:4, cols]) * over * inv

                    def tile(i, j=j, cols=cols, part=part, mean=mean, gain=gain, level=level, tilt=tilt):
                        here = span(j * m.rows + i * step, step)
                        rows = span(r + j * m.rows + i * step, step)
                        d = gain * (up[rows, cols] - level - (zt[here, part] - mean) * tilt)
                        d3[rows, cols] = masked(d, mask).astype(BF16)

                    repeat(2, tile)
            q2[span(r, 2 * m.rows), :] = mm_nt(d3[span(r, 2 * m.rows), :], w3[...])
            for j in range(2):
                crop = m.crop0 + 2 * p + j
                mean, inv = by_view(wv, crop, st2[0:2, :]), by_view(wv, crop, st2[2:4, :])

                def tile(i, sums, j=j, mean=mean, inv=inv):
                    rows = span(r + j * m.rows + i * step, step)
                    n = (z2[rows, :] - mean) * inv
                    v = act_slope(n * norms1[0:1, c3 : 2 * c3] + norms1[1:2, c3 : 2 * c3]) * q2[rows, :]
                    q2[rows, :] = v
                    return (sums[0] + tile_sum(v), sums[1] + tile_sum(v * n))

                zero = jnp.zeros((8, c3), f)
                s, t = lax.fori_loop(0, 2, tile, (zero, zero))
                cs[pl.ds(crop, 1), 0:c3] = jnp.sum(s, axis=0, keepdims=True)
                cm[pl.ds(crop, 1), 0:c3] = jnp.sum(t, axis=0, keepdims=True)

        for p in range(m.count // 2):
            pair(p)
            tick()
    local_sums(blocks[0], (cs, cm), wcol, c3)
    links.send_near(0, blocks[0])

    def outer(n):
        cols = pl.ds(pl.multiple_of(n * 256, 256), 256)
        g3[:, cols] = mm_tn(h2[...], d3[:, cols]).astype(BF16)

    repeat(cin // 512, outer)
    tick()

    def rest():
        repeat(cin // 512, lambda n: outer(n + cin // 512))
        tick()

    meet_sums(links, 0, c3, ((s2, 0), (s2, 2)), rest)

    for i in range(3, 6):
        loads[i].wait()
    for m in sets:

        def pair(p, m=m):
            r = m.row0 + p * 2 * m.rows
            g = m.guard0 + p * 2 * m.guard
            step = m.rows // 2
            mask = keep(c3, 16, m.edge)
            for j in range(2):
                crop = m.crop0 + 2 * p + j
                over = share_of(wv, tally, crop, 1.0)
                mean, inv = by_view(wv, crop, st2[0:2, :]), by_view(wv, crop, st2[2:4, :])
                gain = inv * norms1[0:1, c3 : 2 * c3]
                level = by_view(wv, crop, s2[0:2, :]) * over
                tilt = by_view(wv, crop, s2[2:4, :]) * over * inv

                def tile(i, j=j, mean=mean, gain=gain, level=level, tilt=tilt):
                    rows = span(r + j * m.rows + i * step, step)
                    d = gain * (q2[rows, :] - level - (z2[rows, :] - mean) * tilt)
                    d = masked(d, mask)
                    to = span(g + j * m.guard + i * step, step)
                    d2[to, 0:c3] = pltpu.roll(d, step - 1, 0).astype(BF16)
                    d2[to, c3 : 2 * c3] = d.astype(BF16)
                    d2[to, 2 * c3 : 3 * c3] = pltpu.roll(d, 1, 0).astype(BF16)

                repeat(2, tile)
            size = 2 * m.rows + 16
            value = None
            for a in range(3):
                for b in range(3):
                    part = d2[span(g - (a - 1) * 16, size), b * c3 : (b + 1) * c3]
                    term = mm_nt(part, wsp1[a, b * c3 : (b + 1) * c3, :])
                    value = term if value is None else value + term
            q1[span(r, m.rows), :] = value[0 : m.rows]
            q1[span(r + m.rows, m.rows), :] = value[m.guard : m.guard + m.rows]
            for j in range(2):
                crop = m.crop0 + 2 * p + j
                mean, inv = by_view(wv, crop, st1[0:2, :]), by_view(wv, crop, st1[2:4, :])

                def tile(i, sums, j=j, mean=mean, inv=inv):
                    rows = span(r + j * m.rows + i * step, step)
                    n = (z1[rows, :] - mean) * inv
                    v = act_slope(n * norms1[0:1, 0:c3] + norms1[1:2, 0:c3]) * q1[rows, :]
                    v = masked(v, mask)
                    q1[rows, :] = v
                    return (sums[0] + tile_sum(v), sums[1] + tile_sum(v * n))

                zero = jnp.zeros((8, c3), f)
                s, t = lax.fori_loop(0, 2, tile, (zero, zero))
                cs[pl.ds(crop, 1), 0:c3] = jnp.sum(s, axis=0, keepdims=True)
                cm[pl.ds(crop, 1), 0:c3] = jnp.sum(t, axis=0, keepdims=True)

        for p in range(m.count // 2):
            pair(p)
            tick()
    local_sums(blocks[1], (cs, cm), wcol, c3)
    links.send_near(1, blocks[1])
    inside = guarded - 32

    def taps(a):
        g2[a * 3 * c3 : (a + 1) * 3 * c3, :] = mm_tn(
            h1[a * 16 : a * 16 + inside, :], d2[16 : 16 + inside, c3 : 2 * c3]
        ).astype(BF16)

    taps(0)
    tick()

    def rest():
        taps(1)
        taps(2)
        tick()

    meet_sums(links, 1, c3, ((s1, 0), (s1, 2)), rest)

    loads[6].wait()
    moves = []
    for m, out in zip(sets, (o_gb, o_gs)):
        part = m.rows // 2
        for c in range(m.count):
            i = m.crop0 + c
            own_rows = span(m.row0 + c * m.rows + core * part, part)
            other_rows = span(m.row0 + c * m.rows + (1 - core) * part, part)
            place = out.at[span((core * m.count + c) * part, part)]
            moves.append(
                (
                    pltpu.make_async_copy(d3.at[own_rows], place, own_sem.at[i]),
                    pltpu.make_async_remote_copy(
                        src_ref=d3.at[other_rows],
                        dst_ref=place,
                        send_sem=grad_send.at[i],
                        recv_sem=grad_recv.at[i],
                        device_id=sibling,
                        device_id_type=MESH,
                    ),
                )
            )
    for m in sets:

        def pair(p, m=m):
            r = m.row0 + p * 2 * m.rows
            step = m.rows // 2
            mask = keep(c3, 16, m.edge)
            for j in range(2):
                crop = m.crop0 + 2 * p + j
                over = share_of(wv, tally, crop, 1.0)
                mean, inv = by_view(wv, crop, st1[0:2, :]), by_view(wv, crop, st1[2:4, :])
                gain = inv * norms1[0:1, 0:c3]
                level = by_view(wv, crop, s1[0:2, :]) * over
                tilt = by_view(wv, crop, s1[2:4, :]) * over * inv

                def tile(i, j=j, mean=mean, gain=gain, level=level, tilt=tilt):
                    rows = span(r + j * m.rows + i * step, step)
                    d = gain * (q1[rows, :] - level - (z1[rows, :] - mean) * tilt)
                    d1[rows, :] = masked(d, mask).astype(BF16)

                repeat(2, tile)
            rows = span(r, 2 * m.rows)
            for n in range(cin // 256):
                cols = slice(n * 256, (n + 1) * 256)
                d3[rows, cols] = (up[rows, cols] + mm_nt(d1[rows, :], w1[cols, :])).astype(BF16)

        for p in range(m.count // 2):
            pair(p)
            for c in (2 * p, 2 * p + 1):
                for copy in moves[m.crop0 + c]:
                    copy.start()
            tick()
    loads[7].wait()

    def inner(n):
        part = pl.ds(pl.multiple_of(n * 256, 256), 256)
        g1[part, :] = mm_tn(img[:, part], d1[...]).astype(BF16)

    repeat(cin // 256, inner)
    for src, dst in ((s2, o_s2), (s1, o_s1)):
        puts.put(src, dst)
    while share.at < len(order):
        tick()
    share.finish()
    links.finish()
    for near_copy, far_copy in moves:
        near_copy.wait()
        far_copy.wait()
    puts.finish()


def backward(sets, got, views, w, norms_first, norms_second, total, guarded, outs, idents):
    crops = lax.axis_size("crops")
    w1, wsp1, w3, w4, w5, w6, w7 = w
    cin, c3 = w1.shape
    c4, cout = w6.shape
    (
        f_img, f_z1, f_h1, f_z2, f_h2, f_blk, f_z4, f_x5, f_z5, f_h5, f_xe, f_res, f_d6, f_d7,
        f_st1, f_st2, f_st3, f_st4, f_st7, f_st5, f_st6, f_sq, f_n,
    ) = got
    smem, vmem = pl.BlockSpec(memory_space=pltpu.SMEM), pl.BlockSpec(memory_space=pltpu.VMEM)
    hbm = pl.BlockSpec(memory_space=pl.ANY)
    shape = jax.ShapeDtypeStruct
    most = 2 * sets[0].rows
    pairs = sum(m.count for m in sets) // 2
    count = 2 * pairs

    def like(arrays):
        return [pltpu.VMEM(t.shape, t.dtype) for t in arrays]

    def params(ident):
        return pltpu.CompilerParams(
            collective_id=ident, has_side_effects=True, vmem_limit_bytes=63 * 1024 * 1024
        )

    arrays = [f_d6, w6, f_z5, f_h5, f_d7, f_xe, w7, w5, f_x5, f_z4, w4, f_h2, w3, f_img, f_blk]
    out_shape = [
        shape((total, cin), F32), shape((c4, cout), BF16), shape((cin, cout), BF16), shape((9 * c4, c4), BF16),
        shape((cin, c4), BF16), shape((8, c4), F32), shape((8, c4), F32), shape((8, cin), F32),
    ]
    scratch = like(arrays[:14]) + [
        pltpu.VMEM((outs, c4), F32), pltpu.VMEM((outs, cin), F32), pltpu.VMEM((c4 // 128, total, 128), F32), pltpu.VMEM((total, c4), BF16),
        pltpu.VMEM((most, 512), F32), pltpu.VMEM((cin // 128, most, 128), F32), pltpu.VMEM((2, most, cin), F32),
        pltpu.VMEM((8, c4), F32), pltpu.VMEM((8, c4), F32), pltpu.VMEM((8, cin), F32),
        pltpu.VMEM((16, cin), F32), pltpu.VMEM((16, cin), F32),
        pltpu.SMEM((2, 16), F32), pltpu.VMEM((16, 128), F32),
    ]
    scratch += exchange_shapes((c4, c4, cin), (2, 2, 2), crops)
    scratch += [pltpu.SemaphoreType.DMA((15,)), pltpu.SemaphoreType.DMA((7,)), pltpu.SemaphoreType.DMA((pairs,))]
    shapes = [(cin, cout), (c4, cout), (9 * c4, c4), (cin, c4), (c3, cin), (9 * c3, c3), (cin, c3)]
    chunks = share_plan(shapes, SHARE_CUTS)
    bits = crops.bit_length() - 1
    scratch += share_scratch(chunks[:SHARE_FIRST], bits, [0] * SHARE_FIRST, True)
    up, g_outer2, g_skip, g_spatial2, g_inner2, s5, s4, s3 = pl.pallas_call(
        functools.partial(back_two_kernel, sets, total, outs, crops, (c3, cin, c4, cout), shapes, chunks),
        out_shape=out_shape,
        in_specs=[smem] * 2 + [vmem] * 6 + [hbm] * 15,
        out_specs=[hbm] * len(out_shape),
        scratch_shapes=scratch,
        compiler_params=params(idents[0]),
        name="back_two",
    )(*views, norms_first, norms_second, f_st3, f_st4, f_st5, f_n, *arrays)

    arrays = [f_h2, w3, up, f_z2, f_h1, wsp1, f_z1, w1, f_img]
    out_shape = [
        shape((total_rows(sets[0]), cin), BF16), shape((total_rows(sets[1]), cin), BF16), shape((8, c3), F32),
        shape((8, c3), F32),
    ] + [shape(t, BF16) for t in shapes]
    scratch = like(arrays) + [
        pltpu.VMEM((most, 512), F32), pltpu.VMEM((total, cin), BF16), pltpu.VMEM((total, c3), F32),
        pltpu.VMEM((guarded, 3 * c3), BF16), pltpu.VMEM((total, c3), F32), pltpu.VMEM((total, c3), BF16),
        pltpu.VMEM((c3, cin), BF16), pltpu.VMEM((9 * c3, c3), BF16), pltpu.VMEM((cin, c3), BF16),
        pltpu.VMEM((8, c3), F32), pltpu.VMEM((8, c3), F32), pltpu.VMEM((16, c3), F32), pltpu.VMEM((16, c3), F32),
        pltpu.SMEM((2, 16), F32), pltpu.VMEM((16, 128), F32),
    ]
    scratch += exchange_shapes((c3, c3), (2, 2), crops)
    scratch += [pltpu.SemaphoreType.DMA((9,)), pltpu.SemaphoreType.DMA((2,))]
    scratch += [pltpu.SemaphoreType.DMA((count,))] * 3 + [pltpu.SemaphoreType.DMA((pairs,))]
    scratch += share_scratch(chunks, bits, share_leave(bits) + [0] * (len(chunks) - SHARE_FIRST))
    grad_b, grad_s, s2, s1, *grads = pl.pallas_call(
        functools.partial(back_one_kernel, sets, total, guarded, crops, (c3, cin), shapes, chunks),
        out_shape=out_shape,
        in_specs=[smem] * 2 + [vmem] * 6 + [hbm] * 13,
        out_specs=[hbm] * len(out_shape),
        scratch_shapes=scratch,
        compiler_params=params(idents[1]),
        name="back_one",
    )(*views, norms_first, f_st1, f_st2, f_st3, s3, f_n, *arrays, g_skip, g_outer2, g_spatial2, g_inner2)
    return grad_b, grad_s, grads, (s1, s2, s3, s4, s5)


def widen_kernel(*refs):
    for src, dst in zip(refs[: len(refs) // 2], refs[len(refs) // 2 :]):
        dst[...] = src[...].astype(F32)


def widen(arrays, steps=8):
    def block(t):
        return pl.BlockSpec((t.shape[0] // steps, t.shape[1]), lambda i: (i, 0))

    return pl.pallas_call(
        widen_kernel,
        grid=(steps,),
        out_shape=[jax.ShapeDtypeStruct(t.shape, F32) for t in arrays],
        in_specs=[block(t) for t in arrays],
        out_specs=[block(t) for t in arrays],
        compiler_params=pltpu.CompilerParams(vmem_limit_bytes=48 * 1024 * 1024),
        name="widen",
    )(*arrays)


def total_rows(m):
    return m.count * m.rows


def shards(
    image_big,
    image_small,
    view_big,
    view_small,
    inner_first,
    spatial_first,
    outer_first,
    norms_first,
    inner_second,
    spatial_second,
    outer_second,
    skip_second,
    norms_second,
    cotangent_big,
    cotangent_small,
):
    c3, c4 = inner_first.shape[1], inner_second.shape[1]
    weights = [
        inner_first,
        spatial_first.reshape(3, 3 * c3, c3),
        outer_first,
        inner_second,
        spatial_second.reshape(9 * c4, c4),
        outer_second,
        skip_second,
    ]
    sets, sizes, got = forward(
        [image_big, image_small], [cotangent_big, cotangent_small], (view_big, view_small), weights, norms_first, norms_second, 0
    )
    grad_b, grad_s, grads, sums = backward(
        sets, got, (view_big, view_small), weights, norms_first, norms_second, *sizes, (1, 2)
    )
    s1, s2, s3, s4, s5 = sums
    sq = got[21]

    def both(parts):
        return jnp.concatenate(
            [jnp.stack([t[g] + t[g + 1], t[0] + t[1]]) for t, g in parts], axis=1
        )

    g_skip, g_outer2, g_spatial2, g_inner2, g_outer1, g_spatial1, g_inner1 = widen(grads)
    results = [
        got[11][m.out0 : m.out0 + m.count * m.out].reshape(m.count, m.half, 8, -1)[:, :, : m.half]
        for m in sets
    ]
    gradients = [
        t.reshape(image.shape[0], image.shape[1], 16, -1)[:, :, : image.shape[2]]
        for t, image in ((grad_b, image_big), (grad_s, image_small))
    ]
    return (
        results[0],
        results[1],
        gradients[0],
        gradients[1],
        g_inner1,
        g_spatial1.reshape(spatial_first.shape),
        g_outer1,
        both(((s1, 2), (s2, 2), (s3, 2))),
        g_inner2,
        g_spatial2.reshape(spatial_second.shape),
        g_outer2,
        g_skip,
        both(((s4, 2), (s5, 2), (sq, 2), (sq, 4))),
    )


def solution(mesh):
    maps = P("crops", "rows", None, None)
    whole = P(("crops", "rows"), None, None, None)
    in_specs = (maps, maps, P("crops"), P("crops")) + (P(),) * 9 + (whole, whole)
    out_specs = (whole, whole, maps, maps) + (P(),) * 9
    return jax.shard_map(shards, mesh=mesh, in_specs=in_specs, out_specs=out_specs, check_vma=False)
```

```python
import functools

import jax
import jax.numpy as jnp
from jax import lax
from jax.experimental import pallas as pl
from jax.experimental.pallas import tpu as pltpu
from jax.sharding import PartitionSpec as P

HIGH = lax.Precision.HIGHEST
EPS = 1e-05
MESH = pl.DeviceIdType.MESH
F32 = jnp.float32
BF16 = jnp.bfloat16


class Maps:
    def __init__(self, count, edge, row0, crop0, guard0, out0):
        self.count, self.edge = count, edge
        self.row0, self.crop0, self.guard0, self.out0 = row0, crop0, guard0, out0
        self.rows = edge * 16
        self.guard = (edge + 1) * 16
        self.half = edge // 2
        self.out = self.half * 8
        self.pixels = edge * edge


def geometry(nb, eb, ns, es):
    big = Maps(nb, eb, 0, 0, 16, 0)
    small = Maps(ns, es, nb * big.rows, nb, 16 + nb * big.guard, nb * big.out)
    total = small.row0 + ns * small.rows
    guarded = small.guard0 + ns * small.guard
    out = small.out0 + ns * small.out
    return (big, small), total, guarded, out


def al(x, m=16):
    return x if isinstance(x, int) else pl.multiple_of(x, m)


def span(start, size, m=16):
    return pl.ds(al(start, m), size)


def repeat(count, body):
    def step(i, carry):
        body(i)
        return carry

    lax.fori_loop(0, count, step, 0)


def mm(a, b):
    return jnp.dot(a, b, preferred_element_type=F32)


def mm_nt(a, b):
    return lax.dot_general(a, b, (((1,), (1,)), ((), ())), preferred_element_type=F32)


def mm_tn(a, b):
    return lax.dot_general(a, b, (((0,), (0,)), ((), ())), preferred_element_type=F32)


CA = 0.7978845608028654
CB = 0.7978845608028654 * 0.044715


def act(u):
    t = jnp.tanh(u * (CA + CB * (u * u)))
    return 0.5 * u * (1.0 + t)


def act_slope(u):
    s = u * u
    t = jnp.tanh(u * (CA + CB * s))
    rise = (0.5 * u) * (CA + (3.0 * CB) * s)
    return 0.5 * (1.0 + t) + (1.0 - t * t) * rise


def act_both(u):
    s = u * u
    t = jnp.tanh(u * (CA + CB * s))
    hu = 0.5 * u
    lift = 0.5 * (1.0 + t)
    slope = lift + (1.0 - t * t) * (hu * (CA + (3.0 * CB) * s))
    return u * lift, slope


def keep(width, pitch, edge):
    return lax.broadcasted_iota(jnp.int32, (pitch, width), 0) < edge


def masked(x, mask):
    rows = x.reshape(x.shape[0] // mask.shape[0], mask.shape[0], x.shape[1])
    return jnp.where(mask[None], rows, 0.0).reshape(x.shape)


def tile_sum(x):
    return jnp.sum(x.reshape(x.shape[0] // 8, 8, x.shape[1]), axis=0)


def pieces(width):
    return (4, width // 4) if width >= 512 else (width // 128, 128)


class Links:
    def __init__(self, crops, near, far, near_s, near_r, far_s, far_r):
        self.group = 4 if crops % 4 == 0 else 1
        self.outers = crops // self.group
        self.k, self.r = lax.axis_index("crops"), lax.axis_index("rows")
        inner, self.outer = lax.rem(self.k, self.group), self.k // self.group
        self.wide = 2 * self.group
        self.me = inner * 2 + self.r
        self.inner = inner
        self.peers, self.others, self.places = [], [], []
        for d in range(1, self.wide):
            p = lax.rem(self.me + d, self.wide)
            self.peers.append((self.outer * self.group + p // 2, lax.rem(p, 2)))
            self.places.append(p // 2)
        for d in range(1, self.outers):
            self.others.append((lax.rem(self.outer + d, self.outers) * self.group + inner, self.r))
        self.near, self.far = near, far
        self.sems = (near_s, near_r, far_s, far_r)
        self.live = {}

    def greet(self, extra=()):
        barrier = pltpu.get_barrier_semaphore()
        peers = self.peers + self.others + list(extra)
        for peer in peers:
            pl.semaphore_signal(barrier, inc=1, device_id=peer, device_id_type=MESH)
        pl.semaphore_wait(barrier, len(peers))

    def send_near(self, e, block):
        self.near[e][self.me] = block[...]
        self.live[e, 0] = []
        for d, peer in enumerate(self.peers):
            copy = pltpu.make_async_remote_copy(
                src_ref=block,
                dst_ref=self.near[e].at[self.me],
                send_sem=self.sems[0].at[e, d],
                recv_sem=self.sems[1].at[e, d],
                device_id=peer,
                device_id_type=MESH,
            )
            copy.start()
            self.live[e, 0].append(copy)

    def piece(self, j):
        return pl.ds(pl.multiple_of(j * 128, 128), 128)

    def send_pieces(self, e, block):
        self.near[e][self.me] = block[:, self.piece(self.inner)]
        self.live[e, 0] = []
        for d, peer in enumerate(self.peers):
            copy = pltpu.make_async_remote_copy(
                src_ref=block.at[:, self.piece(self.places[d])],
                dst_ref=self.near[e].at[self.me],
                send_sem=self.sems[0].at[e, d],
                recv_sem=self.sems[1].at[e, d],
                device_id=peer,
                device_id_type=MESH,
            )
            copy.start()
            self.live[e, 0].append(copy)

    def collect(self, e, whole, sems, at):
        place = whole.at[:, self.piece(self.inner)]
        self.live[e, 2] = []
        for d in range(1, self.group):
            copy = pltpu.make_async_remote_copy(
                src_ref=place,
                dst_ref=place,
                send_sem=sems[0].at[at, d - 1],
                recv_sem=sems[1].at[at, d - 1],
                device_id=(self.outer * self.group + lax.rem(self.inner + d, self.group), self.r),
                device_id_type=MESH,
            )
            copy.start()
            self.live[e, 2].append(copy)
        for copy in self.live[e, 2]:
            copy.wait_recv()

    def wait_near(self, e):
        for copy in self.live[e, 0]:
            copy.wait_recv()

    def send_far(self, e):
        self.live[e, 1] = []
        place = self.far[e].at[self.outer]
        for d, peer in enumerate(self.others):
            copy = pltpu.make_async_remote_copy(
                src_ref=place,
                dst_ref=place,
                send_sem=self.sems[2].at[e, d],
                recv_sem=self.sems[3].at[e, d],
                device_id=peer,
                device_id_type=MESH,
            )
            copy.start()
            self.live[e, 1].append(copy)

    def wait_far(self, e):
        for copy in self.live[e, 1]:
            copy.wait_recv()

    def finish(self):
        for copies in self.live.values():
            for copy in copies:
                copy.wait_send()


def fold_moments(buf, tallies, count, scale):
    sums, total = buf[0, 0:8, :], tallies[0]
    for i in range(1, count):
        sums = sums + buf[i, 0:8, :]
        total = total + tallies[i]
    mean = sums * (1.0 / jnp.maximum(total * scale, 1.0))
    spread = None
    for i in range(count):
        n = tallies[i] * scale
        apart = buf[i, 0:8, :] * (1.0 / jnp.maximum(n, 1.0)) - mean
        term = buf[i, 8:16, :] + n * apart * apart
        spread = term if spread is None else spread + term
    return sums, spread, total


def fold_sums(buf, count):
    total = buf[0]
    for i in range(1, count):
        total = total + buf[i]
    return total


def exchange_shapes(widths, tiles, crops, cut=()):
    group = 4 if crops % 4 == 0 else 1
    outers = crops // group
    blocks, near, far = [], [], []
    for at, (width, tile) in enumerate(zip(widths, tiles)):
        lanes = pieces(width)[1]
        blocks.append(pltpu.VMEM((8 * tile, lanes), F32))
        if at in cut:
            lanes = 128
        near.append(pltpu.VMEM((2 * group, 8 * tile, lanes), F32))
        far.append(pltpu.VMEM((outers, 8 * tile, lanes), F32))
    e = len(widths)
    sems = [
        pltpu.SemaphoreType.DMA((e, 2 * group - 1)),
        pltpu.SemaphoreType.DMA((e, 2 * group - 1)),
        pltpu.SemaphoreType.DMA((e, max(outers - 1, 1))),
        pltpu.SemaphoreType.DMA((e, max(outers - 1, 1))),
    ]
    return blocks + near + far + sems


def take(refs, count):
    return list(refs[:count]), refs[count:]


def pack(block, tile, rows, width):
    count, lanes = pieces(width)
    for q in range(count):
        for v in range(2):
            block[tile * 8 + 2 * q + v : tile * 8 + 2 * q + v + 1, :] = rows[v][:, q * lanes : (q + 1) * lanes]


def unpack(table, row, tile, width):
    count, lanes = pieces(width)
    for q in range(count):
        table[row : row + 2, q * lanes : (q + 1) * lanes] = tile[2 * q : 2 * q + 2, :]


def crop_stats(ref, row0, rows, step, width, edge, pitch, pixels, crop, cs, cm, col0=0):
    mask = keep(width, pitch, edge)
    zero = jnp.zeros((8, width), F32)
    cols = pl.ds(col0, width) if isinstance(col0, int) else pl.ds(pl.multiple_of(col0, 128), width)
    near = min(8, edge)
    first = masked(ref[span(row0, 8, 8), cols], keep(width, 8, edge))
    pivot = jnp.sum(first, axis=0, keepdims=True) * (1.0 / near)

    def tile(i, acc):
        d = masked(ref[span(row0 + i * step, step, 8), cols] - pivot, mask)
        return acc[0] + tile_sum(d), acc[1] + tile_sum(d * d)

    if rows == step:
        s, m = tile(0, (zero, zero))
    else:
        s, m = lax.fori_loop(0, rows // step, tile, (zero, zero))
    s = jnp.sum(s, axis=0, keepdims=True)
    m = jnp.sum(m, axis=0, keepdims=True)
    cs[pl.ds(crop, 1), cols] = s + pivot * float(pixels)
    cm[pl.ds(crop, 1), cols] = jnp.maximum(m - s * s * (1.0 / pixels), 0.0)


def local_moments(block, cs, cm, wcol, width, scale, tally=False):
    s, m = cs[:, 0:width], cm[:, 0:width]
    pix = wcol[:, 2:3] * scale
    mean_c = s * (1.0 / pix)
    sums, squares, tallies = [], [], []
    for v in range(2):
        w = wcol[:, v : v + 1]
        total = jnp.sum(w * s, axis=0, keepdims=True)
        n = jnp.sum(w * pix, axis=0, keepdims=True)
        apart = mean_c - total * (1.0 / jnp.maximum(n, 1.0))
        squares.append(jnp.sum(w * (m + pix * apart * apart), axis=0, keepdims=True))
        sums.append(total)
        tallies.append(n)
    pack(block, 0, sums, width)
    pack(block, 1, squares, width)
    if tally:
        lanes = pieces(width)[1]
        for q in range(4):
            for v in range(2):
                block[16 + 2 * q + v : 17 + 2 * q + v, :] = jnp.broadcast_to(tallies[v], (1, lanes))


def local_sums(block, parts, wcol, width):
    for tile, part in enumerate(parts):
        s = part[:, 0:width]
        pack(block, tile, [jnp.sum(wcol[:, v : v + 1] * s, axis=0, keepdims=True) for v in range(2)], width)


def view_tables(sets, core, views, wv, wcol):
    row = lax.broadcasted_iota(jnp.int32, wcol.shape, 0)
    lane = lax.broadcasted_iota(jnp.int32, wcol.shape, 1)
    table = jnp.where(lane == 2, 1.0, 0.0)
    for m, view in zip(sets, views):
        for c in range(m.count):
            second = view[core * m.count + c].astype(F32)
            pair = (1.0 - second, second, float(m.pixels))
            for v in range(3):
                table = jnp.where((row == m.crop0 + c) & (lane == v), pair[v], table)
            wv[0, m.crop0 + c] = pair[0]
            wv[1, m.crop0 + c] = pair[1]
    wcol[...] = table


def by_view(wv, crop, pair):
    return wv[0, crop] * pair[0:1, :] + wv[1, crop] * pair[1:2, :]


FWD_WIDTHS = (256, 256, 1024, 512, 2048, 512, 2048, 2048)


def forward_kernel(sets, total, guarded, outs, crops, dims, *refs):
    c3, cin, c4, cout = dims
    (
        vb, vs, norms1, norms2,
        img_b, img_s, cot_b, cot_s, w1_h, wsp1_h, w3_h, w4_h, w5_h, w6_h, w7_h,
    ), refs = refs[:15], refs[15:]
    (
        o_img, o_z1, o_h1, o_z2, o_h2, o_blk, o_z4, o_x5, o_z5, o_h5, o_xe, o_res, o_d6, o_d7,
        o_st1, o_st2, o_st3, o_st4, o_st7, o_st5, o_st6, o_sq, o_tally,
    ), refs = refs[:23], refs[23:]
    (
        img, z1, h1, z2, h2, zt, blk, eb, z4, xe, z7, hp, x5, z5, h5, z6, cot,
        w1, wsp1, w3, w4, w5, w6, w7, cs, cm, ck,
        st1, st2, st3, st4, st7, st5, st6, sq, tally_v, wv, wcol,
    ), refs = refs[:38], refs[38:]
    e = len(FWD_WIDTHS)
    blocks, refs = take(refs, e)
    near, refs = take(refs, e)
    far, refs = take(refs, e)
    ns_, nr_, fs_, fr_ = refs[:4]
    whole6, whole7, back_s, back_r = refs[4:8]
    load_sem, img_sem, img_send, img_recv, out_sem = refs[8:]
    links = Links(crops, near, far, ns_, nr_, fs_, fr_)
    k, core = links.k, links.r
    sibling = (k, 1 - core)
    f = F32

    loads = []
    for i, (src, dst) in enumerate(
        ((w1_h, w1), (wsp1_h, wsp1), (w3_h, w3), (w4_h, w4), (w5_h, w5), (w6_h, w6), (w7_h, w7),
            (cot_b, cot.at[0 : sets[1].out0]), (cot_s, cot.at[sets[1].out0 : outs]))
    ):
        loads.append(pltpu.make_async_copy(src, dst, load_sem.at[i]))
    own, swaps = [], []
    for at, (m, src) in enumerate(zip(sets, (img_b, img_s))):
        part = m.rows // 2
        for c in range(m.count):
            i = m.crop0 + c
            place = img.at[span(m.row0 + c * m.rows + core * part, part)]
            own.append(
                pltpu.make_async_copy(
                    src.at[span((core * m.count + c) * part, part)], place, img_sem.at[i]
                )
            )
            swaps.append(
                pltpu.make_async_remote_copy(
                    src_ref=src.at[span(((1 - core) * m.count + c) * part, part)],
                    dst_ref=place,
                    send_sem=img_send.at[i],
                    recv_sem=img_recv.at[i],
                    device_id=sibling,
                    device_id_type=MESH,
                )
            )
    for copy in own:
        copy.start()
    loads[0].start()
    links.greet()
    for copy in swaps:
        copy.start()

    view_tables(sets, core, (vb, vs), wv, wcol)
    out_copies = []

    def put(src, dst):
        copy = pltpu.make_async_copy(src, dst, out_sem.at[len(out_copies)])
        copy.start()
        out_copies.append(copy)

    for ref in (cs, cm, ck):
        ref[...] = jnp.zeros(ref.shape, f)
    for block in blocks:
        block[...] = jnp.zeros(block.shape, f)
    h1[0:16, :] = jnp.zeros((16, 3 * c3), BF16)
    for m in sets:
        for c in range(m.count):
            at = m.guard0 + c * m.guard + m.rows
            h1[at : at + 16, :] = jnp.zeros((16, 3 * c3), BF16)

    def near_tallies():
        return [near[0][i, 16:24, 0:1] for i in range(links.wide)]

    def far_tallies():
        return [far[0][i, 16:24, 0:1] for i in range(links.outers)]

    def meet_near(i, scale):
        links.wait_near(i)
        sums, spread, n = fold_moments(near[i], near_tallies(), links.wide, scale)
        place = far[i].at[links.outer]
        place[0:8, :] = sums
        place[8:16, :] = spread
        if i == 0:
            place[16:24, :] = jnp.broadcast_to(n, (8, near[0].shape[2]))
        links.send_far(i)

    def meet_far(i, scale, table, width):
        links.wait_far(i)
        sums, spread, n = fold_moments(far[i], far_tallies(), links.outers, scale)
        over = 1.0 / (n * scale)
        mean = sums * over
        inverse = lax.rsqrt(spread * over + EPS)
        unpack(table, 0, mean, width)
        unpack(table, 2, inverse, width)
        if i == 0:
            tally_v[...] = jnp.broadcast_to(n, (8, 128))

    loads[0].wait()
    for m in sets:

        def pair(p, m=m):
            r = m.row0 + p * 2 * m.rows
            for j in range(2):
                own[m.crop0 + 2 * p + j].wait()
                swaps[m.crop0 + 2 * p + j].wait_recv()
            z1[span(r, 2 * m.rows), :] = mm(img[span(r, 2 * m.rows), :], w1[...])
            for j in range(2):
                crop_stats(z1, r + j * m.rows, m.rows, m.rows // 2, c3, m.edge, 16, m.pixels, m.crop0 + 2 * p + j, cs, cm)

        for p in range(m.count // 2):
            pair(p)
            if m is sets[0] and p == 0:
                for copy in loads[1:]:
                    copy.start()
    local_moments(blocks[0], cs, cm, wcol, c3, 1.0, True)
    links.send_near(0, blocks[0])
    put(img, o_img)
    put(z1, o_z1)
    loads[1].wait()
    meet_near(0, 1.0)
    meet_far(0, 1.0, st1, c3)

    for m in sets:

        def pair(p, m=m):
            r = m.row0 + p * 2 * m.rows
            g = m.guard0 + p * 2 * m.guard
            for j in range(2):
                crop = m.crop0 + 2 * p + j
                mean = by_view(wv, crop, st1[0:2, :])
                scale = by_view(wv, crop, st1[2:4, :]) * norms1[0:1, 0:c3]
                shift = norms1[1:2, 0:c3] - mean * scale
                step = m.rows // 2
                mask = keep(c3, 16, m.edge)

                def tile(i):
                    z = z1[span(r + j * m.rows + i * step, step), :]
                    h = masked(act(z * scale + shift), mask)
                    rows = span(g + j * m.guard + i * step, step)
                    h1[rows, 0:c3] = pltpu.roll(h, 1, 0).astype(BF16)
                    h1[rows, c3 : 2 * c3] = h.astype(BF16)
                    h1[rows, 2 * c3 : 3 * c3] = pltpu.roll(h, step - 1, 0).astype(BF16)

                repeat(2, tile)
            size = 2 * m.rows + 16
            z = mm(h1[span(g - 16, size), :], wsp1[0]) + mm(h1[span(g, size), :], wsp1[1])
            z = z + mm(h1[span(g + 16, size), :], wsp1[2])
            z2[span(r, m.rows), :] = z[0 : m.rows]
            z2[span(r + m.rows, m.rows), :] = z[m.guard : m.guard + m.rows]
            for j in range(2):
                crop_stats(z2, r + j * m.rows, m.rows, m.rows // 2, c3, m.edge, 16, m.pixels, m.crop0 + 2 * p + j, cs, cm)

        repeat(m.count // 2, pair)
    local_moments(blocks[1], cs, cm, wcol, c3, 1.0)
    links.send_near(1, blocks[1])
    put(h1, o_h1)
    put(z2, o_z2)
    loads[2].wait()
    meet_near(1, 1.0)
    meet_far(1, 1.0, st2, c3)

    for m in sets:

        def pair(p, m=m):
            r = m.row0 + p * 2 * m.rows
            for j in range(2):
                crop = m.crop0 + 2 * p + j
                mean = by_view(wv, crop, st2[0:2, :])
                scale = by_view(wv, crop, st2[2:4, :]) * norms1[0:1, c3 : 2 * c3]
                shift = norms1[1:2, c3 : 2 * c3] - mean * scale
                step = m.rows // 2

                def tile(i):
                    rows = span(r + j * m.rows + i * step, step)
                    h2[rows, :] = act(z2[rows, :] * scale + shift).astype(BF16)

                repeat(2, tile)
            zt[0 : 2 * m.rows, :] = mm(h2[span(r, 2 * m.rows), :], w3[...])
            for j in range(2):
                crop_stats(zt, j * m.rows, m.rows, 32, cin, m.edge, 16, m.pixels, m.crop0 + 2 * p + j, cs, cm)

        repeat(m.count // 2, pair)
    local_moments(blocks[2], cs, cm, wcol, cin, 1.0)
    links.send_near(2, blocks[2])
    put(h2, o_h2)
    loads[3].wait()
    meet_near(2, 1.0)
    meet_far(2, 1.0, st3, cin)

    for m in sets:

        def pair(p, m=m):
            r = m.row0 + p * 2 * m.rows
            zt[0 : 2 * m.rows, :] = mm(h2[span(r, 2 * m.rows), :], w3[...])
            for j in range(2):
                crop = m.crop0 + 2 * p + j
                mean = by_view(wv, crop, st3[0:2, :])
                scale = by_view(wv, crop, st3[2:4, :]) * norms1[0:1, 2 * c3 :]
                shift = norms1[1:2, 2 * c3 :] - mean * scale

                def tile(i):
                    here = span(j * m.rows + i * 32, 32)
                    rows = span(r + j * m.rows + i * 32, 32)
                    u = zt[here, :] * scale + shift + img[rows, :].astype(f)
                    b = act(u)
                    blk[rows, :] = b.astype(BF16)
                    for q in range(cin // 128):
                        eb[q, span(j * m.rows // 2 + i * 16, 16), :] = b[0:16, q * 128 : (q + 1) * 128]

                repeat(m.rows // 32, tile)
            for q in range(cin // 128):
                picked = [eb[q, pl.ds(i * 16, 8, stride=2), :] for i in range(2 * m.half)]
                xe[span(m.out0 + p * 2 * m.out, 2 * m.out), q * 128 : (q + 1) * 128] = jnp.concatenate(
                    picked, axis=0
                ).astype(BF16)
            z4[span(r, 2 * m.rows), :] = mm(blk[span(r, 2 * m.rows), :], w4[...])
            for j in range(2):
                crop_stats(z4, r + j * m.rows, m.rows, 32, c4, m.edge, 16, m.pixels, m.crop0 + 2 * p + j, cs, cm)

        repeat(m.count // 2, pair)
    local_moments(blocks[3], cs, cm, wcol, c4, 1.0)
    links.send_near(3, blocks[3])
    put(blk, o_blk)
    put(z4, o_z4)
    put(xe, o_xe)
    loads[6].wait()

    def wide_product(a, w, z):
        def columns(n):
            cols = pl.ds(pl.multiple_of(n * 512, 512), 512)
            z[:, cols] = mm(a[...], w[:, cols])

        repeat(cout // 512, columns)

    def wide_stats(z):
        for m in sets:

            def crop_(c, m=m):
                def columns(n):
                    crop_stats(
                        z, m.out0 + c * m.out, m.out, m.out, 512, m.half, 8, m.half * m.half,
                        m.crop0 + c, cs, cm, n * 512,
                    )

                repeat(cout // 512, columns)

            repeat(m.count, crop_)

    wide_product(xe, w7, z7)
    meet_near(3, 1.0)
    wide_stats(z7)
    local_moments(blocks[4], cs, cm, wcol, cout, 0.25)
    links.send_near(4, blocks[4])
    meet_far(3, 1.0, st4, c4)

    loads[4].wait()
    lots = c4 // 128
    hp[:, 0:24, :] = jnp.zeros((lots, 24, 128), f)
    for m in sets:

        def pair(p, m=m):
            r = m.row0 + p * 2 * m.rows
            for j in range(2):
                crop = m.crop0 + 2 * p + j
                mean = by_view(wv, crop, st4[0:2, :])
                scale = by_view(wv, crop, st4[2:4, :]) * norms2[0:1, 0:c4]
                shift = norms2[1:2, 0:c4] - mean * scale
                mask = keep(c4, 16, m.edge)
                base = 24 + j * m.guard
                hp[:, base + m.rows : base + m.guard, :] = jnp.zeros((lots, 16, 128), f)

                def tile(i):
                    z = z4[span(r + j * m.rows + i * 32, 32), :]
                    h = masked(act(z * scale + shift), mask)
                    for q in range(lots):
                        hp[q, span(base + i * 32, 32, 8), :] = h[:, q * 128 : (q + 1) * 128]

                repeat(m.rows // 32, tile)
            for a in range(3):
                for b in range(3):
                    for q in range(lots):
                        picked = []
                        for j in range(2):
                            for i in range(m.half):
                                at = 24 + j * m.guard + (2 * i + a - 1) * 16 + b - 1
                                picked.append(hp[q, pl.ds(at, 8, stride=2), :])
                        tap = (3 * a + b) * c4 + q * 128
                        x5[span(m.out0 + p * 2 * m.out, 2 * m.out), tap : tap + 128] = jnp.concatenate(
                            picked, axis=0
                        ).astype(BF16)

        repeat(m.count // 2, pair)
    z5[...] = jnp.zeros(z5.shape, f)

    def taps(t):
        part = pl.ds(pl.multiple_of(t * 3 * c4, 128), 3 * c4)
        z5[...] += mm(x5[:, part], w5[part, :])

    repeat(3, taps)
    for m in sets:

        def crop_(c, m=m):
            crop_stats(z5, m.out0 + c * m.out, m.out, m.out, c4, m.half, 8, m.half * m.half, m.crop0 + c, cs, cm)

        repeat(m.count, crop_)
    local_moments(blocks[5], cs, cm, wcol, c4, 0.25)
    links.send_near(5, blocks[5])
    put(x5, o_x5)
    put(z5, o_z5)
    meet_near(4, 0.25)
    meet_near(5, 0.25)
    meet_far(4, 0.25, st7, cout)
    meet_far(5, 0.25, st5, c4)

    loads[5].wait()
    for m in sets:

        def pair(p, m=m):
            o = m.out0 + p * 2 * m.out
            halves = []
            for j in range(2):
                crop = m.crop0 + 2 * p + j
                mean = by_view(wv, crop, st5[0:2, :])
                scale = by_view(wv, crop, st5[2:4, :]) * norms2[0:1, c4 : 2 * c4]
                z = z5[span(o + j * m.out, m.out, 8), :]
                halves.append(act(z * scale + (norms2[1:2, c4 : 2 * c4] - mean * scale)))
            h5[span(o, 2 * m.out), :] = jnp.concatenate(halves, axis=0).astype(BF16)

        repeat(m.count // 2, pair)
    wide_product(h5, w6, z6)
    wide_stats(z6)
    local_moments(blocks[6], cs, cm, wcol, cout, 0.25)
    links.send_pieces(6, blocks[6])
    put(h5, o_h5)
    loads[7].wait()
    loads[8].wait()

    def center(ms):
        for m in ms:

            def crop_(c, m=m):
                def columns(n):
                    cols = pl.ds(pl.multiple_of(n * 512, 512), 512)
                    rows = span(m.out0 + c * m.out, m.out, 8)
                    mean = by_view(wv, m.crop0 + c, st7[0:2, cols])
                    z7[rows, cols] = (z7[rows, cols] - mean) * by_view(wv, m.crop0 + c, st7[2:4, cols])

                repeat(cout // 512, columns)

            repeat(m.count, crop_)

    center(sets[:1])
    meet_near(6, 0.25)
    center(sets[1:])
    links.wait_far(6)
    sums, spread, n = fold_moments(far[6], far_tallies(), links.outers, 0.25)
    over = 4.0 / n
    here = links.piece(links.inner)
    whole6[0:8, here] = sums * over
    whole6[8:16, here] = lax.rsqrt(spread * over + EPS)
    links.collect(6, whole6, (back_s, back_r), 0)
    for t in range(2):
        unpack(st6, 2 * t, whole6[8 * t : 8 * t + 8, :], cout)

    out_copies[6].wait()
    g6, g7 = 2 * c4, 2 * c4 + cout
    lanes = 512
    for m in sets:

        def pair(p, m=m):
            o = m.out0 + p * 2 * m.out

            def columns(n):
                cols = pl.ds(pl.multiple_of(n * lanes, lanes), lanes)
                cols6 = pl.ds(pl.multiple_of(g6 + n * lanes, lanes), lanes)
                cols7 = pl.ds(pl.multiple_of(g7 + n * lanes, lanes), lanes)
                c = cot[span(o, 2 * m.out), cols].astype(f)
                mask = keep(lanes, 8, m.half)
                found = []
                for j in range(2):
                    crop = m.crop0 + 2 * p + j
                    rows = span(o + j * m.out, m.out, 8)
                    n6 = (z6[rows, cols] - by_view(wv, crop, st6[0:2, cols])) * by_view(wv, crop, st6[2:4, cols])
                    n7 = z7[rows, cols]
                    z6[rows, cols] = n6
                    u = n6 * norms2[0:1, cols6] + n7 * norms2[0:1, cols7] + (norms2[1:2, cols6] + norms2[1:2, cols7])
                    a, slope = act_both(u)
                    found.append(a)
                    up = masked(slope * c[j * m.out : (j + 1) * m.out], mask)
                    z4[span(n * outs + o + j * m.out, m.out, 8), :] = up
                    for to, part in ((cs, up), (cm, up * n6), (ck, up * n7)):
                        to[pl.ds(crop, 1), cols] = jnp.sum(tile_sum(part), axis=0, keepdims=True)
                w6[span(o, 2 * m.out), cols] = jnp.concatenate(found, axis=0).astype(BF16)

            repeat(cout // lanes, columns)

        repeat(m.count // 2, pair)
    local_sums(blocks[7], (cs, cm, ck), wcol, cout)
    links.send_pieces(7, blocks[7])
    put(w6.at[0:outs], o_res)
    links.wait_near(7)
    far[7][links.outer] = fold_sums(near[7], links.wide)
    links.send_far(7)
    links.wait_far(7)
    whole7[:, here] = fold_sums(far[7], links.outers)
    links.collect(7, whole7, (back_s, back_r), 1)
    for t in range(3):
        unpack(sq, 2 * t, whole7[8 * t : 8 * t + 8, :], cout)

    for m in sets:

        def pair(p, m=m):
            o = m.out0 + p * 2 * m.out

            def columns(n):
                cols = pl.ds(pl.multiple_of(n * lanes, lanes), lanes)
                mask = keep(lanes, 8, m.half)
                got6, got7 = [], []
                for j in range(2):
                    crop = m.crop0 + 2 * p + j
                    rows = span(o + j * m.out, m.out, 8)
                    up = z4[span(n * outs + o + j * m.out, m.out, 8), :]
                    over = wv[0, crop] * (4.0 / tally_v[0:1, 0:1]) + wv[1, crop] * (4.0 / tally_v[1:2, 0:1])
                    level = by_view(wv, crop, sq[0:2, cols]) * over
                    for got, z, st, at, t in ((got6, z6, st6, g6, 2), (got7, z7, st7, g7, 4)):
                        inv = by_view(wv, crop, st[2:4, cols])
                        gain = inv * norms2[0:1, pl.ds(pl.multiple_of(at + n * lanes, lanes), lanes)]
                        tilt = by_view(wv, crop, sq[t : t + 2, cols]) * over
                        got.append(masked(gain * (up - level - z[rows, cols] * tilt), mask))
                w7[span(o, 2 * m.out), cols] = jnp.concatenate(got6, axis=0).astype(BF16)
                w7[span(cin // 2 + o, 2 * m.out), cols] = jnp.concatenate(got7, axis=0).astype(BF16)

            repeat(cout // lanes, columns)

        repeat(m.count // 2, pair)
    put(w7.at[0:outs], o_d6)
    put(w7.at[cin // 2 : cin // 2 + outs], o_d7)
    for src, dst in (
        (st1, o_st1), (st2, o_st2), (st3, o_st3), (st4, o_st4), (st7, o_st7), (st5, o_st5), (st6, o_st6),
        (sq, o_sq), (tally_v, o_tally),
    ):
        put(src, dst)
    links.finish()
    for copy in swaps:
        copy.wait_send()
    for i, copy in enumerate(out_copies):
        if i != 6:
            copy.wait()


def flat_rows(tensor, pitch):
    n, h, w, c = tensor.shape
    return jnp.pad(tensor, ((0, 0), (0, 0), (0, pitch - w), (0, 0))).reshape(n * h * pitch, c)


def forward(images, cots, views, w, norms_first, norms_second, ident):
    crops = lax.axis_size("crops")
    nb, ns = images[0].shape[0] // 2, images[1].shape[0] // 2
    sets, total, guarded, outs = geometry(nb, images[0].shape[2], ns, images[1].shape[2])
    w1, wsp1, w3, w4, w5, w6, w7 = w
    cin, c3 = w1.shape
    c4, cout = w6.shape
    smem, vmem = pl.BlockSpec(memory_space=pltpu.SMEM), pl.BlockSpec(memory_space=pltpu.VMEM)
    hbm = pl.BlockSpec(memory_space=pl.ANY)
    shape = jax.ShapeDtypeStruct
    out_shape = [
        shape((total, cin), BF16), shape((total, c3), F32), shape((guarded, 3 * c3), BF16), shape((total, c3), F32),
        shape((total, c3), BF16), shape((total, cin), BF16), shape((total, c4), F32), shape((outs, 9 * c4), BF16),
        shape((outs, c4), F32), shape((outs, c4), BF16), shape((outs, cin), BF16), shape((outs, cout), BF16),
        shape((outs, cout), BF16), shape((outs, cout), BF16),
        shape((8, c3), F32), shape((8, c3), F32), shape((8, cin), F32), shape((8, c4), F32), shape((8, cout), F32),
        shape((8, c4), F32), shape((8, cout), F32), shape((8, cout), F32), shape((8, 128), F32),
    ]
    most = 2 * sets[0].rows
    scratch = [
        pltpu.VMEM((total, cin), BF16), pltpu.VMEM((total, c3), F32), pltpu.VMEM((guarded, 3 * c3), BF16),
        pltpu.VMEM((total, c3), F32), pltpu.VMEM((total, c3), BF16), pltpu.VMEM((most, cin), F32),
        pltpu.VMEM((total, cin), BF16), pltpu.VMEM((cin // 128, most // 2, 128), F32), pltpu.VMEM((total, c4), F32),
        pltpu.VMEM((outs, cin), BF16), pltpu.VMEM((outs, cout), F32), pltpu.VMEM((c4 // 128, 24 + 2 * sets[0].guard, 128), F32),
        pltpu.VMEM((outs, 9 * c4), BF16), pltpu.VMEM((outs, c4), F32),
        pltpu.VMEM((outs, c4), BF16), pltpu.VMEM((outs, cout), F32), pltpu.VMEM((outs, cout), BF16),
    ]
    scratch += [pltpu.VMEM(t.shape, BF16) for t in w]
    scratch += [pltpu.VMEM((16, cout), F32)] * 3
    scratch += [pltpu.VMEM((8, n), F32) for n in (c3, c3, cin, c4, cout, c4, cout, cout, 128)]
    scratch += [pltpu.SMEM((2, 16), F32), pltpu.VMEM((16, 128), F32)]
    scratch += exchange_shapes(FWD_WIDTHS, (3, 2, 2, 2, 2, 2, 2, 3), crops, (6, 7))
    scratch += [pltpu.VMEM((16, cout // 4), F32), pltpu.VMEM((24, cout // 4), F32)]
    scratch += [pltpu.SemaphoreType.DMA((2, 3))] * 2
    scratch += [
        pltpu.SemaphoreType.DMA((9,)), pltpu.SemaphoreType.DMA((nb + ns,)), pltpu.SemaphoreType.DMA((nb + ns,)),
        pltpu.SemaphoreType.DMA((nb + ns,)), pltpu.SemaphoreType.DMA((23,)),
    ]
    got = pl.pallas_call(
        functools.partial(forward_kernel, sets, total, guarded, outs, crops, (c3, cin, c4, cout)),
        out_shape=out_shape,
        in_specs=[smem, smem, vmem, vmem] + [hbm] * 11,
        out_specs=[hbm] * len(out_shape),
        scratch_shapes=scratch,
        compiler_params=pltpu.CompilerParams(
            collective_id=ident, has_side_effects=True, vmem_limit_bytes=63 * 1024 * 1024
        ),
        name="forward",
    )(
        *views, norms_first, norms_second,
        flat_rows(images[0], 16), flat_rows(images[1], 16),
        *[flat_rows(t, 8) for t in cots], *w,
    )
    return sets, (total, guarded, outs), got


def share_plan(shapes, cuts):
    chunks = []
    for at, (height, width) in enumerate(shapes):
        down, across = cuts[at]
        half, high = width // 2 // across, height // down
        for c in range(down):
            for p in range(across):
                chunks.append((at, c * high, high, p * half, half))
    return chunks


class Share:
    def __init__(self, shapes, chunks, orders, bits, links, sources, outs, acc, recv0, recvs, sems, begin, leave):
        self.shapes, self.chunks, self.bits = shapes, chunks, bits
        self.k, self.core = links.k, links.r
        self.sources, self.outs, self.acc, self.recv0, self.recvs = sources, outs, acc, recv0, recvs
        self.send_sem, self.recv_sem, self.load_sem, self.store_sem = sems
        self.sibling = (self.k, 1 - self.core)
        self.total = 2 * bits + 2
        self.live, self.loads, self.stores, self.begin, self.leave, self.at = {}, {}, {}, begin, leave, 0
        digit = [lax.rem(self.k // (1 << b), 2) for b in range(bits)]
        self.stages, self.regions, self.kinds, self.slots = [], [], [], []
        for i, (at, row, height, col, width) in enumerate(chunks):
            stages = []
            for a, b in zip(*orders[i]):
                if a == b:
                    mine, step = digit[a], 1 << a
                else:
                    mine = digit[a] * (1 - self.core) + digit[b] * self.core
                    step = (1 << a) * (1 - self.core) + (1 << b) * self.core
                stages.append((mine, self.k + step * (1 - 2 * mine)))
            start, length, used = 0, height, 0
            region, kind, slot = [], [], []
            for s in range(bits):
                region.append((start, length))
                slot.append(used)
                if length % 32 == 0:
                    kind.append(True)
                    length //= 2
                    start = start + stages[s][0] * length
                else:
                    kind.append(False)
                used += length
            region.append((start, length))
            self.stages.append(stages)
            self.regions.append(region)
            self.kinds.append(kind)
            self.slots.append(slot)

    def send(self, i, t, src, dst, device):
        copy = pltpu.make_async_remote_copy(
            src_ref=src,
            dst_ref=dst,
            send_sem=self.send_sem.at[i, t],
            recv_sem=self.recv_sem.at[i, t],
            device_id=device,
            device_id_type=MESH,
        )
        copy.start()
        self.live[i, t] = copy

    def add(self, dst, at, src, src_at, length):
        block = 16
        while length % (block * 2) == 0 and block * 2 * dst.shape[1] <= 65536:
            block *= 2

        def step(j, carry):
            off = j * block
            rows = span(at + off, block)
            dst[rows, :] = dst[rows, :] + src[span(src_at + off, block), :]
            return carry

        lax.fori_loop(0, length // block, step, 0)

    def fetch(self):
        for i, (at, row, height, col, width) in enumerate(self.chunks):
            t = self.begin[i]
            if 1 <= t <= self.bits:
                start, length = self.regions[i][t - 1]
                own = pl.ds(pl.multiple_of(self.core * (self.shapes[at][1] // 2) + col, 128), width)
                self.loads[i] = pltpu.make_async_copy(
                    self.sources[at].at[span(row + start, length), own],
                    self.acc[i].at[span(start, length)],
                    self.load_sem.at[i],
                )
                self.loads[i].start()

    def arrived(self, i, t):
        if (i, t) in self.live:
            self.live[i, t].wait_recv()

    def task(self, i, t):
        at, row, height, col, width = self.chunks[i]
        bits, kinds, regions, stages = self.bits, self.kinds[i], self.regions[i], self.stages[i]
        half = self.shapes[at][1] // 2
        own = pl.ds(pl.multiple_of(self.core * half + col, 128), width)
        rows = pl.ds(row, height)
        if t == 0:
            away = pl.ds(pl.multiple_of((1 - self.core) * half + col, 128), width)
            self.send(i, 0, self.sources[at].at[rows, away], self.recv0[i], self.sibling)
            if self.acc[i] is None:
                self.acc[i] = self.sources[at].at[rows, own]
                return
            copy = pltpu.make_async_copy(self.sources[at].at[rows, own], self.acc[i], self.load_sem.at[i])
            copy.start()
            self.loads[i] = copy
            return
        self.arrived(i, t - 1)
        if t <= bits + 1:
            if t == self.begin[i]:
                if t <= bits:
                    self.loads[i].wait()
            elif t == 1:
                if i in self.loads:
                    self.loads[i].wait()
                self.add(self.acc[i], 0, self.recv0[i], 0, height)
            else:
                s = t - 2
                start, length = regions[s + 1]
                if not kinds[s]:
                    self.live[i, t - 1].wait_send()
                self.add(self.acc[i], start, self.recvs[i], self.slots[i][s], length)
        if t == self.leave[i]:
            start, length = regions[t - 1]
            copy = pltpu.make_async_copy(
                self.acc[i].at[span(start, length)], self.outs[at].at[span(row + start, length), own], self.store_sem.at[i]
            )
            copy.start()
            self.stores[i] = copy
            return
        if t <= bits:
            s = t - 1
            start, length = regions[s]
            give, first = length, start
            if kinds[s]:
                give = length // 2
                first = start + (1 - stages[s][0]) * give
            self.send(
                i, t, self.acc[i].at[span(first, give)], self.recvs[i].at[pl.ds(self.slots[i][s], give)],
                (stages[s][1], self.core),
            )
            return
        if t == bits + 1:
            start, length = regions[bits]
            if t == self.begin[i]:
                mine = self.sources[at].at[span(row + start, length), own]
            else:
                mine = self.acc[i].at[span(start, length)]
            copy = pltpu.make_async_copy(mine, self.outs[at].at[span(row + start, length), own], self.store_sem.at[i])
            copy.start()
            self.stores[i] = copy
        if t == bits + 2:
            self.stores[i].wait()
        if t <= 2 * bits:
            s = bits - 1 - (t - bits - 1)
            start, length = regions[s + 1]
            if kinds[s]:
                place = self.outs[at].at[span(row + start, length), own]
                self.send(i, t, mine if t == bits + 1 else place, place, (stages[s][1], self.core))
            return
        if t == 2 * bits + 1:
            place = self.outs[at].at[rows, own]
            self.send(i, t, place, place, self.sibling)

    def run(self, order):
        while self.at < len(order):
            token = order[self.at]
            self.at += 1
            if token is None:
                return
            i, t = token
            if t == self.total:
                self.arrived(i, t - 1)
            else:
                self.task(i, t)

    def finish(self):
        for (i, t), copy in self.live.items():
            if not (1 <= t <= self.bits and not self.kinds[i][t - 1]):
                copy.wait_send()


def share_scratch(chunks, bits, begin, inside=False):
    acc, recv0, recvs = [], [], []
    for i, (at, row, height, col, width) in enumerate(chunks):
        if begin[i] > bits:
            continue
        acc.append(pltpu.VMEM((height, width), BF16))
        if begin[i] == 0:
            recv0.append(pltpu.VMEM((height, width), BF16))
        length, used = height, 0
        for s in range(bits):
            if length % 32 == 0:
                length //= 2
            used += length
        recvs.append(pltpu.VMEM((used, width), BF16))
    n = len(chunks)
    sems = [pltpu.SemaphoreType.DMA((n, 2 * bits + 2))] * 2 + [pltpu.SemaphoreType.DMA((n,))] * 2
    return ([] if inside else acc) + recv0 + recvs + sems


def share_hold(refs, bits, begin, inside=False):
    n = len(begin)
    acc, recv0, recvs = [None] * n, [None] * n, [None] * n
    for held, most in ((acc, -1 if inside else bits), (recv0, 0), (recvs, bits)):
        for i in range(n):
            if begin[i] <= most:
                held[i], refs = refs[0], refs[1:]
    return acc, recv0, recvs, refs


def share_leave(bits):
    return [bits + 1] * 3 + [min(v, bits + 1) for v in [3, 2, 1]]


def share_orders(bits, path):
    rest = list(range(2, bits))
    if bits < 2:
        return rest or list(range(bits)), rest or list(range(bits))
    if path == 0:
        return [0, 1] + rest, [1, 0] + rest
    if path == 1:
        return [0] + rest + [1], [1] + rest + [0]
    return rest + [0, 1], rest + [1, 0]


SHARE_CUTS = ((1, 2), (1, 1), (3, 1), (1, 1), (1, 1), (1, 1), (1, 1))
SHARE_FIRST = 6
SHARE_PATHS = (1, 0, 1, 0, 0, 0, 0, 1, 0, 0)
SHARE_LATE = (
    51, 37, 81, 21, 66, 96, 5, -1, -1, 52, 38, 22, 97, -1, -1, 82, -1, -1, 53, 98, -1, 83, 23, 112,
    39, -1, 54, -1, 113, -1, 84, 24, -1, -1, 55, 67, -1, -1, 128, 40, 85, 114, -1, 144, 56, 68, -1, 129,
    86, 25, 115, -1, 145, -1, -1, 69, -1, 99, 26, 6, 70, 146, 100, 41, 87, 130, 57, 116, 147, 7, 71, 101,
    117, 42, 88, 58, 131, 148, 72, 149, 132, 89, 150, 8, 118, 133, 151, 73, 102, 90, 119, 134, 152, 74, 103, 120,
    9, 135, 153, 104, 154, 121, 10, 136, 122, 105, 137, 106, 138,
)
SHARE_EARLY = (
    0, -1, -1, -1, 32, 1, -1, -1, 16, 33, -1, 2, -1, 17, -1, -1, 48, 34, -1, -1, -1, 64, 49, 3,
    -1, 18, -1, 80, 35, -1, 65, -1, 81, 50, 19, -1, -1, -1, 20, 51, 66, 4, 36, 5, 37, 21,
)


def share_late_order(pieces, bits, parts, ready):
    if bits == 4:
        return [None if v < 0 else (v // 16, v % 16) for v in SHARE_LATE]
    order, total = [], 2 * bits + 2
    begin = share_leave(bits) + [0] * (pieces - SHARE_FIRST)
    for k in range(parts + total + 1):
        for i in range(pieces):
            t = k - ready[i] + begin[i]
            if k >= ready[i] and t <= total:
                order.append((i, t))
        if k < parts:
            order.append(None)
    return order


def share_early_order(bits):
    if bits == 4:
        return [None if v < 0 else (v // 16, v % 16) for v in SHARE_EARLY]
    order = [None] * 10
    for t in range(bits + 2):
        order += [(i, t) for i in range(SHARE_FIRST) if t <= share_leave(bits)[i]] + [None]
    return order


def meet_sums(links, e, width, tables, between=None):
    links.wait_near(e)
    links.far[e][links.outer] = fold_sums(links.near[e], links.wide)
    links.send_far(e)
    if between is not None:
        between()
    links.wait_far(e)
    sums = fold_sums(links.far[e], links.outers)
    for t, (table, row) in enumerate(tables):
        unpack(table, row, sums[8 * t : 8 * t + 8], width)


def share_of(wv, tally, crop, times):
    return wv[0, crop] * (times / tally[0:1, 0:1]) + wv[1, crop] * (times / tally[1:2, 0:1])


class Puts:
    def __init__(self, sem):
        self.sem, self.copies = sem, []

    def put(self, src, dst):
        copy = pltpu.make_async_copy(src, dst, self.sem.at[len(self.copies)])
        copy.start()
        self.copies.append(copy)

    def finish(self):
        for copy in self.copies:
            copy.wait()


def start_loads(pairs, sem):
    copies = [pltpu.make_async_copy(src, dst, sem.at[i]) for i, (src, dst) in enumerate(pairs)]
    for copy in copies:
        copy.start()
    return copies


def back_two_kernel(sets, total, outs, crops, dims, shapes, chunks, *refs):
    c3, cin, c4, cout = dims
    vb, vs, norms1, norms2, st3, st4, st5, tally = refs[:8]
    sources, refs = refs[8:23], refs[23:]
    (o_up, o_g6, o_g7, o_g5, o_g4, o_s5, o_s4, o_s3), refs = refs[:8], refs[8:]
    held, refs = refs[:14], refs[14:]
    (d7, w7, xe, d6, w6, z5, h5, w5, x5, z4, w4, h2, w3, img) = held
    (q5, t7, dh, d4, zt, bg, up, s5, s4, s3, cs, cm, wv, wcol), refs = refs[:14], refs[14:]
    d5, pv, blk = d6, q5, img
    g6, g7, g5, g4 = w6, w7, w5, w4
    blocks, refs = take(refs, 3)
    near, refs = take(refs, 3)
    far, refs = take(refs, 3)
    links = Links(crops, near, far, *refs[:4])
    load_sem, out_sem, up_sem = refs[4:7]
    refs = refs[7:]
    bits = crops.bit_length() - 1
    early = SHARE_FIRST
    acc, recv0, recvs, refs = share_hold(refs, bits, [0] * early, True)
    share = Share(
        shapes, chunks[:early], [share_orders(bits, v) for v in SHARE_PATHS[:early]], bits, links, [g7, g6, g5], [o_g7, o_g6, o_g5],
        acc, recv0, recvs, refs, [0] * early, share_leave(bits),
    )
    order = share_early_order(bits)

    def tick():
        share.run(order)

    f = F32
    loads = start_loads(list(zip(sources, held)), load_sem)
    links.greet()
    view_tables(sets, links.r, (vb, vs), wv, wcol)
    puts = Puts(out_sem)
    for ref in (cs, cm):
        ref[...] = jnp.zeros(ref.shape, f)
    for block in blocks:
        block[...] = jnp.zeros(block.shape, f)

    for i in range(2):
        loads[i].wait()

    def shortcut(n):
        part = pl.ds(pl.multiple_of(n * 256, 256), 256)
        t7[:, part] = mm_nt(d7[...], w7[part, :])

    repeat(cin // 256, shortcut)
    loads[2].wait()
    for piece in range(2):
        for half in range(2):
            cols = slice(half * (cout // 2) + piece * (cout // 4), half * (cout // 2) + (piece + 1) * (cout // 4))
            g7[:, cols] = mm_tn(xe[...], d7[:, cols]).astype(BF16)
        tick()

    for i in range(3, 6):
        loads[i].wait()
    q5[...] = mm_nt(d6[...], w6[...])
    g5at = c4
    for m in sets:

        def crop_(c, m=m):
            crop = m.crop0 + c
            rows = span(m.out0 + c * m.out, m.out, 8)
            inv = by_view(wv, crop, st5[2:4, :])
            n = (z5[rows, :] - by_view(wv, crop, st5[0:2, :])) * inv
            q = act_slope(n * norms2[0:1, g5at : 2 * c4] + norms2[1:2, g5at : 2 * c4]) * q5[rows, :]
            q5[rows, :] = q
            cs[pl.ds(crop, 1), 0:c4] = jnp.sum(tile_sum(q), axis=0, keepdims=True)
            cm[pl.ds(crop, 1), 0:c4] = jnp.sum(tile_sum(q * n), axis=0, keepdims=True)

        repeat(m.count, crop_)
    local_sums(blocks[0], (cs, cm), wcol, c4)
    links.send_near(0, blocks[0])

    tick()
    loads[6].wait()

    def outer(n):
        cols = pl.ds(pl.multiple_of(n * 512, 512), 512)
        g6[:, cols] = mm_tn(h5[...], d6[:, cols]).astype(BF16)

    repeat(cout // 512, outer)
    tick()
    meet_sums(links, 0, c4, ((s5, 0), (s5, 2)))

    for m in sets:

        def pair(p, m=m):
            o = m.out0 + p * 2 * m.out
            mask = keep(c4, 8, m.half)
            slots = [[], [], [], []]
            for j in range(2):
                crop = m.crop0 + 2 * p + j
                rows = span(o + j * m.out, m.out, 8)
                over = share_of(wv, tally, crop, 4.0)
                inv = by_view(wv, crop, st5[2:4, :])
                n = (z5[rows, :] - by_view(wv, crop, st5[0:2, :])) * inv
                d = (inv * norms2[0:1, g5at : 2 * c4]) * (
                    q5[rows, :] - by_view(wv, crop, s5[0:2, :]) * over - n * (by_view(wv, crop, s5[2:4, :]) * over)
                )
                d = masked(d, mask)
                down = jnp.concatenate([d[8:], jnp.zeros((8, c4), f)], axis=0)
                slots[0].append(d)
                slots[1].append(pltpu.roll(d, m.out - 1, 0))
                slots[2].append(down)
                slots[3].append(pltpu.roll(down, m.out - 1, 0))
            for t in range(4):
                d5[span(o, 2 * m.out), t * c4 : (t + 1) * c4] = jnp.concatenate(slots[t], axis=0).astype(BF16)

        repeat(m.count // 2, pair)

    tick()
    loads[7].wait()
    options = (((1, 0),), ((2, 0), (0, 1)))
    for a in range(2):
        for b in range(2):
            value = None
            for r, down in options[a]:
                for c, side in options[b]:
                    slot, tap = (2 * down + side) * c4, (3 * r + c) * c4
                    term = mm_nt(d5[:, slot : slot + c4], w5[tap : tap + c4, :])
                    value = term if value is None else value + term
            pv[...] = value
            for m in sets:

                def crop_(c, m=m, a=a, b=b):
                    for i in range(m.half):
                        for q in range(c4 // 128):
                            dh[q, pl.ds(m.row0 + c * m.rows + (2 * i + a) * 16 + b, 8, stride=2), :] = pv[
                                span(m.out0 + c * m.out + i * 8, 8, 8), q * 128 : (q + 1) * 128
                            ]

                repeat(m.count, crop_)
        tick()
    loads[9].wait()
    for m in sets:

        def crop_(c, m=m):
            crop = m.crop0 + c
            rows = span(m.row0 + c * m.rows, m.rows)
            mask = keep(128, 16, m.edge)
            levels, tilts = [], []
            for q in range(c4 // 128):
                cols = slice(q * 128, (q + 1) * 128)
                inv = by_view(wv, crop, st4[2:4, cols])
                n = (z4[rows, cols] - by_view(wv, crop, st4[0:2, cols])) * inv
                up_ = masked(act_slope(n * norms2[0:1, cols] + norms2[1:2, cols]) * dh[q, rows, :], mask)
                dh[q, rows, :] = up_
                levels.append(jnp.sum(tile_sum(up_), axis=0, keepdims=True))
                tilts.append(jnp.sum(tile_sum(up_ * n), axis=0, keepdims=True))
            cs[pl.ds(crop, 1), 0:c4] = jnp.concatenate(levels, axis=1)
            cm[pl.ds(crop, 1), 0:c4] = jnp.concatenate(tilts, axis=1)

        repeat(m.count, crop_)
        tick()
    local_sums(blocks[1], (cs, cm), wcol, c4)
    links.send_near(1, blocks[1])
    loads[8].wait()

    def kernel(n):
        for t in range(3 * n, 3 * n + 3):
            part = slice(t * c4, (t + 1) * c4)
            g5[part, :] = mm_tn(x5[:, part], d5[:, 0:c4]).astype(BF16)
        tick()

    kernel(0)

    def rest():
        kernel(1)
        kernel(2)

    meet_sums(links, 1, c4, ((s4, 0), (s4, 2)), rest)
    tick()

    for i in range(10, 14):
        loads[i].wait()
    big_rows = 2 * sets[0].rows
    for at, m in enumerate(sets):

        def pair(p, m=m, at=at):
            r = m.row0 + p * 2 * m.rows
            o = m.out0 + p * 2 * m.out
            mask = keep(128, 16, m.edge)
            for j in range(2):
                crop = m.crop0 + 2 * p + j
                rows = span(r + j * m.rows, m.rows)
                over = share_of(wv, tally, crop, 1.0)
                for q in range(c4 // 128):
                    cols = slice(q * 128, (q + 1) * 128)
                    inv = by_view(wv, crop, st4[2:4, cols])
                    n = (z4[rows, cols] - by_view(wv, crop, st4[0:2, cols])) * inv
                    d = (inv * norms2[0:1, cols]) * (
                        dh[q, rows, :] - by_view(wv, crop, s4[0:2, cols]) * over - n * (by_view(wv, crop, s4[2:4, cols]) * over)
                    )
                    d4[rows, cols] = masked(d, mask).astype(BF16)
            got = mm_nt(d4[span(r, 2 * m.rows), :], w4[...])
            for q in range(cin // 128):
                bg[q, 0 : 2 * m.rows, :] = got[:, q * 128 : (q + 1) * 128]
            for q in range(cin // 128):
                for j in range(2):
                    for i in range(m.half):
                        here = pl.ds(j * m.rows + i * 32, 8, stride=2)
                        bg[q, here, :] = bg[q, here, :] + t7[span(o + j * m.out + i * 8, 8, 8), q * 128 : (q + 1) * 128]
            turn = m.crop0 // 2 + p
            slot = turn % 2

            def left(turn, slot):
                return pltpu.make_async_copy(
                    up.at[slot, 0 : 2 * m.rows], o_up.at[span(r, 2 * m.rows)], up_sem.at[turn]
                )

            if turn >= 2:
                size = big_rows if turn - 2 < sets[0].count // 2 else 2 * m.rows
                pltpu.make_async_copy(up.at[slot, 0:size], o_up.at[pl.ds(0, size)], up_sem.at[turn - 2]).wait()
            step = m.rows // 2
            mask = keep(128, 16, m.edge)
            totals = [[[], []], [[], []]]
            for h, j in [(h, j) for h in range(cin // 512) for j in range(2)]:
                if j == 0:
                    zt[0 : 2 * m.rows, :] = mm(h2[span(r, 2 * m.rows), :], w3[:, h * 512 : (h + 1) * 512])
                crop = m.crop0 + 2 * p + j
                levels, tilts = totals[j]
                for q in range(h * 4, h * 4 + 4):
                    cols = slice(q * 128, (q + 1) * 128)
                    part = slice((q - h * 4) * 128, (q - h * 4 + 1) * 128)
                    at3 = slice(2 * c3 + q * 128, 2 * c3 + (q + 1) * 128)
                    mean, inv = by_view(wv, crop, st3[0:2, cols]), by_view(wv, crop, st3[2:4, cols])
                    gain, bias = norms1[0:1, at3], norms1[1:2, at3]

                    def tile(i, sums, j=j, cols=cols, part=part, q=q, mean=mean, inv=inv, gain=gain, bias=bias):
                        here = span(j * m.rows + i * step, step)
                        rows = span(r + j * m.rows + i * step, step)
                        n = (zt[here, part] - mean) * inv
                        u = n * gain + bias + img[rows, cols].astype(f)
                        got = bg[q, here, :].astype(BF16).astype(f)
                        v = masked(act_slope(u) * got, mask)
                        up[slot, here, cols] = v
                        return (sums[0] + tile_sum(v), sums[1] + tile_sum(v * n))

                    zero = jnp.zeros((8, 128), f)
                    s, t = lax.fori_loop(0, 2, tile, (zero, zero))
                    levels.append(jnp.sum(s, axis=0, keepdims=True))
                    tilts.append(jnp.sum(t, axis=0, keepdims=True))
            for j in range(2):
                crop = m.crop0 + 2 * p + j
                cs[pl.ds(crop, 1), :] = jnp.concatenate(totals[j][0], axis=1)
                cm[pl.ds(crop, 1), :] = jnp.concatenate(totals[j][1], axis=1)
            left(turn, slot).start()

        for p in range(m.count // 2):
            pair(p)
            tick()
    late = pltpu.make_async_copy(sources[14], blk, load_sem.at[14])
    late.start()
    local_sums(blocks[2], (cs, cm), wcol, cin)
    links.send_near(2, blocks[2])
    late.wait()

    def inner(n):
        part = pl.ds(pl.multiple_of(n * 256, 256), 256)
        g4[part, :] = mm_tn(blk[:, part], d4[...]).astype(BF16)

    repeat(2, inner)
    tick()

    def rest():
        repeat(cin // 256 - 2, lambda n: inner(n + 2))
        puts.put(g4, o_g4)
        tick()

    meet_sums(links, 2, cin, ((s3, 0), (s3, 2)), rest)
    for src, dst in ((s5, o_s5), (s4, o_s4), (s3, o_s3)):
        puts.put(src, dst)
    for back in (2, 1):
        size = 2 * sets[1].rows
        turn = (sets[0].count + sets[1].count) // 2 - back
        pltpu.make_async_copy(
            up.at[turn % 2, 0:size], o_up.at[pl.ds(sets[1].row0, size)], up_sem.at[turn]
        ).wait()
    while share.at < len(order):
        tick()
    for copy in share.stores.values():
        copy.wait()
    share.finish()
    links.finish()
    puts.finish()


def back_one_kernel(sets, total, guarded, crops, dims, shapes, chunks, *refs):
    c3, cin = dims
    vb, vs, norms1, st1, st2, st3, s3, tally = refs[:8]
    sources, refs = refs[8:17], refs[17:]
    second, refs = list(refs[:4]), refs[4:]
    (o_gb, o_gs, o_s2, o_s1), refs = refs[:4], refs[4:]
    o_grads, refs = refs[:7], refs[7:]
    held, refs = refs[:9], refs[9:]
    (h2, w3, up, z2, h1, wsp1, z1, w1, img) = held
    (zt, d3, q2, d2, q1, d1, g3, g2, g1, s2, s1, cs, cm, wv, wcol), refs = refs[:15], refs[15:]
    blocks, refs = take(refs, 2)
    near, refs = take(refs, 2)
    far, refs = take(refs, 2)
    links = Links(crops, near, far, *refs[:4])
    load_sem, out_sem, own_sem, grad_send, grad_recv, up_sem = refs[4:10]
    refs = refs[10:]
    n = len(chunks)
    bits = crops.bit_length() - 1
    begin = share_leave(bits) + [0] * (n - SHARE_FIRST)
    acc, recv0, recvs, refs = share_hold(refs, bits, begin)
    share = Share(
        shapes, chunks, [share_orders(bits, v) for v in SHARE_PATHS], bits, links, second + [g3, g2, g1], o_grads,
        acc, recv0, recvs, refs, begin, [2 * bits + 3] * n,
    )
    share.fetch()
    order = share_late_order(n, bits, 20, (0,) * 7 + (7, 14, 15))

    def tick():
        share.run(order)

    core = links.r
    sibling = (links.k, 1 - core)
    f = F32
    loads = start_loads([(a, b) for a, b in zip(sources, held) if b is not up], load_sem)
    ups = []
    for m in sets:
        for p in range(m.count // 2):
            rows = pl.ds(m.row0 + p * 2 * m.rows, 2 * m.rows)
            ups.append(pltpu.make_async_copy(sources[2].at[rows], up.at[rows], up_sem.at[len(ups)]))
    for copy in ups:
        copy.start()
    links.greet()
    tick()
    view_tables(sets, links.r, (vb, vs), wv, wcol)
    puts = Puts(out_sem)
    for ref in (cs, cm):
        ref[...] = jnp.zeros(ref.shape, f)
    for block in blocks:
        block[...] = jnp.zeros(block.shape, f)
    d2[0:16, :] = jnp.zeros((16, 3 * c3), BF16)
    for m in sets:
        for c in range(m.count):
            at = m.guard0 + c * m.guard + m.rows
            d2[at : at + 16, :] = jnp.zeros((16, 3 * c3), BF16)

    for i in range(3):
        loads[i].wait()
    for copy in ups:
        copy.wait()
    for m in sets:

        def pair(p, m=m):
            r = m.row0 + p * 2 * m.rows
            step = m.rows // 2
            mask = keep(128, 16, m.edge)
            for h, j in [(h, j) for h in range(cin // 512) for j in range(2)]:
                if j == 0:
                    zt[0 : 2 * m.rows, :] = mm(h2[span(r, 2 * m.rows), :], w3[:, h * 512 : (h + 1) * 512])
                crop = m.crop0 + 2 * p + j
                over = share_of(wv, tally, crop, 1.0)
                for q in range(h * 4, h * 4 + 4):
                    cols = slice(q * 128, (q + 1) * 128)
                    part = slice((q - h * 4) * 128, (q - h * 4 + 1) * 128)
                    mean, inv = by_view(wv, crop, st3[0:2, cols]), by_view(wv, crop, st3[2:4, cols])
                    gain = inv * norms1[0:1, 2 * c3 + q * 128 : 2 * c3 + (q + 1) * 128]
                    level = by_view(wv, crop, s3[0:2, cols]) * over
                    tilt = by_view(wv, crop, s3[2:4, cols]) * over * inv

                    def tile(i, j=j, cols=cols, part=part, mean=mean, gain=gain, level=level, tilt=tilt):
                        here = span(j * m.rows + i * step, step)
                        rows = span(r + j * m.rows + i * step, step)
                        d = gain * (up[rows, cols] - level - (zt[here, part] - mean) * tilt)
                        d3[rows, cols] = masked(d, mask).astype(BF16)

                    repeat(2, tile)
            q2[span(r, 2 * m.rows), :] = mm_nt(d3[span(r, 2 * m.rows), :], w3[...])
            for j in range(2):
                crop = m.crop0 + 2 * p + j
                mean, inv = by_view(wv, crop, st2[0:2, :]), by_view(wv, crop, st2[2:4, :])

                def tile(i, sums, j=j, mean=mean, inv=inv):
                    rows = span(r + j * m.rows + i * step, step)
                    n = (z2[rows, :] - mean) * inv
                    v = act_slope(n * norms1[0:1, c3 : 2 * c3] + norms1[1:2, c3 : 2 * c3]) * q2[rows, :]
                    q2[rows, :] = v
                    return (sums[0] + tile_sum(v), sums[1] + tile_sum(v * n))

                zero = jnp.zeros((8, c3), f)
                s, t = lax.fori_loop(0, 2, tile, (zero, zero))
                cs[pl.ds(crop, 1), 0:c3] = jnp.sum(s, axis=0, keepdims=True)
                cm[pl.ds(crop, 1), 0:c3] = jnp.sum(t, axis=0, keepdims=True)

        for p in range(m.count // 2):
            pair(p)
            tick()
    local_sums(blocks[0], (cs, cm), wcol, c3)
    links.send_near(0, blocks[0])

    def outer(n):
        cols = pl.ds(pl.multiple_of(n * 256, 256), 256)
        g3[:, cols] = mm_tn(h2[...], d3[:, cols]).astype(BF16)

    repeat(cin // 512, outer)
    tick()

    def rest():
        repeat(cin // 512, lambda n: outer(n + cin // 512))
        tick()

    meet_sums(links, 0, c3, ((s2, 0), (s2, 2)), rest)

    for i in range(3, 6):
        loads[i].wait()
    for m in sets:

        def pair(p, m=m):
            r = m.row0 + p * 2 * m.rows
            g = m.guard0 + p * 2 * m.guard
            step = m.rows // 2
            mask = keep(c3, 16, m.edge)
            for j in range(2):
                crop = m.crop0 + 2 * p + j
                over = share_of(wv, tally, crop, 1.0)
                mean, inv = by_view(wv, crop, st2[0:2, :]), by_view(wv, crop, st2[2:4, :])
                gain = inv * norms1[0:1, c3 : 2 * c3]
                level = by_view(wv, crop, s2[0:2, :]) * over
                tilt = by_view(wv, crop, s2[2:4, :]) * over * inv

                def tile(i, j=j, mean=mean, gain=gain, level=level, tilt=tilt):
                    rows = span(r + j * m.rows + i * step, step)
                    d = gain * (q2[rows, :] - level - (z2[rows, :] - mean) * tilt)
                    d = masked(d, mask)
                    to = span(g + j * m.guard + i * step, step)
                    d2[to, 0:c3] = pltpu.roll(d, step - 1, 0).astype(BF16)
                    d2[to, c3 : 2 * c3] = d.astype(BF16)
                    d2[to, 2 * c3 : 3 * c3] = pltpu.roll(d, 1, 0).astype(BF16)

                repeat(2, tile)
            size = 2 * m.rows + 16
            value = None
            for a in range(3):
                for b in range(3):
                    part = d2[span(g - (a - 1) * 16, size), b * c3 : (b + 1) * c3]
                    term = mm_nt(part, wsp1[a, b * c3 : (b + 1) * c3, :])
                    value = term if value is None else value + term
            q1[span(r, m.rows), :] = value[0 : m.rows]
            q1[span(r + m.rows, m.rows), :] = value[m.guard : m.guard + m.rows]
            for j in range(2):
                crop = m.crop0 + 2 * p + j
                mean, inv = by_view(wv, crop, st1[0:2, :]), by_view(wv, crop, st1[2:4, :])

                def tile(i, sums, j=j, mean=mean, inv=inv):
                    rows = span(r + j * m.rows + i * step, step)
                    n = (z1[rows, :] - mean) * inv
                    v = act_slope(n * norms1[0:1, 0:c3] + norms1[1:2, 0:c3]) * q1[rows, :]
                    v = masked(v, mask)
                    q1[rows, :] = v
                    return (sums[0] + tile_sum(v), sums[1] + tile_sum(v * n))

                zero = jnp.zeros((8, c3), f)
                s, t = lax.fori_loop(0, 2, tile, (zero, zero))
                cs[pl.ds(crop, 1), 0:c3] = jnp.sum(s, axis=0, keepdims=True)
                cm[pl.ds(crop, 1), 0:c3] = jnp.sum(t, axis=0, keepdims=True)

        for p in range(m.count // 2):
            pair(p)
            tick()
    local_sums(blocks[1], (cs, cm), wcol, c3)
    links.send_near(1, blocks[1])
    inside = guarded - 32

    def taps(a):
        g2[a * 3 * c3 : (a + 1) * 3 * c3, :] = mm_tn(
            h1[a * 16 : a * 16 + inside, :], d2[16 : 16 + inside, c3 : 2 * c3]
        ).astype(BF16)

    taps(0)
    tick()

    def rest():
        taps(1)
        taps(2)
        tick()

    meet_sums(links, 1, c3, ((s1, 0), (s1, 2)), rest)

    loads[6].wait()
    moves = []
    for m, out in zip(sets, (o_gb, o_gs)):
        part = m.rows // 2
        for c in range(m.count):
            i = m.crop0 + c
            own_rows = span(m.row0 + c * m.rows + core * part, part)
            other_rows = span(m.row0 + c * m.rows + (1 - core) * part, part)
            place = out.at[span((core * m.count + c) * part, part)]
            moves.append(
                (
                    pltpu.make_async_copy(d3.at[own_rows], place, own_sem.at[i]),
                    pltpu.make_async_remote_copy(
                        src_ref=d3.at[other_rows],
                        dst_ref=place,
                        send_sem=grad_send.at[i],
                        recv_sem=grad_recv.at[i],
                        device_id=sibling,
                        device_id_type=MESH,
                    ),
                )
            )
    for m in sets:

        def pair(p, m=m):
            r = m.row0 + p * 2 * m.rows
            step = m.rows // 2
            mask = keep(c3, 16, m.edge)
            for j in range(2):
                crop = m.crop0 + 2 * p + j
                over = share_of(wv, tally, crop, 1.0)
                mean, inv = by_view(wv, crop, st1[0:2, :]), by_view(wv, crop, st1[2:4, :])
                gain = inv * norms1[0:1, 0:c3]
                level = by_view(wv, crop, s1[0:2, :]) * over
                tilt = by_view(wv, crop, s1[2:4, :]) * over * inv

                def tile(i, j=j, mean=mean, gain=gain, level=level, tilt=tilt):
                    rows = span(r + j * m.rows + i * step, step)
                    d = gain * (q1[rows, :] - level - (z1[rows, :] - mean) * tilt)
                    d1[rows, :] = masked(d, mask).astype(BF16)

                repeat(2, tile)

        repeat(m.count // 2, pair)
    loads[7].wait()

    def inner(n):
        part = pl.ds(pl.multiple_of(n * 256, 256), 256)
        g1[part, :] = mm_tn(img[:, part], d1[...]).astype(BF16)

    repeat(cin // 256, inner)
    tick()
    for m in sets:

        def pair(p, m=m):
            rows = span(m.row0 + p * 2 * m.rows, 2 * m.rows)
            for n in range(cin // 256):
                cols = slice(n * 256, (n + 1) * 256)
                d3[rows, cols] = (up[rows, cols] + mm_nt(d1[rows, :], w1[cols, :])).astype(BF16)

        for p in range(m.count // 2):
            pair(p)
            for c in (2 * p, 2 * p + 1):
                for copy in moves[m.crop0 + c]:
                    copy.start()
            tick()
    for src, dst in ((s2, o_s2), (s1, o_s1)):
        puts.put(src, dst)
    while share.at < len(order):
        tick()
    share.finish()
    links.finish()
    for near_copy, far_copy in moves:
        near_copy.wait()
        far_copy.wait()
    puts.finish()


def backward(sets, got, views, w, norms_first, norms_second, total, guarded, outs, idents):
    crops = lax.axis_size("crops")
    w1, wsp1, w3, w4, w5, w6, w7 = w
    cin, c3 = w1.shape
    c4, cout = w6.shape
    (
        f_img, f_z1, f_h1, f_z2, f_h2, f_blk, f_z4, f_x5, f_z5, f_h5, f_xe, f_res, f_d6, f_d7,
        f_st1, f_st2, f_st3, f_st4, f_st7, f_st5, f_st6, f_sq, f_n,
    ) = got
    smem, vmem = pl.BlockSpec(memory_space=pltpu.SMEM), pl.BlockSpec(memory_space=pltpu.VMEM)
    hbm = pl.BlockSpec(memory_space=pl.ANY)
    shape = jax.ShapeDtypeStruct
    most = 2 * sets[0].rows
    pairs = sum(m.count for m in sets) // 2
    count = 2 * pairs

    def like(arrays):
        return [pltpu.VMEM(t.shape, t.dtype) for t in arrays]

    def params(ident):
        return pltpu.CompilerParams(
            collective_id=ident, has_side_effects=True, vmem_limit_bytes=63 * 1024 * 1024
        )

    arrays = [f_d7, w7, f_xe, f_d6, w6, f_z5, f_h5, w5, f_x5, f_z4, w4, f_h2, w3, f_img, f_blk]
    out_shape = [
        shape((total, cin), F32), shape((c4, cout), BF16), shape((cin, cout), BF16), shape((9 * c4, c4), BF16),
        shape((cin, c4), BF16), shape((8, c4), F32), shape((8, c4), F32), shape((8, cin), F32),
    ]
    scratch = like(arrays[:14]) + [
        pltpu.VMEM((outs, c4), F32), pltpu.VMEM((outs, cin), F32), pltpu.VMEM((c4 // 128, total, 128), F32), pltpu.VMEM((total, c4), BF16),
        pltpu.VMEM((most, 512), F32), pltpu.VMEM((cin // 128, most, 128), F32), pltpu.VMEM((2, most, cin), F32),
        pltpu.VMEM((8, c4), F32), pltpu.VMEM((8, c4), F32), pltpu.VMEM((8, cin), F32),
        pltpu.VMEM((16, cin), F32), pltpu.VMEM((16, cin), F32),
        pltpu.SMEM((2, 16), F32), pltpu.VMEM((16, 128), F32),
    ]
    scratch += exchange_shapes((c4, c4, cin), (2, 2, 2), crops)
    scratch += [pltpu.SemaphoreType.DMA((15,)), pltpu.SemaphoreType.DMA((7,)), pltpu.SemaphoreType.DMA((pairs,))]
    shapes = [(cin, cout), (c4, cout), (9 * c4, c4), (cin, c4), (c3, cin), (9 * c3, c3), (cin, c3)]
    chunks = share_plan(shapes, SHARE_CUTS)
    bits = crops.bit_length() - 1
    scratch += share_scratch(chunks[:SHARE_FIRST], bits, [0] * SHARE_FIRST, True)
    up, g_outer2, g_skip, g_spatial2, g_inner2, s5, s4, s3 = pl.pallas_call(
        functools.partial(back_two_kernel, sets, total, outs, crops, (c3, cin, c4, cout), shapes, chunks),
        out_shape=out_shape,
        in_specs=[smem] * 2 + [vmem] * 6 + [hbm] * 15,
        out_specs=[hbm] * len(out_shape),
        scratch_shapes=scratch,
        compiler_params=params(idents[0]),
        name="back_two",
    )(*views, norms_first, norms_second, f_st3, f_st4, f_st5, f_n, *arrays)

    arrays = [f_h2, w3, up, f_z2, f_h1, wsp1, f_z1, w1, f_img]
    out_shape = [
        shape((total_rows(sets[0]), cin), BF16), shape((total_rows(sets[1]), cin), BF16), shape((8, c3), F32),
        shape((8, c3), F32),
    ] + [shape(t, BF16) for t in shapes]
    scratch = like(arrays) + [
        pltpu.VMEM((most, 512), F32), pltpu.VMEM((total, cin), BF16), pltpu.VMEM((total, c3), F32),
        pltpu.VMEM((guarded, 3 * c3), BF16), pltpu.VMEM((total, c3), F32), pltpu.VMEM((total, c3), BF16),
        pltpu.VMEM((c3, cin), BF16), pltpu.VMEM((9 * c3, c3), BF16), pltpu.VMEM((cin, c3), BF16),
        pltpu.VMEM((8, c3), F32), pltpu.VMEM((8, c3), F32), pltpu.VMEM((16, c3), F32), pltpu.VMEM((16, c3), F32),
        pltpu.SMEM((2, 16), F32), pltpu.VMEM((16, 128), F32),
    ]
    scratch += exchange_shapes((c3, c3), (2, 2), crops)
    scratch += [pltpu.SemaphoreType.DMA((9,)), pltpu.SemaphoreType.DMA((2,))]
    scratch += [pltpu.SemaphoreType.DMA((count,))] * 3 + [pltpu.SemaphoreType.DMA((pairs,))]
    scratch += share_scratch(chunks, bits, share_leave(bits) + [0] * (len(chunks) - SHARE_FIRST))
    grad_b, grad_s, s2, s1, *grads = pl.pallas_call(
        functools.partial(back_one_kernel, sets, total, guarded, crops, (c3, cin), shapes, chunks),
        out_shape=out_shape,
        in_specs=[smem] * 2 + [vmem] * 6 + [hbm] * 13,
        out_specs=[hbm] * len(out_shape),
        scratch_shapes=scratch,
        compiler_params=params(idents[1]),
        name="back_one",
    )(*views, norms_first, f_st1, f_st2, f_st3, s3, f_n, *arrays, g_skip, g_outer2, g_spatial2, g_inner2)
    return grad_b, grad_s, grads, (s1, s2, s3, s4, s5)


def widen_kernel(*refs):
    for src, dst in zip(refs[: len(refs) // 2], refs[len(refs) // 2 :]):
        dst[...] = src[...].astype(F32)


def widen(arrays, steps=8):
    def block(t):
        return pl.BlockSpec((t.shape[0] // steps, t.shape[1]), lambda i: (i, 0))

    return pl.pallas_call(
        widen_kernel,
        grid=(steps,),
        out_shape=[jax.ShapeDtypeStruct(t.shape, F32) for t in arrays],
        in_specs=[block(t) for t in arrays],
        out_specs=[block(t) for t in arrays],
        compiler_params=pltpu.CompilerParams(vmem_limit_bytes=63 * 1024 * 1024),
        name="widen",
    )(*arrays)


def total_rows(m):
    return m.count * m.rows


def shards(
    image_big,
    image_small,
    view_big,
    view_small,
    inner_first,
    spatial_first,
    outer_first,
    norms_first,
    inner_second,
    spatial_second,
    outer_second,
    skip_second,
    norms_second,
    cotangent_big,
    cotangent_small,
):
    c3, c4 = inner_first.shape[1], inner_second.shape[1]
    weights = [
        inner_first,
        spatial_first.reshape(3, 3 * c3, c3),
        outer_first,
        inner_second,
        spatial_second.reshape(9 * c4, c4),
        outer_second,
        skip_second,
    ]
    sets, sizes, got = forward(
        [image_big, image_small], [cotangent_big, cotangent_small], (view_big, view_small), weights, norms_first, norms_second, 0
    )
    grad_b, grad_s, grads, sums = backward(
        sets, got, (view_big, view_small), weights, norms_first, norms_second, *sizes, (1, 2)
    )
    s1, s2, s3, s4, s5 = sums
    sq = got[21]

    def both(parts):
        return jnp.concatenate(
            [jnp.stack([t[g] + t[g + 1], t[0] + t[1]]) for t, g in parts], axis=1
        )

    g_skip, g_outer2, g_spatial2, g_inner2, g_outer1, g_spatial1, g_inner1 = widen(grads)
    results = [
        got[11][m.out0 : m.out0 + m.count * m.out].reshape(m.count, m.half, 8, -1)[:, :, : m.half]
        for m in sets
    ]
    gradients = [
        t.reshape(image.shape[0], image.shape[1], 16, -1)[:, :, : image.shape[2]]
        for t, image in ((grad_b, image_big), (grad_s, image_small))
    ]
    return (
        results[0],
        results[1],
        gradients[0],
        gradients[1],
        g_inner1,
        g_spatial1.reshape(spatial_first.shape),
        g_outer1,
        both(((s1, 2), (s2, 2), (s3, 2))),
        g_inner2,
        g_spatial2.reshape(spatial_second.shape),
        g_outer2,
        g_skip,
        both(((s4, 2), (s5, 2), (sq, 2), (sq, 4))),
    )


def solution(mesh):
    maps = P("crops", "rows", None, None)
    whole = P(("crops", "rows"), None, None, None)
    in_specs = (maps, maps, P("crops"), P("crops")) + (P(),) * 9 + (whole, whole)
    out_specs = (whole, whole, maps, maps) + (P(),) * 9
    return jax.shard_map(shards, mesh=mesh, in_specs=in_specs, out_specs=out_specs, check_vma=False)
```

```python
import functools

import jax
import jax.numpy as jnp
from jax import lax
from jax.experimental import pallas as pl
from jax.experimental.pallas import tpu as pltpu
from jax.sharding import PartitionSpec as P

HIGH = lax.Precision.HIGHEST
EPS = 1e-05
MESH = pl.DeviceIdType.MESH
F32 = jnp.float32
BF16 = jnp.bfloat16


class Maps:
    def __init__(self, count, edge, row0, crop0, guard0, out0):
        self.count, self.edge = count, edge
        self.row0, self.crop0, self.guard0, self.out0 = row0, crop0, guard0, out0
        self.rows = edge * 16
        self.guard = (edge + 1) * 16
        self.half = edge // 2
        self.out = self.half * 8
        self.pixels = edge * edge


def geometry(nb, eb, ns, es):
    big = Maps(nb, eb, 0, 0, 16, 0)
    small = Maps(ns, es, nb * big.rows, nb, 16 + nb * big.guard, nb * big.out)
    total = small.row0 + ns * small.rows
    guarded = small.guard0 + ns * small.guard
    out = small.out0 + ns * small.out
    return (big, small), total, guarded, out


def al(x, m=16):
    return x if isinstance(x, int) else pl.multiple_of(x, m)


def span(start, size, m=16):
    return pl.ds(al(start, m), size)


def repeat(count, body):
    def step(i, carry):
        body(i)
        return carry

    lax.fori_loop(0, count, step, 0)


def mm(a, b):
    return jnp.dot(a, b, preferred_element_type=F32)


def mm_nt(a, b):
    return lax.dot_general(a, b, (((1,), (1,)), ((), ())), preferred_element_type=F32)


def mm_tn(a, b):
    return lax.dot_general(a, b, (((0,), (0,)), ((), ())), preferred_element_type=F32)


CA = 0.7978845608028654
CB = 0.7978845608028654 * 0.044715


def act(u):
    t = jnp.tanh(u * (CA + CB * (u * u)))
    return 0.5 * u * (1.0 + t)


def act_slope(u):
    s = u * u
    t = jnp.tanh(u * (CA + CB * s))
    rise = (0.5 * u) * (CA + (3.0 * CB) * s)
    return 0.5 * (1.0 + t) + (1.0 - t * t) * rise


def act_both(u):
    s = u * u
    t = jnp.tanh(u * (CA + CB * s))
    hu = 0.5 * u
    lift = 0.5 * (1.0 + t)
    slope = lift + (1.0 - t * t) * (hu * (CA + (3.0 * CB) * s))
    return u * lift, slope


def keep(width, pitch, edge):
    return lax.broadcasted_iota(jnp.int32, (pitch, width), 0) < edge


def masked(x, mask):
    rows = x.reshape(x.shape[0] // mask.shape[0], mask.shape[0], x.shape[1])
    return jnp.where(mask[None], rows, 0.0).reshape(x.shape)


def tile_sum(x):
    return jnp.sum(x.reshape(x.shape[0] // 8, 8, x.shape[1]), axis=0)


def pieces(width):
    return (4, width // 4) if width >= 512 else (width // 128, 128)


class Links:
    def __init__(self, crops, near, far, near_s, near_r, far_s, far_r):
        self.group = 4 if crops % 4 == 0 else 1
        self.outers = crops // self.group
        self.k, self.r = lax.axis_index("crops"), lax.axis_index("rows")
        inner, self.outer = lax.rem(self.k, self.group), self.k // self.group
        self.wide = 2 * self.group
        self.me = inner * 2 + self.r
        self.inner = inner
        self.peers, self.others, self.places = [], [], []
        for d in range(1, self.wide):
            p = lax.rem(self.me + d, self.wide)
            self.peers.append((self.outer * self.group + p // 2, lax.rem(p, 2)))
            self.places.append(p // 2)
        for d in range(1, self.outers):
            self.others.append((lax.rem(self.outer + d, self.outers) * self.group + inner, self.r))
        self.near, self.far = near, far
        self.sems = (near_s, near_r, far_s, far_r)
        self.live = {}

    def greet(self, extra=()):
        barrier = pltpu.get_barrier_semaphore()
        peers = self.peers + self.others + list(extra)
        for peer in peers:
            pl.semaphore_signal(barrier, inc=1, device_id=peer, device_id_type=MESH)
        pl.semaphore_wait(barrier, len(peers))

    def send_near(self, e, block):
        self.near[e][self.me] = block[...]
        self.live[e, 0] = []
        for d, peer in enumerate(self.peers):
            copy = pltpu.make_async_remote_copy(
                src_ref=block,
                dst_ref=self.near[e].at[self.me],
                send_sem=self.sems[0].at[e, d],
                recv_sem=self.sems[1].at[e, d],
                device_id=peer,
                device_id_type=MESH,
            )
            copy.start()
            self.live[e, 0].append(copy)

    def piece(self, j):
        return pl.ds(pl.multiple_of(j * 128, 128), 128)

    def send_pieces(self, e, block):
        self.near[e][self.me] = block[:, self.piece(self.inner)]
        self.live[e, 0] = []
        for d, peer in enumerate(self.peers):
            copy = pltpu.make_async_remote_copy(
                src_ref=block.at[:, self.piece(self.places[d])],
                dst_ref=self.near[e].at[self.me],
                send_sem=self.sems[0].at[e, d],
                recv_sem=self.sems[1].at[e, d],
                device_id=peer,
                device_id_type=MESH,
            )
            copy.start()
            self.live[e, 0].append(copy)

    def collect(self, e, whole, sems, at):
        place = whole.at[:, self.piece(self.inner)]
        self.live[e, 2] = []
        for d in range(1, self.group):
            copy = pltpu.make_async_remote_copy(
                src_ref=place,
                dst_ref=place,
                send_sem=sems[0].at[at, d - 1],
                recv_sem=sems[1].at[at, d - 1],
                device_id=(self.outer * self.group + lax.rem(self.inner + d, self.group), self.r),
                device_id_type=MESH,
            )
            copy.start()
            self.live[e, 2].append(copy)
        for copy in self.live[e, 2]:
            copy.wait_recv()

    def wait_near(self, e):
        for copy in self.live[e, 0]:
            copy.wait_recv()

    def send_far(self, e):
        self.live[e, 1] = []
        place = self.far[e].at[self.outer]
        for d, peer in enumerate(self.others):
            copy = pltpu.make_async_remote_copy(
                src_ref=place,
                dst_ref=place,
                send_sem=self.sems[2].at[e, d],
                recv_sem=self.sems[3].at[e, d],
                device_id=peer,
                device_id_type=MESH,
            )
            copy.start()
            self.live[e, 1].append(copy)

    def wait_far(self, e):
        for copy in self.live[e, 1]:
            copy.wait_recv()

    def finish(self):
        for copies in self.live.values():
            for copy in copies:
                copy.wait_send()


def fold_moments(buf, tallies, count, scale):
    sums, total = buf[0, 0:8, :], tallies[0]
    for i in range(1, count):
        sums = sums + buf[i, 0:8, :]
        total = total + tallies[i]
    mean = sums * (1.0 / jnp.maximum(total * scale, 1.0))
    spread = None
    for i in range(count):
        n = tallies[i] * scale
        apart = buf[i, 0:8, :] * (1.0 / jnp.maximum(n, 1.0)) - mean
        term = buf[i, 8:16, :] + n * apart * apart
        spread = term if spread is None else spread + term
    return sums, spread, total


def fold_sums(buf, count):
    total = buf[0]
    for i in range(1, count):
        total = total + buf[i]
    return total


def exchange_shapes(widths, tiles, crops, cut=()):
    group = 4 if crops % 4 == 0 else 1
    outers = crops // group
    blocks, near, far = [], [], []
    for at, (width, tile) in enumerate(zip(widths, tiles)):
        lanes = pieces(width)[1]
        blocks.append(pltpu.VMEM((8 * tile, lanes), F32))
        if at in cut:
            lanes = 128
        near.append(pltpu.VMEM((2 * group, 8 * tile, lanes), F32))
        far.append(pltpu.VMEM((outers, 8 * tile, lanes), F32))
    e = len(widths)
    sems = [
        pltpu.SemaphoreType.DMA((e, 2 * group - 1)),
        pltpu.SemaphoreType.DMA((e, 2 * group - 1)),
        pltpu.SemaphoreType.DMA((e, max(outers - 1, 1))),
        pltpu.SemaphoreType.DMA((e, max(outers - 1, 1))),
    ]
    return blocks + near + far + sems


def take(refs, count):
    return list(refs[:count]), refs[count:]


def pack(block, tile, rows, width):
    count, lanes = pieces(width)
    for q in range(count):
        for v in range(2):
            block[tile * 8 + 2 * q + v : tile * 8 + 2 * q + v + 1, :] = rows[v][:, q * lanes : (q + 1) * lanes]


def unpack(table, row, tile, width):
    count, lanes = pieces(width)
    for q in range(count):
        table[row : row + 2, q * lanes : (q + 1) * lanes] = tile[2 * q : 2 * q + 2, :]


def crop_stats(ref, row0, rows, step, width, edge, pitch, pixels, crop, cs, cm, col0=0):
    mask = keep(width, pitch, edge)
    zero = jnp.zeros((8, width), F32)
    cols = pl.ds(col0, width) if isinstance(col0, int) else pl.ds(pl.multiple_of(col0, 128), width)
    near = min(8, edge)
    first = masked(ref[span(row0, 8, 8), cols], keep(width, 8, edge))
    pivot = jnp.sum(first, axis=0, keepdims=True) * (1.0 / near)

    def tile(i, acc):
        d = masked(ref[span(row0 + i * step, step, 8), cols] - pivot, mask)
        return acc[0] + tile_sum(d), acc[1] + tile_sum(d * d)

    if rows == step:
        s, m = tile(0, (zero, zero))
    else:
        s, m = lax.fori_loop(0, rows // step, tile, (zero, zero))
    s = jnp.sum(s, axis=0, keepdims=True)
    m = jnp.sum(m, axis=0, keepdims=True)
    cs[pl.ds(crop, 1), cols] = s + pivot * float(pixels)
    cm[pl.ds(crop, 1), cols] = jnp.maximum(m - s * s * (1.0 / pixels), 0.0)


def local_moments(block, cs, cm, wcol, width, scale, tally=False):
    s, m = cs[:, 0:width], cm[:, 0:width]
    pix = wcol[:, 2:3] * scale
    mean_c = s * (1.0 / pix)
    sums, squares, tallies = [], [], []
    for v in range(2):
        w = wcol[:, v : v + 1]
        total = jnp.sum(w * s, axis=0, keepdims=True)
        n = jnp.sum(w * pix, axis=0, keepdims=True)
        apart = mean_c - total * (1.0 / jnp.maximum(n, 1.0))
        squares.append(jnp.sum(w * (m + pix * apart * apart), axis=0, keepdims=True))
        sums.append(total)
        tallies.append(n)
    pack(block, 0, sums, width)
    pack(block, 1, squares, width)
    if tally:
        lanes = pieces(width)[1]
        for q in range(4):
            for v in range(2):
                block[16 + 2 * q + v : 17 + 2 * q + v, :] = jnp.broadcast_to(tallies[v], (1, lanes))


def local_sums(block, parts, wcol, width):
    for tile, part in enumerate(parts):
        s = part[:, 0:width]
        pack(block, tile, [jnp.sum(wcol[:, v : v + 1] * s, axis=0, keepdims=True) for v in range(2)], width)


def view_tables(sets, core, views, wv, wcol):
    row = lax.broadcasted_iota(jnp.int32, wcol.shape, 0)
    lane = lax.broadcasted_iota(jnp.int32, wcol.shape, 1)
    table = jnp.where(lane == 2, 1.0, 0.0)
    for m, view in zip(sets, views):
        for c in range(m.count):
            second = view[core * m.count + c].astype(F32)
            pair = (1.0 - second, second, float(m.pixels))
            for v in range(3):
                table = jnp.where((row == m.crop0 + c) & (lane == v), pair[v], table)
            wv[0, m.crop0 + c] = pair[0]
            wv[1, m.crop0 + c] = pair[1]
    wcol[...] = table


def by_view(wv, crop, pair):
    return wv[0, crop] * pair[0:1, :] + wv[1, crop] * pair[1:2, :]


FWD_WIDTHS = (256, 256, 1024, 512, 2048, 512, 2048, 2048)


def forward_kernel(sets, total, guarded, outs, crops, dims, *refs):
    c3, cin, c4, cout = dims
    (
        vb, vs, norms1, norms2,
        img_b, img_s, cot_b, cot_s, w1_h, wsp1_h, w3_h, w4_h, w5_h, w6_h, w7_h,
    ), refs = refs[:15], refs[15:]
    (
        o_img, o_z1, o_h1, o_z2, o_h2, o_blk, o_z4, o_x5, o_z5, o_h5, o_xe, o_res, o_d6, o_d7,
        o_st1, o_st2, o_st3, o_st4, o_st7, o_st5, o_st6, o_sq, o_tally,
    ), refs = refs[:23], refs[23:]
    (
        img, z1, h1, z2, h2, zt, blk, eb, z4, xe, z7, hp, x5, z5, h5, z6, cot,
        w1, wsp1, w3, w4, w5, w6, w7, cs, cm, ck,
        st1, st2, st3, st4, st7, st5, st6, sq, tally_v, wv, wcol,
    ), refs = refs[:38], refs[38:]
    e = len(FWD_WIDTHS)
    blocks, refs = take(refs, e)
    near, refs = take(refs, e)
    far, refs = take(refs, e)
    ns_, nr_, fs_, fr_ = refs[:4]
    whole6, whole7, back_s, back_r = refs[4:8]
    load_sem, img_sem, img_send, img_recv, out_sem = refs[8:]
    links = Links(crops, near, far, ns_, nr_, fs_, fr_)
    k, core = links.k, links.r
    sibling = (k, 1 - core)
    f = F32

    loads = []
    for i, (src, dst) in enumerate(
        ((w1_h, w1), (wsp1_h, wsp1), (w3_h, w3), (w4_h, w4), (w5_h, w5), (w6_h, w6), (w7_h, w7),
            (cot_b, cot.at[0 : sets[1].out0]), (cot_s, cot.at[sets[1].out0 : outs]))
    ):
        loads.append(pltpu.make_async_copy(src, dst, load_sem.at[i]))
    own, swaps = [], []
    for at, (m, src) in enumerate(zip(sets, (img_b, img_s))):
        part = m.rows // 2
        for c in range(m.count):
            i = m.crop0 + c
            place = img.at[span(m.row0 + c * m.rows + core * part, part)]
            own.append(
                pltpu.make_async_copy(
                    src.at[span((core * m.count + c) * part, part)], place, img_sem.at[i]
                )
            )
            swaps.append(
                pltpu.make_async_remote_copy(
                    src_ref=src.at[span(((1 - core) * m.count + c) * part, part)],
                    dst_ref=place,
                    send_sem=img_send.at[i],
                    recv_sem=img_recv.at[i],
                    device_id=sibling,
                    device_id_type=MESH,
                )
            )
    for copy in own:
        copy.start()
    loads[0].start()
    links.greet()
    for copy in swaps:
        copy.start()

    view_tables(sets, core, (vb, vs), wv, wcol)
    out_copies = []

    def put(src, dst):
        copy = pltpu.make_async_copy(src, dst, out_sem.at[len(out_copies)])
        copy.start()
        out_copies.append(copy)

    for ref in (cs, cm, ck):
        ref[...] = jnp.zeros(ref.shape, f)
    for block in blocks:
        block[...] = jnp.zeros(block.shape, f)
    h1[0:16, :] = jnp.zeros((16, 3 * c3), BF16)
    for m in sets:
        for c in range(m.count):
            at = m.guard0 + c * m.guard + m.rows
            h1[at : at + 16, :] = jnp.zeros((16, 3 * c3), BF16)

    def near_tallies():
        return [near[0][i, 16:24, 0:1] for i in range(links.wide)]

    def far_tallies():
        return [far[0][i, 16:24, 0:1] for i in range(links.outers)]

    def meet_near(i, scale):
        links.wait_near(i)
        sums, spread, n = fold_moments(near[i], near_tallies(), links.wide, scale)
        place = far[i].at[links.outer]
        place[0:8, :] = sums
        place[8:16, :] = spread
        if i == 0:
            place[16:24, :] = jnp.broadcast_to(n, (8, near[0].shape[2]))
        links.send_far(i)

    def meet_far(i, scale, table, width):
        links.wait_far(i)
        sums, spread, n = fold_moments(far[i], far_tallies(), links.outers, scale)
        over = 1.0 / (n * scale)
        mean = sums * over
        inverse = lax.rsqrt(spread * over + EPS)
        unpack(table, 0, mean, width)
        unpack(table, 2, inverse, width)
        if i == 0:
            tally_v[...] = jnp.broadcast_to(n, (8, 128))

    loads[0].wait()
    for m in sets:

        def pair(p, m=m):
            r = m.row0 + p * 2 * m.rows
            for j in range(2):
                own[m.crop0 + 2 * p + j].wait()
                swaps[m.crop0 + 2 * p + j].wait_recv()
            z1[span(r, 2 * m.rows), :] = mm(img[span(r, 2 * m.rows), :], w1[...])
            for j in range(2):
                crop_stats(z1, r + j * m.rows, m.rows, m.rows // 2, c3, m.edge, 16, m.pixels, m.crop0 + 2 * p + j, cs, cm)

        for p in range(m.count // 2):
            pair(p)
            if m is sets[0] and p == 0:
                for copy in loads[1:]:
                    copy.start()
    local_moments(blocks[0], cs, cm, wcol, c3, 1.0, True)
    links.send_near(0, blocks[0])
    put(img, o_img)
    put(z1, o_z1)
    loads[1].wait()
    meet_near(0, 1.0)
    meet_far(0, 1.0, st1, c3)

    for m in sets:

        def pair(p, m=m):
            r = m.row0 + p * 2 * m.rows
            g = m.guard0 + p * 2 * m.guard
            for j in range(2):
                crop = m.crop0 + 2 * p + j
                mean = by_view(wv, crop, st1[0:2, :])
                scale = by_view(wv, crop, st1[2:4, :]) * norms1[0:1, 0:c3]
                shift = norms1[1:2, 0:c3] - mean * scale
                step = m.rows // 2
                mask = keep(c3, 16, m.edge)

                def tile(i):
                    z = z1[span(r + j * m.rows + i * step, step), :]
                    h = masked(act(z * scale + shift), mask)
                    rows = span(g + j * m.guard + i * step, step)
                    h1[rows, 0:c3] = pltpu.roll(h, 1, 0).astype(BF16)
                    h1[rows, c3 : 2 * c3] = h.astype(BF16)
                    h1[rows, 2 * c3 : 3 * c3] = pltpu.roll(h, step - 1, 0).astype(BF16)

                repeat(2, tile)
            size = 2 * m.rows + 16
            z = mm(h1[span(g - 16, size), :], wsp1[0]) + mm(h1[span(g, size), :], wsp1[1])
            z = z + mm(h1[span(g + 16, size), :], wsp1[2])
            z2[span(r, m.rows), :] = z[0 : m.rows]
            z2[span(r + m.rows, m.rows), :] = z[m.guard : m.guard + m.rows]
            for j in range(2):
                crop_stats(z2, r + j * m.rows, m.rows, m.rows // 2, c3, m.edge, 16, m.pixels, m.crop0 + 2 * p + j, cs, cm)

        repeat(m.count // 2, pair)
    local_moments(blocks[1], cs, cm, wcol, c3, 1.0)
    links.send_near(1, blocks[1])
    put(h1, o_h1)
    put(z2, o_z2)
    loads[2].wait()
    meet_near(1, 1.0)
    meet_far(1, 1.0, st2, c3)

    for m in sets:

        def pair(p, m=m):
            r = m.row0 + p * 2 * m.rows
            for j in range(2):
                crop = m.crop0 + 2 * p + j
                mean = by_view(wv, crop, st2[0:2, :])
                scale = by_view(wv, crop, st2[2:4, :]) * norms1[0:1, c3 : 2 * c3]
                shift = norms1[1:2, c3 : 2 * c3] - mean * scale
                step = m.rows // 2

                def tile(i):
                    rows = span(r + j * m.rows + i * step, step)
                    h2[rows, :] = act(z2[rows, :] * scale + shift).astype(BF16)

                repeat(2, tile)
            zt[0 : 2 * m.rows, :] = mm(h2[span(r, 2 * m.rows), :], w3[...])
            for j in range(2):
                crop_stats(zt, j * m.rows, m.rows, 32, cin, m.edge, 16, m.pixels, m.crop0 + 2 * p + j, cs, cm)

        repeat(m.count // 2, pair)
    local_moments(blocks[2], cs, cm, wcol, cin, 1.0)
    links.send_near(2, blocks[2])
    put(h2, o_h2)
    loads[3].wait()
    meet_near(2, 1.0)
    meet_far(2, 1.0, st3, cin)

    for m in sets:

        def pair(p, m=m):
            r = m.row0 + p * 2 * m.rows
            zt[0 : 2 * m.rows, :] = mm(h2[span(r, 2 * m.rows), :], w3[...])
            for j in range(2):
                crop = m.crop0 + 2 * p + j
                mean = by_view(wv, crop, st3[0:2, :])
                scale = by_view(wv, crop, st3[2:4, :]) * norms1[0:1, 2 * c3 :]
                shift = norms1[1:2, 2 * c3 :] - mean * scale

                def tile(i):
                    here = span(j * m.rows + i * 32, 32)
                    rows = span(r + j * m.rows + i * 32, 32)
                    u = zt[here, :] * scale + shift + img[rows, :].astype(f)
                    b = act(u)
                    blk[rows, :] = b.astype(BF16)
                    for q in range(cin // 128):
                        eb[q, span(j * m.rows // 2 + i * 16, 16), :] = b[0:16, q * 128 : (q + 1) * 128]

                repeat(m.rows // 32, tile)
            for q in range(cin // 128):
                picked = [eb[q, pl.ds(i * 16, 8, stride=2), :] for i in range(2 * m.half)]
                xe[span(m.out0 + p * 2 * m.out, 2 * m.out), q * 128 : (q + 1) * 128] = jnp.concatenate(
                    picked, axis=0
                ).astype(BF16)
            z4[span(r, 2 * m.rows), :] = mm(blk[span(r, 2 * m.rows), :], w4[...])
            for j in range(2):
                crop_stats(z4, r + j * m.rows, m.rows, 32, c4, m.edge, 16, m.pixels, m.crop0 + 2 * p + j, cs, cm)

        repeat(m.count // 2, pair)
    local_moments(blocks[3], cs, cm, wcol, c4, 1.0)
    links.send_near(3, blocks[3])
    put(blk, o_blk)
    put(z4, o_z4)
    put(xe, o_xe)
    loads[6].wait()

    def wide_product(a, w, z):
        def columns(n):
            cols = pl.ds(pl.multiple_of(n * 512, 512), 512)
            z[:, cols] = mm(a[...], w[:, cols])

        repeat(cout // 512, columns)

    def wide_stats(z):
        for m in sets:

            def crop_(c, m=m):
                def columns(n):
                    crop_stats(
                        z, m.out0 + c * m.out, m.out, m.out, 512, m.half, 8, m.half * m.half,
                        m.crop0 + c, cs, cm, n * 512,
                    )

                repeat(cout // 512, columns)

            repeat(m.count, crop_)

    wide_product(xe, w7, z7)
    meet_near(3, 1.0)
    wide_stats(z7)
    local_moments(blocks[4], cs, cm, wcol, cout, 0.25)
    links.send_near(4, blocks[4])
    meet_far(3, 1.0, st4, c4)

    loads[4].wait()
    lots = c4 // 128
    hp[:, 0:24, :] = jnp.zeros((lots, 24, 128), f)
    for m in sets:

        def pair(p, m=m):
            r = m.row0 + p * 2 * m.rows
            for j in range(2):
                crop = m.crop0 + 2 * p + j
                mean = by_view(wv, crop, st4[0:2, :])
                scale = by_view(wv, crop, st4[2:4, :]) * norms2[0:1, 0:c4]
                shift = norms2[1:2, 0:c4] - mean * scale
                mask = keep(c4, 16, m.edge)
                base = 24 + j * m.guard
                hp[:, base + m.rows : base + m.guard, :] = jnp.zeros((lots, 16, 128), f)

                def tile(i):
                    z = z4[span(r + j * m.rows + i * 32, 32), :]
                    h = masked(act(z * scale + shift), mask)
                    for q in range(lots):
                        hp[q, span(base + i * 32, 32, 8), :] = h[:, q * 128 : (q + 1) * 128]

                repeat(m.rows // 32, tile)
            for a in range(3):
                for b in range(3):
                    for q in range(lots):
                        picked = []
                        for j in range(2):
                            for i in range(m.half):
                                at = 24 + j * m.guard + (2 * i + a - 1) * 16 + b - 1
                                picked.append(hp[q, pl.ds(at, 8, stride=2), :])
                        tap = (3 * a + b) * c4 + q * 128
                        x5[span(m.out0 + p * 2 * m.out, 2 * m.out), tap : tap + 128] = jnp.concatenate(
                            picked, axis=0
                        ).astype(BF16)

        repeat(m.count // 2, pair)
    z5[...] = jnp.zeros(z5.shape, f)

    def taps(t):
        part = pl.ds(pl.multiple_of(t * 3 * c4, 128), 3 * c4)
        z5[...] += mm(x5[:, part], w5[part, :])

    repeat(3, taps)
    for m in sets:

        def crop_(c, m=m):
            crop_stats(z5, m.out0 + c * m.out, m.out, m.out, c4, m.half, 8, m.half * m.half, m.crop0 + c, cs, cm)

        repeat(m.count, crop_)
    local_moments(blocks[5], cs, cm, wcol, c4, 0.25)
    links.send_near(5, blocks[5])
    put(x5, o_x5)
    put(z5, o_z5)
    meet_near(4, 0.25)
    meet_near(5, 0.25)
    meet_far(4, 0.25, st7, cout)
    meet_far(5, 0.25, st5, c4)

    loads[5].wait()
    for m in sets:

        def pair(p, m=m):
            o = m.out0 + p * 2 * m.out
            halves = []
            for j in range(2):
                crop = m.crop0 + 2 * p + j
                mean = by_view(wv, crop, st5[0:2, :])
                scale = by_view(wv, crop, st5[2:4, :]) * norms2[0:1, c4 : 2 * c4]
                z = z5[span(o + j * m.out, m.out, 8), :]
                halves.append(act(z * scale + (norms2[1:2, c4 : 2 * c4] - mean * scale)))
            h5[span(o, 2 * m.out), :] = jnp.concatenate(halves, axis=0).astype(BF16)

        repeat(m.count // 2, pair)
    wide_product(h5, w6, z6)
    wide_stats(z6)
    local_moments(blocks[6], cs, cm, wcol, cout, 0.25)
    links.send_pieces(6, blocks[6])
    put(h5, o_h5)
    loads[7].wait()
    loads[8].wait()

    def center(ms):
        for m in ms:

            def crop_(c, m=m):
                def columns(n):
                    cols = pl.ds(pl.multiple_of(n * 512, 512), 512)
                    rows = span(m.out0 + c * m.out, m.out, 8)
                    mean = by_view(wv, m.crop0 + c, st7[0:2, cols])
                    z7[rows, cols] = (z7[rows, cols] - mean) * by_view(wv, m.crop0 + c, st7[2:4, cols])

                repeat(cout // 512, columns)

            repeat(m.count, crop_)

    center(sets[:1])
    meet_near(6, 0.25)
    center(sets[1:])
    links.wait_far(6)
    sums, spread, n = fold_moments(far[6], far_tallies(), links.outers, 0.25)
    over = 4.0 / n
    here = links.piece(links.inner)
    whole6[0:8, here] = sums * over
    whole6[8:16, here] = lax.rsqrt(spread * over + EPS)
    links.collect(6, whole6, (back_s, back_r), 0)
    for t in range(2):
        unpack(st6, 2 * t, whole6[8 * t : 8 * t + 8, :], cout)

    out_copies[6].wait()
    g6, g7 = 2 * c4, 2 * c4 + cout
    lanes = 512
    for m in sets:

        def pair(p, m=m):
            o = m.out0 + p * 2 * m.out

            def columns(n):
                cols = pl.ds(pl.multiple_of(n * lanes, lanes), lanes)
                cols6 = pl.ds(pl.multiple_of(g6 + n * lanes, lanes), lanes)
                cols7 = pl.ds(pl.multiple_of(g7 + n * lanes, lanes), lanes)
                c = cot[span(o, 2 * m.out), cols].astype(f)
                mask = keep(lanes, 8, m.half)
                found = []
                for j in range(2):
                    crop = m.crop0 + 2 * p + j
                    rows = span(o + j * m.out, m.out, 8)
                    n6 = (z6[rows, cols] - by_view(wv, crop, st6[0:2, cols])) * by_view(wv, crop, st6[2:4, cols])
                    n7 = z7[rows, cols]
                    z6[rows, cols] = n6
                    u = n6 * norms2[0:1, cols6] + n7 * norms2[0:1, cols7] + (norms2[1:2, cols6] + norms2[1:2, cols7])
                    a, slope = act_both(u)
                    found.append(a)
                    up = masked(slope * c[j * m.out : (j + 1) * m.out], mask)
                    z4[span(n * outs + o + j * m.out, m.out, 8), :] = up
                    for to, part in ((cs, up), (cm, up * n6), (ck, up * n7)):
                        to[pl.ds(crop, 1), cols] = jnp.sum(tile_sum(part), axis=0, keepdims=True)
                w6[span(o, 2 * m.out), cols] = jnp.concatenate(found, axis=0).astype(BF16)

            repeat(cout // lanes, columns)

        repeat(m.count // 2, pair)
    local_sums(blocks[7], (cs, cm, ck), wcol, cout)
    links.send_pieces(7, blocks[7])
    put(w6.at[0:outs], o_res)
    links.wait_near(7)
    far[7][links.outer] = fold_sums(near[7], links.wide)
    links.send_far(7)
    links.wait_far(7)
    whole7[:, here] = fold_sums(far[7], links.outers)
    links.collect(7, whole7, (back_s, back_r), 1)
    for t in range(3):
        unpack(sq, 2 * t, whole7[8 * t : 8 * t + 8, :], cout)

    for m in sets:

        def pair(p, m=m):
            o = m.out0 + p * 2 * m.out

            def columns(n):
                cols = pl.ds(pl.multiple_of(n * lanes, lanes), lanes)
                mask = keep(lanes, 8, m.half)
                got6, got7 = [], []
                for j in range(2):
                    crop = m.crop0 + 2 * p + j
                    rows = span(o + j * m.out, m.out, 8)
                    up = z4[span(n * outs + o + j * m.out, m.out, 8), :]
                    over = wv[0, crop] * (4.0 / tally_v[0:1, 0:1]) + wv[1, crop] * (4.0 / tally_v[1:2, 0:1])
                    level = by_view(wv, crop, sq[0:2, cols]) * over
                    for got, z, st, at, t in ((got6, z6, st6, g6, 2), (got7, z7, st7, g7, 4)):
                        inv = by_view(wv, crop, st[2:4, cols])
                        gain = inv * norms2[0:1, pl.ds(pl.multiple_of(at + n * lanes, lanes), lanes)]
                        tilt = by_view(wv, crop, sq[t : t + 2, cols]) * over
                        got.append(masked(gain * (up - level - z[rows, cols] * tilt), mask))
                w7[span(o, 2 * m.out), cols] = jnp.concatenate(got6, axis=0).astype(BF16)
                w7[span(cin // 2 + o, 2 * m.out), cols] = jnp.concatenate(got7, axis=0).astype(BF16)

            repeat(cout // lanes, columns)

        repeat(m.count // 2, pair)
    put(w7.at[0:outs], o_d6)
    put(w7.at[cin // 2 : cin // 2 + outs], o_d7)
    for src, dst in (
        (st1, o_st1), (st2, o_st2), (st3, o_st3), (st4, o_st4), (st7, o_st7), (st5, o_st5), (st6, o_st6),
        (sq, o_sq), (tally_v, o_tally),
    ):
        put(src, dst)
    links.finish()
    for copy in swaps:
        copy.wait_send()
    for i, copy in enumerate(out_copies):
        if i != 6:
            copy.wait()


def flat_rows(tensor, pitch):
    n, h, w, c = tensor.shape
    return jnp.pad(tensor, ((0, 0), (0, 0), (0, pitch - w), (0, 0))).reshape(n * h * pitch, c)


def forward(images, cots, views, w, norms_first, norms_second, ident):
    crops = lax.axis_size("crops")
    nb, ns = images[0].shape[0] // 2, images[1].shape[0] // 2
    sets, total, guarded, outs = geometry(nb, images[0].shape[2], ns, images[1].shape[2])
    w1, wsp1, w3, w4, w5, w6, w7 = w
    cin, c3 = w1.shape
    c4, cout = w6.shape
    smem, vmem = pl.BlockSpec(memory_space=pltpu.SMEM), pl.BlockSpec(memory_space=pltpu.VMEM)
    hbm = pl.BlockSpec(memory_space=pl.ANY)
    shape = jax.ShapeDtypeStruct
    out_shape = [
        shape((total, cin), BF16), shape((total, c3), F32), shape((guarded, 3 * c3), BF16), shape((total, c3), F32),
        shape((total, c3), BF16), shape((total, cin), BF16), shape((total, c4), F32), shape((outs, 9 * c4), BF16),
        shape((outs, c4), F32), shape((outs, c4), BF16), shape((outs, cin), BF16), shape((outs, cout), BF16),
        shape((outs, cout), BF16), shape((outs, cout), BF16),
        shape((8, c3), F32), shape((8, c3), F32), shape((8, cin), F32), shape((8, c4), F32), shape((8, cout), F32),
        shape((8, c4), F32), shape((8, cout), F32), shape((8, cout), F32), shape((8, 128), F32),
    ]
    most = 2 * sets[0].rows
    scratch = [
        pltpu.VMEM((total, cin), BF16), pltpu.VMEM((total, c3), F32), pltpu.VMEM((guarded, 3 * c3), BF16),
        pltpu.VMEM((total, c3), F32), pltpu.VMEM((total, c3), BF16), pltpu.VMEM((most, cin), F32),
        pltpu.VMEM((total, cin), BF16), pltpu.VMEM((cin // 128, most // 2, 128), F32), pltpu.VMEM((total, c4), F32),
        pltpu.VMEM((outs, cin), BF16), pltpu.VMEM((outs, cout), F32), pltpu.VMEM((c4 // 128, 24 + 2 * sets[0].guard, 128), F32),
        pltpu.VMEM((outs, 9 * c4), BF16), pltpu.VMEM((outs, c4), F32),
        pltpu.VMEM((outs, c4), BF16), pltpu.VMEM((outs, cout), F32), pltpu.VMEM((outs, cout), BF16),
    ]
    scratch += [pltpu.VMEM(t.shape, BF16) for t in w]
    scratch += [pltpu.VMEM((16, cout), F32)] * 3
    scratch += [pltpu.VMEM((8, n), F32) for n in (c3, c3, cin, c4, cout, c4, cout, cout, 128)]
    scratch += [pltpu.SMEM((2, 16), F32), pltpu.VMEM((16, 128), F32)]
    scratch += exchange_shapes(FWD_WIDTHS, (3, 2, 2, 2, 2, 2, 2, 3), crops, (6, 7))
    scratch += [pltpu.VMEM((16, cout // 4), F32), pltpu.VMEM((24, cout // 4), F32)]
    scratch += [pltpu.SemaphoreType.DMA((2, 3))] * 2
    scratch += [
        pltpu.SemaphoreType.DMA((9,)), pltpu.SemaphoreType.DMA((nb + ns,)), pltpu.SemaphoreType.DMA((nb + ns,)),
        pltpu.SemaphoreType.DMA((nb + ns,)), pltpu.SemaphoreType.DMA((23,)),
    ]
    got = pl.pallas_call(
        functools.partial(forward_kernel, sets, total, guarded, outs, crops, (c3, cin, c4, cout)),
        out_shape=out_shape,
        in_specs=[smem, smem, vmem, vmem] + [hbm] * 11,
        out_specs=[hbm] * len(out_shape),
        scratch_shapes=scratch,
        compiler_params=pltpu.CompilerParams(
            collective_id=ident, has_side_effects=True, vmem_limit_bytes=63 * 1024 * 1024
        ),
        name="forward",
    )(
        *views, norms_first, norms_second,
        flat_rows(images[0], 16), flat_rows(images[1], 16),
        *[flat_rows(t, 8) for t in cots], *w,
    )
    return sets, (total, guarded, outs), got


def share_plan(shapes, cuts):
    chunks = []
    for at, (height, width) in enumerate(shapes):
        down, across = cuts[at]
        half, high = width // 2 // across, height // down
        for c in range(down):
            for p in range(across):
                chunks.append((at, c * high, high, p * half, half))
    return chunks


class Share:
    def __init__(self, shapes, chunks, orders, bits, links, sources, outs, acc, recv0, recvs, sems, begin, leave):
        self.shapes, self.chunks, self.bits = shapes, chunks, bits
        self.k, self.core = links.k, links.r
        self.sources, self.outs, self.acc, self.recv0, self.recvs = sources, outs, acc, recv0, recvs
        self.send_sem, self.recv_sem, self.load_sem, self.store_sem = sems
        self.sibling = (self.k, 1 - self.core)
        self.total = 2 * bits + 2
        self.live, self.loads, self.stores, self.begin, self.leave, self.at = {}, {}, {}, begin, leave, 0
        digit = [lax.rem(self.k // (1 << b), 2) for b in range(bits)]
        self.stages, self.regions, self.kinds, self.slots = [], [], [], []
        for i, (at, row, height, col, width) in enumerate(chunks):
            stages = []
            for a, b in zip(*orders[i]):
                if a == b:
                    mine, step = digit[a], 1 << a
                else:
                    mine = digit[a] * (1 - self.core) + digit[b] * self.core
                    step = (1 << a) * (1 - self.core) + (1 << b) * self.core
                stages.append((mine, self.k + step * (1 - 2 * mine)))
            start, length, used = 0, height, 0
            region, kind, slot = [], [], []
            for s in range(bits):
                region.append((start, length))
                slot.append(used)
                if length % 32 == 0:
                    kind.append(True)
                    length //= 2
                    start = start + stages[s][0] * length
                else:
                    kind.append(False)
                used += length
            region.append((start, length))
            self.stages.append(stages)
            self.regions.append(region)
            self.kinds.append(kind)
            self.slots.append(slot)

    def send(self, i, t, src, dst, device):
        copy = pltpu.make_async_remote_copy(
            src_ref=src,
            dst_ref=dst,
            send_sem=self.send_sem.at[i, t],
            recv_sem=self.recv_sem.at[i, t],
            device_id=device,
            device_id_type=MESH,
        )
        copy.start()
        self.live[i, t] = copy

    def add(self, dst, at, src, src_at, length):
        block = 16
        while length % (block * 2) == 0 and block * 2 * dst.shape[1] <= 65536:
            block *= 2

        def step(j, carry):
            off = j * block
            rows = span(at + off, block)
            dst[rows, :] = dst[rows, :] + src[span(src_at + off, block), :]
            return carry

        lax.fori_loop(0, length // block, step, 0)

    def fetch(self):
        for i, (at, row, height, col, width) in enumerate(self.chunks):
            t = self.begin[i]
            if 1 <= t <= self.bits:
                start, length = self.regions[i][t - 1]
                own = pl.ds(pl.multiple_of(self.core * (self.shapes[at][1] // 2) + col, 128), width)
                self.loads[i] = pltpu.make_async_copy(
                    self.sources[at].at[span(row + start, length), own],
                    self.acc[i].at[span(start, length)],
                    self.load_sem.at[i],
                )
                self.loads[i].start()

    def arrived(self, i, t):
        if (i, t) in self.live:
            self.live[i, t].wait_recv()

    def task(self, i, t):
        at, row, height, col, width = self.chunks[i]
        bits, kinds, regions, stages = self.bits, self.kinds[i], self.regions[i], self.stages[i]
        half = self.shapes[at][1] // 2
        own = pl.ds(pl.multiple_of(self.core * half + col, 128), width)
        rows = pl.ds(row, height)
        if t == 0:
            away = pl.ds(pl.multiple_of((1 - self.core) * half + col, 128), width)
            self.send(i, 0, self.sources[at].at[rows, away], self.recv0[i], self.sibling)
            if self.acc[i] is None:
                self.acc[i] = self.sources[at].at[rows, own]
                return
            copy = pltpu.make_async_copy(self.sources[at].at[rows, own], self.acc[i], self.load_sem.at[i])
            copy.start()
            self.loads[i] = copy
            return
        self.arrived(i, t - 1)
        if t <= bits + 1:
            if t == self.begin[i]:
                if t <= bits:
                    self.loads[i].wait()
            elif t == 1:
                if i in self.loads:
                    self.loads[i].wait()
                self.add(self.acc[i], 0, self.recv0[i], 0, height)
            else:
                s = t - 2
                start, length = regions[s + 1]
                if not kinds[s]:
                    self.live[i, t - 1].wait_send()
                self.add(self.acc[i], start, self.recvs[i], self.slots[i][s], length)
        if t == self.leave[i]:
            start, length = regions[t - 1]
            copy = pltpu.make_async_copy(
                self.acc[i].at[span(start, length)], self.outs[at].at[span(row + start, length), own], self.store_sem.at[i]
            )
            copy.start()
            self.stores[i] = copy
            return
        if t <= bits:
            s = t - 1
            start, length = regions[s]
            give, first = length, start
            if kinds[s]:
                give = length // 2
                first = start + (1 - stages[s][0]) * give
            self.send(
                i, t, self.acc[i].at[span(first, give)], self.recvs[i].at[pl.ds(self.slots[i][s], give)],
                (stages[s][1], self.core),
            )
            return
        if t == bits + 1:
            start, length = regions[bits]
            if t == self.begin[i]:
                mine = self.sources[at].at[span(row + start, length), own]
            else:
                mine = self.acc[i].at[span(start, length)]
            copy = pltpu.make_async_copy(mine, self.outs[at].at[span(row + start, length), own], self.store_sem.at[i])
            copy.start()
            self.stores[i] = copy
        if t == bits + 2:
            self.stores[i].wait()
        if t <= 2 * bits:
            s = bits - 1 - (t - bits - 1)
            start, length = regions[s + 1]
            if kinds[s]:
                place = self.outs[at].at[span(row + start, length), own]
                self.send(i, t, mine if t == bits + 1 else place, place, (stages[s][1], self.core))
            return
        if t == 2 * bits + 1:
            place = self.outs[at].at[rows, own]
            self.send(i, t, place, place, self.sibling)

    def run(self, order):
        while self.at < len(order):
            token = order[self.at]
            self.at += 1
            if token is None:
                return
            i, t = token
            if t == self.total:
                self.arrived(i, t - 1)
            else:
                self.task(i, t)

    def finish(self):
        for (i, t), copy in self.live.items():
            if not (1 <= t <= self.bits and not self.kinds[i][t - 1]):
                copy.wait_send()


def share_scratch(chunks, bits, begin, inside=False):
    acc, recv0, recvs = [], [], []
    for i, (at, row, height, col, width) in enumerate(chunks):
        if begin[i] > bits:
            continue
        acc.append(pltpu.VMEM((height, width), BF16))
        if begin[i] == 0:
            recv0.append(pltpu.VMEM((height, width), BF16))
        length, used = height, 0
        for s in range(bits):
            if length % 32 == 0:
                length //= 2
            used += length
        recvs.append(pltpu.VMEM((used, width), BF16))
    n = len(chunks)
    sems = [pltpu.SemaphoreType.DMA((n, 2 * bits + 2))] * 2 + [pltpu.SemaphoreType.DMA((n,))] * 2
    return ([] if inside else acc) + recv0 + recvs + sems


def share_hold(refs, bits, begin, inside=False):
    n = len(begin)
    acc, recv0, recvs = [None] * n, [None] * n, [None] * n
    for held, most in ((acc, -1 if inside else bits), (recv0, 0), (recvs, bits)):
        for i in range(n):
            if begin[i] <= most:
                held[i], refs = refs[0], refs[1:]
    return acc, recv0, recvs, refs


def share_leave(bits):
    return [bits + 1] * 3 + [min(v, bits + 1) for v in [3, 3, 3]]


def share_orders(bits, path):
    rest = list(range(2, bits))
    if bits < 2:
        return rest or list(range(bits)), rest or list(range(bits))
    if path == 0:
        return [0, 1] + rest, [1, 0] + rest
    if path == 1:
        return [0] + rest + [1], [1] + rest + [0]
    return rest + [0, 1], rest + [1, 0]


SHARE_CUTS = ((1, 2), (1, 1), (3, 1), (1, 1), (1, 1), (1, 1), (1, 1))
SHARE_FIRST = 6
SHARE_PATHS = (1, 1, 0, 1, 1, 2, 1, 1, 0, 2)
SHARE_LATE = (
    51, 37, 21, 96, 5, 83, 67, -1, 22, 97, 84, -1, 38, -1, 52, 98, 68, 6, 85, -1, 53, 23, -1, 39,
    69, -1, 54, 86, -1, 112, 99, 70, -1, 55, 113, 40, -1, 24, 7, 87, -1, 114, 100, -1, -1, 56, 71, -1,
    -1, 128, 115, -1, 144, 88, 129, 41, -1, 145, 116, 25, -1, -1, 117, 57, 42, 72, -1, 26, -1, 118, 130, 146,
    101, 58, 89, 119, 8, 102, 90, 131, 120, 147, 73, 103, 132, 148, 74, 121, 133, 104, 149, 122, 9, 150, 134, 151,
    105, 135, 10, 106, 152, 136, 153, 137, 154, 138,
)
SHARE_EARLY = (
    0, -1, -1, 16, 1, -1, -1, 17, 32, -1, -1, 2, 33, -1, 18, -1, -1, 48, 3, -1, -1, 34, 80, 49,
    -1, 19, 81, 64, 4, -1, 35, 65, 5, 20, -1, 50, -1, 21, 36, -1, 66, 82, -1, 37, 51, -1, -1, 67,
    83,
)


def share_late_order(pieces, bits, parts, ready):
    if bits == 4:
        return [None if v < 0 else (v // 16, v % 16) for v in SHARE_LATE]
    order, total = [], 2 * bits + 2
    begin = share_leave(bits) + [0] * (pieces - SHARE_FIRST)
    for k in range(parts + total + 1):
        for i in range(pieces):
            t = k - ready[i] + begin[i]
            if k >= ready[i] and t <= total:
                order.append((i, t))
        if k < parts:
            order.append(None)
    return order


def share_early_order(bits):
    if bits == 4:
        return [None if v < 0 else (v // 16, v % 16) for v in SHARE_EARLY]
    order = [None] * 10
    for t in range(bits + 2):
        order += [(i, t) for i in range(SHARE_FIRST) if t <= share_leave(bits)[i]] + [None]
    return order


def meet_sums(links, e, width, tables, between=None):
    links.wait_near(e)
    links.far[e][links.outer] = fold_sums(links.near[e], links.wide)
    links.send_far(e)
    if between is not None:
        between()
    links.wait_far(e)
    sums = fold_sums(links.far[e], links.outers)
    for t, (table, row) in enumerate(tables):
        unpack(table, row, sums[8 * t : 8 * t + 8], width)


def share_of(wv, tally, crop, times):
    return wv[0, crop] * (times / tally[0:1, 0:1]) + wv[1, crop] * (times / tally[1:2, 0:1])


class Puts:
    def __init__(self, sem):
        self.sem, self.copies = sem, []

    def put(self, src, dst):
        copy = pltpu.make_async_copy(src, dst, self.sem.at[len(self.copies)])
        copy.start()
        self.copies.append(copy)

    def finish(self):
        for copy in self.copies:
            copy.wait()


def start_loads(pairs, sem):
    copies = [pltpu.make_async_copy(src, dst, sem.at[i]) for i, (src, dst) in enumerate(pairs)]
    for copy in copies:
        copy.start()
    return copies


def back_two_kernel(sets, total, outs, crops, dims, shapes, chunks, *refs):
    c3, cin, c4, cout = dims
    vb, vs, norms1, norms2, st3, st4, st5, tally = refs[:8]
    sources, refs = refs[8:23], refs[23:]
    (o_up, o_g6, o_g7, o_g5, o_g4, o_s5, o_s4, o_s3), refs = refs[:8], refs[8:]
    held, refs = refs[:14], refs[14:]
    (d7, w7, xe, d6, w6, z5, h5, w5, x5, z4, w4, h2, w3, img) = held
    (q5, t7, dh, d4, zt, bg, up, s5, s4, s3, cs, cm, wv, wcol), refs = refs[:14], refs[14:]
    d5, pv, blk = d6, q5, img
    g6, g7, g5, g4 = w6, w7, w5, w4
    blocks, refs = take(refs, 3)
    near, refs = take(refs, 3)
    far, refs = take(refs, 3)
    links = Links(crops, near, far, *refs[:4])
    load_sem, out_sem, up_sem = refs[4:7]
    refs = refs[7:]
    bits = crops.bit_length() - 1
    early = SHARE_FIRST
    acc, recv0, recvs, refs = share_hold(refs, bits, [0] * early, True)
    share = Share(
        shapes, chunks[:early], [share_orders(bits, v) for v in SHARE_PATHS[:early]], bits, links, [g7, g6, g5], [o_g7, o_g6, o_g5],
        acc, recv0, recvs, refs, [0] * early, share_leave(bits),
    )
    order = share_early_order(bits)

    def tick():
        share.run(order)

    f = F32
    loads = start_loads(list(zip(sources, held)), load_sem)
    links.greet()
    view_tables(sets, links.r, (vb, vs), wv, wcol)
    puts = Puts(out_sem)
    for ref in (cs, cm):
        ref[...] = jnp.zeros(ref.shape, f)
    for block in blocks:
        block[...] = jnp.zeros(block.shape, f)

    for i in range(2):
        loads[i].wait()

    def shortcut(n):
        part = pl.ds(pl.multiple_of(n * 256, 256), 256)
        t7[:, part] = mm_nt(d7[...], w7[part, :])

    repeat(cin // 256, shortcut)
    loads[2].wait()
    for piece in range(2):
        for half in range(2):
            cols = slice(half * (cout // 2) + piece * (cout // 4), half * (cout // 2) + (piece + 1) * (cout // 4))
            g7[:, cols] = mm_tn(xe[...], d7[:, cols]).astype(BF16)
        tick()

    for i in range(3, 6):
        loads[i].wait()
    q5[...] = mm_nt(d6[...], w6[...])
    g5at = c4
    for m in sets:

        def crop_(c, m=m):
            crop = m.crop0 + c
            rows = span(m.out0 + c * m.out, m.out, 8)
            inv = by_view(wv, crop, st5[2:4, :])
            n = (z5[rows, :] - by_view(wv, crop, st5[0:2, :])) * inv
            q = act_slope(n * norms2[0:1, g5at : 2 * c4] + norms2[1:2, g5at : 2 * c4]) * q5[rows, :]
            q5[rows, :] = q
            cs[pl.ds(crop, 1), 0:c4] = jnp.sum(tile_sum(q), axis=0, keepdims=True)
            cm[pl.ds(crop, 1), 0:c4] = jnp.sum(tile_sum(q * n), axis=0, keepdims=True)

        repeat(m.count, crop_)
    local_sums(blocks[0], (cs, cm), wcol, c4)
    links.send_near(0, blocks[0])

    tick()
    loads[6].wait()

    def outer(n):
        cols = pl.ds(pl.multiple_of(n * 512, 512), 512)
        g6[:, cols] = mm_tn(h5[...], d6[:, cols]).astype(BF16)

    repeat(cout // 512, outer)
    tick()
    meet_sums(links, 0, c4, ((s5, 0), (s5, 2)))

    for m in sets:

        def pair(p, m=m):
            o = m.out0 + p * 2 * m.out
            mask = keep(c4, 8, m.half)
            slots = [[], [], [], []]
            for j in range(2):
                crop = m.crop0 + 2 * p + j
                rows = span(o + j * m.out, m.out, 8)
                over = share_of(wv, tally, crop, 4.0)
                inv = by_view(wv, crop, st5[2:4, :])
                n = (z5[rows, :] - by_view(wv, crop, st5[0:2, :])) * inv
                d = (inv * norms2[0:1, g5at : 2 * c4]) * (
                    q5[rows, :] - by_view(wv, crop, s5[0:2, :]) * over - n * (by_view(wv, crop, s5[2:4, :]) * over)
                )
                d = masked(d, mask)
                down = jnp.concatenate([d[8:], jnp.zeros((8, c4), f)], axis=0)
                slots[0].append(d)
                slots[1].append(pltpu.roll(d, m.out - 1, 0))
                slots[2].append(down)
                slots[3].append(pltpu.roll(down, m.out - 1, 0))
            for t in range(4):
                d5[span(o, 2 * m.out), t * c4 : (t + 1) * c4] = jnp.concatenate(slots[t], axis=0).astype(BF16)

        repeat(m.count // 2, pair)

    tick()
    loads[7].wait()
    options = (((1, 0),), ((2, 0), (0, 1)))
    for a in range(2):
        for b in range(2):
            value = None
            for r, down in options[a]:
                for c, side in options[b]:
                    slot, tap = (2 * down + side) * c4, (3 * r + c) * c4
                    term = mm_nt(d5[:, slot : slot + c4], w5[tap : tap + c4, :])
                    value = term if value is None else value + term
            pv[...] = value
            for m in sets:

                def crop_(c, m=m, a=a, b=b):
                    for i in range(m.half):
                        for q in range(c4 // 128):
                            dh[q, pl.ds(m.row0 + c * m.rows + (2 * i + a) * 16 + b, 8, stride=2), :] = pv[
                                span(m.out0 + c * m.out + i * 8, 8, 8), q * 128 : (q + 1) * 128
                            ]

                repeat(m.count, crop_)
        tick()
    loads[9].wait()
    for m in sets:

        def crop_(c, m=m):
            crop = m.crop0 + c
            rows = span(m.row0 + c * m.rows, m.rows)
            mask = keep(128, 16, m.edge)
            levels, tilts = [], []
            for q in range(c4 // 128):
                cols = slice(q * 128, (q + 1) * 128)
                inv = by_view(wv, crop, st4[2:4, cols])
                n = (z4[rows, cols] - by_view(wv, crop, st4[0:2, cols])) * inv
                up_ = masked(act_slope(n * norms2[0:1, cols] + norms2[1:2, cols]) * dh[q, rows, :], mask)
                dh[q, rows, :] = up_
                levels.append(jnp.sum(tile_sum(up_), axis=0, keepdims=True))
                tilts.append(jnp.sum(tile_sum(up_ * n), axis=0, keepdims=True))
            cs[pl.ds(crop, 1), 0:c4] = jnp.concatenate(levels, axis=1)
            cm[pl.ds(crop, 1), 0:c4] = jnp.concatenate(tilts, axis=1)

        repeat(m.count, crop_)
        tick()
    local_sums(blocks[1], (cs, cm), wcol, c4)
    links.send_near(1, blocks[1])
    loads[8].wait()

    def kernel(n):
        for t in range(3 * n, 3 * n + 3):
            part = slice(t * c4, (t + 1) * c4)
            g5[part, :] = mm_tn(x5[:, part], d5[:, 0:c4]).astype(BF16)
        tick()

    kernel(0)

    def rest():
        kernel(1)
        kernel(2)

    meet_sums(links, 1, c4, ((s4, 0), (s4, 2)), rest)
    tick()

    for i in range(10, 14):
        loads[i].wait()
    big_rows = 2 * sets[0].rows
    for at, m in enumerate(sets):

        def pair(p, m=m, at=at):
            r = m.row0 + p * 2 * m.rows
            o = m.out0 + p * 2 * m.out
            mask = keep(128, 16, m.edge)
            for j in range(2):
                crop = m.crop0 + 2 * p + j
                rows = span(r + j * m.rows, m.rows)
                over = share_of(wv, tally, crop, 1.0)
                for q in range(c4 // 128):
                    cols = slice(q * 128, (q + 1) * 128)
                    inv = by_view(wv, crop, st4[2:4, cols])
                    n = (z4[rows, cols] - by_view(wv, crop, st4[0:2, cols])) * inv
                    d = (inv * norms2[0:1, cols]) * (
                        dh[q, rows, :] - by_view(wv, crop, s4[0:2, cols]) * over - n * (by_view(wv, crop, s4[2:4, cols]) * over)
                    )
                    d4[rows, cols] = masked(d, mask).astype(BF16)
            got = mm_nt(d4[span(r, 2 * m.rows), :], w4[...])
            for q in range(cin // 128):
                bg[q, 0 : 2 * m.rows, :] = got[:, q * 128 : (q + 1) * 128]
            for q in range(cin // 128):
                for j in range(2):
                    for i in range(m.half):
                        here = pl.ds(j * m.rows + i * 32, 8, stride=2)
                        bg[q, here, :] = bg[q, here, :] + t7[span(o + j * m.out + i * 8, 8, 8), q * 128 : (q + 1) * 128]
            turn = m.crop0 // 2 + p
            slot = turn % 2

            def left(turn, slot):
                return pltpu.make_async_copy(
                    up.at[slot, 0 : 2 * m.rows], o_up.at[span(r, 2 * m.rows)], up_sem.at[turn]
                )

            if turn >= 2:
                size = big_rows if turn - 2 < sets[0].count // 2 else 2 * m.rows
                pltpu.make_async_copy(up.at[slot, 0:size], o_up.at[pl.ds(0, size)], up_sem.at[turn - 2]).wait()
            step = m.rows // 2
            mask = keep(128, 16, m.edge)
            totals = [[[], []], [[], []]]
            for h, j in [(h, j) for h in range(cin // 512) for j in range(2)]:
                if j == 0:
                    zt[0 : 2 * m.rows, :] = mm(h2[span(r, 2 * m.rows), :], w3[:, h * 512 : (h + 1) * 512])
                crop = m.crop0 + 2 * p + j
                levels, tilts = totals[j]
                for q in range(h * 4, h * 4 + 4):
                    cols = slice(q * 128, (q + 1) * 128)
                    part = slice((q - h * 4) * 128, (q - h * 4 + 1) * 128)
                    at3 = slice(2 * c3 + q * 128, 2 * c3 + (q + 1) * 128)
                    mean, inv = by_view(wv, crop, st3[0:2, cols]), by_view(wv, crop, st3[2:4, cols])
                    gain, bias = norms1[0:1, at3], norms1[1:2, at3]

                    def tile(i, sums, j=j, cols=cols, part=part, q=q, mean=mean, inv=inv, gain=gain, bias=bias):
                        here = span(j * m.rows + i * step, step)
                        rows = span(r + j * m.rows + i * step, step)
                        n = (zt[here, part] - mean) * inv
                        u = n * gain + bias + img[rows, cols].astype(f)
                        got = bg[q, here, :].astype(BF16).astype(f)
                        v = masked(act_slope(u) * got, mask)
                        up[slot, here, cols] = v
                        return (sums[0] + tile_sum(v), sums[1] + tile_sum(v * n))

                    zero = jnp.zeros((8, 128), f)
                    s, t = lax.fori_loop(0, 2, tile, (zero, zero))
                    levels.append(jnp.sum(s, axis=0, keepdims=True))
                    tilts.append(jnp.sum(t, axis=0, keepdims=True))
            for j in range(2):
                crop = m.crop0 + 2 * p + j
                cs[pl.ds(crop, 1), :] = jnp.concatenate(totals[j][0], axis=1)
                cm[pl.ds(crop, 1), :] = jnp.concatenate(totals[j][1], axis=1)
            left(turn, slot).start()

        for p in range(m.count // 2):
            pair(p)
            tick()
    late = pltpu.make_async_copy(sources[14], blk, load_sem.at[14])
    late.start()
    local_sums(blocks[2], (cs, cm), wcol, cin)
    links.send_near(2, blocks[2])
    late.wait()

    def inner(n):
        part = pl.ds(pl.multiple_of(n * 256, 256), 256)
        g4[part, :] = mm_tn(blk[:, part], d4[...]).astype(BF16)

    repeat(2, inner)
    tick()

    def rest():
        repeat(cin // 256 - 2, lambda n: inner(n + 2))
        puts.put(g4, o_g4)
        tick()

    meet_sums(links, 2, cin, ((s3, 0), (s3, 2)), rest)
    for src, dst in ((s5, o_s5), (s4, o_s4), (s3, o_s3)):
        puts.put(src, dst)
    for back in (2, 1):
        size = 2 * sets[1].rows
        turn = (sets[0].count + sets[1].count) // 2 - back
        pltpu.make_async_copy(
            up.at[turn % 2, 0:size], o_up.at[pl.ds(sets[1].row0, size)], up_sem.at[turn]
        ).wait()
    while share.at < len(order):
        tick()
    for copy in share.stores.values():
        copy.wait()
    share.finish()
    links.finish()
    puts.finish()


def back_one_kernel(sets, total, guarded, crops, dims, shapes, chunks, *refs):
    c3, cin = dims
    vb, vs, norms1, st1, st2, st3, s3, tally = refs[:8]
    sources, refs = refs[8:17], refs[17:]
    second, refs = list(refs[:4]), refs[4:]
    (o_gb, o_gs, o_s2, o_s1), refs = refs[:4], refs[4:]
    o_grads, refs = refs[:7], refs[7:]
    held, refs = refs[:9], refs[9:]
    (h2, w3, up, z2, h1, wsp1, z1, w1, img) = held
    (zt, d3, q2, d2, q1, d1, g3, g2, g1, s2, s1, cs, cm, wv, wcol), refs = refs[:15], refs[15:]
    blocks, refs = take(refs, 2)
    near, refs = take(refs, 2)
    far, refs = take(refs, 2)
    links = Links(crops, near, far, *refs[:4])
    load_sem, out_sem, own_sem, grad_send, grad_recv, up_sem = refs[4:10]
    refs = refs[10:]
    n = len(chunks)
    bits = crops.bit_length() - 1
    begin = share_leave(bits) + [0] * (n - SHARE_FIRST)
    acc, recv0, recvs, refs = share_hold(refs, bits, begin)
    share = Share(
        shapes, chunks, [share_orders(bits, v) for v in SHARE_PATHS], bits, links, second + [g3, g2, g1], o_grads,
        acc, recv0, recvs, refs, begin, [2 * bits + 3] * n,
    )
    share.fetch()
    order = share_late_order(n, bits, 20, (0,) * 7 + (7, 14, 15))

    def tick():
        share.run(order)

    core = links.r
    sibling = (links.k, 1 - core)
    f = F32
    loads = start_loads([(a, b) for a, b in zip(sources, held) if b is not up], load_sem)
    ups = []
    for m in sets:
        for p in range(m.count // 2):
            rows = pl.ds(m.row0 + p * 2 * m.rows, 2 * m.rows)
            ups.append(pltpu.make_async_copy(sources[2].at[rows], up.at[rows], up_sem.at[len(ups)]))
    for copy in ups:
        copy.start()
    links.greet()
    tick()
    view_tables(sets, links.r, (vb, vs), wv, wcol)
    puts = Puts(out_sem)
    for ref in (cs, cm):
        ref[...] = jnp.zeros(ref.shape, f)
    for block in blocks:
        block[...] = jnp.zeros(block.shape, f)
    d2[0:16, :] = jnp.zeros((16, 3 * c3), BF16)
    for m in sets:
        for c in range(m.count):
            at = m.guard0 + c * m.guard + m.rows
            d2[at : at + 16, :] = jnp.zeros((16, 3 * c3), BF16)

    for i in range(3):
        loads[i].wait()
    for copy in ups:
        copy.wait()
    for m in sets:

        def pair(p, m=m):
            r = m.row0 + p * 2 * m.rows
            step = m.rows // 2
            mask = keep(128, 16, m.edge)
            for h, j in [(h, j) for h in range(cin // 512) for j in range(2)]:
                if j == 0:
                    zt[0 : 2 * m.rows, :] = mm(h2[span(r, 2 * m.rows), :], w3[:, h * 512 : (h + 1) * 512])
                crop = m.crop0 + 2 * p + j
                over = share_of(wv, tally, crop, 1.0)
                for q in range(h * 4, h * 4 + 4):
                    cols = slice(q * 128, (q + 1) * 128)
                    part = slice((q - h * 4) * 128, (q - h * 4 + 1) * 128)
                    mean, inv = by_view(wv, crop, st3[0:2, cols]), by_view(wv, crop, st3[2:4, cols])
                    gain = inv * norms1[0:1, 2 * c3 + q * 128 : 2 * c3 + (q + 1) * 128]
                    level = by_view(wv, crop, s3[0:2, cols]) * over
                    tilt = by_view(wv, crop, s3[2:4, cols]) * over * inv

                    def tile(i, j=j, cols=cols, part=part, mean=mean, gain=gain, level=level, tilt=tilt):
                        here = span(j * m.rows + i * step, step)
                        rows = span(r + j * m.rows + i * step, step)
                        d = gain * (up[rows, cols] - level - (zt[here, part] - mean) * tilt)
                        d3[rows, cols] = masked(d, mask).astype(BF16)

                    repeat(2, tile)
            q2[span(r, 2 * m.rows), :] = mm_nt(d3[span(r, 2 * m.rows), :], w3[...])
            for j in range(2):
                crop = m.crop0 + 2 * p + j
                mean, inv = by_view(wv, crop, st2[0:2, :]), by_view(wv, crop, st2[2:4, :])

                def tile(i, sums, j=j, mean=mean, inv=inv):
                    rows = span(r + j * m.rows + i * step, step)
                    n = (z2[rows, :] - mean) * inv
                    v = act_slope(n * norms1[0:1, c3 : 2 * c3] + norms1[1:2, c3 : 2 * c3]) * q2[rows, :]
                    q2[rows, :] = v
                    return (sums[0] + tile_sum(v), sums[1] + tile_sum(v * n))

                zero = jnp.zeros((8, c3), f)
                s, t = lax.fori_loop(0, 2, tile, (zero, zero))
                cs[pl.ds(crop, 1), 0:c3] = jnp.sum(s, axis=0, keepdims=True)
                cm[pl.ds(crop, 1), 0:c3] = jnp.sum(t, axis=0, keepdims=True)

        for p in range(m.count // 2):
            pair(p)
            tick()
    local_sums(blocks[0], (cs, cm), wcol, c3)
    links.send_near(0, blocks[0])

    def outer(n):
        cols = pl.ds(pl.multiple_of(n * 256, 256), 256)
        g3[:, cols] = mm_tn(h2[...], d3[:, cols]).astype(BF16)

    repeat(cin // 512, outer)
    tick()

    def rest():
        repeat(cin // 512, lambda n: outer(n + cin // 512))
        tick()

    meet_sums(links, 0, c3, ((s2, 0), (s2, 2)), rest)

    for i in range(3, 6):
        loads[i].wait()
    for m in sets:

        def pair(p, m=m):
            r = m.row0 + p * 2 * m.rows
            g = m.guard0 + p * 2 * m.guard
            step = m.rows // 2
            mask = keep(c3, 16, m.edge)
            for j in range(2):
                crop = m.crop0 + 2 * p + j
                over = share_of(wv, tally, crop, 1.0)
                mean, inv = by_view(wv, crop, st2[0:2, :]), by_view(wv, crop, st2[2:4, :])
                gain = inv * norms1[0:1, c3 : 2 * c3]
                level = by_view(wv, crop, s2[0:2, :]) * over
                tilt = by_view(wv, crop, s2[2:4, :]) * over * inv

                def tile(i, j=j, mean=mean, gain=gain, level=level, tilt=tilt):
                    rows = span(r + j * m.rows + i * step, step)
                    d = gain * (q2[rows, :] - level - (z2[rows, :] - mean) * tilt)
                    d = masked(d, mask)
                    to = span(g + j * m.guard + i * step, step)
                    d2[to, 0:c3] = pltpu.roll(d, step - 1, 0).astype(BF16)
                    d2[to, c3 : 2 * c3] = d.astype(BF16)
                    d2[to, 2 * c3 : 3 * c3] = pltpu.roll(d, 1, 0).astype(BF16)

                repeat(2, tile)
            size = 2 * m.rows + 16
            value = None
            for a in range(3):
                for b in range(3):
                    part = d2[span(g - (a - 1) * 16, size), b * c3 : (b + 1) * c3]
                    term = mm_nt(part, wsp1[a, b * c3 : (b + 1) * c3, :])
                    value = term if value is None else value + term
            q1[span(r, m.rows), :] = value[0 : m.rows]
            q1[span(r + m.rows, m.rows), :] = value[m.guard : m.guard + m.rows]
            for j in range(2):
                crop = m.crop0 + 2 * p + j
                mean, inv = by_view(wv, crop, st1[0:2, :]), by_view(wv, crop, st1[2:4, :])

                def tile(i, sums, j=j, mean=mean, inv=inv):
                    rows = span(r + j * m.rows + i * step, step)
                    n = (z1[rows, :] - mean) * inv
                    v = act_slope(n * norms1[0:1, 0:c3] + norms1[1:2, 0:c3]) * q1[rows, :]
                    v = masked(v, mask)
                    q1[rows, :] = v
                    return (sums[0] + tile_sum(v), sums[1] + tile_sum(v * n))

                zero = jnp.zeros((8, c3), f)
                s, t = lax.fori_loop(0, 2, tile, (zero, zero))
                cs[pl.ds(crop, 1), 0:c3] = jnp.sum(s, axis=0, keepdims=True)
                cm[pl.ds(crop, 1), 0:c3] = jnp.sum(t, axis=0, keepdims=True)

        for p in range(m.count // 2):
            pair(p)
            tick()
    local_sums(blocks[1], (cs, cm), wcol, c3)
    links.send_near(1, blocks[1])
    inside = guarded - 32

    def taps(a):
        g2[a * 3 * c3 : (a + 1) * 3 * c3, :] = mm_tn(
            h1[a * 16 : a * 16 + inside, :], d2[16 : 16 + inside, c3 : 2 * c3]
        ).astype(BF16)

    taps(0)
    tick()

    def rest():
        taps(1)
        taps(2)
        tick()

    meet_sums(links, 1, c3, ((s1, 0), (s1, 2)), rest)

    loads[6].wait()
    moves = []
    for m, out in zip(sets, (o_gb, o_gs)):
        part = m.rows // 2
        for c in range(m.count):
            i = m.crop0 + c
            own_rows = span(m.row0 + c * m.rows + core * part, part)
            other_rows = span(m.row0 + c * m.rows + (1 - core) * part, part)
            place = out.at[span((core * m.count + c) * part, part)]
            moves.append(
                (
                    pltpu.make_async_copy(d3.at[own_rows], place, own_sem.at[i]),
                    pltpu.make_async_remote_copy(
                        src_ref=d3.at[other_rows],
                        dst_ref=place,
                        send_sem=grad_send.at[i],
                        recv_sem=grad_recv.at[i],
                        device_id=sibling,
                        device_id_type=MESH,
                    ),
                )
            )
    for m in sets:

        def pair(p, m=m):
            r = m.row0 + p * 2 * m.rows
            step = m.rows // 2
            mask = keep(c3, 16, m.edge)
            for j in range(2):
                crop = m.crop0 + 2 * p + j
                over = share_of(wv, tally, crop, 1.0)
                mean, inv = by_view(wv, crop, st1[0:2, :]), by_view(wv, crop, st1[2:4, :])
                gain = inv * norms1[0:1, 0:c3]
                level = by_view(wv, crop, s1[0:2, :]) * over
                tilt = by_view(wv, crop, s1[2:4, :]) * over * inv

                def tile(i, j=j, mean=mean, gain=gain, level=level, tilt=tilt):
                    rows = span(r + j * m.rows + i * step, step)
                    d = gain * (q1[rows, :] - level - (z1[rows, :] - mean) * tilt)
                    d1[rows, :] = masked(d, mask).astype(BF16)

                repeat(2, tile)

        repeat(m.count // 2, pair)
    loads[7].wait()

    def inner(n):
        part = pl.ds(pl.multiple_of(n * 256, 256), 256)
        g1[part, :] = mm_tn(img[:, part], d1[...]).astype(BF16)

    repeat(cin // 256, inner)
    tick()
    for m in sets:

        def pair(p, m=m):
            rows = span(m.row0 + p * 2 * m.rows, 2 * m.rows)
            for n in range(cin // 256):
                cols = slice(n * 256, (n + 1) * 256)
                d3[rows, cols] = (up[rows, cols] + mm_nt(d1[rows, :], w1[cols, :])).astype(BF16)

        for p in range(m.count // 2):
            pair(p)
            for c in (2 * p, 2 * p + 1):
                for copy in moves[m.crop0 + c]:
                    copy.start()
            tick()
    for src, dst in ((s2, o_s2), (s1, o_s1)):
        puts.put(src, dst)
    while share.at < len(order):
        tick()
    share.finish()
    links.finish()
    for near_copy, far_copy in moves:
        near_copy.wait()
        far_copy.wait()
    puts.finish()


def backward(sets, got, views, w, norms_first, norms_second, total, guarded, outs, idents):
    crops = lax.axis_size("crops")
    w1, wsp1, w3, w4, w5, w6, w7 = w
    cin, c3 = w1.shape
    c4, cout = w6.shape
    (
        f_img, f_z1, f_h1, f_z2, f_h2, f_blk, f_z4, f_x5, f_z5, f_h5, f_xe, f_res, f_d6, f_d7,
        f_st1, f_st2, f_st3, f_st4, f_st7, f_st5, f_st6, f_sq, f_n,
    ) = got
    smem, vmem = pl.BlockSpec(memory_space=pltpu.SMEM), pl.BlockSpec(memory_space=pltpu.VMEM)
    hbm = pl.BlockSpec(memory_space=pl.ANY)
    shape = jax.ShapeDtypeStruct
    most = 2 * sets[0].rows
    pairs = sum(m.count for m in sets) // 2
    count = 2 * pairs

    def like(arrays):
        return [pltpu.VMEM(t.shape, t.dtype) for t in arrays]

    def params(ident):
        return pltpu.CompilerParams(
            collective_id=ident, has_side_effects=True, vmem_limit_bytes=63 * 1024 * 1024
        )

    arrays = [f_d7, w7, f_xe, f_d6, w6, f_z5, f_h5, w5, f_x5, f_z4, w4, f_h2, w3, f_img, f_blk]
    out_shape = [
        shape((total, cin), F32), shape((c4, cout), BF16), shape((cin, cout), BF16), shape((9 * c4, c4), BF16),
        shape((cin, c4), BF16), shape((8, c4), F32), shape((8, c4), F32), shape((8, cin), F32),
    ]
    scratch = like(arrays[:14]) + [
        pltpu.VMEM((outs, c4), F32), pltpu.VMEM((outs, cin), F32), pltpu.VMEM((c4 // 128, total, 128), F32), pltpu.VMEM((total, c4), BF16),
        pltpu.VMEM((most, 512), F32), pltpu.VMEM((cin // 128, most, 128), F32), pltpu.VMEM((2, most, cin), F32),
        pltpu.VMEM((8, c4), F32), pltpu.VMEM((8, c4), F32), pltpu.VMEM((8, cin), F32),
        pltpu.VMEM((16, cin), F32), pltpu.VMEM((16, cin), F32),
        pltpu.SMEM((2, 16), F32), pltpu.VMEM((16, 128), F32),
    ]
    scratch += exchange_shapes((c4, c4, cin), (2, 2, 2), crops)
    scratch += [pltpu.SemaphoreType.DMA((15,)), pltpu.SemaphoreType.DMA((7,)), pltpu.SemaphoreType.DMA((pairs,))]
    shapes = [(cin, cout), (c4, cout), (9 * c4, c4), (cin, c4), (c3, cin), (9 * c3, c3), (cin, c3)]
    chunks = share_plan(shapes, SHARE_CUTS)
    bits = crops.bit_length() - 1
    scratch += share_scratch(chunks[:SHARE_FIRST], bits, [0] * SHARE_FIRST, True)
    up, g_outer2, g_skip, g_spatial2, g_inner2, s5, s4, s3 = pl.pallas_call(
        functools.partial(back_two_kernel, sets, total, outs, crops, (c3, cin, c4, cout), shapes, chunks),
        out_shape=out_shape,
        in_specs=[smem] * 2 + [vmem] * 6 + [hbm] * 15,
        out_specs=[hbm] * len(out_shape),
        scratch_shapes=scratch,
        compiler_params=params(idents[0]),
        name="back_two",
    )(*views, norms_first, norms_second, f_st3, f_st4, f_st5, f_n, *arrays)

    arrays = [f_h2, w3, up, f_z2, f_h1, wsp1, f_z1, w1, f_img]
    out_shape = [
        shape((total_rows(sets[0]), cin), BF16), shape((total_rows(sets[1]), cin), BF16), shape((8, c3), F32),
        shape((8, c3), F32),
    ] + [shape(t, BF16) for t in shapes]
    scratch = like(arrays) + [
        pltpu.VMEM((most, 512), F32), pltpu.VMEM((total, cin), BF16), pltpu.VMEM((total, c3), F32),
        pltpu.VMEM((guarded, 3 * c3), BF16), pltpu.VMEM((total, c3), F32), pltpu.VMEM((total, c3), BF16),
        pltpu.VMEM((c3, cin), BF16), pltpu.VMEM((9 * c3, c3), BF16), pltpu.VMEM((cin, c3), BF16),
        pltpu.VMEM((8, c3), F32), pltpu.VMEM((8, c3), F32), pltpu.VMEM((16, c3), F32), pltpu.VMEM((16, c3), F32),
        pltpu.SMEM((2, 16), F32), pltpu.VMEM((16, 128), F32),
    ]
    scratch += exchange_shapes((c3, c3), (2, 2), crops)
    scratch += [pltpu.SemaphoreType.DMA((9,)), pltpu.SemaphoreType.DMA((2,))]
    scratch += [pltpu.SemaphoreType.DMA((count,))] * 3 + [pltpu.SemaphoreType.DMA((pairs,))]
    scratch += share_scratch(chunks, bits, share_leave(bits) + [0] * (len(chunks) - SHARE_FIRST))
    grad_b, grad_s, s2, s1, *grads = pl.pallas_call(
        functools.partial(back_one_kernel, sets, total, guarded, crops, (c3, cin), shapes, chunks),
        out_shape=out_shape,
        in_specs=[smem] * 2 + [vmem] * 6 + [hbm] * 13,
        out_specs=[hbm] * len(out_shape),
        scratch_shapes=scratch,
        compiler_params=params(idents[1]),
        name="back_one",
    )(*views, norms_first, f_st1, f_st2, f_st3, s3, f_n, *arrays, g_skip, g_outer2, g_spatial2, g_inner2)
    return grad_b, grad_s, grads, (s1, s2, s3, s4, s5)


def widen_kernel(*refs):
    for src, dst in zip(refs[: len(refs) // 2], refs[len(refs) // 2 :]):
        dst[...] = src[...].astype(F32)


def widen(arrays, steps=8):
    def block(t):
        return pl.BlockSpec((t.shape[0] // steps, t.shape[1]), lambda i: (i, 0))

    return pl.pallas_call(
        widen_kernel,
        grid=(steps,),
        out_shape=[jax.ShapeDtypeStruct(t.shape, F32) for t in arrays],
        in_specs=[block(t) for t in arrays],
        out_specs=[block(t) for t in arrays],
        compiler_params=pltpu.CompilerParams(vmem_limit_bytes=63 * 1024 * 1024),
        name="widen",
    )(*arrays)


def total_rows(m):
    return m.count * m.rows


def shards(
    image_big,
    image_small,
    view_big,
    view_small,
    inner_first,
    spatial_first,
    outer_first,
    norms_first,
    inner_second,
    spatial_second,
    outer_second,
    skip_second,
    norms_second,
    cotangent_big,
    cotangent_small,
):
    c3, c4 = inner_first.shape[1], inner_second.shape[1]
    weights = [
        inner_first,
        spatial_first.reshape(3, 3 * c3, c3),
        outer_first,
        inner_second,
        spatial_second.reshape(9 * c4, c4),
        outer_second,
        skip_second,
    ]
    sets, sizes, got = forward(
        [image_big, image_small], [cotangent_big, cotangent_small], (view_big, view_small), weights, norms_first, norms_second, 0
    )
    grad_b, grad_s, grads, sums = backward(
        sets, got, (view_big, view_small), weights, norms_first, norms_second, *sizes, (1, 2)
    )
    s1, s2, s3, s4, s5 = sums
    sq = got[21]

    def both(parts):
        return jnp.concatenate(
            [jnp.stack([t[g] + t[g + 1], t[0] + t[1]]) for t, g in parts], axis=1
        )

    g_skip, g_outer2, g_spatial2, g_inner2, g_outer1, g_spatial1, g_inner1 = widen(grads)
    results = [
        got[11][m.out0 : m.out0 + m.count * m.out].reshape(m.count, m.half, 8, -1)[:, :, : m.half]
        for m in sets
    ]
    gradients = [
        t.reshape(image.shape[0], image.shape[1], 16, -1)[:, :, : image.shape[2]]
        for t, image in ((grad_b, image_big), (grad_s, image_small))
    ]
    return (
        results[0],
        results[1],
        gradients[0],
        gradients[1],
        g_inner1,
        g_spatial1.reshape(spatial_first.shape),
        g_outer1,
        both(((s1, 2), (s2, 2), (s3, 2))),
        g_inner2,
        g_spatial2.reshape(spatial_second.shape),
        g_outer2,
        g_skip,
        both(((s4, 2), (s5, 2), (sq, 2), (sq, 4))),
    )


def solution(mesh):
    maps = P("crops", "rows", None, None)
    whole = P(("crops", "rows"), None, None, None)
    in_specs = (maps, maps, P("crops"), P("crops")) + (P(),) * 9 + (whole, whole)
    out_specs = (whole, whole, maps, maps) + (P(),) * 9
    return jax.shard_map(shards, mesh=mesh, in_specs=in_specs, out_specs=out_specs, check_vma=False)
```

```python
import functools

import jax
import jax.numpy as jnp
from jax import lax
from jax.experimental import pallas as pl
from jax.experimental.pallas import tpu as pltpu
from jax.sharding import PartitionSpec as P

HIGH = lax.Precision.HIGHEST
EPS = 1e-05
MESH = pl.DeviceIdType.MESH
F32 = jnp.float32
BF16 = jnp.bfloat16


class Maps:
    def __init__(self, count, edge, row0, crop0, guard0, out0):
        self.count, self.edge = count, edge
        self.row0, self.crop0, self.guard0, self.out0 = row0, crop0, guard0, out0
        self.rows = edge * 16
        self.guard = (edge + 1) * 16
        self.half = edge // 2
        self.out = self.half * 8
        self.pixels = edge * edge


def geometry(nb, eb, ns, es):
    big = Maps(nb, eb, 0, 0, 16, 0)
    small = Maps(ns, es, nb * big.rows, nb, 16 + nb * big.guard, nb * big.out)
    total = small.row0 + ns * small.rows
    guarded = small.guard0 + ns * small.guard
    out = small.out0 + ns * small.out
    return (big, small), total, guarded, out


def al(x, m=16):
    return x if isinstance(x, int) else pl.multiple_of(x, m)


def span(start, size, m=16):
    return pl.ds(al(start, m), size)


def repeat(count, body):
    def step(i, carry):
        body(i)
        return carry

    lax.fori_loop(0, count, step, 0)


def mm(a, b):
    return jnp.dot(a, b, preferred_element_type=F32)


def mm_nt(a, b):
    return lax.dot_general(a, b, (((1,), (1,)), ((), ())), preferred_element_type=F32)


def mm_tn(a, b):
    return lax.dot_general(a, b, (((0,), (0,)), ((), ())), preferred_element_type=F32)


CA = 0.7978845608028654
CB = 0.7978845608028654 * 0.044715


def act(u):
    t = jnp.tanh(u * (CA + CB * (u * u)))
    return 0.5 * u * (1.0 + t)


def act_slope(u):
    s = u * u
    t = jnp.tanh(u * (CA + CB * s))
    rise = (0.5 * u) * (CA + (3.0 * CB) * s)
    return 0.5 * (1.0 + t) + (1.0 - t * t) * rise


def act_both(u):
    s = u * u
    t = jnp.tanh(u * (CA + CB * s))
    hu = 0.5 * u
    lift = 0.5 * (1.0 + t)
    slope = lift + (1.0 - t * t) * (hu * (CA + (3.0 * CB) * s))
    return u * lift, slope


def keep(width, pitch, edge):
    return lax.broadcasted_iota(jnp.int32, (pitch, width), 0) < edge


def masked(x, mask):
    rows = x.reshape(x.shape[0] // mask.shape[0], mask.shape[0], x.shape[1])
    return jnp.where(mask[None], rows, 0.0).reshape(x.shape)


def tile_sum(x):
    return jnp.sum(x.reshape(x.shape[0] // 8, 8, x.shape[1]), axis=0)


def pieces(width):
    return (4, width // 4) if width >= 512 else (width // 128, 128)


class Links:
    def __init__(self, crops, near, far, near_s, near_r, far_s, far_r):
        self.group = 4 if crops % 4 == 0 else 1
        self.outers = crops // self.group
        self.k, self.r = lax.axis_index("crops"), lax.axis_index("rows")
        inner, self.outer = lax.rem(self.k, self.group), self.k // self.group
        self.wide = 2 * self.group
        self.me = inner * 2 + self.r
        self.peers, self.others = [], []
        for d in range(1, self.wide):
            p = lax.rem(self.me + d, self.wide)
            self.peers.append((self.outer * self.group + p // 2, lax.rem(p, 2)))
        for d in range(1, self.outers):
            self.others.append((lax.rem(self.outer + d, self.outers) * self.group + inner, self.r))
        self.near, self.far = near, far
        self.sems = (near_s, near_r, far_s, far_r)
        self.live = {}

    def greet(self, extra=()):
        barrier = pltpu.get_barrier_semaphore()
        peers = self.peers + self.others + list(extra)
        for peer in peers:
            pl.semaphore_signal(barrier, inc=1, device_id=peer, device_id_type=MESH)
        pl.semaphore_wait(barrier, len(peers))

    def send_near(self, e, block):
        self.near[e][self.me] = block[...]
        self.live[e, 0] = []
        for d, peer in enumerate(self.peers):
            copy = pltpu.make_async_remote_copy(
                src_ref=block,
                dst_ref=self.near[e].at[self.me],
                send_sem=self.sems[0].at[e, d],
                recv_sem=self.sems[1].at[e, d],
                device_id=peer,
                device_id_type=MESH,
            )
            copy.start()
            self.live[e, 0].append(copy)

    def wait_near(self, e):
        for copy in self.live[e, 0]:
            copy.wait_recv()

    def send_far(self, e):
        self.live[e, 1] = []
        place = self.far[e].at[self.outer]
        for d, peer in enumerate(self.others):
            copy = pltpu.make_async_remote_copy(
                src_ref=place,
                dst_ref=place,
                send_sem=self.sems[2].at[e, d],
                recv_sem=self.sems[3].at[e, d],
                device_id=peer,
                device_id_type=MESH,
            )
            copy.start()
            self.live[e, 1].append(copy)

    def wait_far(self, e):
        for copy in self.live[e, 1]:
            copy.wait_recv()

    def finish(self):
        for copies in self.live.values():
            for copy in copies:
                copy.wait_send()


def fold_moments(buf, tallies, count, scale):
    sums, total = buf[0, 0:8, :], tallies[0]
    for i in range(1, count):
        sums = sums + buf[i, 0:8, :]
        total = total + tallies[i]
    mean = sums * (1.0 / jnp.maximum(total * scale, 1.0))
    spread = None
    for i in range(count):
        n = tallies[i] * scale
        apart = buf[i, 0:8, :] * (1.0 / jnp.maximum(n, 1.0)) - mean
        term = buf[i, 8:16, :] + n * apart * apart
        spread = term if spread is None else spread + term
    return sums, spread, total


def fold_sums(buf, count):
    total = buf[0]
    for i in range(1, count):
        total = total + buf[i]
    return total


def exchange_shapes(widths, tiles, crops):
    group = 4 if crops % 4 == 0 else 1
    outers = crops // group
    blocks, near, far = [], [], []
    for width, tile in zip(widths, tiles):
        lanes = pieces(width)[1]
        blocks.append(pltpu.VMEM((8 * tile, lanes), F32))
        near.append(pltpu.VMEM((2 * group, 8 * tile, lanes), F32))
        far.append(pltpu.VMEM((outers, 8 * tile, lanes), F32))
    e = len(widths)
    sems = [
        pltpu.SemaphoreType.DMA((e, 2 * group - 1)),
        pltpu.SemaphoreType.DMA((e, 2 * group - 1)),
        pltpu.SemaphoreType.DMA((e, max(outers - 1, 1))),
        pltpu.SemaphoreType.DMA((e, max(outers - 1, 1))),
    ]
    return blocks + near + far + sems


def take(refs, count):
    return list(refs[:count]), refs[count:]


def pack(block, tile, rows, width):
    count, lanes = pieces(width)
    for q in range(count):
        for v in range(2):
            block[tile * 8 + 2 * q + v : tile * 8 + 2 * q + v + 1, :] = rows[v][:, q * lanes : (q + 1) * lanes]


def unpack(table, row, tile, width):
    count, lanes = pieces(width)
    for q in range(count):
        table[row : row + 2, q * lanes : (q + 1) * lanes] = tile[2 * q : 2 * q + 2, :]


def crop_stats(ref, row0, rows, step, width, edge, pitch, pixels, crop, cs, cm, col0=0):
    mask = keep(width, pitch, edge)
    zero = jnp.zeros((8, width), F32)
    cols = pl.ds(col0, width) if isinstance(col0, int) else pl.ds(pl.multiple_of(col0, 128), width)
    near = min(8, edge)
    first = masked(ref[span(row0, 8, 8), cols], keep(width, 8, edge))
    pivot = jnp.sum(first, axis=0, keepdims=True) * (1.0 / near)

    def tile(i, acc):
        d = masked(ref[span(row0 + i * step, step, 8), cols] - pivot, mask)
        return acc[0] + tile_sum(d), acc[1] + tile_sum(d * d)

    if rows == step:
        s, m = tile(0, (zero, zero))
    else:
        s, m = lax.fori_loop(0, rows // step, tile, (zero, zero))
    s = jnp.sum(s, axis=0, keepdims=True)
    m = jnp.sum(m, axis=0, keepdims=True)
    cs[pl.ds(crop, 1), cols] = s + pivot * float(pixels)
    cm[pl.ds(crop, 1), cols] = jnp.maximum(m - s * s * (1.0 / pixels), 0.0)


def local_moments(block, cs, cm, wcol, width, scale, tally=False):
    s, m = cs[:, 0:width], cm[:, 0:width]
    pix = wcol[:, 2:3] * scale
    mean_c = s * (1.0 / pix)
    sums, squares, tallies = [], [], []
    for v in range(2):
        w = wcol[:, v : v + 1]
        total = jnp.sum(w * s, axis=0, keepdims=True)
        n = jnp.sum(w * pix, axis=0, keepdims=True)
        apart = mean_c - total * (1.0 / jnp.maximum(n, 1.0))
        squares.append(jnp.sum(w * (m + pix * apart * apart), axis=0, keepdims=True))
        sums.append(total)
        tallies.append(n)
    pack(block, 0, sums, width)
    pack(block, 1, squares, width)
    if tally:
        lanes = pieces(width)[1]
        for q in range(4):
            for v in range(2):
                block[16 + 2 * q + v : 17 + 2 * q + v, :] = jnp.broadcast_to(tallies[v], (1, lanes))


def local_sums(block, parts, wcol, width):
    for tile, part in enumerate(parts):
        s = part[:, 0:width]
        pack(block, tile, [jnp.sum(wcol[:, v : v + 1] * s, axis=0, keepdims=True) for v in range(2)], width)


def view_tables(sets, core, views, wv, wcol):
    row = lax.broadcasted_iota(jnp.int32, wcol.shape, 0)
    lane = lax.broadcasted_iota(jnp.int32, wcol.shape, 1)
    table = jnp.where(lane == 2, 1.0, 0.0)
    for m, view in zip(sets, views):
        for c in range(m.count):
            second = view[core * m.count + c].astype(F32)
            pair = (1.0 - second, second, float(m.pixels))
            for v in range(3):
                table = jnp.where((row == m.crop0 + c) & (lane == v), pair[v], table)
            wv[0, m.crop0 + c] = pair[0]
            wv[1, m.crop0 + c] = pair[1]
    wcol[...] = table


def by_view(wv, crop, pair):
    return wv[0, crop] * pair[0:1, :] + wv[1, crop] * pair[1:2, :]


FWD_WIDTHS = (256, 256, 1024, 512, 2048, 512, 2048, 2048)


def forward_kernel(sets, total, guarded, outs, crops, dims, *refs):
    c3, cin, c4, cout = dims
    (
        vb, vs, norms1, norms2,
        img_b, img_s, cot_b, cot_s, w1_h, wsp1_h, w3_h, w4_h, w5_h, w6_h, w7_h,
    ), refs = refs[:15], refs[15:]
    (
        o_img, o_z1, o_h1, o_z2, o_h2, o_blk, o_z4, o_x5, o_z5, o_h5, o_xe, o_res, o_d6, o_d7,
        o_st1, o_st2, o_st3, o_st4, o_st7, o_st5, o_st6, o_sq, o_tally,
    ), refs = refs[:23], refs[23:]
    (
        img, z1, h1, z2, h2, zt, blk, eb, z4, xe, z7, hp, x5, z5, h5, z6, cot,
        w1, wsp1, w3, w4, w5, w6, w7, cs, cm, ck,
        st1, st2, st3, st4, st7, st5, st6, sq, tally_v, wv, wcol,
    ), refs = refs[:38], refs[38:]
    e = len(FWD_WIDTHS)
    blocks, refs = take(refs, e)
    near, refs = take(refs, e)
    far, refs = take(refs, e)
    ns_, nr_, fs_, fr_ = refs[:4]
    load_sem, img_sem, img_send, img_recv, out_sem = refs[4:]
    links = Links(crops, near, far, ns_, nr_, fs_, fr_)
    k, core = links.k, links.r
    sibling = (k, 1 - core)
    f = F32

    loads = []
    for i, (src, dst) in enumerate(
        ((w1_h, w1), (wsp1_h, wsp1), (w3_h, w3), (w4_h, w4), (w5_h, w5), (w6_h, w6), (w7_h, w7),
            (cot_b, cot.at[0 : sets[1].out0]), (cot_s, cot.at[sets[1].out0 : outs]))
    ):
        loads.append(pltpu.make_async_copy(src, dst, load_sem.at[i]))
    own, swaps = [], []
    for at, (m, src) in enumerate(zip(sets, (img_b, img_s))):
        part = m.rows // 2
        for c in range(m.count):
            i = m.crop0 + c
            place = img.at[span(m.row0 + c * m.rows + core * part, part)]
            own.append(
                pltpu.make_async_copy(
                    src.at[span((core * m.count + c) * part, part)], place, img_sem.at[i]
                )
            )
            swaps.append(
                pltpu.make_async_remote_copy(
                    src_ref=src.at[span(((1 - core) * m.count + c) * part, part)],
                    dst_ref=place,
                    send_sem=img_send.at[i],
                    recv_sem=img_recv.at[i],
                    device_id=sibling,
                    device_id_type=MESH,
                )
            )
    for copy in own:
        copy.start()
    loads[0].start()
    links.greet()
    for copy in swaps:
        copy.start()

    view_tables(sets, core, (vb, vs), wv, wcol)
    out_copies = []

    def put(src, dst):
        copy = pltpu.make_async_copy(src, dst, out_sem.at[len(out_copies)])
        copy.start()
        out_copies.append(copy)

    for ref in (cs, cm, ck):
        ref[...] = jnp.zeros(ref.shape, f)
    for block in blocks:
        block[...] = jnp.zeros(block.shape, f)
    h1[0:16, :] = jnp.zeros((16, 3 * c3), BF16)
    for m in sets:
        for c in range(m.count):
            at = m.guard0 + c * m.guard + m.rows
            h1[at : at + 16, :] = jnp.zeros((16, 3 * c3), BF16)

    def near_tallies():
        return [near[0][i, 16:24, 0:1] for i in range(links.wide)]

    def far_tallies():
        return [far[0][i, 16:24, 0:1] for i in range(links.outers)]

    def meet_near(i, scale):
        links.wait_near(i)
        sums, spread, n = fold_moments(near[i], near_tallies(), links.wide, scale)
        place = far[i].at[links.outer]
        place[0:8, :] = sums
        place[8:16, :] = spread
        if i == 0:
            place[16:24, :] = jnp.broadcast_to(n, (8, near[0].shape[2]))
        links.send_far(i)

    def meet_far(i, scale, table, width):
        links.wait_far(i)
        sums, spread, n = fold_moments(far[i], far_tallies(), links.outers, scale)
        over = 1.0 / (n * scale)
        mean = sums * over
        inverse = lax.rsqrt(spread * over + EPS)
        unpack(table, 0, mean, width)
        unpack(table, 2, inverse, width)
        if i == 0:
            tally_v[...] = jnp.broadcast_to(n, (8, 128))

    loads[0].wait()
    for m in sets:

        def pair(p, m=m):
            r = m.row0 + p * 2 * m.rows
            for j in range(2):
                own[m.crop0 + 2 * p + j].wait()
                swaps[m.crop0 + 2 * p + j].wait_recv()
            z1[span(r, 2 * m.rows), :] = mm(img[span(r, 2 * m.rows), :], w1[...])
            for j in range(2):
                crop_stats(z1, r + j * m.rows, m.rows, m.rows // 2, c3, m.edge, 16, m.pixels, m.crop0 + 2 * p + j, cs, cm)

        for p in range(m.count // 2):
            pair(p)
            if m is sets[0] and p == 0:
                for copy in loads[1:]:
                    copy.start()
    local_moments(blocks[0], cs, cm, wcol, c3, 1.0, True)
    links.send_near(0, blocks[0])
    put(img, o_img)
    put(z1, o_z1)
    loads[1].wait()
    meet_near(0, 1.0)
    meet_far(0, 1.0, st1, c3)

    for m in sets:

        def pair(p, m=m):
            r = m.row0 + p * 2 * m.rows
            g = m.guard0 + p * 2 * m.guard
            for j in range(2):
                crop = m.crop0 + 2 * p + j
                mean = by_view(wv, crop, st1[0:2, :])
                scale = by_view(wv, crop, st1[2:4, :]) * norms1[0:1, 0:c3]
                shift = norms1[1:2, 0:c3] - mean * scale
                step = m.rows // 2
                mask = keep(c3, 16, m.edge)

                def tile(i):
                    z = z1[span(r + j * m.rows + i * step, step), :]
                    h = masked(act(z * scale + shift), mask)
                    rows = span(g + j * m.guard + i * step, step)
                    h1[rows, 0:c3] = pltpu.roll(h, 1, 0).astype(BF16)
                    h1[rows, c3 : 2 * c3] = h.astype(BF16)
                    h1[rows, 2 * c3 : 3 * c3] = pltpu.roll(h, step - 1, 0).astype(BF16)

                repeat(2, tile)
            size = 2 * m.rows + 16
            z = mm(h1[span(g - 16, size), :], wsp1[0]) + mm(h1[span(g, size), :], wsp1[1])
            z = z + mm(h1[span(g + 16, size), :], wsp1[2])
            z2[span(r, m.rows), :] = z[0 : m.rows]
            z2[span(r + m.rows, m.rows), :] = z[m.guard : m.guard + m.rows]
            for j in range(2):
                crop_stats(z2, r + j * m.rows, m.rows, m.rows // 2, c3, m.edge, 16, m.pixels, m.crop0 + 2 * p + j, cs, cm)

        repeat(m.count // 2, pair)
    local_moments(blocks[1], cs, cm, wcol, c3, 1.0)
    links.send_near(1, blocks[1])
    put(h1, o_h1)
    put(z2, o_z2)
    loads[2].wait()
    meet_near(1, 1.0)
    meet_far(1, 1.0, st2, c3)

    for m in sets:

        def pair(p, m=m):
            r = m.row0 + p * 2 * m.rows
            for j in range(2):
                crop = m.crop0 + 2 * p + j
                mean = by_view(wv, crop, st2[0:2, :])
                scale = by_view(wv, crop, st2[2:4, :]) * norms1[0:1, c3 : 2 * c3]
                shift = norms1[1:2, c3 : 2 * c3] - mean * scale
                step = m.rows // 2

                def tile(i):
                    rows = span(r + j * m.rows + i * step, step)
                    h2[rows, :] = act(z2[rows, :] * scale + shift).astype(BF16)

                repeat(2, tile)
            zt[0 : 2 * m.rows, :] = mm(h2[span(r, 2 * m.rows), :], w3[...])
            for j in range(2):
                crop_stats(zt, j * m.rows, m.rows, 32, cin, m.edge, 16, m.pixels, m.crop0 + 2 * p + j, cs, cm)

        repeat(m.count // 2, pair)
    local_moments(blocks[2], cs, cm, wcol, cin, 1.0)
    links.send_near(2, blocks[2])
    put(h2, o_h2)
    loads[3].wait()
    meet_near(2, 1.0)
    meet_far(2, 1.0, st3, cin)

    for m in sets:

        def pair(p, m=m):
            r = m.row0 + p * 2 * m.rows
            zt[0 : 2 * m.rows, :] = mm(h2[span(r, 2 * m.rows), :], w3[...])
            for j in range(2):
                crop = m.crop0 + 2 * p + j
                mean = by_view(wv, crop, st3[0:2, :])
                scale = by_view(wv, crop, st3[2:4, :]) * norms1[0:1, 2 * c3 :]
                shift = norms1[1:2, 2 * c3 :] - mean * scale

                def tile(i):
                    here = span(j * m.rows + i * 32, 32)
                    rows = span(r + j * m.rows + i * 32, 32)
                    u = zt[here, :] * scale + shift + img[rows, :].astype(f)
                    b = act(u)
                    blk[rows, :] = b.astype(BF16)
                    for q in range(cin // 128):
                        eb[q, span(j * m.rows // 2 + i * 16, 16), :] = b[0:16, q * 128 : (q + 1) * 128]

                repeat(m.rows // 32, tile)
            for q in range(cin // 128):
                picked = [eb[q, pl.ds(i * 16, 8, stride=2), :] for i in range(2 * m.half)]
                xe[span(m.out0 + p * 2 * m.out, 2 * m.out), q * 128 : (q + 1) * 128] = jnp.concatenate(
                    picked, axis=0
                ).astype(BF16)
            z4[span(r, 2 * m.rows), :] = mm(blk[span(r, 2 * m.rows), :], w4[...])
            for j in range(2):
                crop_stats(z4, r + j * m.rows, m.rows, 32, c4, m.edge, 16, m.pixels, m.crop0 + 2 * p + j, cs, cm)

        repeat(m.count // 2, pair)
    local_moments(blocks[3], cs, cm, wcol, c4, 1.0)
    links.send_near(3, blocks[3])
    put(blk, o_blk)
    put(z4, o_z4)
    put(xe, o_xe)
    loads[6].wait()

    def wide_product(a, w, z):
        def columns(n):
            cols = pl.ds(pl.multiple_of(n * 512, 512), 512)
            z[:, cols] = mm(a[...], w[:, cols])

        repeat(cout // 512, columns)

    def wide_stats(z):
        for m in sets:

            def crop_(c, m=m):
                def columns(n):
                    crop_stats(
                        z, m.out0 + c * m.out, m.out, m.out, 512, m.half, 8, m.half * m.half,
                        m.crop0 + c, cs, cm, n * 512,
                    )

                repeat(cout // 512, columns)

            repeat(m.count, crop_)

    wide_product(xe, w7, z7)
    meet_near(3, 1.0)
    wide_stats(z7)
    local_moments(blocks[4], cs, cm, wcol, cout, 0.25)
    links.send_near(4, blocks[4])
    meet_far(3, 1.0, st4, c4)

    loads[4].wait()
    lots = c4 // 128
    hp[:, 0:24, :] = jnp.zeros((lots, 24, 128), f)
    for m in sets:

        def pair(p, m=m):
            r = m.row0 + p * 2 * m.rows
            for j in range(2):
                crop = m.crop0 + 2 * p + j
                mean = by_view(wv, crop, st4[0:2, :])
                scale = by_view(wv, crop, st4[2:4, :]) * norms2[0:1, 0:c4]
                shift = norms2[1:2, 0:c4] - mean * scale
                mask = keep(c4, 16, m.edge)
                base = 24 + j * m.guard
                hp[:, base + m.rows : base + m.guard, :] = jnp.zeros((lots, 16, 128), f)

                def tile(i):
                    z = z4[span(r + j * m.rows + i * 32, 32), :]
                    h = masked(act(z * scale + shift), mask)
                    for q in range(lots):
                        hp[q, span(base + i * 32, 32, 8), :] = h[:, q * 128 : (q + 1) * 128]

                repeat(m.rows // 32, tile)
            for a in range(3):
                for b in range(3):
                    for q in range(lots):
                        picked = []
                        for j in range(2):
                            for i in range(m.half):
                                at = 24 + j * m.guard + (2 * i + a - 1) * 16 + b - 1
                                picked.append(hp[q, pl.ds(at, 8, stride=2), :])
                        tap = (3 * a + b) * c4 + q * 128
                        x5[span(m.out0 + p * 2 * m.out, 2 * m.out), tap : tap + 128] = jnp.concatenate(
                            picked, axis=0
                        ).astype(BF16)

        repeat(m.count // 2, pair)
    z5[...] = jnp.zeros(z5.shape, f)

    def taps(t):
        part = pl.ds(pl.multiple_of(t * 3 * c4, 128), 3 * c4)
        z5[...] += mm(x5[:, part], w5[part, :])

    repeat(3, taps)
    for m in sets:

        def crop_(c, m=m):
            crop_stats(z5, m.out0 + c * m.out, m.out, m.out, c4, m.half, 8, m.half * m.half, m.crop0 + c, cs, cm)

        repeat(m.count, crop_)
    local_moments(blocks[5], cs, cm, wcol, c4, 0.25)
    links.send_near(5, blocks[5])
    put(x5, o_x5)
    put(z5, o_z5)
    meet_near(4, 0.25)
    meet_near(5, 0.25)
    meet_far(4, 0.25, st7, cout)
    meet_far(5, 0.25, st5, c4)

    loads[5].wait()
    for m in sets:

        def pair(p, m=m):
            o = m.out0 + p * 2 * m.out
            halves = []
            for j in range(2):
                crop = m.crop0 + 2 * p + j
                mean = by_view(wv, crop, st5[0:2, :])
                scale = by_view(wv, crop, st5[2:4, :]) * norms2[0:1, c4 : 2 * c4]
                z = z5[span(o + j * m.out, m.out, 8), :]
                halves.append(act(z * scale + (norms2[1:2, c4 : 2 * c4] - mean * scale)))
            h5[span(o, 2 * m.out), :] = jnp.concatenate(halves, axis=0).astype(BF16)

        repeat(m.count // 2, pair)
    wide_product(h5, w6, z6)
    wide_stats(z6)
    local_moments(blocks[6], cs, cm, wcol, cout, 0.25)
    links.send_near(6, blocks[6])
    put(h5, o_h5)
    loads[7].wait()
    loads[8].wait()

    def center(ms):
        for m in ms:

            def crop_(c, m=m):
                def columns(n):
                    cols = pl.ds(pl.multiple_of(n * 512, 512), 512)
                    rows = span(m.out0 + c * m.out, m.out, 8)
                    mean = by_view(wv, m.crop0 + c, st7[0:2, cols])
                    z7[rows, cols] = (z7[rows, cols] - mean) * by_view(wv, m.crop0 + c, st7[2:4, cols])

                repeat(cout // 512, columns)

            repeat(m.count, crop_)

    center(sets[:1])
    meet_near(6, 0.25)
    center(sets[1:])
    meet_far(6, 0.25, st6, cout)

    out_copies[6].wait()
    g6, g7 = 2 * c4, 2 * c4 + cout
    lanes = 512
    for m in sets:

        def pair(p, m=m):
            o = m.out0 + p * 2 * m.out

            def columns(n):
                cols = pl.ds(pl.multiple_of(n * lanes, lanes), lanes)
                cols6 = pl.ds(pl.multiple_of(g6 + n * lanes, lanes), lanes)
                cols7 = pl.ds(pl.multiple_of(g7 + n * lanes, lanes), lanes)
                c = cot[span(o, 2 * m.out), cols].astype(f)
                mask = keep(lanes, 8, m.half)
                found = []
                for j in range(2):
                    crop = m.crop0 + 2 * p + j
                    rows = span(o + j * m.out, m.out, 8)
                    n6 = (z6[rows, cols] - by_view(wv, crop, st6[0:2, cols])) * by_view(wv, crop, st6[2:4, cols])
                    n7 = z7[rows, cols]
                    z6[rows, cols] = n6
                    u = n6 * norms2[0:1, cols6] + n7 * norms2[0:1, cols7] + (norms2[1:2, cols6] + norms2[1:2, cols7])
                    a, slope = act_both(u)
                    found.append(a)
                    up = masked(slope * c[j * m.out : (j + 1) * m.out], mask)
                    z4[span(n * outs + o + j * m.out, m.out, 8), :] = up
                    for to, part in ((cs, up), (cm, up * n6), (ck, up * n7)):
                        to[pl.ds(crop, 1), cols] = jnp.sum(tile_sum(part), axis=0, keepdims=True)
                w6[span(o, 2 * m.out), cols] = jnp.concatenate(found, axis=0).astype(BF16)

            repeat(cout // lanes, columns)

        repeat(m.count // 2, pair)
    local_sums(blocks[7], (cs, cm, ck), wcol, cout)
    links.send_near(7, blocks[7])
    put(w6.at[0:outs], o_res)
    links.wait_near(7)
    far[7][links.outer] = fold_sums(near[7], links.wide)
    links.send_far(7)
    links.wait_far(7)
    sums = fold_sums(far[7], links.outers)
    for t in range(3):
        unpack(sq, 2 * t, sums[8 * t : 8 * t + 8], cout)

    for m in sets:

        def pair(p, m=m):
            o = m.out0 + p * 2 * m.out

            def columns(n):
                cols = pl.ds(pl.multiple_of(n * lanes, lanes), lanes)
                mask = keep(lanes, 8, m.half)
                got6, got7 = [], []
                for j in range(2):
                    crop = m.crop0 + 2 * p + j
                    rows = span(o + j * m.out, m.out, 8)
                    up = z4[span(n * outs + o + j * m.out, m.out, 8), :]
                    over = wv[0, crop] * (4.0 / tally_v[0:1, 0:1]) + wv[1, crop] * (4.0 / tally_v[1:2, 0:1])
                    level = by_view(wv, crop, sq[0:2, cols]) * over
                    for got, z, st, at, t in ((got6, z6, st6, g6, 2), (got7, z7, st7, g7, 4)):
                        inv = by_view(wv, crop, st[2:4, cols])
                        gain = inv * norms2[0:1, pl.ds(pl.multiple_of(at + n * lanes, lanes), lanes)]
                        tilt = by_view(wv, crop, sq[t : t + 2, cols]) * over
                        got.append(masked(gain * (up - level - z[rows, cols] * tilt), mask))
                w7[span(o, 2 * m.out), cols] = jnp.concatenate(got6, axis=0).astype(BF16)
                w7[span(cin // 2 + o, 2 * m.out), cols] = jnp.concatenate(got7, axis=0).astype(BF16)

            repeat(cout // lanes, columns)

        repeat(m.count // 2, pair)
    put(w7.at[0:outs], o_d6)
    put(w7.at[cin // 2 : cin // 2 + outs], o_d7)
    for src, dst in (
        (st1, o_st1), (st2, o_st2), (st3, o_st3), (st4, o_st4), (st7, o_st7), (st5, o_st5), (st6, o_st6),
        (sq, o_sq), (tally_v, o_tally),
    ):
        put(src, dst)
    links.finish()
    for copy in swaps:
        copy.wait_send()
    for i, copy in enumerate(out_copies):
        if i != 6:
            copy.wait()


def flat_rows(tensor, pitch):
    n, h, w, c = tensor.shape
    return jnp.pad(tensor, ((0, 0), (0, 0), (0, pitch - w), (0, 0))).reshape(n * h * pitch, c)


def forward(images, cots, views, w, norms_first, norms_second, ident):
    crops = lax.axis_size("crops")
    nb, ns = images[0].shape[0] // 2, images[1].shape[0] // 2
    sets, total, guarded, outs = geometry(nb, images[0].shape[2], ns, images[1].shape[2])
    w1, wsp1, w3, w4, w5, w6, w7 = w
    cin, c3 = w1.shape
    c4, cout = w6.shape
    smem, vmem = pl.BlockSpec(memory_space=pltpu.SMEM), pl.BlockSpec(memory_space=pltpu.VMEM)
    hbm = pl.BlockSpec(memory_space=pl.ANY)
    shape = jax.ShapeDtypeStruct
    out_shape = [
        shape((total, cin), BF16), shape((total, c3), F32), shape((guarded, 3 * c3), BF16), shape((total, c3), F32),
        shape((total, c3), BF16), shape((total, cin), BF16), shape((total, c4), F32), shape((outs, 9 * c4), BF16),
        shape((outs, c4), F32), shape((outs, c4), BF16), shape((outs, cin), BF16), shape((outs, cout), BF16),
        shape((outs, cout), BF16), shape((outs, cout), BF16),
        shape((8, c3), F32), shape((8, c3), F32), shape((8, cin), F32), shape((8, c4), F32), shape((8, cout), F32),
        shape((8, c4), F32), shape((8, cout), F32), shape((8, cout), F32), shape((8, 128), F32),
    ]
    most = 2 * sets[0].rows
    scratch = [
        pltpu.VMEM((total, cin), BF16), pltpu.VMEM((total, c3), F32), pltpu.VMEM((guarded, 3 * c3), BF16),
        pltpu.VMEM((total, c3), F32), pltpu.VMEM((total, c3), BF16), pltpu.VMEM((most, cin), F32),
        pltpu.VMEM((total, cin), BF16), pltpu.VMEM((cin // 128, most // 2, 128), F32), pltpu.VMEM((total, c4), F32),
        pltpu.VMEM((outs, cin), BF16), pltpu.VMEM((outs, cout), F32), pltpu.VMEM((c4 // 128, 24 + 2 * sets[0].guard, 128), F32),
        pltpu.VMEM((outs, 9 * c4), BF16), pltpu.VMEM((outs, c4), F32),
        pltpu.VMEM((outs, c4), BF16), pltpu.VMEM((outs, cout), F32), pltpu.VMEM((outs, cout), BF16),
    ]
    scratch += [pltpu.VMEM(t.shape, BF16) for t in w]
    scratch += [pltpu.VMEM((16, cout), F32)] * 3
    scratch += [pltpu.VMEM((8, n), F32) for n in (c3, c3, cin, c4, cout, c4, cout, cout, 128)]
    scratch += [pltpu.SMEM((2, 16), F32), pltpu.VMEM((16, 128), F32)]
    scratch += exchange_shapes(FWD_WIDTHS, (3, 2, 2, 2, 2, 2, 2, 3), crops)
    scratch += [
        pltpu.SemaphoreType.DMA((9,)), pltpu.SemaphoreType.DMA((nb + ns,)), pltpu.SemaphoreType.DMA((nb + ns,)),
        pltpu.SemaphoreType.DMA((nb + ns,)), pltpu.SemaphoreType.DMA((23,)),
    ]
    got = pl.pallas_call(
        functools.partial(forward_kernel, sets, total, guarded, outs, crops, (c3, cin, c4, cout)),
        out_shape=out_shape,
        in_specs=[smem, smem, vmem, vmem] + [hbm] * 11,
        out_specs=[hbm] * len(out_shape),
        scratch_shapes=scratch,
        compiler_params=pltpu.CompilerParams(
            collective_id=ident, has_side_effects=True, vmem_limit_bytes=63 * 1024 * 1024
        ),
        name="forward",
    )(
        *views, norms_first, norms_second,
        flat_rows(images[0], 16), flat_rows(images[1], 16),
        *[flat_rows(t, 8) for t in cots], *w,
    )
    return sets, (total, guarded, outs), got


def share_plan(shapes, cuts):
    chunks = []
    for at, (height, width) in enumerate(shapes):
        down, across = cuts[at]
        half, high = width // 2 // across, height // down
        for c in range(down):
            for p in range(across):
                chunks.append((at, c * high, high, p * half, half))
    return chunks


class Share:
    def __init__(self, shapes, chunks, orders, bits, links, sources, outs, acc, recv0, recvs, sems, begin, leave):
        self.shapes, self.chunks, self.bits = shapes, chunks, bits
        self.k, self.core = links.k, links.r
        self.sources, self.outs, self.acc, self.recv0, self.recvs = sources, outs, acc, recv0, recvs
        self.send_sem, self.recv_sem, self.load_sem, self.store_sem = sems
        self.sibling = (self.k, 1 - self.core)
        self.total = 2 * bits + 2
        self.live, self.loads, self.stores, self.begin, self.leave, self.at = {}, {}, {}, begin, leave, 0
        digit = [lax.rem(self.k // (1 << b), 2) for b in range(bits)]
        self.stages, self.regions, self.kinds, self.slots = [], [], [], []
        for i, (at, row, height, col, width) in enumerate(chunks):
            stages = []
            for a, b in zip(*orders[i]):
                if a == b:
                    mine, step = digit[a], 1 << a
                else:
                    mine = digit[a] * (1 - self.core) + digit[b] * self.core
                    step = (1 << a) * (1 - self.core) + (1 << b) * self.core
                stages.append((mine, self.k + step * (1 - 2 * mine)))
            start, length, used = 0, height, 0
            region, kind, slot = [], [], []
            for s in range(bits):
                region.append((start, length))
                slot.append(used)
                if length % 32 == 0:
                    kind.append(True)
                    length //= 2
                    start = start + stages[s][0] * length
                else:
                    kind.append(False)
                used += length
            region.append((start, length))
            self.stages.append(stages)
            self.regions.append(region)
            self.kinds.append(kind)
            self.slots.append(slot)

    def send(self, i, t, src, dst, device):
        copy = pltpu.make_async_remote_copy(
            src_ref=src,
            dst_ref=dst,
            send_sem=self.send_sem.at[i, t],
            recv_sem=self.recv_sem.at[i, t],
            device_id=device,
            device_id_type=MESH,
        )
        copy.start()
        self.live[i, t] = copy

    def add(self, dst, at, src, src_at, length):
        block = 16
        while length % (block * 2) == 0 and block * 2 * dst.shape[1] <= 65536:
            block *= 2

        def step(j, carry):
            off = j * block
            rows = span(at + off, block)
            dst[rows, :] = dst[rows, :] + src[span(src_at + off, block), :]
            return carry

        lax.fori_loop(0, length // block, step, 0)

    def fetch(self):
        for i, (at, row, height, col, width) in enumerate(self.chunks):
            t = self.begin[i]
            if 1 <= t <= self.bits:
                start, length = self.regions[i][t - 1]
                own = pl.ds(pl.multiple_of(self.core * (self.shapes[at][1] // 2) + col, 128), width)
                self.loads[i] = pltpu.make_async_copy(
                    self.sources[at].at[span(row + start, length), own],
                    self.acc[i].at[span(start, length)],
                    self.load_sem.at[i],
                )
                self.loads[i].start()

    def arrived(self, i, t):
        if (i, t) in self.live:
            self.live[i, t].wait_recv()

    def task(self, i, t):
        at, row, height, col, width = self.chunks[i]
        bits, kinds, regions, stages = self.bits, self.kinds[i], self.regions[i], self.stages[i]
        half = self.shapes[at][1] // 2
        own = pl.ds(pl.multiple_of(self.core * half + col, 128), width)
        rows = pl.ds(row, height)
        if t == 0:
            away = pl.ds(pl.multiple_of((1 - self.core) * half + col, 128), width)
            self.send(i, 0, self.sources[at].at[rows, away], self.recv0[i], self.sibling)
            if self.acc[i] is None:
                self.acc[i] = self.sources[at].at[rows, own]
                return
            copy = pltpu.make_async_copy(self.sources[at].at[rows, own], self.acc[i], self.load_sem.at[i])
            copy.start()
            self.loads[i] = copy
            return
        self.arrived(i, t - 1)
        if t <= bits + 1:
            if t == self.begin[i]:
                if t <= bits:
                    self.loads[i].wait()
            elif t == 1:
                if i in self.loads:
                    self.loads[i].wait()
                self.add(self.acc[i], 0, self.recv0[i], 0, height)
            else:
                s = t - 2
                start, length = regions[s + 1]
                if not kinds[s]:
                    self.live[i, t - 1].wait_send()
                self.add(self.acc[i], start, self.recvs[i], self.slots[i][s], length)
        if t == self.leave[i]:
            start, length = regions[t - 1]
            copy = pltpu.make_async_copy(
                self.acc[i].at[span(start, length)], self.outs[at].at[span(row + start, length), own], self.store_sem.at[i]
            )
            copy.start()
            self.stores[i] = copy
            return
        if t <= bits:
            s = t - 1
            start, length = regions[s]
            give, first = length, start
            if kinds[s]:
                give = length // 2
                first = start + (1 - stages[s][0]) * give
            self.send(
                i, t, self.acc[i].at[span(first, give)], self.recvs[i].at[pl.ds(self.slots[i][s], give)],
                (stages[s][1], self.core),
            )
            return
        if t == bits + 1:
            start, length = regions[bits]
            if t == self.begin[i]:
                mine = self.sources[at].at[span(row + start, length), own]
            else:
                mine = self.acc[i].at[span(start, length)]
            copy = pltpu.make_async_copy(mine, self.outs[at].at[span(row + start, length), own], self.store_sem.at[i])
            copy.start()
            self.stores[i] = copy
        if t == bits + 2:
            self.stores[i].wait()
        if t <= 2 * bits:
            s = bits - 1 - (t - bits - 1)
            start, length = regions[s + 1]
            if kinds[s]:
                place = self.outs[at].at[span(row + start, length), own]
                self.send(i, t, mine if t == bits + 1 else place, place, (stages[s][1], self.core))
            return
        if t == 2 * bits + 1:
            place = self.outs[at].at[rows, own]
            self.send(i, t, place, place, self.sibling)

    def run(self, order):
        while self.at < len(order):
            token = order[self.at]
            self.at += 1
            if token is None:
                return
            i, t = token
            if t == self.total:
                self.arrived(i, t - 1)
            else:
                self.task(i, t)

    def finish(self):
        for (i, t), copy in self.live.items():
            if not (1 <= t <= self.bits and not self.kinds[i][t - 1]):
                copy.wait_send()


def share_scratch(chunks, bits, begin, inside=False):
    acc, recv0, recvs = [], [], []
    for i, (at, row, height, col, width) in enumerate(chunks):
        if begin[i] > bits:
            continue
        acc.append(pltpu.VMEM((height, width), BF16))
        if begin[i] == 0:
            recv0.append(pltpu.VMEM((height, width), BF16))
        length, used = height, 0
        for s in range(bits):
            if length % 32 == 0:
                length //= 2
            used += length
        recvs.append(pltpu.VMEM((used, width), BF16))
    n = len(chunks)
    sems = [pltpu.SemaphoreType.DMA((n, 2 * bits + 2))] * 2 + [pltpu.SemaphoreType.DMA((n,))] * 2
    return ([] if inside else acc) + recv0 + recvs + sems


def share_hold(refs, bits, begin, inside=False):
    n = len(begin)
    acc, recv0, recvs = [None] * n, [None] * n, [None] * n
    for held, most in ((acc, -1 if inside else bits), (recv0, 0), (recvs, bits)):
        for i in range(n):
            if begin[i] <= most:
                held[i], refs = refs[0], refs[1:]
    return acc, recv0, recvs, refs


def share_leave(bits):
    return [bits + 1] * 3 + [min(3, bits + 1)] * 3


def share_orders(bits, path):
    rest = list(range(2, bits))
    if bits < 2:
        return rest or list(range(bits)), rest or list(range(bits))
    if path == 0:
        return [0, 1] + rest, [1, 0] + rest
    if path == 1:
        return [0] + rest + [1], [1] + rest + [0]
    return rest + [0, 1], rest + [1, 0]


SHARE_CUTS = ((1, 2), (1, 1), (3, 1), (1, 1), (1, 1), (1, 1), (1, 1))
SHARE_FIRST = 6
SHARE_PATHS = (0, 1, 1, 0, 1, 0, 0, 0, 0, 1)
SHARE_LATE = (
    5, 51, 67, 96, 37, 21, -1, 97, -1, 6, -1, 52, 68, 98, 83, -1, -1, 7, 69, 38, -1, 99, -1, 112,
    53, -1, 8, 113, 100, -1, 54, 84, -1, 114, 101, -1, -1, 55, 70, 85, -1, 9, 102, -1, 128, -1, 10, 56,
    -1, 103, 115, 129, 39, 71, -1, -1, 116, -1, -1, 144, 104, 117, 145, 57, 118, 130, 86, 72, 58, 22, 146, 119,
    105, 40, 131, 87, 106, 120, 147, 23, 132, 133, 148, 121, 73, 88, 149, 122, 134, 24, 41, 74, 150, 135, 42, 151,
    89, 152, 136, 90, 25, 153, 26, 137, 154, 138,
)
SHARE_EARLY = (
    32, -1, 0, 33, 16, -1, 1, 17, -1, -1, -1, 34, -1, -1, 48, -1, 64, -1, -1, 80, 2, 18, 65, 35,
    49, -1, -1, 81, 3, -1, 19, -1, -1, 4, 66, 50, 36, -1, 82, -1, 20, 5, 51, 37, 83, 67, 21,
)


def share_late_order(pieces, bits, parts, ready):
    if bits == 4:
        return [None if v < 0 else (v // 16, v % 16) for v in SHARE_LATE]
    order, total = [], 2 * bits + 2
    begin = share_leave(bits) + [0] * (pieces - SHARE_FIRST)
    for k in range(parts + total + 1):
        for i in range(pieces):
            t = k - ready[i] + begin[i]
            if k >= ready[i] and t <= total:
                order.append((i, t))
        if k < parts:
            order.append(None)
    return order


def share_early_order(bits):
    if bits == 4:
        return [None if v < 0 else (v // 16, v % 16) for v in SHARE_EARLY]
    order = [None] * 10
    for t in range(bits + 2):
        order += [(i, t) for i in range(SHARE_FIRST) if t <= share_leave(bits)[i]] + [None]
    return order


def meet_sums(links, e, width, tables, between=None):
    links.wait_near(e)
    links.far[e][links.outer] = fold_sums(links.near[e], links.wide)
    links.send_far(e)
    if between is not None:
        between()
    links.wait_far(e)
    sums = fold_sums(links.far[e], links.outers)
    for t, (table, row) in enumerate(tables):
        unpack(table, row, sums[8 * t : 8 * t + 8], width)


def share_of(wv, tally, crop, times):
    return wv[0, crop] * (times / tally[0:1, 0:1]) + wv[1, crop] * (times / tally[1:2, 0:1])


class Puts:
    def __init__(self, sem):
        self.sem, self.copies = sem, []

    def put(self, src, dst):
        copy = pltpu.make_async_copy(src, dst, self.sem.at[len(self.copies)])
        copy.start()
        self.copies.append(copy)

    def finish(self):
        for copy in self.copies:
            copy.wait()


def start_loads(pairs, sem):
    copies = [pltpu.make_async_copy(src, dst, sem.at[i]) for i, (src, dst) in enumerate(pairs)]
    for copy in copies:
        copy.start()
    return copies


def back_two_kernel(sets, total, outs, crops, dims, shapes, chunks, *refs):
    c3, cin, c4, cout = dims
    vb, vs, norms1, norms2, st3, st4, st5, tally = refs[:8]
    sources, refs = refs[8:23], refs[23:]
    (o_up, o_g6, o_g7, o_g5, o_g4, o_s5, o_s4, o_s3), refs = refs[:8], refs[8:]
    held, refs = refs[:14], refs[14:]
    (d6, w6, z5, h5, d7, xe, w7, w5, x5, z4, w4, h2, w3, img) = held
    (q5, t7, dh, d4, zt, bg, up, s5, s4, s3, cs, cm, wv, wcol), refs = refs[:14], refs[14:]
    d5, pv, blk = d6, q5, img
    g6, g7, g5, g4 = w6, w7, w5, w4
    blocks, refs = take(refs, 3)
    near, refs = take(refs, 3)
    far, refs = take(refs, 3)
    links = Links(crops, near, far, *refs[:4])
    load_sem, out_sem, up_sem = refs[4:7]
    refs = refs[7:]
    bits = crops.bit_length() - 1
    early = SHARE_FIRST
    acc, recv0, recvs, refs = share_hold(refs, bits, [0] * early, True)
    share = Share(
        shapes, chunks[:early], [share_orders(bits, v) for v in SHARE_PATHS[:early]], bits, links, [g7, g6, g5], [o_g7, o_g6, o_g5],
        acc, recv0, recvs, refs, [0] * early, share_leave(bits),
    )
    order = share_early_order(bits)

    def tick():
        share.run(order)

    f = F32
    loads = start_loads(list(zip(sources, held)), load_sem)
    links.greet()
    view_tables(sets, links.r, (vb, vs), wv, wcol)
    puts = Puts(out_sem)
    for ref in (cs, cm):
        ref[...] = jnp.zeros(ref.shape, f)
    for block in blocks:
        block[...] = jnp.zeros(block.shape, f)

    for i in range(3):
        loads[i].wait()
    q5[...] = mm_nt(d6[...], w6[...])
    g5at = c4
    for m in sets:

        def crop_(c, m=m):
            crop = m.crop0 + c
            rows = span(m.out0 + c * m.out, m.out, 8)
            inv = by_view(wv, crop, st5[2:4, :])
            n = (z5[rows, :] - by_view(wv, crop, st5[0:2, :])) * inv
            q = act_slope(n * norms2[0:1, g5at : 2 * c4] + norms2[1:2, g5at : 2 * c4]) * q5[rows, :]
            q5[rows, :] = q
            cs[pl.ds(crop, 1), 0:c4] = jnp.sum(tile_sum(q), axis=0, keepdims=True)
            cm[pl.ds(crop, 1), 0:c4] = jnp.sum(tile_sum(q * n), axis=0, keepdims=True)

        repeat(m.count, crop_)
    local_sums(blocks[0], (cs, cm), wcol, c4)
    links.send_near(0, blocks[0])

    loads[3].wait()

    def outer(n):
        cols = pl.ds(pl.multiple_of(n * 512, 512), 512)
        g6[:, cols] = mm_tn(h5[...], d6[:, cols]).astype(BF16)

    repeat(cout // 512, outer)
    tick()

    def rest():
        for i in (4, 5, 6):
            loads[i].wait()

        def shortcut(n):
            part = pl.ds(pl.multiple_of(n * 256, 256), 256)
            t7[:, part] = mm_nt(d7[...], w7[part, :])

        repeat(cin // 256, shortcut)

        def skip(n):
            cols = pl.ds(pl.multiple_of(n * 512, 512), 512)
            g7[:, cols] = mm_tn(xe[...], d7[:, cols]).astype(BF16)

        repeat(cout // 512, skip)
        tick()

    meet_sums(links, 0, c4, ((s5, 0), (s5, 2)), rest)

    for m in sets:

        def pair(p, m=m):
            o = m.out0 + p * 2 * m.out
            mask = keep(c4, 8, m.half)
            slots = [[], [], [], []]
            for j in range(2):
                crop = m.crop0 + 2 * p + j
                rows = span(o + j * m.out, m.out, 8)
                over = share_of(wv, tally, crop, 4.0)
                inv = by_view(wv, crop, st5[2:4, :])
                n = (z5[rows, :] - by_view(wv, crop, st5[0:2, :])) * inv
                d = (inv * norms2[0:1, g5at : 2 * c4]) * (
                    q5[rows, :] - by_view(wv, crop, s5[0:2, :]) * over - n * (by_view(wv, crop, s5[2:4, :]) * over)
                )
                d = masked(d, mask)
                down = jnp.concatenate([d[8:], jnp.zeros((8, c4), f)], axis=0)
                slots[0].append(d)
                slots[1].append(pltpu.roll(d, m.out - 1, 0))
                slots[2].append(down)
                slots[3].append(pltpu.roll(down, m.out - 1, 0))
            for t in range(4):
                d5[span(o, 2 * m.out), t * c4 : (t + 1) * c4] = jnp.concatenate(slots[t], axis=0).astype(BF16)

        repeat(m.count // 2, pair)

    tick()
    loads[7].wait()
    options = (((1, 0),), ((2, 0), (0, 1)))
    for a in range(2):
        for b in range(2):
            value = None
            for r, down in options[a]:
                for c, side in options[b]:
                    slot, tap = (2 * down + side) * c4, (3 * r + c) * c4
                    term = mm_nt(d5[:, slot : slot + c4], w5[tap : tap + c4, :])
                    value = term if value is None else value + term
            pv[...] = value
            for m in sets:

                def crop_(c, m=m, a=a, b=b):
                    for i in range(m.half):
                        for q in range(c4 // 128):
                            dh[q, pl.ds(m.row0 + c * m.rows + (2 * i + a) * 16 + b, 8, stride=2), :] = pv[
                                span(m.out0 + c * m.out + i * 8, 8, 8), q * 128 : (q + 1) * 128
                            ]

                repeat(m.count, crop_)
        tick()
    loads[9].wait()
    for m in sets:

        def crop_(c, m=m):
            crop = m.crop0 + c
            rows = span(m.row0 + c * m.rows, m.rows)
            mask = keep(128, 16, m.edge)
            levels, tilts = [], []
            for q in range(c4 // 128):
                cols = slice(q * 128, (q + 1) * 128)
                inv = by_view(wv, crop, st4[2:4, cols])
                n = (z4[rows, cols] - by_view(wv, crop, st4[0:2, cols])) * inv
                up_ = masked(act_slope(n * norms2[0:1, cols] + norms2[1:2, cols]) * dh[q, rows, :], mask)
                dh[q, rows, :] = up_
                levels.append(jnp.sum(tile_sum(up_), axis=0, keepdims=True))
                tilts.append(jnp.sum(tile_sum(up_ * n), axis=0, keepdims=True))
            cs[pl.ds(crop, 1), 0:c4] = jnp.concatenate(levels, axis=1)
            cm[pl.ds(crop, 1), 0:c4] = jnp.concatenate(tilts, axis=1)

        repeat(m.count, crop_)
        tick()
    local_sums(blocks[1], (cs, cm), wcol, c4)
    links.send_near(1, blocks[1])
    loads[8].wait()

    def kernel(n):
        for t in range(3 * n, 3 * n + 3):
            part = slice(t * c4, (t + 1) * c4)
            g5[part, :] = mm_tn(x5[:, part], d5[:, 0:c4]).astype(BF16)
        tick()

    kernel(0)

    def rest():
        kernel(1)
        kernel(2)

    meet_sums(links, 1, c4, ((s4, 0), (s4, 2)), rest)
    tick()

    for i in range(10, 14):
        loads[i].wait()
    big_rows = 2 * sets[0].rows
    for at, m in enumerate(sets):

        def pair(p, m=m, at=at):
            r = m.row0 + p * 2 * m.rows
            o = m.out0 + p * 2 * m.out
            mask = keep(128, 16, m.edge)
            for j in range(2):
                crop = m.crop0 + 2 * p + j
                rows = span(r + j * m.rows, m.rows)
                over = share_of(wv, tally, crop, 1.0)
                for q in range(c4 // 128):
                    cols = slice(q * 128, (q + 1) * 128)
                    inv = by_view(wv, crop, st4[2:4, cols])
                    n = (z4[rows, cols] - by_view(wv, crop, st4[0:2, cols])) * inv
                    d = (inv * norms2[0:1, cols]) * (
                        dh[q, rows, :] - by_view(wv, crop, s4[0:2, cols]) * over - n * (by_view(wv, crop, s4[2:4, cols]) * over)
                    )
                    d4[rows, cols] = masked(d, mask).astype(BF16)
            got = mm_nt(d4[span(r, 2 * m.rows), :], w4[...])
            for q in range(cin // 128):
                bg[q, 0 : 2 * m.rows, :] = got[:, q * 128 : (q + 1) * 128]
            for q in range(cin // 128):
                for j in range(2):
                    for i in range(m.half):
                        here = pl.ds(j * m.rows + i * 32, 8, stride=2)
                        bg[q, here, :] = bg[q, here, :] + t7[span(o + j * m.out + i * 8, 8, 8), q * 128 : (q + 1) * 128]
            turn = m.crop0 // 2 + p
            slot = turn % 2

            def left(turn, slot):
                return pltpu.make_async_copy(
                    up.at[slot, 0 : 2 * m.rows], o_up.at[span(r, 2 * m.rows)], up_sem.at[turn]
                )

            if turn >= 2:
                size = big_rows if turn - 2 < sets[0].count // 2 else 2 * m.rows
                pltpu.make_async_copy(up.at[slot, 0:size], o_up.at[pl.ds(0, size)], up_sem.at[turn - 2]).wait()
            step = m.rows // 2
            mask = keep(128, 16, m.edge)
            totals = [[[], []], [[], []]]
            for h, j in [(h, j) for h in range(cin // 512) for j in range(2)]:
                if j == 0:
                    zt[0 : 2 * m.rows, :] = mm(h2[span(r, 2 * m.rows), :], w3[:, h * 512 : (h + 1) * 512])
                crop = m.crop0 + 2 * p + j
                levels, tilts = totals[j]
                for q in range(h * 4, h * 4 + 4):
                    cols = slice(q * 128, (q + 1) * 128)
                    part = slice((q - h * 4) * 128, (q - h * 4 + 1) * 128)
                    at3 = slice(2 * c3 + q * 128, 2 * c3 + (q + 1) * 128)
                    mean, inv = by_view(wv, crop, st3[0:2, cols]), by_view(wv, crop, st3[2:4, cols])
                    gain, bias = norms1[0:1, at3], norms1[1:2, at3]

                    def tile(i, sums, j=j, cols=cols, part=part, q=q, mean=mean, inv=inv, gain=gain, bias=bias):
                        here = span(j * m.rows + i * step, step)
                        rows = span(r + j * m.rows + i * step, step)
                        n = (zt[here, part] - mean) * inv
                        u = n * gain + bias + img[rows, cols].astype(f)
                        got = bg[q, here, :].astype(BF16).astype(f)
                        v = masked(act_slope(u) * got, mask)
                        up[slot, here, cols] = v
                        return (sums[0] + tile_sum(v), sums[1] + tile_sum(v * n))

                    zero = jnp.zeros((8, 128), f)
                    s, t = lax.fori_loop(0, 2, tile, (zero, zero))
                    levels.append(jnp.sum(s, axis=0, keepdims=True))
                    tilts.append(jnp.sum(t, axis=0, keepdims=True))
            for j in range(2):
                crop = m.crop0 + 2 * p + j
                cs[pl.ds(crop, 1), :] = jnp.concatenate(totals[j][0], axis=1)
                cm[pl.ds(crop, 1), :] = jnp.concatenate(totals[j][1], axis=1)
            left(turn, slot).start()

        for p in range(m.count // 2):
            pair(p)
            tick()
    late = pltpu.make_async_copy(sources[14], blk, load_sem.at[14])
    late.start()
    local_sums(blocks[2], (cs, cm), wcol, cin)
    links.send_near(2, blocks[2])
    late.wait()

    def inner(n):
        part = pl.ds(pl.multiple_of(n * 256, 256), 256)
        g4[part, :] = mm_tn(blk[:, part], d4[...]).astype(BF16)

    repeat(2, inner)
    tick()

    def rest():
        repeat(cin // 256 - 2, lambda n: inner(n + 2))
        puts.put(g4, o_g4)
        tick()

    meet_sums(links, 2, cin, ((s3, 0), (s3, 2)), rest)
    for src, dst in ((s5, o_s5), (s4, o_s4), (s3, o_s3)):
        puts.put(src, dst)
    for back in (2, 1):
        size = 2 * sets[1].rows
        turn = (sets[0].count + sets[1].count) // 2 - back
        pltpu.make_async_copy(
            up.at[turn % 2, 0:size], o_up.at[pl.ds(sets[1].row0, size)], up_sem.at[turn]
        ).wait()
    while share.at < len(order):
        tick()
    for copy in share.stores.values():
        copy.wait()
    share.finish()
    links.finish()
    puts.finish()


def back_one_kernel(sets, total, guarded, crops, dims, shapes, chunks, *refs):
    c3, cin = dims
    vb, vs, norms1, st1, st2, st3, s3, tally = refs[:8]
    sources, refs = refs[8:17], refs[17:]
    second, refs = list(refs[:4]), refs[4:]
    (o_gb, o_gs, o_s2, o_s1), refs = refs[:4], refs[4:]
    o_grads, refs = refs[:7], refs[7:]
    held, refs = refs[:9], refs[9:]
    (h2, w3, up, z2, h1, wsp1, z1, w1, img) = held
    (zt, d3, q2, d2, q1, d1, g3, g2, g1, s2, s1, cs, cm, wv, wcol), refs = refs[:15], refs[15:]
    blocks, refs = take(refs, 2)
    near, refs = take(refs, 2)
    far, refs = take(refs, 2)
    links = Links(crops, near, far, *refs[:4])
    load_sem, out_sem, own_sem, grad_send, grad_recv, up_sem = refs[4:10]
    refs = refs[10:]
    n = len(chunks)
    bits = crops.bit_length() - 1
    begin = share_leave(bits) + [0] * (n - SHARE_FIRST)
    acc, recv0, recvs, refs = share_hold(refs, bits, begin)
    share = Share(
        shapes, chunks, [share_orders(bits, v) for v in SHARE_PATHS], bits, links, second + [g3, g2, g1], o_grads,
        acc, recv0, recvs, refs, begin, [2 * bits + 3] * n,
    )
    share.fetch()
    order = share_late_order(n, bits, 20, (0,) * 7 + (7, 14, 20))

    def tick():
        share.run(order)

    core = links.r
    sibling = (links.k, 1 - core)
    f = F32
    loads = start_loads([(a, b) for a, b in zip(sources, held) if b is not up], load_sem)
    ups = []
    for m in sets:
        for p in range(m.count // 2):
            rows = pl.ds(m.row0 + p * 2 * m.rows, 2 * m.rows)
            ups.append(pltpu.make_async_copy(sources[2].at[rows], up.at[rows], up_sem.at[len(ups)]))
    for copy in ups:
        copy.start()
    links.greet()
    tick()
    view_tables(sets, links.r, (vb, vs), wv, wcol)
    puts = Puts(out_sem)
    for ref in (cs, cm):
        ref[...] = jnp.zeros(ref.shape, f)
    for block in blocks:
        block[...] = jnp.zeros(block.shape, f)
    d2[0:16, :] = jnp.zeros((16, 3 * c3), BF16)
    for m in sets:
        for c in range(m.count):
            at = m.guard0 + c * m.guard + m.rows
            d2[at : at + 16, :] = jnp.zeros((16, 3 * c3), BF16)

    for i in range(3):
        loads[i].wait()
    for copy in ups:
        copy.wait()
    for m in sets:

        def pair(p, m=m):
            r = m.row0 + p * 2 * m.rows
            step = m.rows // 2
            mask = keep(128, 16, m.edge)
            for h, j in [(h, j) for h in range(cin // 512) for j in range(2)]:
                if j == 0:
                    zt[0 : 2 * m.rows, :] = mm(h2[span(r, 2 * m.rows), :], w3[:, h * 512 : (h + 1) * 512])
                crop = m.crop0 + 2 * p + j
                over = share_of(wv, tally, crop, 1.0)
                for q in range(h * 4, h * 4 + 4):
                    cols = slice(q * 128, (q + 1) * 128)
                    part = slice((q - h * 4) * 128, (q - h * 4 + 1) * 128)
                    mean, inv = by_view(wv, crop, st3[0:2, cols]), by_view(wv, crop, st3[2:4, cols])
                    gain = inv * norms1[0:1, 2 * c3 + q * 128 : 2 * c3 + (q + 1) * 128]
                    level = by_view(wv, crop, s3[0:2, cols]) * over
                    tilt = by_view(wv, crop, s3[2:4, cols]) * over * inv

                    def tile(i, j=j, cols=cols, part=part, mean=mean, gain=gain, level=level, tilt=tilt):
                        here = span(j * m.rows + i * step, step)
                        rows = span(r + j * m.rows + i * step, step)
                        d = gain * (up[rows, cols] - level - (zt[here, part] - mean) * tilt)
                        d3[rows, cols] = masked(d, mask).astype(BF16)

                    repeat(2, tile)
            q2[span(r, 2 * m.rows), :] = mm_nt(d3[span(r, 2 * m.rows), :], w3[...])
            for j in range(2):
                crop = m.crop0 + 2 * p + j
                mean, inv = by_view(wv, crop, st2[0:2, :]), by_view(wv, crop, st2[2:4, :])

                def tile(i, sums, j=j, mean=mean, inv=inv):
                    rows = span(r + j * m.rows + i * step, step)
                    n = (z2[rows, :] - mean) * inv
                    v = act_slope(n * norms1[0:1, c3 : 2 * c3] + norms1[1:2, c3 : 2 * c3]) * q2[rows, :]
                    q2[rows, :] = v
                    return (sums[0] + tile_sum(v), sums[1] + tile_sum(v * n))

                zero = jnp.zeros((8, c3), f)
                s, t = lax.fori_loop(0, 2, tile, (zero, zero))
                cs[pl.ds(crop, 1), 0:c3] = jnp.sum(s, axis=0, keepdims=True)
                cm[pl.ds(crop, 1), 0:c3] = jnp.sum(t, axis=0, keepdims=True)

        for p in range(m.count // 2):
            pair(p)
            tick()
    local_sums(blocks[0], (cs, cm), wcol, c3)
    links.send_near(0, blocks[0])

    def outer(n):
        cols = pl.ds(pl.multiple_of(n * 256, 256), 256)
        g3[:, cols] = mm_tn(h2[...], d3[:, cols]).astype(BF16)

    repeat(cin // 512, outer)
    tick()

    def rest():
        repeat(cin // 512, lambda n: outer(n + cin // 512))
        tick()

    meet_sums(links, 0, c3, ((s2, 0), (s2, 2)), rest)

    for i in range(3, 6):
        loads[i].wait()
    for m in sets:

        def pair(p, m=m):
            r = m.row0 + p * 2 * m.rows
            g = m.guard0 + p * 2 * m.guard
            step = m.rows // 2
            mask = keep(c3, 16, m.edge)
            for j in range(2):
                crop = m.crop0 + 2 * p + j
                over = share_of(wv, tally, crop, 1.0)
                mean, inv = by_view(wv, crop, st2[0:2, :]), by_view(wv, crop, st2[2:4, :])
                gain = inv * norms1[0:1, c3 : 2 * c3]
                level = by_view(wv, crop, s2[0:2, :]) * over
                tilt = by_view(wv, crop, s2[2:4, :]) * over * inv

                def tile(i, j=j, mean=mean, gain=gain, level=level, tilt=tilt):
                    rows = span(r + j * m.rows + i * step, step)
                    d = gain * (q2[rows, :] - level - (z2[rows, :] - mean) * tilt)
                    d = masked(d, mask)
                    to = span(g + j * m.guard + i * step, step)
                    d2[to, 0:c3] = pltpu.roll(d, step - 1, 0).astype(BF16)
                    d2[to, c3 : 2 * c3] = d.astype(BF16)
                    d2[to, 2 * c3 : 3 * c3] = pltpu.roll(d, 1, 0).astype(BF16)

                repeat(2, tile)
            size = 2 * m.rows + 16
            value = None
            for a in range(3):
                for b in range(3):
                    part = d2[span(g - (a - 1) * 16, size), b * c3 : (b + 1) * c3]
                    term = mm_nt(part, wsp1[a, b * c3 : (b + 1) * c3, :])
                    value = term if value is None else value + term
            q1[span(r, m.rows), :] = value[0 : m.rows]
            q1[span(r + m.rows, m.rows), :] = value[m.guard : m.guard + m.rows]
            for j in range(2):
                crop = m.crop0 + 2 * p + j
                mean, inv = by_view(wv, crop, st1[0:2, :]), by_view(wv, crop, st1[2:4, :])

                def tile(i, sums, j=j, mean=mean, inv=inv):
                    rows = span(r + j * m.rows + i * step, step)
                    n = (z1[rows, :] - mean) * inv
                    v = act_slope(n * norms1[0:1, 0:c3] + norms1[1:2, 0:c3]) * q1[rows, :]
                    v = masked(v, mask)
                    q1[rows, :] = v
                    return (sums[0] + tile_sum(v), sums[1] + tile_sum(v * n))

                zero = jnp.zeros((8, c3), f)
                s, t = lax.fori_loop(0, 2, tile, (zero, zero))
                cs[pl.ds(crop, 1), 0:c3] = jnp.sum(s, axis=0, keepdims=True)
                cm[pl.ds(crop, 1), 0:c3] = jnp.sum(t, axis=0, keepdims=True)

        for p in range(m.count // 2):
            pair(p)
            tick()
    local_sums(blocks[1], (cs, cm), wcol, c3)
    links.send_near(1, blocks[1])
    inside = guarded - 32

    def taps(a):
        g2[a * 3 * c3 : (a + 1) * 3 * c3, :] = mm_tn(
            h1[a * 16 : a * 16 + inside, :], d2[16 : 16 + inside, c3 : 2 * c3]
        ).astype(BF16)

    taps(0)
    tick()

    def rest():
        taps(1)
        taps(2)
        tick()

    meet_sums(links, 1, c3, ((s1, 0), (s1, 2)), rest)

    loads[6].wait()
    moves = []
    for m, out in zip(sets, (o_gb, o_gs)):
        part = m.rows // 2
        for c in range(m.count):
            i = m.crop0 + c
            own_rows = span(m.row0 + c * m.rows + core * part, part)
            other_rows = span(m.row0 + c * m.rows + (1 - core) * part, part)
            place = out.at[span((core * m.count + c) * part, part)]
            moves.append(
                (
                    pltpu.make_async_copy(d3.at[own_rows], place, own_sem.at[i]),
                    pltpu.make_async_remote_copy(
                        src_ref=d3.at[other_rows],
                        dst_ref=place,
                        send_sem=grad_send.at[i],
                        recv_sem=grad_recv.at[i],
                        device_id=sibling,
                        device_id_type=MESH,
                    ),
                )
            )
    for m in sets:

        def pair(p, m=m):
            r = m.row0 + p * 2 * m.rows
            step = m.rows // 2
            mask = keep(c3, 16, m.edge)
            for j in range(2):
                crop = m.crop0 + 2 * p + j
                over = share_of(wv, tally, crop, 1.0)
                mean, inv = by_view(wv, crop, st1[0:2, :]), by_view(wv, crop, st1[2:4, :])
                gain = inv * norms1[0:1, 0:c3]
                level = by_view(wv, crop, s1[0:2, :]) * over
                tilt = by_view(wv, crop, s1[2:4, :]) * over * inv

                def tile(i, j=j, mean=mean, gain=gain, level=level, tilt=tilt):
                    rows = span(r + j * m.rows + i * step, step)
                    d = gain * (q1[rows, :] - level - (z1[rows, :] - mean) * tilt)
                    d1[rows, :] = masked(d, mask).astype(BF16)

                repeat(2, tile)
            rows = span(r, 2 * m.rows)
            for n in range(cin // 256):
                cols = slice(n * 256, (n + 1) * 256)
                d3[rows, cols] = (up[rows, cols] + mm_nt(d1[rows, :], w1[cols, :])).astype(BF16)

        for p in range(m.count // 2):
            pair(p)
            for c in (2 * p, 2 * p + 1):
                for copy in moves[m.crop0 + c]:
                    copy.start()
            tick()
    loads[7].wait()

    def inner(n):
        part = pl.ds(pl.multiple_of(n * 256, 256), 256)
        g1[part, :] = mm_tn(img[:, part], d1[...]).astype(BF16)

    repeat(cin // 256, inner)
    for src, dst in ((s2, o_s2), (s1, o_s1)):
        puts.put(src, dst)
    while share.at < len(order):
        tick()
    share.finish()
    links.finish()
    for near_copy, far_copy in moves:
        near_copy.wait()
        far_copy.wait()
    puts.finish()


def backward(sets, got, views, w, norms_first, norms_second, total, guarded, outs, idents):
    crops = lax.axis_size("crops")
    w1, wsp1, w3, w4, w5, w6, w7 = w
    cin, c3 = w1.shape
    c4, cout = w6.shape
    (
        f_img, f_z1, f_h1, f_z2, f_h2, f_blk, f_z4, f_x5, f_z5, f_h5, f_xe, f_res, f_d6, f_d7,
        f_st1, f_st2, f_st3, f_st4, f_st7, f_st5, f_st6, f_sq, f_n,
    ) = got
    smem, vmem = pl.BlockSpec(memory_space=pltpu.SMEM), pl.BlockSpec(memory_space=pltpu.VMEM)
    hbm = pl.BlockSpec(memory_space=pl.ANY)
    shape = jax.ShapeDtypeStruct
    most = 2 * sets[0].rows
    pairs = sum(m.count for m in sets) // 2
    count = 2 * pairs

    def like(arrays):
        return [pltpu.VMEM(t.shape, t.dtype) for t in arrays]

    def params(ident):
        return pltpu.CompilerParams(
            collective_id=ident, has_side_effects=True, vmem_limit_bytes=63 * 1024 * 1024
        )

    arrays = [f_d6, w6, f_z5, f_h5, f_d7, f_xe, w7, w5, f_x5, f_z4, w4, f_h2, w3, f_img, f_blk]
    out_shape = [
        shape((total, cin), F32), shape((c4, cout), BF16), shape((cin, cout), BF16), shape((9 * c4, c4), BF16),
        shape((cin, c4), BF16), shape((8, c4), F32), shape((8, c4), F32), shape((8, cin), F32),
    ]
    scratch = like(arrays[:14]) + [
        pltpu.VMEM((outs, c4), F32), pltpu.VMEM((outs, cin), F32), pltpu.VMEM((c4 // 128, total, 128), F32), pltpu.VMEM((total, c4), BF16),
        pltpu.VMEM((most, 512), F32), pltpu.VMEM((cin // 128, most, 128), F32), pltpu.VMEM((2, most, cin), F32),
        pltpu.VMEM((8, c4), F32), pltpu.VMEM((8, c4), F32), pltpu.VMEM((8, cin), F32),
        pltpu.VMEM((16, cin), F32), pltpu.VMEM((16, cin), F32),
        pltpu.SMEM((2, 16), F32), pltpu.VMEM((16, 128), F32),
    ]
    scratch += exchange_shapes((c4, c4, cin), (2, 2, 2), crops)
    scratch += [pltpu.SemaphoreType.DMA((15,)), pltpu.SemaphoreType.DMA((7,)), pltpu.SemaphoreType.DMA((pairs,))]
    shapes = [(cin, cout), (c4, cout), (9 * c4, c4), (cin, c4), (c3, cin), (9 * c3, c3), (cin, c3)]
    chunks = share_plan(shapes, SHARE_CUTS)
    bits = crops.bit_length() - 1
    scratch += share_scratch(chunks[:SHARE_FIRST], bits, [0] * SHARE_FIRST, True)
    up, g_outer2, g_skip, g_spatial2, g_inner2, s5, s4, s3 = pl.pallas_call(
        functools.partial(back_two_kernel, sets, total, outs, crops, (c3, cin, c4, cout), shapes, chunks),
        out_shape=out_shape,
        in_specs=[smem] * 2 + [vmem] * 6 + [hbm] * 15,
        out_specs=[hbm] * len(out_shape),
        scratch_shapes=scratch,
        compiler_params=params(idents[0]),
        name="back_two",
    )(*views, norms_first, norms_second, f_st3, f_st4, f_st5, f_n, *arrays)

    arrays = [f_h2, w3, up, f_z2, f_h1, wsp1, f_z1, w1, f_img]
    out_shape = [
        shape((total_rows(sets[0]), cin), BF16), shape((total_rows(sets[1]), cin), BF16), shape((8, c3), F32),
        shape((8, c3), F32),
    ] + [shape(t, BF16) for t in shapes]
    scratch = like(arrays) + [
        pltpu.VMEM((most, 512), F32), pltpu.VMEM((total, cin), BF16), pltpu.VMEM((total, c3), F32),
        pltpu.VMEM((guarded, 3 * c3), BF16), pltpu.VMEM((total, c3), F32), pltpu.VMEM((total, c3), BF16),
        pltpu.VMEM((c3, cin), BF16), pltpu.VMEM((9 * c3, c3), BF16), pltpu.VMEM((cin, c3), BF16),
        pltpu.VMEM((8, c3), F32), pltpu.VMEM((8, c3), F32), pltpu.VMEM((16, c3), F32), pltpu.VMEM((16, c3), F32),
        pltpu.SMEM((2, 16), F32), pltpu.VMEM((16, 128), F32),
    ]
    scratch += exchange_shapes((c3, c3), (2, 2), crops)
    scratch += [pltpu.SemaphoreType.DMA((9,)), pltpu.SemaphoreType.DMA((2,))]
    scratch += [pltpu.SemaphoreType.DMA((count,))] * 3 + [pltpu.SemaphoreType.DMA((pairs,))]
    scratch += share_scratch(chunks, bits, share_leave(bits) + [0] * (len(chunks) - SHARE_FIRST))
    grad_b, grad_s, s2, s1, *grads = pl.pallas_call(
        functools.partial(back_one_kernel, sets, total, guarded, crops, (c3, cin), shapes, chunks),
        out_shape=out_shape,
        in_specs=[smem] * 2 + [vmem] * 6 + [hbm] * 13,
        out_specs=[hbm] * len(out_shape),
        scratch_shapes=scratch,
        compiler_params=params(idents[1]),
        name="back_one",
    )(*views, norms_first, f_st1, f_st2, f_st3, s3, f_n, *arrays, g_skip, g_outer2, g_spatial2, g_inner2)
    return grad_b, grad_s, grads, (s1, s2, s3, s4, s5)


def widen_kernel(*refs):
    for src, dst in zip(refs[: len(refs) // 2], refs[len(refs) // 2 :]):
        dst[...] = src[...].astype(F32)


def widen(arrays, steps=8):
    def block(t):
        return pl.BlockSpec((t.shape[0] // steps, t.shape[1]), lambda i: (i, 0))

    return pl.pallas_call(
        widen_kernel,
        grid=(steps,),
        out_shape=[jax.ShapeDtypeStruct(t.shape, F32) for t in arrays],
        in_specs=[block(t) for t in arrays],
        out_specs=[block(t) for t in arrays],
        compiler_params=pltpu.CompilerParams(vmem_limit_bytes=48 * 1024 * 1024),
        name="widen",
    )(*arrays)


def total_rows(m):
    return m.count * m.rows


def shards(
    image_big,
    image_small,
    view_big,
    view_small,
    inner_first,
    spatial_first,
    outer_first,
    norms_first,
    inner_second,
    spatial_second,
    outer_second,
    skip_second,
    norms_second,
    cotangent_big,
    cotangent_small,
):
    c3, c4 = inner_first.shape[1], inner_second.shape[1]
    weights = [
        inner_first,
        spatial_first.reshape(3, 3 * c3, c3),
        outer_first,
        inner_second,
        spatial_second.reshape(9 * c4, c4),
        outer_second,
        skip_second,
    ]
    sets, sizes, got = forward(
        [image_big, image_small], [cotangent_big, cotangent_small], (view_big, view_small), weights, norms_first, norms_second, 0
    )
    grad_b, grad_s, grads, sums = backward(
        sets, got, (view_big, view_small), weights, norms_first, norms_second, *sizes, (1, 2)
    )
    s1, s2, s3, s4, s5 = sums
    sq = got[21]

    def both(parts):
        return jnp.concatenate(
            [jnp.stack([t[g] + t[g + 1], t[0] + t[1]]) for t, g in parts], axis=1
        )

    g_skip, g_outer2, g_spatial2, g_inner2, g_outer1, g_spatial1, g_inner1 = widen(grads)
    results = [
        got[11][m.out0 : m.out0 + m.count * m.out].reshape(m.count, m.half, 8, -1)[:, :, : m.half]
        for m in sets
    ]
    gradients = [
        t.reshape(image.shape[0], image.shape[1], 16, -1)[:, :, : image.shape[2]]
        for t, image in ((grad_b, image_big), (grad_s, image_small))
    ]
    return (
        results[0],
        results[1],
        gradients[0],
        gradients[1],
        g_inner1,
        g_spatial1.reshape(spatial_first.shape),
        g_outer1,
        both(((s1, 2), (s2, 2), (s3, 2))),
        g_inner2,
        g_spatial2.reshape(spatial_second.shape),
        g_outer2,
        g_skip,
        both(((s4, 2), (s5, 2), (sq, 2), (sq, 4))),
    )


def solution(mesh):
    maps = P("crops", "rows", None, None)
    whole = P(("crops", "rows"), None, None, None)
    in_specs = (maps, maps, P("crops"), P("crops")) + (P(),) * 9 + (whole, whole)
    out_specs = (whole, whole, maps, maps) + (P(),) * 9
    return jax.shard_map(shards, mesh=mesh, in_specs=in_specs, out_specs=out_specs, check_vma=False)
```
